32 devices in a mesh: region: 2 (over y), cell: 16 (over z, x, core).
Axes of the slice: x: 2, y: 2, z: 4, core: 2. Of those that a mesh axis runs over, the one named last changes fastest.
Arguments:
- position: float32 [3, 256, 128], P(None, ('region', 'cell')), may hold values from 0 to 1
- velocity: float32 [3, 256, 128], P(None, ('region', 'cell')), may hold values from -6 to 6
- smoothing: float32 [256, 128], P(('region', 'cell')), may hold values from 0.3 to 0.5
- particle_mass: float32 [256, 128], P(('region', 'cell')), may hold values from 0.004 to 0.012
- energy: float32 [256, 128], P(('region', 'cell')), may hold values from 0.5 to 2
- density_old: float32 [256, 128], P(('region', 'cell')), may hold values from 0.3 to 1.2
- cell_count: int32 [256], P(('region', 'cell')), may hold values from 8 to 128, as said below
- active: int32 [256, 128], P(('region', 'cell')), may hold values from 0 to 1, as said below
- time_bin: int32 [256, 128], P(('region', 'cell')), may hold values from 0 to 5
- pair_source: int32 [256, 27], P(('region', 'cell')), may hold values from 0 to 41, as said below
- pair_shift: int32 [256, 27], P(('region', 'cell')), may hold values from 0 to 26, as said below
- export: int32 [512, 2], P(('region', 'cell')), may hold values from 0 to 7
Outputs:
- density: float32 [256, 128], P(('region', 'cell'))
- acceleration: float32 [3, 256, 128], P(None, ('region', 'cell'))
- kicked_velocity: float32 [3, 256, 128], P(None, ('region', 'cell'))
The draws below stay inside these ranges and needn't reach their ends.
Inputs may be any that keep to these rules, and one draw needn't show every extreme that they name: `cell_count`: every device has a cell of exactly 128 particles. `active`: 0 in the slots past a cell's count. `pair_source`: pair 0 of a device's cell k names source k; a device's pairs name every one of its 42 sources. `pair_shift`: pair 0 has code 13; a cell's 27 codes are distinct.
All inputs are finite; a program needn't handle non-finite values.
Results may differ from the reference program's by a relative error of at most 0.0003.
Values sent between devices are 32-bit elements; how exact they have to be, the bound alone decides.
No kernel may reach another device: no remote copies, remote signals or barrier semaphores. Data moves between devices by JAX's collectives and lax.ppermute only.
A program may use at most 64 MiB of HBM per device.

```python
import math
import jax
import jax.numpy as jnp
from jax import lax

C_DEV = 8
CAP = 128
NB = 27
PROXY = 2
DEVS = 32
CELLS = 256
TABLE = 42
EXPORTS = 512
N_REGION = 2
N_CELL = 16


def count_table(key):
    device_total = CELLS // C_DEV
    key_low, key_raw, key_full = jax.random.split(key, 3)
    low_count = jax.random.randint(key_low, (device_total, 1), CAP // 16, CAP // 2 + 1)
    raw_draws = jax.random.randint(key_raw, (device_total, C_DEV), 0, 1 << 20)
    counts = low_count + raw_draws % (CAP + 1 - low_count)
    full_slot = jax.random.randint(key_full, (device_total, 1), 0, C_DEV)
    counts = jnp.where(jnp.arange(C_DEV)[None, :] == full_slot, CAP, counts)
    return counts.reshape(CELLS).astype(jnp.int32)


def draw_cell_count(key, part):
    return count_table(key)


def draw_active(key, part):
    counts = count_table(key)
    key = jax.random.fold_in(key, 2)
    device_total = CELLS // C_DEV
    key_share, key_roll = jax.random.split(key, 2)
    percent = jax.random.randint(key_share, (device_total, 1, 1), 3, 31)
    rolled = jax.random.randint(key_roll, (device_total, C_DEV, CAP), 0, 100)
    chosen = (rolled < percent).reshape(CELLS, CAP)
    live_slot = jnp.arange(CAP)[None, :] < counts[:, None]
    return (chosen & live_slot).astype(jnp.int32)


def draw_pair_source(key, part):
    key = jax.random.fold_in(key, 3)
    device_total = CELLS // C_DEV
    others = C_DEV * (NB - 1)
    key_perm, key_fill, key_mix = jax.random.split(key, 3)

    def covering(one_key):
        return jax.random.permutation(one_key, TABLE)
    covered = jax.vmap(covering)(jax.random.split(key_perm, device_total))
    filler = jax.random.randint(key_fill, (device_total, others - TABLE), 0, TABLE)
    listed = jnp.concatenate([covered, filler], axis=1)

    def mixing(one_key, one_row):
        return one_row[jax.random.permutation(one_key, others)]
    placed = jax.vmap(mixing)(jax.random.split(key_mix, device_total), listed)
    own_cells = jnp.broadcast_to(jnp.arange(C_DEV)[None, :, None], (device_total, C_DEV, 1))
    joined = jnp.concatenate([own_cells, placed.reshape(device_total, C_DEV, NB - 1)], axis=2)
    return joined.reshape(CELLS, NB).astype(jnp.int32)


def draw_pair_shift(key, part):
    key = jax.random.fold_in(key, 4)

    def ordering(one_key):
        return jax.random.permutation(one_key, 26)
    shift_codes = jax.vmap(ordering)(jax.random.split(key, CELLS))
    shift_codes = shift_codes + (shift_codes >= 13).astype(shift_codes.dtype)
    centre = jnp.full((CELLS, 1), 13, shift_codes.dtype)
    return jnp.concatenate([centre, shift_codes], axis=1).astype(jnp.int32)


def place_ends(values, own_key, smallest, largest):
    longest = values.shape.index(max(values.shape))
    spots = []
    for shift in (0, 1):
        where = [jax.random.randint(jax.random.fold_in(own_key, axis), (), 0, length) for axis, length in enumerate(values.shape)]
        where[longest] = (where[longest] + shift) % values.shape[longest]
        spots.append(tuple(where))
    return values.at[spots[0]].set(smallest).at[spots[1]].set(largest)


def block_scale(rng, shape, cuts, low, largest):
    level, own = 1.0, jax.random.fold_in(rng, 6)
    for axis_at, shards_of in cuts:
        draws = jnp.exp(jax.random.uniform(jax.random.fold_in(own, axis_at), (shards_of,), jnp.float32, low / len(cuts), largest / len(cuts)))
        level = level * jnp.repeat(draws, shape[axis_at] // shards_of).reshape([-1 if axis == axis_at else 1 for axis in range(len(shape))])
    return level


def normal_values(rng, shape, spread, reach, pieces=(), kind=jnp.bfloat16):
    result = spread * jax.random.normal(rng, shape, jnp.float32)
    if pieces:
        result = result * block_scale(rng, shape, pieces, -0.22, 0.18)
    return jnp.clip(result, -reach, reach).astype(kind)


def setup_inputs(seed: int = 0) -> dict:
    streams_of = jax.random.split(jax.random.key(seed), 13)
    position = jnp.clip(1.0 * jax.random.uniform(streams_of[0], (3, CELLS, CAP), jnp.float32) ** block_scale(streams_of[0], (3, CELLS, CAP), ((1, 32),), -0.2, 0.2), 0.0, 1.0)
    velocity = normal_values(streams_of[1], (3, CELLS, CAP), 1.0, 6.0, ((1, 32),), jnp.float32)
    smoothing = jnp.clip(0.3 + 0.19999999 * jax.random.uniform(streams_of[2], (CELLS, CAP), jnp.float32) ** block_scale(streams_of[2], (CELLS, CAP), ((0, 32),), -0.2, 0.2), 0.3, 0.5)
    particle_mass = jnp.clip(jnp.exp(math.log(0.012) - 1.09861225 * jax.random.uniform(streams_of[3], (CELLS, CAP), jnp.float32) ** block_scale(streams_of[3], (CELLS, CAP), ((0, 32),), -0.2, 0.2)), 0.004, 0.012)
    energy = jnp.clip(jnp.exp(math.log(2.0) - 1.3862944 * jax.random.uniform(streams_of[4], (CELLS, CAP), jnp.float32) ** block_scale(streams_of[4], (CELLS, CAP), ((0, 32),), -0.2, 0.2)), 0.5, 2.0)
    density_old = jnp.clip(jnp.exp(math.log(1.2) - 1.3862944 * jax.random.uniform(streams_of[5], (CELLS, CAP), jnp.float32) ** block_scale(streams_of[5], (CELLS, CAP), ((0, 32),), -0.2, 0.2)), 0.3, 1.2)
    cell_count = draw_cell_count(jax.random.fold_in(streams_of[12], 71), 0)
    active = draw_active(jax.random.fold_in(streams_of[12], 71), 0)
    time_bin = place_ends(jax.random.randint(streams_of[8], (CELLS, CAP), 0, 6), jax.random.fold_in(streams_of[8], 1), 0, 5).astype(jnp.int32)
    pair_source = draw_pair_source(jax.random.fold_in(streams_of[12], 71), 0)
    pair_shift = draw_pair_shift(jax.random.fold_in(streams_of[12], 71), 0)
    export = place_ends(jax.random.randint(streams_of[11], (EXPORTS, PROXY), 0, C_DEV), jax.random.fold_in(streams_of[11], 1), 0, C_DEV - 1).astype(jnp.int32)
    return {"position": position, "velocity": velocity, "smoothing": smoothing, "particle_mass": particle_mass, "energy": energy, "density_old": density_old, "cell_count": cell_count, "active": active, "time_bin": time_bin, "pair_source": pair_source, "pair_shift": pair_shift, "export": export}


ADIABATIC = 5.0 / 3.0
VISC_ALPHA = 1.0
VISC_BETA = 2.0
STEP_MAX = 0.2

def kernel_value(radius, smooth):
    scaled = radius / smooth
    factor = 1.0 / (math.pi * smooth * smooth * smooth)
    inner_part = 1.0 - 1.5 * scaled * scaled + 0.75 * scaled * scaled * scaled
    outer_part = 0.25 * jnp.maximum(2.0 - scaled, 0.0) ** 3
    return factor * jnp.where(scaled < 1.0, inner_part, outer_part)

def kernel_slope(radius, smooth):
    scaled = radius / smooth
    factor = 1.0 / (math.pi * smooth * smooth * smooth * smooth * smooth)
    inner_part = -3.0 + 2.25 * scaled
    bounded = jnp.maximum(scaled, 1.0)
    outer_part = -0.75 * jnp.maximum(2.0 - bounded, 0.0) ** 2 / bounded
    return factor * jnp.where(scaled < 1.0, inner_part, outer_part)

def shift_offsets(shift_codes):
    first = shift_codes // 9 - 1
    second = shift_codes // 3 % 3 - 1
    third = shift_codes % 3 - 1
    return jnp.stack([first, second, third], axis=-1).astype(jnp.float32)

def density_terms(target_pos, target_smooth, source_pos, source_mass):
    square = sum(((target_pos[component] - source_pos[component]) ** 2 for component in range(3)))
    radius = jnp.sqrt(square)
    return source_mass * kernel_value(radius, target_smooth)

def force_terms(target_pos, target_vel, target_smooth, target_press, target_sound, target_dens, source_pos, source_vel, source_smooth, source_mass, source_press, source_sound, source_dens):
    separation = [target_pos[component] - source_pos[component] for component in range(3)]
    square = sum((piece * piece for piece in separation))
    radius = jnp.sqrt(square)
    mean_slope = 0.5 * (kernel_slope(radius, target_smooth) + kernel_slope(radius, source_smooth))
    approach = sum(((target_vel[component] - source_vel[component]) * separation[component] for component in range(3)))
    mean_smooth = 0.5 * (target_smooth + source_smooth)
    mu_term = mean_smooth * jnp.minimum(approach, 0.0) / (square + 0.01 * mean_smooth * mean_smooth)
    viscous = (-VISC_ALPHA * 0.5 * (target_sound + source_sound) * mu_term + VISC_BETA * mu_term * mu_term) / (0.5 * (target_dens + source_dens))
    weight = source_mass * (target_press + source_press + viscous) * mean_slope
    return [-weight * piece for piece in separation]

def source_tables(export):
    device_ids = jnp.arange(DEVS)
    region_ids = device_ids // N_CELL
    column_ids = device_ids % N_CELL
    own_cells = device_ids[:, None] * C_DEV + jnp.arange(C_DEV)[None, :]
    peer_ids = region_ids[:, None] * N_CELL + jnp.arange(N_CELL)[None, :]
    chosen = export[peer_ids * N_CELL + column_ids[:, None]]
    proxies = (peer_ids[:, :, None] * C_DEV + chosen).reshape(DEVS, N_CELL * PROXY)
    before = ((region_ids - 1) % N_REGION * N_CELL + column_ids) * C_DEV + C_DEV - 1
    after = ((region_ids + 1) % N_REGION * N_CELL + column_ids) * C_DEV
    return jnp.concatenate([own_cells, proxies, before[:, None], after[:, None]], axis=1).astype(jnp.int32)

def reference(position, velocity, smoothing, particle_mass, energy, density_old, cell_count, active, time_bin, pair_source, pair_shift, export):
    slot_index = jnp.arange(CAP)
    live_slot = slot_index[None, :] < cell_count[:, None]
    mass_live = jnp.where(live_slot, particle_mass, 0.0)
    is_active = active > 0
    tables = source_tables(export)
    owner_device = (jnp.arange(CELLS) // C_DEV).astype(jnp.int32)
    global_source = jnp.take_along_axis(tables[owner_device], pair_source, axis=1)
    offsets = shift_offsets(pair_shift)
    cell_ids = jnp.arange(CELLS).astype(jnp.int32)

    def cell_density(cell_item):
        target, sources, shifts = cell_item
        target_pos = [position[component, target][:, None, None] for component in range(3)]
        source_pos = [position[component][sources][None, :, :] + shifts[:, component][None, :, None] for component in range(3)]
        pair_terms = density_terms(target_pos, smoothing[target][:, None, None], source_pos, mass_live[sources][None])
        return lax.optimization_barrier(jnp.sum(pair_terms, axis=(1, 2)))
    summed = lax.map(cell_density, (cell_ids, global_source, offsets))
    density = jnp.where(is_active, summed, density_old)
    press_term = (ADIABATIC - 1.0) * energy / density
    sound_speed = jnp.sqrt(ADIABATIC * (ADIABATIC - 1.0) * energy)

    def cell_force(cell_item):
        target, sources, shifts = cell_item
        target_pos = [position[component, target][:, None, None] for component in range(3)]
        target_vel = [velocity[component, target][:, None, None] for component in range(3)]
        source_pos = [position[component][sources][None, :, :] + shifts[:, component][None, :, None] for component in range(3)]
        source_vel = [velocity[component][sources][None] for component in range(3)]
        pair_terms = force_terms(target_pos, target_vel, smoothing[target][:, None, None], press_term[target][:, None, None], sound_speed[target][:, None, None], density[target][:, None, None], source_pos, source_vel, smoothing[sources][None], mass_live[sources][None], press_term[sources][None], sound_speed[sources][None], density[sources][None])
        return jnp.stack([lax.optimization_barrier(jnp.sum(piece, axis=(1, 2))) for piece in pair_terms], axis=0)
    accel_cells = lax.map(cell_force, (cell_ids, global_source, offsets))
    accel_cells = jnp.transpose(accel_cells, (1, 0, 2))
    acceleration = jnp.where(is_active[None], accel_cells, 0.0)
    step_size = STEP_MAX * jnp.exp2(-time_bin.astype(jnp.float32))
    kicked_velocity = velocity + acceleration * step_size[None]
    return (density, acceleration, kicked_velocity)
```

```python
import functools
import math

import jax
import jax.numpy as jnp
from jax import lax
from jax.experimental import pallas as pl
from jax.experimental.pallas import tpu as pltpu
from jax.sharding import PartitionSpec as P

ADIABATIC = 5.0 / 3.0
STEP_MAX = 0.2
LANES = 128
FIELDS = 16
CHUNK = 16
UNROLL = 4

X, Y, Z, MASS, VX, VY, VZ, WIDE, INV6, HALF, SOUND, DENS4, PRESS, HEAT, COUNT, LIVE = range(FIELDS)


def lane_gather(values, index):
    return jnp.take_along_axis(values, index, axis=1, mode="promise_in_bounds")


def lanes_of(shape):
    return lax.broadcasted_iota(jnp.int32, shape, len(shape) - 1)


def scaled_density(density):
    return 4.0 * density


def pressure_of(heat, density):
    return heat / density


def pack_kernel(
    count, export, position, velocity, smoothing, mass, energy, density_old, active,
    own, rank_out, outgoing, border,
):
    cells = smoothing.shape[0]
    shape = smoothing.shape
    lane = lanes_of(shape)
    row = lax.broadcasted_iota(jnp.int32, shape, 0)
    counts = jnp.zeros(shape, jnp.int32)
    for cell in range(cells):
        counts = jnp.where(row == cell, count[cell], counts)
    is_active = active[...] > 0
    flags = jnp.where(is_active, 1.0, 0.0).astype(jnp.bfloat16)
    square = (LANES, LANES)
    upper = lax.broadcasted_iota(jnp.int32, square, 0) <= lanes_of(square)
    upper = jnp.where(upper, 1.0, 0.0).astype(jnp.bfloat16)
    seen = jnp.dot(flags, upper, preferred_element_type=jnp.float32).astype(jnp.int32)
    chosen = lane_gather(seen, jnp.full(shape, LANES - 1, jnp.int32))
    others = lane + 1 - seen
    rank = jnp.where(is_active, seen - 1, chosen + others - 1)
    first_part = lane < chosen
    wanted = jnp.where(first_part, lane, lane - chosen)
    slot = jnp.zeros(shape, jnp.int32)
    step = LANES // 2
    while step:
        probe = slot + (step - 1)
        found = jnp.where(first_part, lane_gather(seen, probe), lane_gather(others, probe))
        slot = jnp.where(found <= wanted, slot + step, slot)
        step //= 2
    sort = lambda values: lane_gather(values, slot)
    mass_live = jnp.where(lane < counts, mass[...], 0.0)
    smooth = smoothing[...]
    inverse = 1.0 / smooth
    inverse = inverse * inverse * inverse
    heat = (ADIABATIC - 1.0) * energy[...]
    old = density_old[...]
    rows = {
        X: position[0], Y: position[1], Z: position[2], MASS: mass_live,
        VX: 40.0 * velocity[0], VY: 40.0 * velocity[1], VZ: 40.0 * velocity[2],
        WIDE: 2.0 * smooth, INV6: inverse * inverse, HALF: 0.05 * smooth,
        SOUND: jnp.sqrt(ADIABATIC * heat), DENS4: scaled_density(old),
        PRESS: pressure_of(heat, old), HEAT: heat,
    }
    for field, values in rows.items():
        own[:, field, :] = sort(values)
    own[:, COUNT, :] = chosen.astype(jnp.float32)
    own[:, LIVE, :] = jnp.where(lane == 1, chosen, counts).astype(jnp.float32)
    rank_out[...] = rank
    for peer in range(export.shape[0]):
        for entry in range(export.shape[1]):
            outgoing[peer * export.shape[1] + entry] = own[export[peer, entry]]
    border[0] = own[cells - 1]
    border[1] = own[0]


def fill_table(table, shifts, meta_values, meta, meta_sem, own, incoming, border):
    cells = own.shape[0]
    imported = incoming.shape[0]
    for cell in range(cells):
        table[cell] = own[cell]
    for cell in range(imported):
        table[cells + cell] = incoming[cell]
    table[cells + imported] = border[0]
    table[cells + imported + 1] = border[1]
    for cell in range(table.shape[0]):
        meta_values[pl.ds(cell, 1), :] = table[cell, LIVE : LIVE + 1, :].astype(jnp.int32)
    copy = pltpu.make_async_copy(meta_values, meta, meta_sem)
    copy.start()
    row = lax.broadcasted_iota(jnp.int32, (FIELDS, LANES), 0)
    for code in range(shifts.shape[0]):
        first, second, third = code // 9 - 1.0, code // 3 % 3 - 1.0, code % 3 - 1.0
        shifts[code] = jnp.where(
            row == X, first, jnp.where(row == Y, second, jnp.where(row == Z, third, 0.0))
        )
    copy.wait()


def fill_stream(stream, table, shifts, meta, pair_source, pair_shift, cell):
    shape = (FIELDS, LANES)
    lane = lanes_of(shape)
    block = jnp.int32(0)
    offset = jnp.int32(0)
    current = jnp.zeros(shape, jnp.float32)
    for pair in range(pair_source.shape[1]):
        source = pair_source[cell, pair]
        code = pair_shift[cell, pair]
        rolled = pltpu.roll(table[source] + shifts[code], offset, 1)
        current = jnp.where(lane >= offset, rolled, current)
        stream[block] = current
        offset = offset + meta[source, 0]
        full = offset >= LANES
        current = jnp.where(full, rolled, current)
        block = jnp.where(full, block + 1, block)
        offset = jnp.where(full, offset - LANES, offset)
    stream[block] = jnp.where(lane < offset, current, 0.0)
    for extra in range(1, UNROLL):
        stream[block + extra] = jnp.zeros(shape, jnp.float32)
    used = jnp.where(offset > 0, block + 1, block)
    return (used + UNROLL - 1) // UNROLL


def spread(values, field):
    return jnp.broadcast_to(values[:, field : field + 1], (values.shape[0], LANES))


def line(stream, block, field):
    return stream[block, field : field + 1, :]


def density_kernel(
    pair_source, pair_shift, export, own, incoming, border, rank, active, density_old,
    density, sorted_density, outgoing, outgoing_border,
    table, shifts, meta_values, meta, meta_sem, stream, targets, sums, lines,
):
    cells = own.shape[0]
    fill_table(table, shifts, meta_values, meta, meta_sem, own, incoming, border)
    for cell in range(cells):
        targets[cell] = own[cell].T

    def one_cell(cell, carry):
        rounds = fill_stream(stream, table, shifts, meta, pair_source, pair_shift, cell)
        chunks = (meta[cell, 1] + CHUNK - 1) // CHUNK

        def one_chunk(chunk, carry):
            base = pl.multiple_of(chunk * CHUNK, CHUNK)
            mine = targets[cell, pl.ds(base, CHUNK), :]
            place = [spread(mine, field) for field in (X, Y, Z)]
            wide = spread(mine, WIDE)
            smooth = 0.5 * wide

            def blocks(index, total):
                for sub in range(UNROLL):
                    block = index * UNROLL + sub
                    apart = [place[c] - line(stream, block, c) for c in range(3)]
                    square = apart[0] * apart[0] + apart[1] * apart[1] + apart[2] * apart[2]
                    radius = square * lax.rsqrt(jnp.maximum(square, 1e-24))
                    outer = jnp.maximum(wide - radius, 0.0)
                    inner = jnp.maximum(smooth - radius, 0.0)
                    value = outer * outer * outer - 4.0 * (inner * inner * inner)
                    total = total + line(stream, block, MASS) * value
                return total

            total = lax.fori_loop(0, rounds, blocks, jnp.zeros((CHUNK, LANES), jnp.float32))
            summed = jnp.sum(total, axis=1, keepdims=True)
            sums[pl.ds(base, CHUNK), 0:1] = summed * (0.25 / math.pi) * mine[:, INV6 : INV6 + 1]
            return carry

        lax.fori_loop(0, chunks, one_chunk, 0)
        lines[pl.ds(cell, 1), :] = sums[...].T[0:1, :]
        return carry

    lax.fori_loop(0, cells, one_cell, 0)
    shape = density.shape
    old_sorted = jnp.zeros(shape, jnp.float32)
    row = lax.broadcasted_iota(jnp.int32, shape, 0)
    chosen = jnp.zeros(shape, jnp.float32)
    for cell in range(cells):
        old_sorted = jnp.where(row == cell, own[cell, DENS4 : DENS4 + 1, :], old_sorted)
        chosen = jnp.where(row == cell, own[cell, COUNT : COUNT + 1, :], chosen)
    summed = lines[...]
    density[...] = jnp.where(active[...] > 0, lane_gather(summed, rank[...]), density_old[...])
    lane = lanes_of(shape).astype(jnp.float32)
    sorted_density[...] = jnp.where(lane < chosen, summed, 0.25 * old_sorted)
    for peer in range(export.shape[0]):
        for entry in range(export.shape[1]):
            outgoing[peer, pl.ds(entry, 1), :] = sorted_density[pl.ds(export[peer, entry], 1), :]
    outgoing_border[0:1, :] = sorted_density[cells - 1 : cells, :]
    outgoing_border[1:2, :] = sorted_density[0:1, :]


def force_kernel(
    pair_source, pair_shift, own, incoming, border, own_density, new_density, new_border,
    rank, active, velocity, time_bin,
    acceleration, kicked,
    table, shifts, meta_values, meta, meta_sem, stream, targets, sums, lines,
):
    cells = own.shape[0]
    imported = incoming.shape[0]
    fill_table(table, shifts, meta_values, meta, meta_sem, own, incoming, border)

    def renew(cell, density):
        table[cell, DENS4 : DENS4 + 1, :] = scaled_density(density)
        table[cell, PRESS : PRESS + 1, :] = pressure_of(table[cell, HEAT : HEAT + 1, :], density)

    for cell in range(cells):
        renew(cell, own_density[cell : cell + 1, :])
    per = new_density.shape[1]
    for cell in range(imported):
        renew(cells + cell, new_density[cell // per, cell % per : cell % per + 1, :])
    for cell in range(2):
        renew(cells + imported + cell, new_border[cell : cell + 1, :])
    for cell in range(cells):
        targets[cell] = table[cell].T

    def one_cell(cell, carry):
        rounds = fill_stream(stream, table, shifts, meta, pair_source, pair_shift, cell)
        chunks = (meta[cell, 1] + CHUNK - 1) // CHUNK

        def one_chunk(chunk, carry):
            base = pl.multiple_of(chunk * CHUNK, CHUNK)
            mine = targets[cell, pl.ds(base, CHUNK), :]
            t = {
                field: spread(mine, field)
                for field in (X, Y, Z, VX, VY, VZ, WIDE, INV6, HALF, SOUND, DENS4, PRESS)
            }

            def blocks(index, totals):
                for sub in range(UNROLL):
                    s = functools.partial(line, stream, index * UNROLL + sub)
                    apart = [t[c] - s(c) for c in (X, Y, Z)]
                    square = apart[0] * apart[0] + apart[1] * apart[1] + apart[2] * apart[2]
                    inverse = lax.rsqrt(jnp.maximum(square, 1e-24))
                    radius = square * inverse
                    double = radius + radius
                    outer = jnp.maximum(t[WIDE] - radius, 0.0)
                    inner = jnp.maximum(t[WIDE] - double, 0.0)
                    slope = t[INV6] * (outer * outer - inner * inner)
                    outer = jnp.maximum(s(WIDE) - radius, 0.0)
                    inner = jnp.maximum(s(WIDE) - double, 0.0)
                    slope = slope + s(INV6) * (outer * outer - inner * inner)
                    approach = (
                        (t[VX] - s(VX)) * apart[0]
                        + (t[VY] - s(VY)) * apart[1]
                        + (t[VZ] - s(VZ)) * apart[2]
                    )
                    half = t[HALF] + s(HALF)
                    mu = half * jnp.minimum(approach, 0.0) * (1.0 / (square + half * half))
                    viscous = mu * (mu - (t[SOUND] + s(SOUND))) * (1.0 / (t[DENS4] + s(DENS4)))
                    weight = (t[PRESS] + s(PRESS) + viscous) * (slope * (inverse * s(MASS)))
                    totals = tuple(total + weight * a for total, a in zip(totals, apart))
                return totals

            zero = jnp.zeros((CHUNK, LANES), jnp.float32)
            totals = lax.fori_loop(0, rounds, blocks, (zero, zero, zero))
            for c in range(3):
                sums[pl.ds(base, CHUNK), c : c + 1] = jnp.sum(totals[c], axis=1, keepdims=True) * (
                    0.375 / math.pi
                )
            return carry

        lax.fori_loop(0, chunks, one_chunk, 0)
        turned = sums[...].T
        for c in range(3):
            lines[c, pl.ds(cell, 1), :] = turned[c : c + 1, :]
        return carry

    lax.fori_loop(0, cells, one_cell, 0)
    step = STEP_MAX * jnp.exp2(-time_bin[...].astype(jnp.float32))
    for c in range(3):
        gathered = lane_gather(lines[c], rank[...])
        value = jnp.where(active[...] > 0, gathered, 0.0)
        acceleration[c] = value
        kicked[c] = velocity[c] + value * step


def shards(
    position, velocity, smoothing, particle_mass, energy, density_old, cell_count, active,
    time_bin, pair_source, pair_shift, export,
):
    cells, capacity = smoothing.shape
    peers, per_peer = export.shape
    sources = cells + peers * per_peer + 2
    f32 = lambda *shape: jax.ShapeDtypeStruct(shape, jnp.float32)
    smem = pl.BlockSpec(memory_space=pltpu.SMEM)
    vmem = pl.BlockSpec(memory_space=pltpu.VMEM)
    params = pltpu.CompilerParams(vmem_limit_bytes=32 * 2**20)

    own, rank, outgoing, border = pl.pallas_call(
        pack_kernel,
        out_shape=(
            f32(cells, FIELDS, capacity),
            jax.ShapeDtypeStruct((cells, capacity), jnp.int32),
            f32(peers * per_peer, FIELDS, capacity),
            f32(2, FIELDS, capacity),
        ),
        in_specs=[smem] * 2 + [vmem] * 7,
        out_specs=(vmem,) * 4,
        compiler_params=params,
        name="pack",
    )(cell_count, export, position, velocity, smoothing, particle_mass, energy, density_old, active)

    def swap_border(pieces):
        size = lax.axis_size("region")
        up = [(i, (i + 1) % size) for i in range(size)]
        down = [(j, i) for i, j in up]
        if size == 2:
            return lax.ppermute(pieces, "region", up)
        before = lax.ppermute(pieces[0:1], "region", up)
        after = lax.ppermute(pieces[1:2], "region", down)
        return jnp.concatenate([before, after], axis=0)

    incoming = lax.all_to_all(outgoing, "cell", split_axis=0, concat_axis=0, tiled=True)
    other = swap_border(border)

    def scratch(result_rows):
        return [
            pltpu.VMEM((sources, FIELDS, capacity), jnp.float32),
            pltpu.VMEM((27, FIELDS, capacity), jnp.float32),
            pltpu.VMEM((-(-sources // 8) * 8, capacity), jnp.int32),
            pltpu.SMEM((-(-sources // 8) * 8, capacity), jnp.int32),
            pltpu.SemaphoreType.DMA,
            pltpu.VMEM((pair_source.shape[1] + UNROLL + 1, FIELDS, capacity), jnp.float32),
            pltpu.VMEM((cells, capacity, FIELDS), jnp.float32),
            pltpu.VMEM((capacity, 8), jnp.float32),
            pltpu.VMEM(result_rows + (cells, capacity), jnp.float32),
        ]

    density, sorted_density, outgoing_density, border_density = pl.pallas_call(
        density_kernel,
        out_shape=(
            f32(cells, capacity),
            f32(cells, capacity),
            f32(peers, per_peer, capacity),
            f32(2, capacity),
        ),
        in_specs=[smem] * 3 + [vmem] * 6,
        out_specs=(vmem,) * 4,
        scratch_shapes=scratch(()),
        compiler_params=params,
        name="density",
    )(pair_source, pair_shift, export, own, incoming, other, rank, active, density_old)

    new_density = lax.all_to_all(outgoing_density, "cell", split_axis=0, concat_axis=0, tiled=True)
    new_border = swap_border(border_density)

    acceleration, kicked = pl.pallas_call(
        force_kernel,
        out_shape=(f32(3, cells, capacity), f32(3, cells, capacity)),
        in_specs=[smem] * 2 + [vmem] * 10,
        out_specs=(vmem,) * 2,
        scratch_shapes=scratch((3,)),
        compiler_params=params,
        name="force",
    )(
        pair_source, pair_shift, own, incoming, other, sorted_density, new_density, new_border,
        rank, active, velocity, time_bin,
    )
    return density, acceleration, kicked


def solution(mesh):
    rows = P(("region", "cell"), None)
    planes = P(None, ("region", "cell"), None)
    return jax.shard_map(
        shards,
        mesh=mesh,
        in_specs=(
            planes, planes, rows, rows, rows, rows, P(("region", "cell")), rows, rows, rows, rows,
            rows,
        ),
        out_specs=(rows, planes, planes),
        check_vma=False,
    )
```

```python
import functools
import math

import jax
import jax.numpy as jnp
from jax import lax
from jax.experimental import pallas as pl
from jax.experimental.pallas import tpu as pltpu
from jax.sharding import PartitionSpec as P

ADIABATIC = 5.0 / 3.0
STEP_MAX = 0.2
LANES = 128
FIELDS = 16
CHUNK = 16
UNROLL = 4

X, Y, Z, MASS, VX, VY, VZ, WIDE, INV6, HALF, SOUND, DENS4, PRESS, HEAT, COUNT, LIVE = range(FIELDS)


def lane_gather(values, index):
    return jnp.take_along_axis(values, index, axis=1, mode="promise_in_bounds")


def lanes_of(shape):
    return lax.broadcasted_iota(jnp.int32, shape, len(shape) - 1)


def scaled_density(density):
    return 4.0 * density


def pressure_of(heat, density):
    return heat / density


def pack_kernel(
    count, *refs
):
    arrays, (own, rank_out, border), landed, sem = refs[:8], refs[8:11], refs[11:-1], refs[-1]
    copies = [
        pltpu.make_async_copy(array, place, sem.at[index])
        for index, (array, place) in enumerate(zip(arrays, landed))
    ]
    for copy in copies:
        copy.start()
    for copy in copies:
        copy.wait()
    position, velocity, smoothing, mass, energy, density_old, active, export = landed
    cells = smoothing.shape[0]
    shape = smoothing.shape
    lane = lanes_of(shape)
    row = lax.broadcasted_iota(jnp.int32, shape, 0)
    counts = jnp.zeros(shape, jnp.int32)
    for cell in range(cells):
        counts = jnp.where(row == cell, count[cell], counts)
    is_active = active[...] > 0
    flags = jnp.where(is_active, 1.0, 0.0).astype(jnp.bfloat16)
    square = (LANES, LANES)
    upper = lax.broadcasted_iota(jnp.int32, square, 0) <= lanes_of(square)
    upper = jnp.where(upper, 1.0, 0.0).astype(jnp.bfloat16)
    seen = jnp.dot(flags, upper, preferred_element_type=jnp.float32).astype(jnp.int32)
    chosen = lane_gather(seen, jnp.full(shape, LANES - 1, jnp.int32))
    others = lane + 1 - seen
    rank = jnp.where(is_active, seen - 1, chosen + others - 1)
    first_part = lane < chosen
    wanted = jnp.where(first_part, lane, lane - chosen)
    slot = jnp.zeros(shape, jnp.int32)
    step = LANES // 2
    while step:
        probe = slot + (step - 1)
        found = jnp.where(first_part, lane_gather(seen, probe), lane_gather(others, probe))
        slot = jnp.where(found <= wanted, slot + step, slot)
        step //= 2
    sort = lambda values: lane_gather(values, slot)
    mass_live = jnp.where(lane < counts, mass[...], 0.0)
    smooth = smoothing[...]
    inverse = 1.0 / smooth
    inverse = inverse * inverse * inverse
    heat = (ADIABATIC - 1.0) * energy[...]
    old = density_old[...]
    rows = {
        X: position[0], Y: position[1], Z: position[2], MASS: mass_live,
        VX: 40.0 * velocity[0], VY: 40.0 * velocity[1], VZ: 40.0 * velocity[2],
        WIDE: 2.0 * smooth, INV6: inverse * inverse, HALF: 0.05 * smooth,
        SOUND: jnp.sqrt(ADIABATIC * heat), DENS4: scaled_density(old),
        PRESS: pressure_of(heat, old), HEAT: heat,
    }
    for field, values in rows.items():
        own[0:cells, field, :] = sort(values)
    own[0:cells, COUNT, :] = chosen.astype(jnp.float32)
    own[0:cells, LIVE, :] = jnp.where(lane == 1, chosen, counts).astype(jnp.float32)
    rank_out[...] = rank
    own[cells] = jnp.zeros((FIELDS, LANES), jnp.float32)
    own[cells, 0 : export.shape[0], 0 : export.shape[1]] = export[...].astype(jnp.float32)
    border[0] = own[cells - 1]
    border[1] = own[0]


def find_sources(lists, lists_smem, sem, incoming, cells, per_peer):
    span = cells + 1
    peers = incoming.shape[0] // span
    for peer in range(peers):
        lists[pl.ds(peer * 8, 8), :] = incoming[peer * span + cells, 0:8, :].astype(jnp.int32)
    copy = pltpu.make_async_copy(lists, lists_smem, sem)
    copy.start()
    copy.wait()
    column = lax.axis_index("cell")
    return lambda peer, entry: lists_smem[peer * 8 + entry, column]


def fill_table(table, shifts, meta_values, meta, meta_sem, own, incoming, border, picked, peers, per_peer):
    cells = own.shape[0] - 1
    for cell in range(cells):
        table[cell] = own[cell]
    for peer in range(peers):
        for entry in range(per_peer):
            table[cells + peer * per_peer + entry] = incoming[
                peer * (cells + 1) + picked(peer, entry)
            ]
    imported = peers * per_peer
    table[cells + imported] = border[0]
    table[cells + imported + 1] = border[1]
    for cell in range(table.shape[0]):
        meta_values[pl.ds(cell, 1), :] = table[cell, LIVE : LIVE + 1, :].astype(jnp.int32)
    copy = pltpu.make_async_copy(meta_values, meta, meta_sem)
    copy.start()
    row = lax.broadcasted_iota(jnp.int32, (FIELDS, LANES), 0)
    for code in range(shifts.shape[0]):
        first, second, third = code // 9 - 1.0, code // 3 % 3 - 1.0, code % 3 - 1.0
        shifts[code] = jnp.where(
            row == X, first, jnp.where(row == Y, second, jnp.where(row == Z, third, 0.0))
        )
    copy.wait()


def fill_stream(stream, table, shifts, meta, pair_source, pair_shift, cell):
    shape = (FIELDS, LANES)
    lane = lanes_of(shape)
    block = jnp.int32(0)
    offset = jnp.int32(0)
    current = jnp.zeros(shape, jnp.float32)
    for pair in range(pair_source.shape[1]):
        source = pair_source[cell, pair]
        code = pair_shift[cell, pair]
        rolled = pltpu.roll(table[source] + shifts[code], offset, 1)
        current = jnp.where(lane >= offset, rolled, current)
        stream[block] = current
        offset = offset + meta[source, 0]
        full = offset >= LANES
        current = jnp.where(full, rolled, current)
        block = jnp.where(full, block + 1, block)
        offset = jnp.where(full, offset - LANES, offset)
    stream[block] = jnp.where(lane < offset, current, 0.0)
    for extra in range(1, UNROLL):
        stream[block + extra] = jnp.zeros(shape, jnp.float32)
    used = jnp.where(offset > 0, block + 1, block)
    return (used + UNROLL - 1) // UNROLL


def spread(values, field):
    return jnp.broadcast_to(values[:, field : field + 1], (values.shape[0], LANES))


def line(stream, block, field):
    return stream[block, field : field + 1, :]


def density_kernel(
    per_peer, pair_source, pair_shift, own, incoming, border, rank, active, density_old,
    density, sorted_density, outgoing_border,
    table, shifts, meta_values, meta, meta_sem, stream, targets, sums, lines, lists, lists_smem,
):
    cells = own.shape[0] - 1
    peers = incoming.shape[0] // (cells + 1)
    picked = find_sources(lists, lists_smem, meta_sem, incoming, cells, per_peer)
    fill_table(
        table, shifts, meta_values, meta, meta_sem, own, incoming, border, picked, peers, per_peer
    )
    for cell in range(cells):
        targets[cell] = own[cell].T

    def one_cell(cell, carry):
        rounds = fill_stream(stream, table, shifts, meta, pair_source, pair_shift, cell)
        chunks = (meta[cell, 1] + CHUNK - 1) // CHUNK

        def one_chunk(chunk, carry):
            base = pl.multiple_of(chunk * CHUNK, CHUNK)
            mine = targets[cell, pl.ds(base, CHUNK), :]
            place = [spread(mine, field) for field in (X, Y, Z)]
            wide = spread(mine, WIDE)
            smooth = 0.5 * wide

            def blocks(index, total):
                for sub in range(UNROLL):
                    block = index * UNROLL + sub
                    apart = [place[c] - line(stream, block, c) for c in range(3)]
                    square = apart[0] * apart[0] + apart[1] * apart[1] + apart[2] * apart[2]
                    radius = square * lax.rsqrt(jnp.maximum(square, 1e-24))
                    outer = jnp.maximum(wide - radius, 0.0)
                    inner = jnp.maximum(smooth - radius, 0.0)
                    value = outer * outer * outer - 4.0 * (inner * inner * inner)
                    total = total + line(stream, block, MASS) * value
                return total

            total = lax.fori_loop(0, rounds, blocks, jnp.zeros((CHUNK, LANES), jnp.float32))
            summed = jnp.sum(total, axis=1, keepdims=True)
            sums[pl.ds(base, CHUNK), 0:1] = summed * (0.25 / math.pi) * mine[:, INV6 : INV6 + 1]
            return carry

        lax.fori_loop(0, chunks, one_chunk, 0)
        lines[pl.ds(cell, 1), :] = sums[...].T[0:1, :]
        return carry

    lax.fori_loop(0, cells, one_cell, 0)
    shape = density.shape
    old_sorted = jnp.zeros(shape, jnp.float32)
    row = lax.broadcasted_iota(jnp.int32, shape, 0)
    chosen = jnp.zeros(shape, jnp.float32)
    for cell in range(cells):
        old_sorted = jnp.where(row == cell, own[cell, DENS4 : DENS4 + 1, :], old_sorted)
        chosen = jnp.where(row == cell, own[cell, COUNT : COUNT + 1, :], chosen)
    summed = lines[...]
    density[...] = jnp.where(active[...] > 0, lane_gather(summed, rank[...]), density_old[...])
    lane = lanes_of(shape).astype(jnp.float32)
    sorted_density[...] = jnp.where(lane < chosen, summed, 0.25 * old_sorted)
    outgoing_border[0:1, :] = sorted_density[cells - 1 : cells, :]
    outgoing_border[1:2, :] = sorted_density[0:1, :]


def force_kernel(
    per_peer, pair_source, pair_shift, own, incoming, border, own_density, new_density, new_border,
    rank, active, velocity, time_bin,
    acceleration, kicked,
    table, shifts, meta_values, meta, meta_sem, stream, targets, sums, lines, lists, lists_smem,
):
    cells = own.shape[0] - 1
    peers = incoming.shape[0] // (cells + 1)
    imported = peers * per_peer
    picked = find_sources(lists, lists_smem, meta_sem, incoming, cells, per_peer)
    fill_table(
        table, shifts, meta_values, meta, meta_sem, own, incoming, border, picked, peers, per_peer
    )

    def renew(cell, density):
        table[cell, DENS4 : DENS4 + 1, :] = scaled_density(density)
        table[cell, PRESS : PRESS + 1, :] = pressure_of(table[cell, HEAT : HEAT + 1, :], density)

    for cell in range(cells):
        renew(cell, own_density[cell : cell + 1, :])
    for peer in range(peers):
        for entry in range(per_peer):
            place = peer * cells + picked(peer, entry)
            renew(cells + peer * per_peer + entry, new_density[pl.ds(place, 1), :])
    for cell in range(2):
        renew(cells + imported + cell, new_border[cell : cell + 1, :])
    for cell in range(cells):
        targets[cell] = table[cell].T

    def one_cell(cell, carry):
        rounds = fill_stream(stream, table, shifts, meta, pair_source, pair_shift, cell)
        chunks = (meta[cell, 1] + CHUNK - 1) // CHUNK

        def one_chunk(chunk, carry):
            base = pl.multiple_of(chunk * CHUNK, CHUNK)
            mine = targets[cell, pl.ds(base, CHUNK), :]
            t = {
                field: spread(mine, field)
                for field in (X, Y, Z, VX, VY, VZ, WIDE, INV6, HALF, SOUND, DENS4, PRESS)
            }

            def blocks(index, totals):
                for sub in range(UNROLL):
                    s = functools.partial(line, stream, index * UNROLL + sub)
                    apart = [t[c] - s(c) for c in (X, Y, Z)]
                    square = apart[0] * apart[0] + apart[1] * apart[1] + apart[2] * apart[2]
                    inverse = lax.rsqrt(jnp.maximum(square, 1e-24))
                    radius = square * inverse
                    double = radius + radius
                    outer = jnp.maximum(t[WIDE] - radius, 0.0)
                    inner = jnp.maximum(t[WIDE] - double, 0.0)
                    slope = t[INV6] * (outer * outer - inner * inner)
                    outer = jnp.maximum(s(WIDE) - radius, 0.0)
                    inner = jnp.maximum(s(WIDE) - double, 0.0)
                    slope = slope + s(INV6) * (outer * outer - inner * inner)
                    approach = (
                        (t[VX] - s(VX)) * apart[0]
                        + (t[VY] - s(VY)) * apart[1]
                        + (t[VZ] - s(VZ)) * apart[2]
                    )
                    half = t[HALF] + s(HALF)
                    mu = half * jnp.minimum(approach, 0.0) * (1.0 / (square + half * half))
                    viscous = mu * (mu - (t[SOUND] + s(SOUND))) * (1.0 / (t[DENS4] + s(DENS4)))
                    weight = (t[PRESS] + s(PRESS) + viscous) * (slope * (inverse * s(MASS)))
                    totals = tuple(total + weight * a for total, a in zip(totals, apart))
                return totals

            zero = jnp.zeros((CHUNK, LANES), jnp.float32)
            totals = lax.fori_loop(0, rounds, blocks, (zero, zero, zero))
            for c in range(3):
                sums[pl.ds(base, CHUNK), c : c + 1] = jnp.sum(totals[c], axis=1, keepdims=True) * (
                    0.375 / math.pi
                )
            return carry

        lax.fori_loop(0, chunks, one_chunk, 0)
        turned = sums[...].T
        for c in range(3):
            lines[c, pl.ds(cell, 1), :] = turned[c : c + 1, :]
        return carry

    lax.fori_loop(0, cells, one_cell, 0)
    step = STEP_MAX * jnp.exp2(-time_bin[...].astype(jnp.float32))
    for c in range(3):
        gathered = lane_gather(lines[c], rank[...])
        value = jnp.where(active[...] > 0, gathered, 0.0)
        acceleration[c] = value
        kicked[c] = velocity[c] + value * step


def shards(
    position, velocity, smoothing, particle_mass, energy, density_old, cell_count, active,
    time_bin, pair_source, pair_shift, export,
):
    cells, capacity = smoothing.shape
    peers, per_peer = export.shape
    sources = cells + peers * per_peer + 2
    f32 = lambda *shape: jax.ShapeDtypeStruct(shape, jnp.float32)
    smem = pl.BlockSpec(memory_space=pltpu.SMEM)
    vmem = pl.BlockSpec(memory_space=pltpu.VMEM)
    params = pltpu.CompilerParams(vmem_limit_bytes=64 * 2**20)

    hbm = pl.BlockSpec(memory_space=pltpu.HBM)
    arrays = (position, velocity, smoothing, particle_mass, energy, density_old, active, export.T)
    own, rank, border = pl.pallas_call(
        pack_kernel,
        out_shape=(
            f32(cells + 1, FIELDS, capacity),
            jax.ShapeDtypeStruct((cells, capacity), jnp.int32),
            f32(2, FIELDS, capacity),
        ),
        in_specs=[smem] + [hbm] * 8,
        out_specs=(vmem,) * 3,
        scratch_shapes=[pltpu.VMEM(a.shape, a.dtype) for a in arrays]
        + [pltpu.SemaphoreType.DMA((8,))],
        compiler_params=params,
        name="pack",
    )(cell_count, *arrays)

    def swap_border(pieces):
        size = lax.axis_size("region")
        up = [(i, (i + 1) % size) for i in range(size)]
        down = [(j, i) for i, j in up]
        if size == 2:
            return lax.ppermute(pieces, "region", up)
        before = lax.ppermute(pieces[0:1], "region", up)
        after = lax.ppermute(pieces[1:2], "region", down)
        return jnp.concatenate([before, after], axis=0)

    incoming = lax.all_gather(own, "cell", axis=0, tiled=True)
    other = swap_border(border)

    def scratch(result_rows):
        return [
            pltpu.VMEM((sources, FIELDS, capacity), jnp.float32),
            pltpu.VMEM((27, FIELDS, capacity), jnp.float32),
            pltpu.VMEM((-(-sources // 8) * 8, capacity), jnp.int32),
            pltpu.SMEM((-(-sources // 8) * 8, capacity), jnp.int32),
            pltpu.SemaphoreType.DMA,
            pltpu.VMEM((pair_source.shape[1] + UNROLL + 1, FIELDS, capacity), jnp.float32),
            pltpu.VMEM((cells, capacity, FIELDS), jnp.float32),
            pltpu.VMEM((capacity, 8), jnp.float32),
            pltpu.VMEM(result_rows + (cells, capacity), jnp.float32),
            pltpu.VMEM((peers * 8, capacity), jnp.int32),
            pltpu.SMEM((peers * 8, capacity), jnp.int32),
        ]

    density, sorted_density, border_density = pl.pallas_call(
        functools.partial(density_kernel, per_peer),
        out_shape=(f32(cells, capacity), f32(cells, capacity), f32(2, capacity)),
        in_specs=[smem] * 2 + [vmem] * 6,
        out_specs=(vmem,) * 3,
        scratch_shapes=scratch(()),
        compiler_params=params,
        name="density",
    )(pair_source, pair_shift, own, incoming, other, rank, active, density_old)

    new_density = lax.all_gather(sorted_density, "cell", axis=0, tiled=True)
    new_border = swap_border(border_density)

    acceleration, kicked = pl.pallas_call(
        functools.partial(force_kernel, per_peer),
        out_shape=(f32(3, cells, capacity), f32(3, cells, capacity)),
        in_specs=[smem] * 2 + [vmem] * 10,
        out_specs=(vmem,) * 2,
        scratch_shapes=scratch((3,)),
        compiler_params=params,
        name="force",
    )(
        pair_source, pair_shift, own, incoming, other, sorted_density, new_density, new_border,
        rank, active, velocity, time_bin,
    )
    return density, acceleration, kicked


def solution(mesh):
    rows = P(("region", "cell"), None)
    planes = P(None, ("region", "cell"), None)
    return jax.shard_map(
        shards,
        mesh=mesh,
        in_specs=(
            planes, planes, rows, rows, rows, rows, P(("region", "cell")), rows, rows, rows, rows,
            rows,
        ),
        out_specs=(rows, planes, planes),
        check_vma=False,
    )
```

```python
import functools
import math

import jax
import jax.numpy as jnp
from jax import lax
from jax.experimental import pallas as pl
from jax.experimental.pallas import tpu as pltpu
from jax.sharding import PartitionSpec as P

ADIABATIC = 5.0 / 3.0
STEP_MAX = 0.2
LANES = 128
ROWS = 8
DENSITY_UNROLL = 6
FORCE_UNROLL = 4
SPARE = 8

X, Y, Z, MASS, VX, VY, VZ, WIDE = range(ROWS)
HEAT, DENS, COUNT, LIVE = range(4)
SENT = 4
INV6, HALF, SOUND, DENS4, PRESS = range(5)


def lane_gather(values, index):
    return jnp.take_along_axis(values, index, axis=1, mode="promise_in_bounds")


def lanes_of(shape):
    return lax.broadcasted_iota(jnp.int32, shape, len(shape) - 1)


def split_of(peers):
    low = 1
    while low * low < peers:
        low *= 2
    return (peers // low, low) if peers % low == 0 else (peers, 1)


def place_of(peer, peers):
    high, low = split_of(peers)
    return (peer % low) * high + peer // low


def pack_kernel(count, export, *refs):
    arrays, (own, own_sent, rank_out, outgoing, border) = refs[:7], refs[7:12]
    landed, sem = refs[12:-1], refs[-1]
    copies = [
        pltpu.make_async_copy(array, place, sem.at[index])
        for index, (array, place) in enumerate(zip(arrays, landed))
    ]
    for copy in copies:
        copy.start()
    for copy in copies:
        copy.wait()
    position, velocity, smoothing, mass, energy, density_old, active = landed
    cells = smoothing.shape[0]
    shape = smoothing.shape
    lane = lanes_of(shape)
    row = lax.broadcasted_iota(jnp.int32, shape, 0)
    counts = jnp.zeros(shape, jnp.int32)
    for cell in range(cells):
        counts = jnp.where(row == cell, count[cell], counts)
    is_active = active[...] > 0
    flags = jnp.where(is_active, 1.0, 0.0).astype(jnp.bfloat16)
    square = (LANES, LANES)
    upper = lax.broadcasted_iota(jnp.int32, square, 0) <= lanes_of(square)
    upper = jnp.where(upper, 1.0, 0.0).astype(jnp.bfloat16)
    seen = jnp.dot(flags, upper, preferred_element_type=jnp.float32).astype(jnp.int32)
    chosen = lane_gather(seen, jnp.full(shape, LANES - 1, jnp.int32))
    others = lane + 1 - seen
    rank_out[...] = jnp.where(is_active, seen - 1, chosen + others - 1)
    first_part = lane < chosen
    wanted = jnp.where(first_part, lane, lane - chosen)
    slot = jnp.zeros(shape, jnp.int32)
    step = LANES // 2
    while step:
        probe = slot + (step - 1)
        found = jnp.where(first_part, lane_gather(seen, probe), lane_gather(others, probe))
        slot = jnp.where(found <= wanted, slot + step, slot)
        step //= 2
    mass_live = jnp.where(lane < counts, mass[...], 0.0)
    rows = (
        position[0], position[1], position[2], mass_live,
        40.0 * velocity[0], 40.0 * velocity[1], 40.0 * velocity[2], 2.0 * smoothing[...],
    )
    for field, values in enumerate(rows):
        own[:, field, :] = lane_gather(values, slot)
    own_sent[:, HEAT, :] = lane_gather((ADIABATIC - 1.0) * energy[...], slot)
    own_sent[:, DENS, :] = lane_gather(density_old[...], slot)
    own_sent[:, COUNT, :] = chosen.astype(jnp.float32)
    own_sent[:, LIVE, :] = jnp.where(lane == 1, chosen, counts).astype(jnp.float32)
    per_peer, peers = export.shape
    for peer in range(peers):
        place = place_of(peer, peers)
        for entry in range(per_peer):
            cell = export[entry, peer]
            outgoing[place, entry * ROWS : (entry + 1) * ROWS, :] = own[cell]
            start = per_peer * ROWS + entry * SENT
            outgoing[place, start : start + SENT, :] = own_sent[cell]
    for side, cell in enumerate((cells - 1, 0)):
        border[side, 0:ROWS, :] = own[cell]
        border[side, ROWS : ROWS + SENT, :] = own_sent[cell]


def fill_meta(meta_values, meta, meta_sem, own_sent, incoming, border, per_peer):
    cells, peers = own_sent.shape[0], incoming.shape[0]
    for cell in range(cells):
        meta_values[cell : cell + 1, :] = own_sent[cell, LIVE : LIVE + 1, :].astype(jnp.int32)
    for peer in range(peers):
        for entry in range(per_peer):
            row = per_peer * ROWS + entry * SENT + LIVE
            place = cells + peer * per_peer + entry
            meta_values[place : place + 1, :] = incoming[peer, row : row + 1, :].astype(jnp.int32)
    for side in range(2):
        place = cells + peers * per_peer + side
        row = ROWS + LIVE
        meta_values[place : place + 1, :] = border[side, row : row + 1, :].astype(jnp.int32)
    copy = pltpu.make_async_copy(meta_values, meta, meta_sem)
    copy.start()
    return copy


def fill_stream(stream, table, shifts, meta, pair_source, pair_shift, cell):
    shape = (ROWS, LANES)
    lane = lanes_of(shape)
    block = jnp.int32(0)
    offset = jnp.int32(0)
    current = jnp.zeros(shape, jnp.float32)
    for pair in range(pair_source.shape[1]):
        source = pair_source[cell, pair]
        values = table[source]
        if shifts is not None:
            values = values + shifts[pair_shift[cell, pair]]
        rolled = pltpu.roll(values, offset, 1)
        current = jnp.where(lane >= offset, rolled, current)
        stream[block] = current
        offset = offset + meta[source, 0]
        full = offset >= LANES
        current = jnp.where(full, rolled, current)
        block = jnp.where(full, block + 1, block)
        offset = jnp.where(full, offset - LANES, offset)
    stream[block] = jnp.where(lane < offset, current, 0.0)
    for extra in range(1, SPARE):
        stream[block + extra] = jnp.zeros(shape, jnp.float32)
    return jnp.where(offset > 0, block + 1, block)


def spread(values, field):
    return jnp.broadcast_to(values[:, field : field + 1], (values.shape[0], LANES))


def over_targets(active, one_chunk):
    groups = (active + ROWS - 1) // ROWS

    def large(chunk, carry):
        one_chunk(pl.multiple_of(chunk * 4 * ROWS, ROWS), 4)
        return carry

    lax.fori_loop(0, groups // 4, large, 0)
    for size in (2, 1):

        @pl.when((groups & size) != 0)
        def _(size=size):
            done = groups & -(2 * size)
            one_chunk(pl.multiple_of(done * ROWS, ROWS), size)


def lane_sums(parts):
    ones = jnp.ones((ROWS, LANES), jnp.float32)
    sums = lax.dot_general(
        ones, parts, (((1,), (1,)), ((), ())),
        precision=lax.Precision.HIGHEST, preferred_element_type=jnp.float32,
    )
    return sums[0:1, :]


def density_kernel(
    per_peer, pair_source, pair_shift, export, own, own_sent, incoming, border, rank, active,
    density_old,
    density, sorted_density, outgoing, outgoing_border, streams,
    table, shifts, meta_values, meta, meta_sem, targets, parts, lines,
):
    cells, peers = own.shape[0], incoming.shape[0]
    copy = fill_meta(meta_values, meta, meta_sem, own_sent, incoming, border, per_peer)
    for cell in range(cells):
        table[cell] = own[cell]
    for peer in range(peers):
        for entry in range(per_peer):
            table[cells + peer * per_peer + entry] = incoming[
                peer, entry * ROWS : (entry + 1) * ROWS, :
            ]
    for side in range(2):
        table[cells + peers * per_peer + side] = border[side, 0:ROWS, :]
    row = lax.broadcasted_iota(jnp.int32, (ROWS, LANES), 0)
    for code in range(shifts.shape[0]):
        first, second, third = code // 9 - 1.0, code // 3 % 3 - 1.0, code % 3 - 1.0
        shifts[code] = jnp.where(
            row == X, first, jnp.where(row == Y, second, jnp.where(row == Z, third, 0.0))
        )
    for cell in range(cells):
        targets[cell] = own[cell].T
    copy.wait()

    def one_cell(cell, carry):
        stream = streams.at[cell]
        used = fill_stream(stream, table, shifts, meta, pair_source, pair_shift, cell)
        rounds = (used + DENSITY_UNROLL - 1) // DENSITY_UNROLL

        def one_chunk(base, groups):
            size = groups * ROWS
            mine = targets[cell, pl.ds(base, size), :]
            place = [spread(mine, field) for field in (X, Y, Z)]
            wide = spread(mine, WIDE)
            smooth = 0.5 * wide

            def blocks(index, total):
                for sub in range(DENSITY_UNROLL):
                    s = lambda field: stream[index * DENSITY_UNROLL + sub, field : field + 1, :]
                    apart = [place[c] - s(c) for c in range(3)]
                    square = apart[0] * apart[0] + apart[1] * apart[1] + apart[2] * apart[2]
                    radius = square * lax.rsqrt(jnp.maximum(square, 1e-24))
                    outer = jnp.maximum(wide - radius, 0.0)
                    inner = jnp.maximum(smooth - radius, 0.0)
                    value = outer * outer * outer - 4.0 * (inner * inner * inner)
                    total = total + s(MASS) * value
                return total

            total = lax.fori_loop(0, rounds, blocks, jnp.zeros((size, LANES), jnp.float32))
            parts[pl.ds(base, size), :] = total

        over_targets(meta[cell, 1], one_chunk)
        lines[pl.ds(cell, 1), :] = lane_sums(parts[...])
        return carry

    lax.fori_loop(0, cells, one_cell, 0)
    shape = density.shape
    old_sorted = jnp.zeros(shape, jnp.float32)
    wide = jnp.zeros(shape, jnp.float32)
    chosen = jnp.zeros(shape, jnp.float32)
    row = lax.broadcasted_iota(jnp.int32, shape, 0)
    for cell in range(cells):
        old_sorted = jnp.where(row == cell, own_sent[cell, DENS : DENS + 1, :], old_sorted)
        chosen = jnp.where(row == cell, own_sent[cell, COUNT : COUNT + 1, :], chosen)
        wide = jnp.where(row == cell, own[cell, WIDE : WIDE + 1, :], wide)
    inverse = 2.0 / wide
    inverse = inverse * inverse * inverse
    summed = lines[...] * (0.25 / math.pi) * (inverse * inverse)
    density[...] = jnp.where(active[...] > 0, lane_gather(summed, rank[...]), density_old[...])
    lane = lanes_of(shape).astype(jnp.float32)
    sorted_density[...] = jnp.where(lane < chosen, summed, old_sorted)
    for peer in range(peers):
        for entry in range(per_peer):
            outgoing[place_of(peer, peers), entry : entry + 1, :] = sorted_density[
                pl.ds(export[entry, peer], 1), :
            ]
    outgoing_border[0:1, :] = sorted_density[cells - 1 : cells, :]
    outgoing_border[1:2, :] = sorted_density[0:1, :]


def force_kernel(
    per_peer, pair_source, own, own_sent, incoming, border, streams, own_density, new_density,
    new_border, rank, active, velocity, time_bin,
    acceleration, kicked,
    table, meta_values, meta, meta_sem, stream, targets, more_targets, parts, lines,
):
    cells, peers = own.shape[0], incoming.shape[0]
    copy = fill_meta(meta_values, meta, meta_sem, own_sent, incoming, border, per_peer)

    def entry_of(place, wide, heat, density):
        inverse = 2.0 / wide
        inverse = inverse * inverse * inverse
        table[place, INV6 : INV6 + 1, :] = inverse * inverse
        table[place, HALF : HALF + 1, :] = 0.025 * wide
        table[place, SOUND : SOUND + 1, :] = jnp.sqrt(ADIABATIC * heat)
        table[place, DENS4 : DENS4 + 1, :] = 4.0 * density
        table[place, PRESS : PRESS + 1, :] = heat / density

    for cell in range(cells):
        entry_of(
            cell, own[cell, WIDE : WIDE + 1, :], own_sent[cell, HEAT : HEAT + 1, :],
            own_density[cell : cell + 1, :],
        )
    for peer in range(peers):
        for entry in range(per_peer):
            wide = entry * ROWS + WIDE
            heat = per_peer * ROWS + entry * SENT + HEAT
            entry_of(
                cells + peer * per_peer + entry, incoming[peer, wide : wide + 1, :],
                incoming[peer, heat : heat + 1, :], new_density[peer, entry : entry + 1, :],
            )
    for side in range(2):
        entry_of(
            cells + peers * per_peer + side, border[side, WIDE : WIDE + 1, :],
            border[side, ROWS + HEAT : ROWS + HEAT + 1, :], new_border[side : side + 1, :],
        )
    for cell in range(cells):
        targets[cell] = own[cell].T
        more_targets[cell] = table[cell].T
    copy.wait()

    def one_cell(cell, carry):
        near = streams.at[cell]
        used = fill_stream(stream, table, None, meta, pair_source, None, cell)
        rounds = (used + FORCE_UNROLL - 1) // FORCE_UNROLL

        def one_chunk(base, groups):
            size = groups * ROWS
            mine = targets[cell, pl.ds(base, size), :]
            more = more_targets[cell, pl.ds(base, size), :]
            place = [spread(mine, field) for field in (X, Y, Z)]
            speed = [spread(mine, field) for field in (VX, VY, VZ)]
            wide = spread(mine, WIDE)
            inv6, half_, sound, dens4, press = [spread(more, field) for field in range(5)]

            def blocks(index, totals):
                for sub in range(FORCE_UNROLL):
                    block = index * FORCE_UNROLL + sub
                    s = lambda field: near[block, field : field + 1, :]
                    o = lambda field: stream[block, field : field + 1, :]
                    apart = [place[c] - s(c) for c in range(3)]
                    square = apart[0] * apart[0] + apart[1] * apart[1] + apart[2] * apart[2]
                    inverse = lax.rsqrt(jnp.maximum(square, 1e-24))
                    radius = square * inverse
                    double = radius + radius
                    outer = jnp.maximum(wide - radius, 0.0)
                    inner = jnp.maximum(wide - double, 0.0)
                    slope = inv6 * (outer * outer - inner * inner)
                    outer = jnp.maximum(s(WIDE) - radius, 0.0)
                    inner = jnp.maximum(s(WIDE) - double, 0.0)
                    slope = slope + o(INV6) * (outer * outer - inner * inner)
                    approach = (
                        (speed[0] - s(VX)) * apart[0]
                        + (speed[1] - s(VY)) * apart[1]
                        + (speed[2] - s(VZ)) * apart[2]
                    )
                    half = half_ + o(HALF)
                    mu = half * jnp.minimum(approach, 0.0) * (1.0 / (square + half * half))
                    viscous = mu * (mu - (sound + o(SOUND))) * (1.0 / (dens4 + o(DENS4)))
                    weight = (press + o(PRESS) + viscous) * (slope * (inverse * s(MASS)))
                    totals = tuple(total + weight * a for total, a in zip(totals, apart))
                return totals

            zero = jnp.zeros((size, LANES), jnp.float32)
            totals = lax.fori_loop(0, rounds, blocks, (zero, zero, zero))
            for c in range(3):
                parts[c, pl.ds(base, size), :] = totals[c]

        over_targets(meta[cell, 1], one_chunk)
        for c in range(3):
            lines[c, pl.ds(cell, 1), :] = lane_sums(parts[c])
        return carry

    lax.fori_loop(0, cells, one_cell, 0)
    step = STEP_MAX * jnp.exp2(-time_bin[...].astype(jnp.float32))
    for c in range(3):
        gathered = lane_gather(lines[c] * (0.375 / math.pi), rank[...])
        value = jnp.where(active[...] > 0, gathered, 0.0)
        acceleration[c] = value
        kicked[c] = velocity[c] + value * step


def shards(
    position, velocity, smoothing, particle_mass, energy, density_old, cell_count, active,
    time_bin, pair_source, pair_shift, export,
):
    cells, capacity = smoothing.shape
    peers, per_peer = export.shape
    sources = cells + peers * per_peer + 2
    codes = 27
    f32 = lambda *shape: jax.ShapeDtypeStruct(shape, jnp.float32)
    smem = pl.BlockSpec(memory_space=pltpu.SMEM)
    vmem = pl.BlockSpec(memory_space=pltpu.VMEM)
    hbm = pl.BlockSpec(memory_space=pltpu.HBM)
    whole = pltpu.CompilerParams(vmem_limit_bytes=64 * 2**20)
    params = pltpu.CompilerParams(vmem_limit_bytes=48 * 2**20)
    sent_rows = per_peer * (ROWS + SENT)
    turned = export.T

    arrays = (position, velocity, smoothing, particle_mass, energy, density_old, active)
    own, own_sent, rank, outgoing, border = pl.pallas_call(
        pack_kernel,
        out_shape=(
            f32(cells, ROWS, capacity),
            f32(cells, SENT, capacity),
            jax.ShapeDtypeStruct((cells, capacity), jnp.int32),
            f32(peers, sent_rows, capacity),
            f32(2, ROWS + SENT, capacity),
        ),
        in_specs=[smem] * 2 + [hbm] * 7,
        out_specs=(vmem,) * 5,
        scratch_shapes=[pltpu.VMEM(a.shape, a.dtype) for a in arrays]
        + [pltpu.SemaphoreType.DMA((7,))],
        compiler_params=whole,
        name="pack",
    )(cell_count, turned, *arrays)

    def exchange(pieces):
        high, low = split_of(peers)
        if high == 1 or low == 1:
            return lax.all_to_all(pieces, "cell", split_axis=0, concat_axis=0, tiled=True)
        near = [[h * low + i for i in range(low)] for h in range(high)]
        far = [[h * low + i for h in range(high)] for i in range(low)]
        pieces = pieces.reshape((low, high) + pieces.shape[1:])
        pieces = lax.all_to_all(
            pieces, "cell", split_axis=0, concat_axis=0, axis_index_groups=near, tiled=True
        )
        pieces = lax.all_to_all(
            pieces, "cell", split_axis=1, concat_axis=0, axis_index_groups=far, tiled=True
        )
        return pieces.reshape((peers,) + pieces.shape[2:])

    def swap_border(pieces):
        size = lax.axis_size("region")
        up = [(i, (i + 1) % size) for i in range(size)]
        down = [(j, i) for i, j in up]
        if size == 2:
            return lax.ppermute(pieces, "region", up)
        before = lax.ppermute(pieces[0:1], "region", up)
        after = lax.ppermute(pieces[1:2], "region", down)
        return jnp.concatenate([before, after], axis=0)

    incoming = exchange(outgoing)
    other = swap_border(border)
    blocks = pair_source.shape[1] + SPARE + 1
    meta_rows = -(-sources // 8) * 8
    meta_scratch = [
        pltpu.VMEM((meta_rows, capacity), jnp.int32),
        pltpu.SMEM((meta_rows, capacity), jnp.int32),
        pltpu.SemaphoreType.DMA,
    ]
    density, sorted_density, outgoing_density, border_density, streams = pl.pallas_call(
        functools.partial(density_kernel, per_peer),
        out_shape=(
            f32(cells, capacity),
            f32(cells, capacity),
            f32(peers, per_peer, capacity),
            f32(2, capacity),
            f32(cells, blocks, ROWS, capacity),
        ),
        in_specs=[smem] * 3 + [vmem] * 7,
        out_specs=(vmem,) * 5,
        scratch_shapes=[
            pltpu.VMEM((sources, ROWS, capacity), jnp.float32),
            pltpu.VMEM((codes, ROWS, capacity), jnp.float32),
            *meta_scratch,
            pltpu.VMEM((cells, capacity, ROWS), jnp.float32),
            pltpu.VMEM((capacity, LANES), jnp.float32),
            pltpu.VMEM((cells, capacity), jnp.float32),
        ],
        compiler_params=params,
        name="density",
    )(
        pair_source, pair_shift, turned, own, own_sent, incoming, other, rank, active, density_old,
    )

    new_density = exchange(outgoing_density)
    new_border = swap_border(border_density)

    acceleration, kicked = pl.pallas_call(
        functools.partial(force_kernel, per_peer),
        out_shape=(f32(3, cells, capacity), f32(3, cells, capacity)),
        in_specs=[smem] + [vmem] * 12,
        out_specs=(vmem,) * 2,
        scratch_shapes=[
            pltpu.VMEM((sources, ROWS, capacity), jnp.float32),
            *meta_scratch,
            pltpu.VMEM((blocks, ROWS, capacity), jnp.float32),
            pltpu.VMEM((cells, capacity, ROWS), jnp.float32),
            pltpu.VMEM((cells, capacity, ROWS), jnp.float32),
            pltpu.VMEM((3, capacity, LANES), jnp.float32),
            pltpu.VMEM((3, cells, capacity), jnp.float32),
        ],
        compiler_params=params,
        name="force",
    )(
        pair_source, own, own_sent, incoming, other, streams, sorted_density, new_density,
        new_border, rank, active, velocity, time_bin,
    )
    return density, acceleration, kicked


def solution(mesh):
    rows = P(("region", "cell"), None)
    planes = P(None, ("region", "cell"), None)
    return jax.shard_map(
        shards,
        mesh=mesh,
        in_specs=(
            planes, planes, rows, rows, rows, rows, P(("region", "cell")), rows, rows, rows, rows,
            rows,
        ),
        out_specs=(rows, planes, planes),
        check_vma=False,
    )
```

```python
import functools
import math

import jax
import jax.numpy as jnp
from jax import lax
from jax.experimental import pallas as pl
from jax.experimental.pallas import tpu as pltpu
from jax.sharding import PartitionSpec as P

ADIABATIC = 5.0 / 3.0
STEP_MAX = 0.2
LANES = 128
ROWS = 8
DENSITY_UNROLL = 9
FORCE_UNROLL = 4
SPARE = 8

X, Y, Z, MASS, VX, VY, VZ, WIDE = range(ROWS)
HEAT, DENS, LIVE = range(3)
SENT = 4
INV6, HALF, SOUND, WARM = range(4)
T_INV6, T_HALF, T_SOUND, T_DENS4, T_PRESS = range(5)


def lane_gather(values, index):
    return jnp.take_along_axis(values, index, axis=1, mode="promise_in_bounds")


def lanes_of(shape):
    return lax.broadcasted_iota(jnp.int32, shape, len(shape) - 1)


def pack_kernel(count, export, *refs):
    arrays, (own, own_sent, outgoing, border) = refs[:6], refs[6:10]
    landed, sem = refs[10:-1], refs[-1]
    copies = [
        pltpu.make_async_copy(array, place, sem.at[index])
        for index, (array, place) in enumerate(zip(arrays, landed))
    ]
    for copy in copies:
        copy.start()
    for copy in copies:
        copy.wait()
    position, velocity, smoothing, mass, energy, density_old = landed
    cells = smoothing.shape[0]
    shape = smoothing.shape
    lane = lanes_of(shape)
    row = lax.broadcasted_iota(jnp.int32, shape, 0)
    counts = jnp.zeros(shape, jnp.int32)
    for cell in range(cells):
        counts = jnp.where(row == cell, count[cell], counts)
    mass_live = jnp.where(lane < counts, mass[...], 0.0)
    rows = (
        position[0], position[1], position[2], mass_live,
        40.0 * velocity[0], 40.0 * velocity[1], 40.0 * velocity[2], 2.0 * smoothing[...],
    )
    for field, values in enumerate(rows):
        own[:, field, :] = values
    own_sent[:, HEAT, :] = (ADIABATIC - 1.0) * energy[...]
    own_sent[:, DENS, :] = density_old[...]
    own_sent[:, LIVE, :] = counts.astype(jnp.float32)
    own_sent[:, SENT - 1, :] = jnp.zeros(shape, jnp.float32)
    per_peer, peers = export.shape
    for peer in range(peers):
        for entry in range(per_peer):
            cell = export[entry, peer]
            outgoing[peer, entry * ROWS : (entry + 1) * ROWS, :] = own[cell]
            start = per_peer * ROWS + entry * SENT
            outgoing[peer, start : start + SENT, :] = own_sent[cell]
    for side, cell in enumerate((cells - 1, 0)):
        border[side, 0:ROWS, :] = own[cell]
        border[side, ROWS : ROWS + SENT, :] = own_sent[cell]


def sort_kernel(own, own_sent, active, rank_out, actives, columns, heat_sorted, wide_sorted):
    shape = active.shape
    cells = shape[0]
    lane = lanes_of(shape)
    is_active = active[...] > 0
    ones = jnp.where(is_active, 1.0, 0.0)
    for cell in range(cells):
        actives[cell] = jnp.sum(ones[cell : cell + 1, :]).astype(jnp.int32)
    square = (LANES, LANES)
    upper = lax.broadcasted_iota(jnp.int32, square, 0) <= lanes_of(square)
    upper = jnp.where(upper, 1.0, 0.0).astype(jnp.bfloat16)
    seen = jnp.dot(ones.astype(jnp.bfloat16), upper, preferred_element_type=jnp.float32)
    seen = seen.astype(jnp.int32)
    chosen = lane_gather(seen, jnp.full(shape, LANES - 1, jnp.int32))
    others = lane + 1 - seen
    rank_out[...] = jnp.where(is_active, seen - 1, chosen + others - 1)
    first_part = lane < chosen
    wanted = jnp.where(first_part, lane, lane - chosen)
    slot = jnp.zeros(shape, jnp.int32)
    step = LANES // 2
    while step:
        probe = slot + (step - 1)
        found = jnp.where(first_part, lane_gather(seen, probe), lane_gather(others, probe))
        slot = jnp.where(found <= wanted, slot + step, slot)
        step //= 2
    for cell in range(cells):
        order = jnp.broadcast_to(slot[cell : cell + 1, :], (ROWS, LANES))
        tile = lane_gather(own[cell], order)
        columns[cell] = tile.T
        wide_sorted[cell : cell + 1, :] = tile[WIDE : WIDE + 1, :]
        warm = jnp.broadcast_to(own_sent[cell, HEAT : HEAT + 1, :], (ROWS, LANES))
        heat_sorted[cell : cell + 1, :] = lane_gather(warm, order)[0:1, :]


def source_tiles(own, incoming, border, per_peer):
    cells, peers = own[0].shape[0], incoming.shape[0]
    for cell in range(cells):
        yield cell, lambda c=cell: own[0][c], lambda c=cell: own[1][c]
    for peer in range(peers):
        for entry in range(per_peer):
            near, sent = entry * ROWS, per_peer * ROWS + entry * SENT
            yield (
                cells + peer * per_peer + entry,
                lambda p=peer, n=near: incoming[p, n : n + ROWS, :],
                lambda p=peer, n=sent: incoming[p, n : n + SENT, :],
            )
    for side in range(2):
        yield (
            cells + peers * per_peer + side,
            lambda b=side: border[b, 0:ROWS, :],
            lambda b=side: border[b, ROWS : ROWS + SENT, :],
        )


def fill_shifts(shifts):
    row = lax.broadcasted_iota(jnp.int32, (ROWS, LANES), 0)
    for code in range(shifts.shape[0]):
        first, second, third = code // 9 - 1.0, code // 3 % 3 - 1.0, code % 3 - 1.0
        shifts[code] = jnp.where(
            row == X, first, jnp.where(row == Y, second, jnp.where(row == Z, third, 0.0))
        )


def fill_streams(streams, tables, counts, sources, cell):
    shape = (ROWS, LANES)
    lane = lanes_of(shape)
    pairs = sources.shape[1]
    start = jnp.int32(0)
    starts, rolled = [], []
    for pair in range(pairs):
        source = sources[cell, pair]
        starts.append(start)
        rolled.append([pltpu.roll(load(source, pair), start & (LANES - 1), 1) for load in tables])
        start = start + counts[source >> 7, source & (LANES - 1)]
    starts.append(start)
    current = [jnp.zeros(shape, jnp.float32) for _ in tables]
    for pair in range(pairs):
        block = starts[pair] >> 7
        fresh = lane >= (starts[pair] & (LANES - 1))
        full = (starts[pair + 1] >> 7) > block
        for which, stream in enumerate(streams):
            merged = jnp.where(fresh, rolled[pair][which], current[which])
            stream[block] = merged
            current[which] = jnp.where(full, rolled[pair][which], merged)
    block = start >> 7
    for which, stream in enumerate(streams):
        stream[block] = jnp.where(lane < (start & (LANES - 1)), current[which], 0.0)
        for extra in range(1, SPARE):
            stream[block + extra] = jnp.zeros(shape, jnp.float32)
    return (start + LANES - 1) >> 7


def spread(values, field):
    return jnp.broadcast_to(values[:, field : field + 1], (values.shape[0], LANES))


def over_targets(active, one_chunk):
    groups = (active + ROWS - 1) // ROWS

    def large(chunk, carry):
        one_chunk(pl.multiple_of(chunk * 4 * ROWS, ROWS), 4)
        return carry

    lax.fori_loop(0, groups // 4, large, 0)
    for size in (2, 1):

        @pl.when((groups & size) != 0)
        def _(size=size):
            done = groups & -(2 * size)
            one_chunk(pl.multiple_of(done * ROWS, ROWS), size)


def density_kernel(
    per_peer, pair_source, pair_shift, export, actives, own, own_sent, incoming, border, rank,
    columns, wide_sorted, active, density_old,
    density, sorted_density, outgoing, outgoing_border,
    table, shifts, sums, lines,
):
    cells, peers = own.shape[0], incoming.shape[0]
    for place, near, _ in source_tiles((own, own_sent), incoming, border, per_peer):
        table[place] = near()
    fill_shifts(shifts)

    def one_cell(cell, carry):
        def one_chunk(base, groups):
            size = groups * ROWS
            mine = columns[cell, pl.ds(base, size), :]
            place = [spread(mine, field) for field in (X, Y, Z)]
            wide = spread(mine, WIDE)
            smooth = 0.5 * wide

            def blocks(index, total):
                for sub in range(DENSITY_UNROLL):
                    pair = index * DENSITY_UNROLL + sub
                    source, code = pair_source[cell, pair], pair_shift[cell, pair]
                    s = lambda field: table[source, field : field + 1, :]
                    shift = lambda field: shifts[code, field : field + 1, :]
                    apart = [place[c] - (s(c) + shift(c)) for c in range(3)]
                    square = apart[0] * apart[0] + apart[1] * apart[1] + apart[2] * apart[2]
                    radius = square * lax.rsqrt(jnp.maximum(square, 1e-24))
                    outer = jnp.maximum(wide - radius, 0.0)
                    inner = jnp.maximum(smooth - radius, 0.0)
                    value = outer * outer * outer - 4.0 * (inner * inner * inner)
                    total = total + s(MASS) * value
                return total

            total = lax.fori_loop(
                0, pair_source.shape[1] // DENSITY_UNROLL, blocks,
                jnp.zeros((size, LANES), jnp.float32),
            )
            sums[cell, pl.ds(base, size), 0:1] = jnp.sum(total, axis=1, keepdims=True)

        over_targets(actives[cell], one_chunk)
        return carry

    lax.fori_loop(0, cells, one_cell, 0)
    for cell in range(cells):
        lines[cell : cell + 1, :] = sums[cell].T[0:1, :]
    inverse = 2.0 / wide_sorted[...]
    inverse = inverse * inverse * inverse
    summed = lines[...] * (0.25 / math.pi) * (inverse * inverse)
    sorted_density[...] = summed
    density[...] = jnp.where(active[...] > 0, lane_gather(summed, rank[...]), density_old[...])
    for peer in range(peers):
        for entry in range(per_peer):
            outgoing[peer, entry : entry + 1, :] = density[pl.ds(export[entry, peer], 1), :]
    outgoing_border[0:1, :] = density[cells - 1 : cells, :]
    outgoing_border[1:2, :] = density[0:1, :]


def stream_kernel(
    per_peer, pair_source, pair_shift, own, own_sent, incoming, border,
    near_streams, far_streams, counts,
    near_table, far_table, shifts, count_row, sem,
):
    lane = lanes_of((1, LANES))
    packed = [jnp.zeros((1, LANES), jnp.float32) for _ in range(count_row.shape[0])]
    for place, near, sent in source_tiles((own, own_sent), incoming, border, per_peer):
        tile, other = near(), sent()
        near_table[place] = tile
        wide, heat = tile[WIDE : WIDE + 1, :], other[HEAT : HEAT + 1, :]
        inverse = 2.0 / wide
        inverse = inverse * inverse * inverse
        far_table[place, INV6 : INV6 + 1, :] = inverse * inverse
        far_table[place, HALF : HALF + 1, :] = 0.025 * wide
        far_table[place, SOUND : SOUND + 1, :] = jnp.sqrt(ADIABATIC * heat)
        far_table[place, WARM : WARM + 1, :] = heat
        line = place // LANES
        packed[line] = jnp.where(lane == place % LANES, other[LIVE : LIVE + 1, :], packed[line])
    for line, values in enumerate(packed):
        count_row[line : line + 1, :] = values.astype(jnp.int32)
    copy = pltpu.make_async_copy(count_row, counts, sem)
    copy.start()
    fill_shifts(shifts)
    copy.wait()

    def one_cell(cell, carry):
        tables = (
            lambda source, pair: near_table[source] + shifts[pair_shift[cell, pair]],
            lambda source, pair: far_table[source],
        )
        fill_streams(
            (near_streams.at[cell], far_streams.at[cell]), tables, counts, pair_source, cell
        )
        return carry

    lax.fori_loop(0, own.shape[0], one_cell, 0)


def force_kernel(
    per_peer, pair_source, counts, actives, near_streams, far_streams, columns, wide_sorted,
    heat_sorted, own_density, sorted_density, new_density, new_border, rank, active, velocity,
    time_bin,
    acceleration, kicked,
    table, stream, more, sums, lines,
):
    cells, peers = own_density.shape[0], new_density.shape[0]
    for cell in range(cells):
        table[cell, 0:1, :] = own_density[cell : cell + 1, :]
    for peer in range(peers):
        for entry in range(per_peer):
            place = cells + peer * per_peer + entry
            table[place, 0:1, :] = new_density[peer, entry : entry + 1, :]
    for side in range(2):
        table[cells + peers * per_peer + side, 0:1, :] = new_border[side : side + 1, :]
    inverse = 2.0 / wide_sorted[...]
    inverse = inverse * inverse * inverse
    row = lax.broadcasted_iota(jnp.int32, (ROWS, LANES), 0)
    fields = (
        inverse * inverse, 0.025 * wide_sorted[...], jnp.sqrt(ADIABATIC * heat_sorted[...]),
        4.0 * sorted_density[...], heat_sorted[...] / sorted_density[...],
    )
    for cell in range(cells):
        tile = jnp.zeros((ROWS, LANES), jnp.float32)
        for which, values in enumerate(fields):
            tile = jnp.where(row == which, values[cell : cell + 1, :], tile)
        more[cell] = tile.T

    def one_cell(cell, carry):
        near, far = near_streams.at[cell], far_streams.at[cell]
        used = fill_streams(
            (stream,), (lambda source, pair: table[source],), counts, pair_source, cell
        )
        rounds = (used + FORCE_UNROLL - 1) // FORCE_UNROLL

        def one_chunk(base, groups):
            size = groups * ROWS
            mine = columns[cell, pl.ds(base, size), :]
            mine_more = more[cell, pl.ds(base, size), :]
            place = [spread(mine, field) for field in (X, Y, Z)]
            speed = [spread(mine, field) for field in (VX, VY, VZ)]
            wide = spread(mine, WIDE)
            inv6, half_, sound, dens4, press = [spread(mine_more, field) for field in range(5)]

            def blocks(index, totals):
                for sub in range(FORCE_UNROLL):
                    block = index * FORCE_UNROLL + sub
                    s = lambda field: near[block, field : field + 1, :]
                    o = lambda field: far[block, field : field + 1, :]
                    dens = stream[block, 0:1, :]
                    their_press = o(WARM) * (1.0 / jnp.maximum(dens, 1e-30))
                    apart = [place[c] - s(c) for c in range(3)]
                    square = apart[0] * apart[0] + apart[1] * apart[1] + apart[2] * apart[2]
                    inverse = lax.rsqrt(jnp.maximum(square, 1e-24))
                    radius = square * inverse
                    double = radius + radius
                    outer = jnp.maximum(wide - radius, 0.0)
                    inner = jnp.maximum(wide - double, 0.0)
                    slope = inv6 * (outer * outer - inner * inner)
                    outer = jnp.maximum(s(WIDE) - radius, 0.0)
                    inner = jnp.maximum(s(WIDE) - double, 0.0)
                    slope = slope + o(INV6) * (outer * outer - inner * inner)
                    approach = (
                        (speed[0] - s(VX)) * apart[0]
                        + (speed[1] - s(VY)) * apart[1]
                        + (speed[2] - s(VZ)) * apart[2]
                    )
                    half = half_ + o(HALF)
                    mu = half * jnp.minimum(approach, 0.0) * (1.0 / (square + half * half))
                    viscous = mu * (mu - (sound + o(SOUND))) * (1.0 / (dens4 + 4.0 * dens))
                    weight = (press + their_press + viscous) * (slope * (inverse * s(MASS)))
                    totals = tuple(total + weight * a for total, a in zip(totals, apart))
                return totals

            zero = jnp.zeros((size, LANES), jnp.float32)
            totals = lax.fori_loop(0, rounds, blocks, (zero, zero, zero))
            for c in range(3):
                sums[cell, pl.ds(base, size), c : c + 1] = jnp.sum(
                    totals[c], axis=1, keepdims=True
                )

        over_targets(actives[cell], one_chunk)
        return carry

    lax.fori_loop(0, cells, one_cell, 0)
    for cell in range(cells):
        turned = sums[cell].T
        for c in range(3):
            lines[c, cell : cell + 1, :] = turned[c : c + 1, :]
    step = STEP_MAX * jnp.exp2(-time_bin[...].astype(jnp.float32))
    for c in range(3):
        gathered = lane_gather(lines[c] * (0.375 / math.pi), rank[...])
        value = jnp.where(active[...] > 0, gathered, 0.0)
        acceleration[c] = value
        kicked[c] = velocity[c] + value * step


def shards(
    position, velocity, smoothing, particle_mass, energy, density_old, cell_count, active,
    time_bin, pair_source, pair_shift, export,
):
    cells, capacity = smoothing.shape
    peers, per_peer = export.shape
    sources = cells + peers * per_peer + 2
    codes = 27
    f32 = lambda *shape: jax.ShapeDtypeStruct(shape, jnp.float32)
    smem = pl.BlockSpec(memory_space=pltpu.SMEM)
    vmem = pl.BlockSpec(memory_space=pltpu.VMEM)
    hbm = pl.BlockSpec(memory_space=pltpu.HBM)
    whole = pltpu.CompilerParams(vmem_limit_bytes=64 * 2**20)
    params = pltpu.CompilerParams(vmem_limit_bytes=40 * 2**20)
    i32 = lambda *shape: jax.ShapeDtypeStruct(shape, jnp.int32)
    sent_rows = per_peer * (ROWS + SENT)
    turned = export.T

    arrays = (position, velocity, smoothing, particle_mass, energy, density_old)
    own, own_sent, outgoing, border = pl.pallas_call(
        pack_kernel,
        out_shape=(
            f32(cells, ROWS, capacity),
            f32(cells, SENT, capacity),
            f32(peers, sent_rows, capacity),
            f32(2, ROWS + SENT, capacity),
        ),
        in_specs=[smem] * 2 + [hbm] * 6,
        out_specs=(vmem,) * 4,
        scratch_shapes=[pltpu.VMEM(a.shape, a.dtype) for a in arrays]
        + [pltpu.SemaphoreType.DMA((6,))],
        compiler_params=whole,
        name="pack",
    )(cell_count, turned, *arrays)

    def exchange(pieces):
        return lax.all_to_all(pieces, "cell", split_axis=0, concat_axis=0, tiled=True)

    def swap_border(pieces):
        size = lax.axis_size("region")
        up = [(i, (i + 1) % size) for i in range(size)]
        down = [(j, i) for i, j in up]
        if size == 2:
            return lax.ppermute(pieces, "region", up)
        before = lax.ppermute(pieces[0:1], "region", up)
        after = lax.ppermute(pieces[1:2], "region", down)
        return jnp.concatenate([before, after], axis=0)

    incoming = exchange(outgoing)
    other = swap_border(border)
    rank, actives, columns, heat_sorted, wide_sorted = pl.pallas_call(
        sort_kernel,
        out_shape=(
            i32(cells, capacity),
            i32(cells),
            f32(cells, capacity, ROWS),
            f32(cells, capacity),
            f32(cells, capacity),
        ),
        in_specs=[vmem] * 3,
        out_specs=(vmem, smem, vmem, vmem, vmem),
        compiler_params=params,
        name="sort",
    )(own, own_sent, active)

    density, sorted_density, outgoing_density, border_density = pl.pallas_call(
        functools.partial(density_kernel, per_peer),
        out_shape=(
            f32(cells, capacity),
            f32(cells, capacity),
            f32(peers, per_peer, capacity),
            f32(2, capacity),
        ),
        in_specs=[smem] * 4 + [vmem] * 9,
        out_specs=(vmem,) * 4,
        scratch_shapes=[
            pltpu.VMEM((sources, ROWS, capacity), jnp.float32),
            pltpu.VMEM((codes, ROWS, capacity), jnp.float32),
            pltpu.VMEM((cells, capacity, ROWS), jnp.float32),
            pltpu.VMEM((cells, capacity), jnp.float32),
        ],
        compiler_params=params,
        name="density",
    )(
        pair_source, pair_shift, turned, actives, own, own_sent, incoming, other, rank, columns,
        wide_sorted, active, density_old,
    )

    new_density = exchange(outgoing_density)
    new_border = swap_border(border_density)
    blocks = pair_source.shape[1] + SPARE
    count_rows = -(-sources // capacity)
    near_streams, far_streams, counts = pl.pallas_call(
        functools.partial(stream_kernel, per_peer),
        out_shape=(
            f32(cells, blocks, ROWS, capacity),
            f32(cells, blocks, ROWS, capacity),
            i32(count_rows, capacity),
        ),
        in_specs=[smem] * 2 + [vmem] * 4,
        out_specs=(vmem, vmem, smem),
        scratch_shapes=[
            pltpu.VMEM((sources, ROWS, capacity), jnp.float32),
            pltpu.VMEM((sources, ROWS, capacity), jnp.float32),
            pltpu.VMEM((codes, ROWS, capacity), jnp.float32),
            pltpu.VMEM((count_rows, capacity), jnp.int32),
            pltpu.SemaphoreType.DMA,
        ],
        compiler_params=params,
        name="streams",
    )(pair_source, pair_shift, own, own_sent, incoming, other)

    acceleration, kicked = pl.pallas_call(
        functools.partial(force_kernel, per_peer),
        out_shape=(f32(3, cells, capacity), f32(3, cells, capacity)),
        in_specs=[smem] * 3 + [vmem] * 13,
        out_specs=(vmem,) * 2,
        scratch_shapes=[
            pltpu.VMEM((sources, ROWS, capacity), jnp.float32),
            pltpu.VMEM((blocks, ROWS, capacity), jnp.float32),
            pltpu.VMEM((cells, capacity, ROWS), jnp.float32),
            pltpu.VMEM((cells, capacity, ROWS), jnp.float32),
            pltpu.VMEM((3, cells, capacity), jnp.float32),
        ],
        compiler_params=params,
        name="force",
    )(
        pair_source, counts, actives, near_streams, far_streams, columns, wide_sorted, heat_sorted,
        density, sorted_density, new_density, new_border, rank, active, velocity, time_bin,
    )
    return density, acceleration, kicked


def solution(mesh):
    rows = P(("region", "cell"), None)
    planes = P(None, ("region", "cell"), None)
    return jax.shard_map(
        shards,
        mesh=mesh,
        in_specs=(
            planes, planes, rows, rows, rows, rows, P(("region", "cell")), rows, rows, rows, rows,
            rows,
        ),
        out_specs=(rows, planes, planes),
        check_vma=False,
    )
```

```python
import functools
import math

import jax
import jax.numpy as jnp
from jax import lax
from jax.experimental import pallas as pl
from jax.experimental.pallas import tpu as pltpu
from jax.sharding import PartitionSpec as P

ADIABATIC = 5.0 / 3.0
STEP_MAX = 0.2
LANES = 128
ROWS = 8
FORCE_UNROLL = 10
SPARE = FORCE_UNROLL

X, Y, Z, MASS, VX, VY, VZ, WIDE = range(ROWS)
HEAT, DENS, LIVE = range(3)
SENT = 4
INV6, HALF, SOUND, WARM = range(4)


def lane_gather(values, index):
    return jnp.take_along_axis(values, index, axis=1, mode="promise_in_bounds")


def lanes_of(shape):
    return lax.broadcasted_iota(jnp.int32, shape, len(shape) - 1)


def start_copies(arrays, landed, sem):
    copies = [
        pltpu.make_async_copy(array, place, sem.at[index])
        for index, (array, place) in enumerate(zip(arrays, landed))
    ]
    for copy in copies:
        copy.start()
    return copies


def pack_kernel(count, export, *refs):
    arrays, (own, own_sent, outgoing, border) = refs[:6], refs[6:10]
    landed, sem = refs[10:-1], refs[-1]
    for copy in start_copies(arrays, landed, sem):
        copy.wait()
    position, velocity, smoothing, mass, energy, density_old = landed
    cells = smoothing.shape[0]
    shape = smoothing.shape
    lane = lanes_of(shape)
    row = lax.broadcasted_iota(jnp.int32, shape, 0)
    counts = jnp.zeros(shape, jnp.int32)
    for cell in range(cells):
        counts = jnp.where(row == cell, count[cell], counts)
    mass_live = jnp.where(lane < counts, mass[...], 0.0)
    rows = (
        position[0], position[1], position[2], mass_live,
        40.0 * velocity[0], 40.0 * velocity[1], 40.0 * velocity[2], 2.0 * smoothing[...],
    )
    for field, values in enumerate(rows):
        own[:, field, :] = values
    own_sent[:, HEAT, :] = (ADIABATIC - 1.0) * energy[...]
    own_sent[:, DENS, :] = density_old[...]
    own_sent[:, LIVE, :] = counts.astype(jnp.float32)
    own_sent[:, SENT - 1, :] = jnp.zeros(shape, jnp.float32)
    per_peer, peers = export.shape
    for peer in range(peers):
        for entry in range(per_peer):
            cell = export[entry, peer]
            outgoing[peer, entry * ROWS : (entry + 1) * ROWS, :] = own[cell]
            start = per_peer * ROWS + entry * SENT
            outgoing[peer, start : start + SENT, :] = own_sent[cell]
    for side, cell in enumerate((cells - 1, 0)):
        border[side, 0:ROWS, :] = own[cell]
        border[side, ROWS : ROWS + SENT, :] = own_sent[cell]


def sort_kernel(*refs):
    (rank_out, actives, columns, heat_sorted, wide_sorted), landed, sem = refs[3:8], refs[8:11], refs[11]
    for copy in start_copies(refs[:3], landed, sem):
        copy.wait()
    own, own_sent, active = landed
    shape = active.shape
    cells = shape[0]
    lane = lanes_of(shape)
    is_active = active[...] > 0
    ones = jnp.where(is_active, 1.0, 0.0)
    for cell in range(cells):
        actives[cell] = jnp.sum(ones[cell : cell + 1, :]).astype(jnp.int32)
    square = (LANES, LANES)
    upper = lax.broadcasted_iota(jnp.int32, square, 0) <= lanes_of(square)
    upper = jnp.where(upper, 1.0, 0.0).astype(jnp.bfloat16)
    seen = jnp.dot(ones.astype(jnp.bfloat16), upper, preferred_element_type=jnp.float32)
    seen = seen.astype(jnp.int32)
    chosen = lane_gather(seen, jnp.full(shape, LANES - 1, jnp.int32))
    others = lane + 1 - seen
    rank_out[...] = jnp.where(is_active, seen - 1, chosen + others - 1)
    first_part = lane < chosen
    wanted = jnp.where(first_part, lane, lane - chosen)
    slot = jnp.zeros(shape, jnp.int32)
    step = LANES // 2
    while step:
        probe = slot + (step - 1)
        found = jnp.where(first_part, lane_gather(seen, probe), lane_gather(others, probe))
        slot = jnp.where(found <= wanted, slot + step, slot)
        step //= 2
    for cell in range(cells):
        order = jnp.broadcast_to(slot[cell : cell + 1, :], (ROWS, LANES))
        tile = lane_gather(own[cell], order)
        columns[cell] = tile.T
        wide_sorted[cell : cell + 1, :] = tile[WIDE : WIDE + 1, :]
        warm = jnp.broadcast_to(own_sent[cell, HEAT : HEAT + 1, :], (ROWS, LANES))
        heat_sorted[cell : cell + 1, :] = lane_gather(warm, order)[0:1, :]


def source_tiles(own, incoming, border, per_peer):
    cells, peers = own[0].shape[0], incoming.shape[0]
    for cell in range(cells):
        yield cell, lambda c=cell: own[0][c], lambda c=cell: own[1][c]
    for peer in range(peers):
        for entry in range(per_peer):
            near, sent = entry * ROWS, per_peer * ROWS + entry * SENT
            yield (
                cells + peer * per_peer + entry,
                lambda p=peer, n=near: incoming[p, n : n + ROWS, :],
                lambda p=peer, n=sent: incoming[p, n : n + SENT, :],
            )
    for side in range(2):
        yield (
            cells + peers * per_peer + side,
            lambda b=side: border[b, 0:ROWS, :],
            lambda b=side: border[b, ROWS : ROWS + SENT, :],
        )


def fill_shifts(shifts):
    row = lax.broadcasted_iota(jnp.int32, (ROWS, LANES), 0)
    for code in range(shifts.shape[0]):
        first, second, third = code // 9 - 1.0, code // 3 % 3 - 1.0, code % 3 - 1.0
        shifts[code] = jnp.where(
            row == X, first, jnp.where(row == Y, second, jnp.where(row == Z, third, 0.0))
        )


def fill_streams(streams, tables, sources, starts, cell):
    shape = (ROWS, LANES)
    lane = lanes_of(shape)
    pairs = sources.shape[1]
    rolled = []
    for pair in range(pairs):
        source = sources[cell, pair]
        offset = starts[cell, pair] & (LANES - 1)
        rolled.append([pltpu.roll(load(source, pair), offset, 1) for load in tables])
    for pair in range(pairs):
        start = starts[cell, pair]
        block = start >> 7
        fresh = lane >= (start & (LANES - 1))
        for which, stream in enumerate(streams):
            stream[block + 1] = rolled[pair][which]
            pltpu.store(stream.at[block], rolled[pair][which], mask=fresh)
    end = starts[cell, pairs]
    block = end >> 7
    for stream in streams:
        stream[block] = jnp.where(lane < (end & (LANES - 1)), stream[block], 0.0)
        for extra in range(1, SPARE):
            stream[block + extra] = jnp.zeros(shape, jnp.float32)
    return (end + LANES - 1) >> 7


def spread(values, field):
    return jnp.broadcast_to(values[:, field : field + 1], (values.shape[0], LANES))


def over_targets(active, one_chunk):
    groups = (active + ROWS - 1) // ROWS

    def large(chunk, carry):
        one_chunk(pl.multiple_of(chunk * 4 * ROWS, ROWS), 4)
        return carry

    lax.fori_loop(0, groups // 4, large, 0)
    for size in (2, 1):

        @pl.when((groups & size) != 0)
        def _(size=size):
            done = groups & -(2 * size)
            one_chunk(pl.multiple_of(done * ROWS, ROWS), size)


def density_kernel(per_peer, pair_source, pair_shift, export, actives, *refs):
    arrays, (density, sorted_density, outgoing, outgoing_border) = refs[:9], refs[9:13]
    landed, (sem, table, shifts, sums, lines) = refs[13:22], refs[22:]
    copies = start_copies(arrays, landed, sem)
    fill_shifts(shifts)
    for copy in copies:
        copy.wait()
    own, own_sent, incoming, border, rank, columns, wide_sorted, active, density_old = landed
    cells, peers = own.shape[0], incoming.shape[0]
    for place, near, _ in source_tiles((own, own_sent), incoming, border, per_peer):
        table[place] = near()

    def one_cell(cell, carry):
        def one_chunk(base, groups):
            size = groups * ROWS
            mine = columns[cell, pl.ds(base, size), :]
            place = [spread(mine, field) for field in (X, Y, Z)]
            wide = spread(mine, WIDE)
            smooth = 0.5 * wide

            total = jnp.zeros((size, LANES), jnp.float32)
            for pair in range(pair_source.shape[1]):
                source, code = pair_source[cell, pair], pair_shift[cell, pair]
                s = lambda field: table[source, field : field + 1, :]
                shift = lambda field: shifts[code, field : field + 1, :]
                apart = [place[c] - (s(c) + shift(c)) for c in range(3)]
                square = apart[0] * apart[0] + apart[1] * apart[1] + apart[2] * apart[2]
                radius = square * lax.rsqrt(jnp.maximum(square, 1e-24))
                outer = jnp.maximum(wide - radius, 0.0)
                inner = jnp.maximum(smooth - radius, 0.0)
                value = outer * outer * outer - 4.0 * (inner * inner * inner)
                total = total + s(MASS) * value
            sums[cell, pl.ds(base, size), 0:1] = jnp.sum(total, axis=1, keepdims=True)

        over_targets(actives[cell], one_chunk)
        return carry

    lax.fori_loop(0, cells, one_cell, 0)
    for cell in range(cells):
        lines[cell : cell + 1, :] = sums[cell].T[0:1, :]
    inverse = 2.0 / wide_sorted[...]
    inverse = inverse * inverse * inverse
    summed = lines[...] * (0.25 / math.pi) * (inverse * inverse)
    sorted_density[...] = summed
    density[...] = jnp.where(active[...] > 0, lane_gather(summed, rank[...]), density_old[...])
    for peer in range(peers):
        for entry in range(per_peer):
            outgoing[peer, entry : entry + 1, :] = density[pl.ds(export[entry, peer], 1), :]
    outgoing_border[0:1, :] = density[cells - 1 : cells, :]
    outgoing_border[1:2, :] = density[0:1, :]


def stream_kernel(per_peer, pair_source, pair_shift, *refs):
    arrays, (near_streams, far_streams, starts, more) = refs[:7], refs[7:11]
    landed, (sems, near_table, far_table, shifts, count_row, counts, sem) = refs[11:18], refs[18:]
    copies = start_copies(arrays, landed, sems)
    fill_shifts(shifts)
    for copy in copies:
        copy.wait()
    own, own_sent, incoming, border, wide_sorted, heat_sorted, sorted_density = landed
    lane = lanes_of((1, LANES))
    packed = [jnp.zeros((1, LANES), jnp.float32) for _ in range(count_row.shape[0])]
    for place, near, sent in source_tiles((own, own_sent), incoming, border, per_peer):
        tile, other = near(), sent()
        near_table[place] = tile
        wide, heat = tile[WIDE : WIDE + 1, :], other[HEAT : HEAT + 1, :]
        inverse = 2.0 / wide
        inverse = inverse * inverse * inverse
        far_table[place, INV6 : INV6 + 1, :] = inverse * inverse
        far_table[place, HALF : HALF + 1, :] = 0.025 * wide
        far_table[place, SOUND : SOUND + 1, :] = jnp.sqrt(ADIABATIC * heat)
        far_table[place, WARM : WARM + 1, :] = heat
        line = place // LANES
        packed[line] = jnp.where(lane == place % LANES, other[LIVE : LIVE + 1, :], packed[line])
    for line, values in enumerate(packed):
        count_row[line : line + 1, :] = values.astype(jnp.int32)
    copy = pltpu.make_async_copy(count_row, counts, sem)
    copy.start()
    inverse = 2.0 / wide_sorted[...]
    inverse = inverse * inverse * inverse
    row = lax.broadcasted_iota(jnp.int32, (ROWS, LANES), 0)
    fields = (
        inverse * inverse, 0.025 * wide_sorted[...], jnp.sqrt(ADIABATIC * heat_sorted[...]),
        4.0 * sorted_density[...], heat_sorted[...] / sorted_density[...],
    )
    for cell in range(own.shape[0]):
        tile = jnp.zeros((ROWS, LANES), jnp.float32)
        for which, values in enumerate(fields):
            tile = jnp.where(row == which, values[cell : cell + 1, :], tile)
        more[cell] = tile.T
    copy.wait()

    def one_cell(cell, carry):
        tables = (
            lambda source, pair: near_table[source] + shifts[pair_shift[cell, pair]],
            lambda source, pair: far_table[source],
        )
        start = jnp.int32(0)
        for pair in range(pair_source.shape[1]):
            starts[cell, pair] = start
            source = pair_source[cell, pair]
            start = start + counts[source >> 7, source & (LANES - 1)]
        starts[cell, pair_source.shape[1]] = start
        fill_streams(
            (near_streams.at[cell], far_streams.at[cell]), tables, pair_source, starts, cell
        )
        return carry

    lax.fori_loop(0, own.shape[0], one_cell, 0)


def force_kernel(per_peer, pair_source, starts, actives, *refs):
    arrays, streams, (acceleration, kicked) = refs[:9], refs[9:11], refs[11:13]
    landed, sem, landed_streams, stream_sems = refs[13:22], refs[22], refs[23:25], refs[25:27]
    table, stream, sums, lines = refs[27:]
    copies = start_copies(arrays, landed, sem)

    def stream_copies(cell):
        return [
            pltpu.make_async_copy(source.at[cell], place.at[cell], sems.at[cell])
            for source, place, sems in zip(streams, landed_streams, stream_sems)
        ]

    for cell in range(actives.shape[0]):
        for copy in stream_copies(cell):
            copy.start()
    for copy in copies:
        copy.wait()
    columns, more, own_density, new_density, new_border, rank, active, velocity, time_bin = landed
    near_streams, far_streams = landed_streams
    cells, peers = own_density.shape[0], new_density.shape[0]
    for cell in range(cells):
        table[cell, 0:1, :] = own_density[cell : cell + 1, :]
    for peer in range(peers):
        for entry in range(per_peer):
            place = cells + peer * per_peer + entry
            table[place, 0:1, :] = new_density[peer, entry : entry + 1, :]
    for side in range(2):
        table[cells + peers * per_peer + side, 0:1, :] = new_border[side : side + 1, :]

    def one_cell(cell, carry):
        near, far = near_streams.at[cell], far_streams.at[cell]
        used = fill_streams(
            (stream,), (lambda source, pair: table[source],), pair_source, starts, cell
        )
        for copy in stream_copies(cell):
            copy.wait()
        rounds = (used + FORCE_UNROLL - 1) // FORCE_UNROLL

        def one_chunk(base, groups):
            size = groups * ROWS
            mine = columns[cell, pl.ds(base, size), :]
            mine_more = more[cell, pl.ds(base, size), :]
            place = [spread(mine, field) for field in (X, Y, Z)]
            speed = [spread(mine, field) for field in (VX, VY, VZ)]
            wide = spread(mine, WIDE)
            inv6, half_, sound, dens4, press = [spread(mine_more, field) for field in range(5)]

            def blocks(index, totals):
                for sub in range(FORCE_UNROLL):
                    block = index * FORCE_UNROLL + sub
                    s = lambda field: near[block, field : field + 1, :]
                    o = lambda field: far[block, field : field + 1, :]
                    dens = stream[block, 0:1, :]
                    their_press = o(WARM) * (1.0 / jnp.maximum(dens, 1e-30))
                    apart = [place[c] - s(c) for c in range(3)]
                    square = apart[0] * apart[0] + apart[1] * apart[1] + apart[2] * apart[2]
                    inverse = lax.rsqrt(jnp.maximum(square, 1e-24))
                    radius = square * inverse
                    double = radius + radius
                    outer = jnp.maximum(wide - radius, 0.0)
                    inner = jnp.maximum(wide - double, 0.0)
                    slope = inv6 * (outer * outer - inner * inner)
                    outer = jnp.maximum(s(WIDE) - radius, 0.0)
                    inner = jnp.maximum(s(WIDE) - double, 0.0)
                    slope = slope + o(INV6) * (outer * outer - inner * inner)
                    approach = (
                        (speed[0] - s(VX)) * apart[0]
                        + (speed[1] - s(VY)) * apart[1]
                        + (speed[2] - s(VZ)) * apart[2]
                    )
                    half = half_ + o(HALF)
                    mu = half * jnp.minimum(approach, 0.0) * (1.0 / (square + half * half))
                    viscous = mu * (mu - (sound + o(SOUND))) * (1.0 / (dens4 + 4.0 * dens))
                    weight = (press + their_press + viscous) * (slope * (inverse * s(MASS)))
                    totals = tuple(total + weight * a for total, a in zip(totals, apart))
                return totals

            zero = jnp.zeros((size, LANES), jnp.float32)
            totals = lax.fori_loop(0, rounds, blocks, (zero, zero, zero))
            for c in range(3):
                sums[cell, pl.ds(base, size), c : c + 1] = jnp.sum(
                    totals[c], axis=1, keepdims=True
                )

        over_targets(actives[cell], one_chunk)
        return carry

    lax.fori_loop(0, cells, one_cell, 0)
    for cell in range(cells):
        turned = sums[cell].T
        for c in range(3):
            lines[c, cell : cell + 1, :] = turned[c : c + 1, :]
    step = STEP_MAX * jnp.exp2(-time_bin[...].astype(jnp.float32))
    for c in range(3):
        gathered = lane_gather(lines[c] * (0.375 / math.pi), rank[...])
        value = jnp.where(active[...] > 0, gathered, 0.0)
        acceleration[c] = value
        kicked[c] = velocity[c] + value * step


def shards(
    position, velocity, smoothing, particle_mass, energy, density_old, cell_count, active,
    time_bin, pair_source, pair_shift, export,
):
    cells, capacity = smoothing.shape
    peers, per_peer = export.shape
    sources = cells + peers * per_peer + 2
    codes = 27
    f32 = lambda *shape: jax.ShapeDtypeStruct(shape, jnp.float32)
    smem = pl.BlockSpec(memory_space=pltpu.SMEM)
    vmem = pl.BlockSpec(memory_space=pltpu.VMEM)
    hbm = pl.BlockSpec(memory_space=pltpu.HBM)
    whole = pltpu.CompilerParams(vmem_limit_bytes=64 * 2**20)
    i32 = lambda *shape: jax.ShapeDtypeStruct(shape, jnp.int32)
    sent_rows = per_peer * (ROWS + SENT)
    turned = export.T

    def landing(*arrays):
        return [pltpu.VMEM(a.shape, a.dtype) for a in arrays] + [
            pltpu.SemaphoreType.DMA((len(arrays),))
        ]

    arrays = (position, velocity, smoothing, particle_mass, energy, density_old)
    own, own_sent, outgoing, border = pl.pallas_call(
        pack_kernel,
        out_shape=(
            f32(cells, ROWS, capacity),
            f32(cells, SENT, capacity),
            f32(peers, sent_rows, capacity),
            f32(2, ROWS + SENT, capacity),
        ),
        in_specs=[smem] * 2 + [hbm] * 6,
        out_specs=(vmem,) * 4,
        scratch_shapes=landing(*arrays),
        compiler_params=whole,
        name="pack",
    )(cell_count, turned, *arrays)

    def exchange(pieces):
        return lax.all_to_all(pieces, "cell", split_axis=0, concat_axis=0, tiled=True)

    def swap_border(pieces):
        size = lax.axis_size("region")
        up = [(i, (i + 1) % size) for i in range(size)]
        down = [(j, i) for i, j in up]
        if size == 2:
            return lax.ppermute(pieces, "region", up)
        before = lax.ppermute(pieces[0:1], "region", up)
        after = lax.ppermute(pieces[1:2], "region", down)
        return jnp.concatenate([before, after], axis=0)

    incoming = exchange(outgoing)
    other = swap_border(border)
    rank, actives, columns, heat_sorted, wide_sorted = pl.pallas_call(
        sort_kernel,
        out_shape=(
            i32(cells, capacity),
            i32(cells),
            f32(cells, capacity, ROWS),
            f32(cells, capacity),
            f32(cells, capacity),
        ),
        in_specs=[hbm] * 3,
        out_specs=(vmem, smem, vmem, vmem, vmem),
        scratch_shapes=landing(own, own_sent, active),
        compiler_params=whole,
        name="sort",
    )(own, own_sent, active)

    arrays = (own, own_sent, incoming, other, rank, columns, wide_sorted, active, density_old)
    density, sorted_density, outgoing_density, border_density = pl.pallas_call(
        functools.partial(density_kernel, per_peer),
        out_shape=(
            f32(cells, capacity),
            f32(cells, capacity),
            f32(peers, per_peer, capacity),
            f32(2, capacity),
        ),
        in_specs=[smem] * 4 + [hbm] * 9,
        out_specs=(vmem,) * 4,
        scratch_shapes=landing(*arrays)
        + [
            pltpu.VMEM((sources, ROWS, capacity), jnp.float32),
            pltpu.VMEM((codes, ROWS, capacity), jnp.float32),
            pltpu.VMEM((cells, capacity, ROWS), jnp.float32),
            pltpu.VMEM((cells, capacity), jnp.float32),
        ],
        compiler_params=whole,
        name="density",
    )(pair_source, pair_shift, turned, actives, *arrays)

    new_density = exchange(outgoing_density)
    new_border = swap_border(border_density)
    blocks = pair_source.shape[1] + SPARE
    count_rows = -(-sources // capacity)
    arrays = (own, own_sent, incoming, other, wide_sorted, heat_sorted, sorted_density)
    near_streams, far_streams, starts, more = pl.pallas_call(
        functools.partial(stream_kernel, per_peer),
        out_shape=(
            f32(cells, blocks, ROWS, capacity),
            f32(cells, blocks, ROWS, capacity),
            i32(cells, pair_source.shape[1] + 1),
            f32(cells, capacity, ROWS),
        ),
        in_specs=[smem] * 2 + [hbm] * 7,
        out_specs=(vmem, vmem, smem, vmem),
        scratch_shapes=landing(*arrays)
        + [
            pltpu.VMEM((sources, ROWS, capacity), jnp.float32),
            pltpu.VMEM((sources, ROWS, capacity), jnp.float32),
            pltpu.VMEM((codes, ROWS, capacity), jnp.float32),
            pltpu.VMEM((count_rows, capacity), jnp.int32),
            pltpu.SMEM((count_rows, capacity), jnp.int32),
            pltpu.SemaphoreType.DMA,
        ],
        compiler_params=whole,
        name="streams",
    )(pair_source, pair_shift, *arrays)

    arrays = (
        columns, more, density, new_density, new_border, rank, active, velocity, time_bin,
    )
    acceleration, kicked = pl.pallas_call(
        functools.partial(force_kernel, per_peer),
        out_shape=(f32(3, cells, capacity), f32(3, cells, capacity)),
        in_specs=[smem] * 3 + [hbm] * 11,
        out_specs=(vmem,) * 2,
        scratch_shapes=landing(*arrays)
        + [pltpu.VMEM(near_streams.shape, jnp.float32)] * 2
        + [pltpu.SemaphoreType.DMA((cells,))] * 2
        + [
            pltpu.VMEM((sources, ROWS, capacity), jnp.float32),
            pltpu.VMEM((blocks, ROWS, capacity), jnp.float32),
            pltpu.VMEM((cells, capacity, ROWS), jnp.float32),
            pltpu.VMEM((3, cells, capacity), jnp.float32),
        ],
        compiler_params=whole,
        name="force",
    )(pair_source, starts, actives, *arrays, near_streams, far_streams)
    return density, acceleration, kicked


def solution(mesh):
    rows = P(("region", "cell"), None)
    planes = P(None, ("region", "cell"), None)
    return jax.shard_map(
        shards,
        mesh=mesh,
        in_specs=(
            planes, planes, rows, rows, rows, rows, P(("region", "cell")), rows, rows, rows, rows,
            rows,
        ),
        out_specs=(rows, planes, planes),
        check_vma=False,
    )
```

```python
import functools
import math

import jax
import jax.numpy as jnp
from jax import lax
from jax.experimental import pallas as pl
from jax.experimental.pallas import tpu as pltpu
from jax.sharding import PartitionSpec as P

ADIABATIC = 5.0 / 3.0
STEP_MAX = 0.2
LANES = 128
ROWS = 8
FORCE_UNROLL = 7
PAIR_ROWS = 32
FAR_AWAY = 1e9
SPARE = FORCE_UNROLL

X, Y, Z, MASS, VX, VY, VZ, WIDE = range(ROWS)
HEAT, DENS, LIVE = range(3)
SENT = 4
INV6, HALF, SOUND, WARM, SUPPORT = range(5)


def lane_gather(values, index):
    return jnp.take_along_axis(values, index, axis=1, mode="promise_in_bounds")


def lanes_of(shape):
    return lax.broadcasted_iota(jnp.int32, shape, len(shape) - 1)


def start_copies(arrays, landed, sem):
    copies = [
        pltpu.make_async_copy(array, place, sem.at[index])
        for index, (array, place) in enumerate(zip(arrays, landed))
    ]
    for copy in copies:
        copy.start()
    return copies


def pack_kernel(count, *refs):
    arrays, (own, own_sent, outgoing, border) = refs[:7], refs[7:11]
    landed, sem = refs[11:-1], refs[-1]
    for copy in start_copies(arrays, landed, sem):
        copy.wait()
    export, position, velocity, smoothing, mass, energy, density_old = landed
    cells = smoothing.shape[0]
    shape = smoothing.shape
    lane = lanes_of(shape)
    row = lax.broadcasted_iota(jnp.int32, shape, 0)
    counts = jnp.zeros(shape, jnp.int32)
    for cell in range(cells):
        counts = jnp.where(row == cell, count[cell], counts)
    mass_live = jnp.where(lane < counts, mass[...], 0.0)
    rows = (
        position[0], position[1], position[2], mass_live,
        40.0 * velocity[0], 40.0 * velocity[1], 40.0 * velocity[2], 2.0 * smoothing[...],
    )
    for field, values in enumerate(rows):
        own[:, field, :] = values
    own_sent[:, HEAT, :] = (ADIABATIC - 1.0) * energy[...]
    own_sent[:, DENS, :] = density_old[...]
    own_sent[:, LIVE, :] = counts.astype(jnp.float32)
    own_sent[:, SENT - 1, :] = jnp.zeros(shape, jnp.float32)
    per_peer, peers = export.shape
    for peer in range(peers):
        for entry in range(per_peer):
            cell = export[entry, peer]
            outgoing[peer, entry * ROWS : (entry + 1) * ROWS, :] = own[cell]
            start = per_peer * ROWS + entry * SENT
            outgoing[peer, start : start + SENT, :] = own_sent[cell]
    for side, cell in enumerate((cells - 1, 0)):
        border[side, 0:ROWS, :] = own[cell]
        border[side, ROWS : ROWS + SENT, :] = own_sent[cell]


def sort_kernel(*refs):
    rank_out, actives, columns, heat_sorted, wide_sorted, lowest, highest, reach = refs[3:11]
    landed, sem = refs[11:14], refs[14]
    for copy in start_copies(refs[:3], landed, sem):
        copy.wait()
    own, own_sent, active = landed
    shape = active.shape
    cells = shape[0]
    lane = lanes_of(shape)
    is_active = active[...] > 0
    ones = jnp.where(is_active, 1.0, 0.0)
    for cell in range(cells):
        actives[0, cell] = jnp.sum(ones[cell : cell + 1, :]).astype(jnp.int32)
    square = (LANES, LANES)
    upper = lax.broadcasted_iota(jnp.int32, square, 0) <= lanes_of(square)
    upper = jnp.where(upper, 1.0, 0.0).astype(jnp.bfloat16)
    seen = jnp.dot(ones.astype(jnp.bfloat16), upper, preferred_element_type=jnp.float32)
    seen = seen.astype(jnp.int32)
    chosen = lane_gather(seen, jnp.full(shape, LANES - 1, jnp.int32))
    others = lane + 1 - seen
    rank_out[...] = jnp.where(is_active, seen - 1, chosen + others - 1)
    first_part = lane < chosen
    wanted = jnp.where(first_part, lane, lane - chosen)
    slot = jnp.zeros(shape, jnp.int32)
    step = LANES // 2
    while step:
        probe = slot + (step - 1)
        found = jnp.where(first_part, lane_gather(seen, probe), lane_gather(others, probe))
        slot = jnp.where(found <= wanted, slot + step, slot)
        step //= 2
    for cell in range(cells):
        order = jnp.broadcast_to(slot[cell : cell + 1, :], (ROWS, LANES))
        tile = lane_gather(own[cell], order)
        columns[cell] = tile.T
        target = lane < chosen[cell : cell + 1, :]
        low = jnp.min(jnp.where(target, tile, FAR_AWAY), axis=1, keepdims=True)
        high = jnp.max(jnp.where(target, tile, -FAR_AWAY), axis=1, keepdims=True)
        place = lax.broadcasted_iota(jnp.int32, shape, 0) <= Z
        lowest[cell] = jnp.where(place, low, -FAR_AWAY)
        highest[cell] = jnp.where(place, high, FAR_AWAY)
        reach[cell : cell + 1, :] = jnp.broadcast_to(high[WIDE : WIDE + 1, :], (1, LANES))
        wide_sorted[cell : cell + 1, :] = tile[WIDE : WIDE + 1, :]
        warm = jnp.broadcast_to(own_sent[cell, HEAT : HEAT + 1, :], (ROWS, LANES))
        heat_sorted[cell : cell + 1, :] = lane_gather(warm, order)[0:1, :]


def source_tiles(own, incoming, border, per_peer):
    cells, peers = own[0].shape[0], incoming.shape[0]
    for cell in range(cells):
        yield cell, lambda c=cell: own[0][c], lambda c=cell: own[1][c]
    for peer in range(peers):
        for entry in range(per_peer):
            near, sent = entry * ROWS, per_peer * ROWS + entry * SENT
            yield (
                cells + peer * per_peer + entry,
                lambda p=peer, n=near: incoming[p, n : n + ROWS, :],
                lambda p=peer, n=sent: incoming[p, n : n + SENT, :],
            )
    for side in range(2):
        yield (
            cells + peers * per_peer + side,
            lambda b=side: border[b, 0:ROWS, :],
            lambda b=side: border[b, ROWS : ROWS + SENT, :],
        )


def fill_shifts(shifts):
    row = lax.broadcasted_iota(jnp.int32, (ROWS, LANES), 0)
    for code in range(shifts.shape[0]):
        first, second, third = code // 9 - 1.0, code // 3 % 3 - 1.0, code % 3 - 1.0
        shifts[code] = jnp.where(
            row == X, first, jnp.where(row == Y, second, jnp.where(row == Z, third, 0.0))
        )


def fill_streams(streams, tables, sources, starts, orders, cell):
    shape = (ROWS, LANES)
    lane = lanes_of(shape)
    pairs = sources.shape[1]
    moved = []
    for pair in range(pairs):
        order = jnp.broadcast_to(orders(pair), shape)
        moved.append([lane_gather(load(sources[cell, pair], pair), order) for load in tables])
    for pair in range(pairs):
        start = starts[cell, pair]
        block = start >> 7
        fresh = lane >= (start & (LANES - 1))
        for which, stream in enumerate(streams):
            stream[block + 1] = moved[pair][which]
            pltpu.store(stream.at[block], moved[pair][which], mask=fresh)
    end = starts[cell, pairs]
    block = end >> 7
    for stream in streams:
        stream[block] = jnp.where(lane < (end & (LANES - 1)), stream[block], 0.0)
        for extra in range(1, SPARE):
            stream[block + extra] = jnp.zeros(shape, jnp.float32)
    return (end + LANES - 1) >> 7


def spread(values, field):
    return jnp.broadcast_to(values[:, field : field + 1], (values.shape[0], LANES))


def over_targets(active, one_chunk):
    groups = (active + ROWS - 1) // ROWS

    def large(chunk, carry):
        one_chunk(pl.multiple_of(chunk * 4 * ROWS, ROWS), 4)
        return carry

    lax.fori_loop(0, groups // 4, large, 0)
    for size in (2, 1):

        @pl.when((groups & size) != 0)
        def _(size=size):
            done = groups & -(2 * size)
            one_chunk(pl.multiple_of(done * ROWS, ROWS), size)


def density_kernel(per_peer, *refs):
    arrays, (density, sorted_density, outgoing, outgoing_border) = refs[:13], refs[13:17]
    landed, (sem, table, shifts, sums, lines) = refs[17:30], refs[30:]
    copies = start_copies(arrays, landed, sem)
    fill_shifts(shifts)
    for copy in copies:
        copy.wait()
    pair_source, pair_shift, export, actives = landed[:4]
    own, own_sent, incoming, border, rank, columns, wide_sorted, active, density_old = landed[4:]
    cells, peers = own.shape[0], incoming.shape[0]
    for place, near, _ in source_tiles((own, own_sent), incoming, border, per_peer):
        table[place] = near()

    def one_cell(cell, carry):
        def one_chunk(base, groups):
            size = groups * ROWS
            mine = columns[cell, pl.ds(base, size), :]
            place = [spread(mine, field) for field in (X, Y, Z)]
            wide = spread(mine, WIDE)
            smooth = 0.5 * wide

            total = jnp.zeros((size, LANES), jnp.float32)
            for pair in range(pair_source.shape[1]):
                source, code = pair_source[cell, pair], pair_shift[cell, pair]
                s = lambda field: table[source, field : field + 1, :]
                shift = lambda field: shifts[code, field : field + 1, :]
                apart = [place[c] - (s(c) + shift(c)) for c in range(3)]
                square = apart[0] * apart[0] + apart[1] * apart[1] + apart[2] * apart[2]
                radius = square * lax.rsqrt(jnp.maximum(square, 1e-24))
                outer = jnp.maximum(wide - radius, 0.0)
                inner = jnp.maximum(smooth - radius, 0.0)
                value = outer * outer * outer - 4.0 * (inner * inner * inner)
                total = total + s(MASS) * value
            sums[cell, pl.ds(base, size), 0:1] = jnp.sum(total, axis=1, keepdims=True)

        over_targets(actives[0, cell], one_chunk)
        return carry

    lax.fori_loop(0, cells, one_cell, 0)
    for cell in range(cells):
        lines[cell : cell + 1, :] = sums[cell].T[0:1, :]
    inverse = 2.0 / wide_sorted[...]
    inverse = inverse * inverse * inverse
    summed = lines[...] * (0.25 / math.pi) * (inverse * inverse)
    sorted_density[...] = summed
    density[...] = jnp.where(active[...] > 0, lane_gather(summed, rank[...]), density_old[...])
    for peer in range(peers):
        for entry in range(per_peer):
            outgoing[peer, entry : entry + 1, :] = density[pl.ds(export[entry, peer], 1), :]
    outgoing_border[0:1, :] = density[cells - 1 : cells, :]
    outgoing_border[1:2, :] = density[0:1, :]


def stream_kernel(per_peer, *refs):
    arrays, (near_out, far_out, starts, orders, more) = refs[:12], refs[12:17]
    landed, refs = refs[17:29], refs[29:]
    sems, near_table, far_table, shifts, inside, totals_row, totals, sem = refs[:8]
    near_streams, far_streams, out_sems = refs[8:]
    copies = start_copies(arrays, landed, sems)
    fill_shifts(shifts)
    for copy in copies:
        copy.wait()
    pair_source, pair_shift, own, own_sent, incoming, border = landed[:6]
    wide_sorted, heat_sorted, sorted_density, lowest, highest, reach = landed[6:]
    cells, pairs = pair_source.shape
    tile_shape = (ROWS, LANES)
    row = lax.broadcasted_iota(jnp.int32, tile_shape, 0)
    lane = lanes_of(tile_shape).astype(jnp.float32)
    for place, near, sent in source_tiles((own, own_sent), incoming, border, per_peer):
        tile, other = near(), sent()
        near_table[place] = tile
        wide, heat = tile[WIDE : WIDE + 1, :], other[HEAT : HEAT + 1, :]
        inverse = 2.0 * pl.reciprocal(wide, approx=True)
        inverse = inverse * inverse * inverse
        far_table[place, INV6 : INV6 + 1, :] = inverse * inverse
        far_table[place, HALF : HALF + 1, :] = 0.025 * wide
        far_table[place, SOUND : SOUND + 1, :] = jnp.sqrt(ADIABATIC * heat)
        far_table[place, WARM : WARM + 1, :] = heat
        far_table[place, SUPPORT : SUPPORT + 1, :] = jnp.where(
            lane[0:1, :] < other[LIVE : LIVE + 1, :], wide, -FAR_AWAY
        )

    def choose(cell, carry):
        low, high = lowest[cell], highest[cell]
        widest = reach[pl.ds(cell, 1), :]
        for pair in range(pairs):
            source = pair_source[cell, pair]
            tile = near_table[source] + shifts[pair_shift[cell, pair]]
            away = jnp.maximum(jnp.maximum(low - tile, tile - high), 0.0)
            distance = jnp.sum(away * away, axis=0, keepdims=True)
            support = far_table[source, SUPPORT : SUPPORT + 1, :]
            limit = jnp.maximum(support, widest)
            keep = (distance < limit * limit) & (support > 0.0)
            inside[pl.ds(cell * PAIR_ROWS + pair, 1), :] = jnp.where(keep, 1.0, 0.0)
        for pair in range(pairs, PAIR_ROWS):
            inside[pl.ds(cell * PAIR_ROWS + pair, 1), :] = jnp.zeros((1, LANES), jnp.float32)
        return carry

    lax.fori_loop(0, cells, choose, 0)
    flags = inside[...].astype(jnp.bfloat16)
    all_lanes = jnp.ones((ROWS, LANES), jnp.bfloat16)
    sums = lax.dot_general(
        all_lanes, flags, (((1,), (1,)), ((), ())), preferred_element_type=jnp.float32
    )
    for line in range(totals_row.shape[0]):
        totals_row[line : line + 1, :] = sums[0:1, line * LANES : (line + 1) * LANES].astype(
            jnp.int32
        )
    copy = pltpu.make_async_copy(totals_row, totals, sem)
    copy.start()
    square = (LANES, LANES)
    upper = lax.broadcasted_iota(jnp.int32, square, 0) <= lanes_of(square)
    upper = jnp.where(upper, 1.0, 0.0).astype(jnp.bfloat16)
    seen = jnp.dot(flags, upper, preferred_element_type=jnp.float32)
    wanted = lanes_of(seen.shape).astype(jnp.float32)
    slot = jnp.zeros(seen.shape, jnp.int32)
    step = LANES // 2
    while step:
        found = lane_gather(seen, slot + (step - 1))
        slot = jnp.where(found <= wanted, slot + step, slot)
        step //= 2
    orders[...] = slot
    inverse = 2.0 * pl.reciprocal(wide_sorted[...], approx=True)
    inverse = inverse * inverse * inverse
    fields = (
        inverse * inverse, 0.025 * wide_sorted[...], jnp.sqrt(ADIABATIC * heat_sorted[...]),
        4.0 * sorted_density[...], heat_sorted[...] / sorted_density[...],
    )
    for cell in range(cells):
        tile = jnp.zeros(tile_shape, jnp.float32)
        for which, values in enumerate(fields):
            tile = jnp.where(row == which, values[cell : cell + 1, :], tile)
        more[cell] = tile.T
    copy.wait()

    def leave(cell):
        return [
            pltpu.make_async_copy(stream.at[cell], out.at[cell], sems.at[cell])
            for stream, out, sems in (
                (near_streams, near_out, out_sems.at[0]), (far_streams, far_out, out_sems.at[1]),
            )
        ]

    def one_cell(cell, carry):
        tables = (
            lambda source, pair: near_table[source] + shifts[pair_shift[cell, pair]],
            lambda source, pair: far_table[source],
        )
        start = jnp.int32(0)
        for pair in range(pairs):
            starts[cell, pair] = start
            place = cell * PAIR_ROWS + pair
            turn = pl.ds(place, 1)
            orders[turn, :] = pltpu.roll(orders[turn, :], start & (LANES - 1), 1)
            start = start + totals[place >> 7, place & (LANES - 1)]
        starts[cell, pairs] = start
        fill_streams(
            (near_streams.at[cell], far_streams.at[cell]), tables, pair_source, starts,
            lambda pair: orders[pl.ds(cell * PAIR_ROWS + pair, 1), :], cell,
        )
        for copy in leave(cell):
            copy.start()
        return carry

    lax.fori_loop(0, cells, one_cell, 0)
    for cell in range(cells):
        for copy in leave(cell):
            copy.wait()


def force_kernel(per_peer, *refs):
    arrays, streams, (acceleration, kicked) = refs[:13], refs[13:15], refs[15:17]
    landed, sem, landed_streams, stream_sems = refs[17:30], refs[30], refs[31:33], refs[33:35]
    table, stream, sums, lines = refs[35:]
    copies = start_copies(arrays, landed, sem)

    def stream_copies(cell):
        return [
            pltpu.make_async_copy(source.at[cell], place.at[cell], sems.at[cell])
            for source, place, sems in zip(streams, landed_streams, stream_sems)
        ]

    for cell in range(streams[0].shape[0]):
        for copy in stream_copies(cell):
            copy.start()
    for copy in copies:
        copy.wait()
    pair_source, starts, actives, columns, more, orders, own_density = landed[:7]
    new_density, new_border, rank, active, velocity, time_bin = landed[7:]
    near_streams, far_streams = landed_streams
    cells, peers = own_density.shape[0], new_density.shape[0]
    for cell in range(cells):
        table[cell, 0:1, :] = own_density[cell : cell + 1, :]
    for peer in range(peers):
        for entry in range(per_peer):
            place = cells + peer * per_peer + entry
            table[place, 0:1, :] = new_density[peer, entry : entry + 1, :]
    for side in range(2):
        table[cells + peers * per_peer + side, 0:1, :] = new_border[side : side + 1, :]

    def one_cell(cell, carry):
        near, far = near_streams.at[cell], far_streams.at[cell]
        used = fill_streams(
            (stream,), (lambda source, pair: table[source],), pair_source, starts,
            lambda pair: orders[pl.ds(cell * PAIR_ROWS + pair, 1), :], cell,
        )
        for copy in stream_copies(cell):
            copy.wait()
        rounds = (used + FORCE_UNROLL - 1) // FORCE_UNROLL

        def one_chunk(base, groups):
            size = groups * ROWS
            mine = columns[cell, pl.ds(base, size), :]
            mine_more = more[cell, pl.ds(base, size), :]
            place = [spread(mine, field) for field in (X, Y, Z)]
            speed = [spread(mine, field) for field in (VX, VY, VZ)]
            wide = spread(mine, WIDE)
            inv6, half_, sound, dens4, press = [spread(mine_more, field) for field in range(5)]

            def blocks(index, totals):
                for sub in range(FORCE_UNROLL):
                    block = index * FORCE_UNROLL + sub
                    s = lambda field: near[block, field : field + 1, :]
                    o = lambda field: far[block, field : field + 1, :]
                    dens = stream[block, 0:1, :]
                    their_press = o(WARM) * pl.reciprocal(jnp.maximum(dens, 1e-30), approx=True)
                    apart = [place[c] - s(c) for c in range(3)]
                    square = apart[0] * apart[0] + apart[1] * apart[1] + apart[2] * apart[2]
                    inverse = lax.rsqrt(jnp.maximum(square, 1e-24))
                    radius = square * inverse
                    double = radius + radius
                    outer = jnp.maximum(wide - radius, 0.0)
                    inner = jnp.maximum(wide - double, 0.0)
                    slope = inv6 * (outer * outer - inner * inner)
                    outer = jnp.maximum(s(WIDE) - radius, 0.0)
                    inner = jnp.maximum(s(WIDE) - double, 0.0)
                    slope = slope + o(INV6) * (outer * outer - inner * inner)
                    approach = (
                        (speed[0] - s(VX)) * apart[0]
                        + (speed[1] - s(VY)) * apart[1]
                        + (speed[2] - s(VZ)) * apart[2]
                    )
                    half = half_ + o(HALF)
                    slow = pl.reciprocal(square + half * half, approx=True)
                    mu = half * jnp.minimum(approach, 0.0) * slow
                    light = pl.reciprocal(dens4 + 4.0 * dens, approx=True)
                    viscous = mu * (mu - (sound + o(SOUND))) * light
                    weight = (press + their_press + viscous) * (slope * (inverse * s(MASS)))
                    totals = tuple(total + weight * a for total, a in zip(totals, apart))
                return totals

            zero = jnp.zeros((size, LANES), jnp.float32)
            totals = lax.fori_loop(0, rounds, blocks, (zero, zero, zero))
            for c in range(3):
                sums[cell, pl.ds(base, size), c : c + 1] = jnp.sum(
                    totals[c], axis=1, keepdims=True
                )

        over_targets(actives[0, cell], one_chunk)
        return carry

    lax.fori_loop(0, cells, one_cell, 0)
    for cell in range(cells):
        turned = sums[cell].T
        for c in range(3):
            lines[c, cell : cell + 1, :] = turned[c : c + 1, :]
    step = STEP_MAX * jnp.exp2(-time_bin[...].astype(jnp.float32))
    for c in range(3):
        gathered = lane_gather(lines[c] * (0.375 / math.pi), rank[...])
        value = jnp.where(active[...] > 0, gathered, 0.0)
        acceleration[c] = value
        kicked[c] = velocity[c] + value * step


def shards(
    position, velocity, smoothing, particle_mass, energy, density_old, cell_count, active,
    time_bin, pair_source, pair_shift, export,
):
    cells, capacity = smoothing.shape
    peers, per_peer = export.shape
    sources = cells + peers * per_peer + 2
    codes = 27
    f32 = lambda *shape: jax.ShapeDtypeStruct(shape, jnp.float32)
    smem = pl.BlockSpec(memory_space=pltpu.SMEM)
    vmem = pl.BlockSpec(memory_space=pltpu.VMEM)
    hbm = pl.BlockSpec(memory_space=pltpu.HBM)
    whole = pltpu.CompilerParams(vmem_limit_bytes=64 * 2**20)
    i32 = lambda *shape: jax.ShapeDtypeStruct(shape, jnp.int32)
    sent_rows = per_peer * (ROWS + SENT)
    turned = export.T

    def landing(scalars, *arrays):
        return (
            [pltpu.SMEM(a.shape, a.dtype) for a in arrays[:scalars]]
            + [pltpu.VMEM(a.shape, a.dtype) for a in arrays[scalars:]]
            + [pltpu.SemaphoreType.DMA((len(arrays),))]
        )

    arrays = (turned, position, velocity, smoothing, particle_mass, energy, density_old)
    own, own_sent, outgoing, border = pl.pallas_call(
        pack_kernel,
        out_shape=(
            f32(cells, ROWS, capacity),
            f32(cells, SENT, capacity),
            f32(peers, sent_rows, capacity),
            f32(2, ROWS + SENT, capacity),
        ),
        in_specs=[smem] + [hbm] * 7,
        out_specs=(vmem,) * 4,
        scratch_shapes=landing(1, *arrays),
        compiler_params=whole,
        name="pack",
    )(cell_count, *arrays)

    def exchange(pieces):
        return lax.all_to_all(pieces, "cell", split_axis=0, concat_axis=0, tiled=True)

    def swap_border(pieces):
        size = lax.axis_size("region")
        up = [(i, (i + 1) % size) for i in range(size)]
        down = [(j, i) for i, j in up]
        if size == 2:
            return lax.ppermute(pieces, "region", up)
        before = lax.ppermute(pieces[0:1], "region", up)
        after = lax.ppermute(pieces[1:2], "region", down)
        return jnp.concatenate([before, after], axis=0)

    incoming = exchange(outgoing)
    other = swap_border(border)
    rank, actives, columns, heat_sorted, wide_sorted, lowest, highest, reach = pl.pallas_call(
        sort_kernel,
        out_shape=(
            i32(cells, capacity),
            i32(1, cells),
            f32(cells, capacity, ROWS),
            f32(cells, capacity),
            f32(cells, capacity),
            f32(cells, ROWS, capacity),
            f32(cells, ROWS, capacity),
            f32(cells, capacity),
        ),
        in_specs=[hbm] * 3,
        out_specs=(vmem, smem) + (vmem,) * 6,
        scratch_shapes=landing(0, own, own_sent, active),
        compiler_params=whole,
        name="sort",
    )(own, own_sent, active)

    arrays = (
        pair_source, pair_shift, turned, actives,
        own, own_sent, incoming, other, rank, columns, wide_sorted, active, density_old,
    )
    density, sorted_density, outgoing_density, border_density = pl.pallas_call(
        functools.partial(density_kernel, per_peer),
        out_shape=(
            f32(cells, capacity),
            f32(cells, capacity),
            f32(peers, per_peer, capacity),
            f32(2, capacity),
        ),
        in_specs=[hbm] * 13,
        out_specs=(vmem,) * 4,
        scratch_shapes=landing(4, *arrays)
        + [
            pltpu.VMEM((sources, ROWS, capacity), jnp.float32),
            pltpu.VMEM((codes, ROWS, capacity), jnp.float32),
            pltpu.VMEM((cells, capacity, ROWS), jnp.float32),
            pltpu.VMEM((cells, capacity), jnp.float32),
        ],
        compiler_params=whole,
        name="density",
    )(*arrays)

    new_density = exchange(outgoing_density)
    new_border = swap_border(border_density)
    pairs = pair_source.shape[1]
    blocks = pairs + SPARE
    pair_rows = cells * PAIR_ROWS
    arrays = (
        pair_source, pair_shift, own, own_sent, incoming, other, wide_sorted, heat_sorted,
        sorted_density, lowest, highest, reach,
    )
    near_streams, far_streams, starts, orders, more = pl.pallas_call(
        functools.partial(stream_kernel, per_peer),
        out_shape=(
            f32(cells, blocks, ROWS, capacity),
            f32(cells, blocks, ROWS, capacity),
            i32(cells, pairs + 1),
            i32(pair_rows, capacity),
            f32(cells, capacity, ROWS),
        ),
        in_specs=[hbm] * 12,
        out_specs=(hbm, hbm, smem, vmem, vmem),
        scratch_shapes=landing(2, *arrays)
        + [
            pltpu.VMEM((sources, ROWS, capacity), jnp.float32),
            pltpu.VMEM((sources, ROWS, capacity), jnp.float32),
            pltpu.VMEM((codes, ROWS, capacity), jnp.float32),
            pltpu.VMEM((pair_rows, capacity), jnp.float32),
            pltpu.VMEM((pair_rows // capacity, capacity), jnp.int32),
            pltpu.SMEM((pair_rows // capacity, capacity), jnp.int32),
            pltpu.SemaphoreType.DMA,
            pltpu.VMEM((cells, blocks, ROWS, capacity), jnp.float32),
            pltpu.VMEM((cells, blocks, ROWS, capacity), jnp.float32),
            pltpu.SemaphoreType.DMA((2, cells)),
        ],
        compiler_params=whole,
        name="streams",
    )(*arrays)

    arrays = (
        pair_source, starts, actives,
        columns, more, orders, density, new_density, new_border, rank, active, velocity, time_bin,
    )
    acceleration, kicked = pl.pallas_call(
        functools.partial(force_kernel, per_peer),
        out_shape=(f32(3, cells, capacity), f32(3, cells, capacity)),
        in_specs=[hbm] * 15,
        out_specs=(vmem,) * 2,
        scratch_shapes=landing(3, *arrays)
        + [pltpu.VMEM(near_streams.shape, jnp.float32)] * 2
        + [pltpu.SemaphoreType.DMA((cells,))] * 2
        + [
            pltpu.VMEM((sources, ROWS, capacity), jnp.float32),
            pltpu.VMEM((blocks, ROWS, capacity), jnp.float32),
            pltpu.VMEM((cells, capacity, ROWS), jnp.float32),
            pltpu.VMEM((3, cells, capacity), jnp.float32),
        ],
        compiler_params=whole,
        name="force",
    )(*arrays, near_streams, far_streams)
    return density, acceleration, kicked


def solution(mesh):
    rows = P(("region", "cell"), None)
    planes = P(None, ("region", "cell"), None)
    return jax.shard_map(
        shards,
        mesh=mesh,
        in_specs=(
            planes, planes, rows, rows, rows, rows, P(("region", "cell")), rows, rows, rows, rows,
            rows,
        ),
        out_specs=(rows, planes, planes),
        check_vma=False,
    )
```

```python
import functools
import math

import jax
import jax.numpy as jnp
from jax import lax
from jax.experimental import pallas as pl
from jax.experimental.pallas import tpu as pltpu
from jax.sharding import PartitionSpec as P

ADIABATIC = 5.0 / 3.0
STEP_MAX = 0.2
LANES = 128
ROWS = 8
FORCE_UNROLL = 7
PAIR_ROWS = 32
FAR_AWAY = 1e9
SPARE = FORCE_UNROLL

X, Y, Z, MASS, VX, VY, VZ, WIDE = range(ROWS)
HEAT, DENS, LIVE = range(3)
SENT = 4
INV6, HALF, SOUND, WARM, SUPPORT = range(5)


def lane_gather(values, index):
    return jnp.take_along_axis(values, index, axis=1, mode="promise_in_bounds")


def lanes_of(shape):
    return lax.broadcasted_iota(jnp.int32, shape, len(shape) - 1)


def start_copies(arrays, landed, sem):
    copies = [
        pltpu.make_async_copy(array, place, sem.at[index])
        for index, (array, place) in enumerate(zip(arrays, landed))
    ]
    for copy in copies:
        copy.start()
    return copies


def pack_kernel(count, *refs):
    arrays, (own, own_sent, outgoing, border) = refs[:7], refs[7:11]
    landed, sem = refs[11:-1], refs[-1]
    for copy in start_copies(arrays, landed, sem):
        copy.wait()
    export, position, velocity, smoothing, mass, energy, density_old = landed
    cells = smoothing.shape[0]
    shape = smoothing.shape
    lane = lanes_of(shape)
    row = lax.broadcasted_iota(jnp.int32, shape, 0)
    counts = jnp.zeros(shape, jnp.int32)
    for cell in range(cells):
        counts = jnp.where(row == cell, count[cell], counts)
    mass_live = jnp.where(lane < counts, mass[...], 0.0)
    rows = (
        position[0], position[1], position[2], mass_live,
        40.0 * velocity[0], 40.0 * velocity[1], 40.0 * velocity[2], 2.0 * smoothing[...],
    )
    for field, values in enumerate(rows):
        own[:, field, :] = values
    own_sent[:, HEAT, :] = (ADIABATIC - 1.0) * energy[...]
    own_sent[:, DENS, :] = density_old[...]
    own_sent[:, LIVE, :] = counts.astype(jnp.float32)
    own_sent[:, SENT - 1, :] = jnp.zeros(shape, jnp.float32)
    per_peer, peers = export.shape
    for peer in range(peers):
        for entry in range(per_peer):
            cell = export[entry, peer]
            outgoing[peer, entry * ROWS : (entry + 1) * ROWS, :] = own[cell]
            start = per_peer * ROWS + entry * SENT
            outgoing[peer, start : start + SENT, :] = own_sent[cell]
    for side, cell in enumerate((cells - 1, 0)):
        border[side, 0:ROWS, :] = own[cell]
        border[side, ROWS : ROWS + SENT, :] = own_sent[cell]


def sort_kernel(*refs):
    rank_out, actives, columns, heat_sorted, wide_sorted, lowest, highest, reach = refs[3:11]
    landed, sem = refs[11:14], refs[14]
    for copy in start_copies(refs[:3], landed, sem):
        copy.wait()
    own, own_sent, active = landed
    shape = active.shape
    cells = shape[0]
    lane = lanes_of(shape)
    is_active = active[...] > 0
    ones = jnp.where(is_active, 1.0, 0.0)
    for cell in range(cells):
        actives[0, cell] = jnp.sum(ones[cell : cell + 1, :]).astype(jnp.int32)
    square = (LANES, LANES)
    upper = lax.broadcasted_iota(jnp.int32, square, 0) <= lanes_of(square)
    upper = jnp.where(upper, 1.0, 0.0).astype(jnp.bfloat16)
    seen = jnp.dot(ones.astype(jnp.bfloat16), upper, preferred_element_type=jnp.float32)
    seen = seen.astype(jnp.int32)
    chosen = lane_gather(seen, jnp.full(shape, LANES - 1, jnp.int32))
    others = lane + 1 - seen
    rank_out[...] = jnp.where(is_active, seen - 1, chosen + others - 1)
    first_part = lane < chosen
    wanted = jnp.where(first_part, lane, lane - chosen)
    slot = jnp.zeros(shape, jnp.int32)
    step = LANES // 2
    while step:
        probe = slot + (step - 1)
        found = jnp.where(first_part, lane_gather(seen, probe), lane_gather(others, probe))
        slot = jnp.where(found <= wanted, slot + step, slot)
        step //= 2
    for cell in range(cells):
        order = jnp.broadcast_to(slot[cell : cell + 1, :], (ROWS, LANES))
        tile = lane_gather(own[cell], order)
        columns[cell] = tile.T
        target = lane < chosen[cell : cell + 1, :]
        low = jnp.min(jnp.where(target, tile, FAR_AWAY), axis=1, keepdims=True)
        high = jnp.max(jnp.where(target, tile, -FAR_AWAY), axis=1, keepdims=True)
        place = lax.broadcasted_iota(jnp.int32, shape, 0) <= Z
        lowest[cell] = jnp.where(place, low, -FAR_AWAY)
        highest[cell] = jnp.where(place, high, FAR_AWAY)
        reach[cell : cell + 1, :] = jnp.broadcast_to(high[WIDE : WIDE + 1, :], (1, LANES))
        wide_sorted[cell : cell + 1, :] = tile[WIDE : WIDE + 1, :]
        warm = jnp.broadcast_to(own_sent[cell, HEAT : HEAT + 1, :], (ROWS, LANES))
        heat_sorted[cell : cell + 1, :] = lane_gather(warm, order)[0:1, :]


def source_tiles(own, incoming, border, per_peer):
    cells, peers = own[0].shape[0], incoming.shape[0]
    for cell in range(cells):
        yield cell, lambda c=cell: own[0][c], lambda c=cell: own[1][c]
    for peer in range(peers):
        for entry in range(per_peer):
            near, sent = entry * ROWS, per_peer * ROWS + entry * SENT
            yield (
                cells + peer * per_peer + entry,
                lambda p=peer, n=near: incoming[p, n : n + ROWS, :],
                lambda p=peer, n=sent: incoming[p, n : n + SENT, :],
            )
    for side in range(2):
        yield (
            cells + peers * per_peer + side,
            lambda b=side: border[b, 0:ROWS, :],
            lambda b=side: border[b, ROWS : ROWS + SENT, :],
        )


def fill_shifts(shifts):
    row = lax.broadcasted_iota(jnp.int32, (ROWS, LANES), 0)
    for code in range(shifts.shape[0]):
        first, second, third = code // 9 - 1.0, code // 3 % 3 - 1.0, code % 3 - 1.0
        shifts[code] = jnp.where(
            row == X, first, jnp.where(row == Y, second, jnp.where(row == Z, third, 0.0))
        )


def fill_streams(streams, tables, sources, starts, orders, cell):
    shape = (ROWS, LANES)
    lane = lanes_of(shape)
    pairs = sources.shape[1]
    moved = []
    for pair in range(pairs):
        order = jnp.broadcast_to(orders(pair), shape)
        moved.append([lane_gather(load(sources[cell, pair], pair), order) for load in tables])
    for pair in range(pairs):
        start = starts(pair)
        block = start >> 7
        fresh = lane >= (start & (LANES - 1))
        for which, stream in enumerate(streams):
            stream[block + 1] = moved[pair][which]
            pltpu.store(stream.at[block], moved[pair][which], mask=fresh)
    end = starts(pairs)
    block = end >> 7
    for stream in streams:
        stream[block] = jnp.where(lane < (end & (LANES - 1)), stream[block], 0.0)
        for extra in range(1, SPARE):
            stream[block + extra] = jnp.zeros(shape, jnp.float32)
    return (end + LANES - 1) >> 7


def spread(values, field):
    return jnp.broadcast_to(values[:, field : field + 1], (values.shape[0], LANES))


def over_targets(active, one_chunk):
    groups = (active + ROWS - 1) // ROWS

    def large(chunk, carry):
        one_chunk(pl.multiple_of(chunk * 4 * ROWS, ROWS), 4)
        return carry

    lax.fori_loop(0, groups // 4, large, 0)
    for size in (2, 1):

        @pl.when((groups & size) != 0)
        def _(size=size):
            done = groups & -(2 * size)
            one_chunk(pl.multiple_of(done * ROWS, ROWS), size)


def density_kernel(per_peer, *refs):
    arrays, (density, sorted_density, outgoing, outgoing_border) = refs[:13], refs[13:17]
    landed, (sem, table, shifts, sums, lines) = refs[17:30], refs[30:]
    copies = start_copies(arrays, landed, sem)
    fill_shifts(shifts)
    for copy in copies:
        copy.wait()
    pair_source, pair_shift, export, actives = landed[:4]
    own, own_sent, incoming, border, rank, columns, wide_sorted, active, density_old = landed[4:]
    cells, peers = own.shape[0], incoming.shape[0]
    for place, near, _ in source_tiles((own, own_sent), incoming, border, per_peer):
        table[place] = near()

    def one_cell(cell, carry):
        def one_chunk(base, groups):
            size = groups * ROWS
            mine = columns[cell, pl.ds(base, size), :]
            place = [spread(mine, field) for field in (X, Y, Z)]
            wide = spread(mine, WIDE)
            smooth = 0.5 * wide

            total = jnp.zeros((size, LANES), jnp.float32)
            for pair in range(pair_source.shape[1]):
                source, code = pair_source[cell, pair], pair_shift[cell, pair]
                s = lambda field: table[source, field : field + 1, :]
                shift = lambda field: shifts[code, field : field + 1, :]
                apart = [place[c] - (s(c) + shift(c)) for c in range(3)]
                square = apart[0] * apart[0] + apart[1] * apart[1] + apart[2] * apart[2]
                radius = square * lax.rsqrt(jnp.maximum(square, 1e-24))
                outer = jnp.maximum(wide - radius, 0.0)
                inner = jnp.maximum(smooth - radius, 0.0)
                value = outer * outer * outer - 4.0 * (inner * inner * inner)
                total = total + s(MASS) * value
            sums[cell, pl.ds(base, size), 0:1] = jnp.sum(total, axis=1, keepdims=True)

        over_targets(actives[0, cell], one_chunk)
        return carry

    lax.fori_loop(0, cells, one_cell, 0)
    for cell in range(cells):
        lines[cell : cell + 1, :] = sums[cell].T[0:1, :]
    inverse = 2.0 / wide_sorted[...]
    inverse = inverse * inverse * inverse
    summed = lines[...] * (0.25 / math.pi) * (inverse * inverse)
    sorted_density[...] = summed
    density[...] = jnp.where(active[...] > 0, lane_gather(summed, rank[...]), density_old[...])
    for peer in range(peers):
        for entry in range(per_peer):
            outgoing[peer, entry : entry + 1, :] = density[pl.ds(export[entry, peer], 1), :]
    outgoing_border[0:1, :] = density[cells - 1 : cells, :]
    outgoing_border[1:2, :] = density[0:1, :]


def stream_kernel(per_peer, *refs):
    arrays, (near_out, far_out, starts, orders, more) = refs[:12], refs[12:17]
    landed, refs = refs[17:29], refs[29:]
    sems, near_table, far_table, shifts, inside, totals_row, totals, sem = refs[:8]
    near_streams, far_streams, out_sems = refs[8:]
    copies = start_copies(arrays, landed, sems)
    fill_shifts(shifts)
    for copy in copies:
        copy.wait()
    pair_source, pair_shift, own, own_sent, incoming, border = landed[:6]
    wide_sorted, heat_sorted, sorted_density, lowest, highest, reach = landed[6:]
    cells, pairs = pair_source.shape
    tile_shape = (ROWS, LANES)
    row = lax.broadcasted_iota(jnp.int32, tile_shape, 0)
    lane = lanes_of(tile_shape).astype(jnp.float32)
    for place, near, sent in source_tiles((own, own_sent), incoming, border, per_peer):
        tile, other = near(), sent()
        near_table[place] = tile
        wide, heat = tile[WIDE : WIDE + 1, :], other[HEAT : HEAT + 1, :]
        inverse = 2.0 * pl.reciprocal(wide, approx=True)
        inverse = inverse * inverse * inverse
        far_table[place, INV6 : INV6 + 1, :] = inverse * inverse
        far_table[place, HALF : HALF + 1, :] = 0.025 * wide
        far_table[place, SOUND : SOUND + 1, :] = jnp.sqrt(ADIABATIC * heat)
        far_table[place, WARM : WARM + 1, :] = heat
        far_table[place, SUPPORT : SUPPORT + 1, :] = jnp.where(
            lane[0:1, :] < other[LIVE : LIVE + 1, :], wide, -FAR_AWAY
        )

    def choose(cell, carry):
        low, high = lowest[cell], highest[cell]
        widest = reach[pl.ds(cell, 1), :]
        kept = []
        for pair in range(pairs):
            source = pair_source[cell, pair]
            tile = near_table[source] + shifts[pair_shift[cell, pair]]
            away = jnp.maximum(jnp.maximum(low - tile, tile - high), 0.0)
            distance = jnp.sum(away * away, axis=0, keepdims=True)
            support = far_table[source, SUPPORT : SUPPORT + 1, :]
            limit = jnp.maximum(support, widest)
            keep = (distance < limit * limit) & (support > 0.0)
            kept.append(jnp.where(keep, 1.0, 0.0))
        kept += [jnp.zeros((1, LANES), jnp.float32)] * (PAIR_ROWS - pairs)
        base = pl.multiple_of(cell * PAIR_ROWS, PAIR_ROWS)
        inside[pl.ds(base, PAIR_ROWS), :] = jnp.concatenate(kept, axis=0)
        return carry

    lax.fori_loop(0, cells, choose, 0)
    flags = inside[...].astype(jnp.bfloat16)
    all_lanes = jnp.ones((ROWS, LANES), jnp.bfloat16)
    sums = lax.dot_general(
        all_lanes, flags, (((1,), (1,)), ((), ())), preferred_element_type=jnp.float32
    )
    for line in range(totals_row.shape[0]):
        totals_row[line : line + 1, :] = sums[0:1, line * LANES : (line + 1) * LANES].astype(
            jnp.int32
        )
    copy = pltpu.make_async_copy(totals_row, totals, sem)
    copy.start()
    square = (LANES, LANES)
    upper = lax.broadcasted_iota(jnp.int32, square, 0) <= lanes_of(square)
    upper = jnp.where(upper, 1.0, 0.0).astype(jnp.bfloat16)
    seen = jnp.dot(flags, upper, preferred_element_type=jnp.float32)
    wanted = lanes_of(seen.shape).astype(jnp.float32)
    slot = jnp.zeros(seen.shape, jnp.int32)
    step = LANES // 2
    while step:
        found = lane_gather(seen, slot + (step - 1))
        slot = jnp.where(found <= wanted, slot + step, slot)
        step //= 2
    orders[...] = slot
    inverse = 2.0 * pl.reciprocal(wide_sorted[...], approx=True)
    inverse = inverse * inverse * inverse
    fields = (
        inverse * inverse, 0.025 * wide_sorted[...], jnp.sqrt(ADIABATIC * heat_sorted[...]),
        4.0 * sorted_density[...], heat_sorted[...] / sorted_density[...],
    )
    for cell in range(cells):
        tile = jnp.zeros(tile_shape, jnp.float32)
        for which, values in enumerate(fields):
            tile = jnp.where(row == which, values[cell : cell + 1, :], tile)
        more[cell] = tile.T
    copy.wait()

    def leave(cell):
        return [
            pltpu.make_async_copy(stream.at[cell], out.at[cell], sems.at[cell])
            for stream, out, sems in (
                (near_streams, near_out, out_sems.at[0]), (far_streams, far_out, out_sems.at[1]),
            )
        ]

    def one_cell(cell, carry):
        tables = (
            lambda source, pair: near_table[source] + shifts[pair_shift[cell, pair]],
            lambda source, pair: far_table[source],
        )
        start = jnp.int32(0)
        begins, turned = [], []
        for pair in range(pairs):
            begins.append(start)
            place = cell * PAIR_ROWS + pair
            turned.append(pltpu.roll(orders[pl.ds(place, 1), :], start & (LANES - 1), 1))
            start = start + totals[place >> 7, place & (LANES - 1)]
        begins.append(start)
        turned += [turned[-1]] * (PAIR_ROWS - pairs)
        for pair, begin in enumerate(begins):
            starts[cell, pair] = begin
        fill_streams(
            (near_streams.at[cell], far_streams.at[cell]), tables, pair_source,
            lambda pair: begins[pair], lambda pair: turned[pair], cell,
        )
        base = pl.multiple_of(cell * PAIR_ROWS, PAIR_ROWS)
        orders[pl.ds(base, PAIR_ROWS), :] = jnp.concatenate(turned, axis=0)
        for copy in leave(cell):
            copy.start()
        return carry

    lax.fori_loop(0, cells, one_cell, 0)
    for cell in range(cells):
        for copy in leave(cell):
            copy.wait()


def force_kernel(per_peer, *refs):
    arrays, streams, (acceleration, kicked) = refs[:13], refs[13:15], refs[15:17]
    landed, sem, landed_streams, stream_sems = refs[17:30], refs[30], refs[31:33], refs[33:35]
    table, stream, sums, lines = refs[35:]
    copies = start_copies(arrays, landed, sem)

    def stream_copies(cell):
        return [
            pltpu.make_async_copy(source.at[cell], place.at[cell], sems.at[cell])
            for source, place, sems in zip(streams, landed_streams, stream_sems)
        ]

    for cell in range(streams[0].shape[0]):
        for copy in stream_copies(cell):
            copy.start()
    for copy in copies:
        copy.wait()
    pair_source, starts, actives, columns, more, orders, own_density = landed[:7]
    new_density, new_border, rank, active, velocity, time_bin = landed[7:]
    near_streams, far_streams = landed_streams
    cells, peers = own_density.shape[0], new_density.shape[0]
    for cell in range(cells):
        table[cell, 0:1, :] = own_density[cell : cell + 1, :]
    for peer in range(peers):
        for entry in range(per_peer):
            place = cells + peer * per_peer + entry
            table[place, 0:1, :] = new_density[peer, entry : entry + 1, :]
    for side in range(2):
        table[cells + peers * per_peer + side, 0:1, :] = new_border[side : side + 1, :]

    def one_cell(cell, carry):
        near, far = near_streams.at[cell], far_streams.at[cell]
        used = fill_streams(
            (stream,), (lambda source, pair: table[source],), pair_source,
            lambda pair: starts[cell, pair],
            lambda pair: orders[pl.ds(cell * PAIR_ROWS + pair, 1), :], cell,
        )
        for copy in stream_copies(cell):
            copy.wait()
        rounds = (used + FORCE_UNROLL - 1) // FORCE_UNROLL

        def one_chunk(base, groups):
            size = groups * ROWS
            mine = columns[cell, pl.ds(base, size), :]
            mine_more = more[cell, pl.ds(base, size), :]
            place = [spread(mine, field) for field in (X, Y, Z)]
            speed = [spread(mine, field) for field in (VX, VY, VZ)]
            wide = spread(mine, WIDE)
            inv6, half_, sound, dens4, press = [spread(mine_more, field) for field in range(5)]

            def blocks(index, totals):
                for sub in range(FORCE_UNROLL):
                    block = index * FORCE_UNROLL + sub
                    s = lambda field: near[block, field : field + 1, :]
                    o = lambda field: far[block, field : field + 1, :]
                    dens = stream[block, 0:1, :]
                    their_press = o(WARM) * pl.reciprocal(jnp.maximum(dens, 1e-30), approx=True)
                    apart = [place[c] - s(c) for c in range(3)]
                    square = apart[0] * apart[0] + apart[1] * apart[1] + apart[2] * apart[2]
                    inverse = lax.rsqrt(jnp.maximum(square, 1e-24))
                    radius = square * inverse
                    double = radius + radius
                    outer = jnp.maximum(wide - radius, 0.0)
                    inner = jnp.maximum(wide - double, 0.0)
                    slope = inv6 * (outer * outer - inner * inner)
                    outer = jnp.maximum(s(WIDE) - radius, 0.0)
                    inner = jnp.maximum(s(WIDE) - double, 0.0)
                    slope = slope + o(INV6) * (outer * outer - inner * inner)
                    approach = (
                        (speed[0] - s(VX)) * apart[0]
                        + (speed[1] - s(VY)) * apart[1]
                        + (speed[2] - s(VZ)) * apart[2]
                    )
                    half = half_ + o(HALF)
                    slow = pl.reciprocal(square + half * half, approx=True)
                    mu = half * jnp.minimum(approach, 0.0) * slow
                    light = pl.reciprocal(dens4 + 4.0 * dens, approx=True)
                    viscous = mu * (mu - (sound + o(SOUND))) * light
                    weight = (press + their_press + viscous) * (slope * (inverse * s(MASS)))
                    totals = tuple(total + weight * a for total, a in zip(totals, apart))
                return totals

            zero = jnp.zeros((size, LANES), jnp.float32)
            totals = lax.fori_loop(0, rounds, blocks, (zero, zero, zero))
            for c in range(3):
                sums[cell, pl.ds(base, size), c : c + 1] = jnp.sum(
                    totals[c], axis=1, keepdims=True
                )

        over_targets(actives[0, cell], one_chunk)
        return carry

    lax.fori_loop(0, cells, one_cell, 0)
    for cell in range(cells):
        turned = sums[cell].T
        for c in range(3):
            lines[c, cell : cell + 1, :] = turned[c : c + 1, :]
    step = STEP_MAX * jnp.exp2(-time_bin[...].astype(jnp.float32))
    for c in range(3):
        gathered = lane_gather(lines[c] * (0.375 / math.pi), rank[...])
        value = jnp.where(active[...] > 0, gathered, 0.0)
        acceleration[c] = value
        kicked[c] = velocity[c] + value * step


def shards(
    position, velocity, smoothing, particle_mass, energy, density_old, cell_count, active,
    time_bin, pair_source, pair_shift, export,
):
    cells, capacity = smoothing.shape
    peers, per_peer = export.shape
    sources = cells + peers * per_peer + 2
    codes = 27
    f32 = lambda *shape: jax.ShapeDtypeStruct(shape, jnp.float32)
    smem = pl.BlockSpec(memory_space=pltpu.SMEM)
    vmem = pl.BlockSpec(memory_space=pltpu.VMEM)
    hbm = pl.BlockSpec(memory_space=pltpu.HBM)
    whole = pltpu.CompilerParams(vmem_limit_bytes=64 * 2**20)
    i32 = lambda *shape: jax.ShapeDtypeStruct(shape, jnp.int32)
    sent_rows = per_peer * (ROWS + SENT)
    turned = export.T

    def landing(scalars, *arrays):
        return (
            [pltpu.SMEM(a.shape, a.dtype) for a in arrays[:scalars]]
            + [pltpu.VMEM(a.shape, a.dtype) for a in arrays[scalars:]]
            + [pltpu.SemaphoreType.DMA((len(arrays),))]
        )

    arrays = (turned, position, velocity, smoothing, particle_mass, energy, density_old)
    own, own_sent, outgoing, border = pl.pallas_call(
        pack_kernel,
        out_shape=(
            f32(cells, ROWS, capacity),
            f32(cells, SENT, capacity),
            f32(peers, sent_rows, capacity),
            f32(2, ROWS + SENT, capacity),
        ),
        in_specs=[smem] + [hbm] * 7,
        out_specs=(vmem,) * 4,
        scratch_shapes=landing(1, *arrays),
        compiler_params=whole,
        name="pack",
    )(cell_count, *arrays)

    def exchange(pieces):
        return lax.all_to_all(pieces, "cell", split_axis=0, concat_axis=0, tiled=True)

    def swap_border(pieces):
        size = lax.axis_size("region")
        up = [(i, (i + 1) % size) for i in range(size)]
        down = [(j, i) for i, j in up]
        if size == 2:
            return lax.ppermute(pieces, "region", up)
        before = lax.ppermute(pieces[0:1], "region", up)
        after = lax.ppermute(pieces[1:2], "region", down)
        return jnp.concatenate([before, after], axis=0)

    incoming = exchange(outgoing)
    other = swap_border(border)
    rank, actives, columns, heat_sorted, wide_sorted, lowest, highest, reach = pl.pallas_call(
        sort_kernel,
        out_shape=(
            i32(cells, capacity),
            i32(1, cells),
            f32(cells, capacity, ROWS),
            f32(cells, capacity),
            f32(cells, capacity),
            f32(cells, ROWS, capacity),
            f32(cells, ROWS, capacity),
            f32(cells, capacity),
        ),
        in_specs=[hbm] * 3,
        out_specs=(vmem, smem) + (vmem,) * 6,
        scratch_shapes=landing(0, own, own_sent, active),
        compiler_params=whole,
        name="sort",
    )(own, own_sent, active)

    arrays = (
        pair_source, pair_shift, turned, actives,
        own, own_sent, incoming, other, rank, columns, wide_sorted, active, density_old,
    )
    density, sorted_density, outgoing_density, border_density = pl.pallas_call(
        functools.partial(density_kernel, per_peer),
        out_shape=(
            f32(cells, capacity),
            f32(cells, capacity),
            f32(peers, per_peer, capacity),
            f32(2, capacity),
        ),
        in_specs=[hbm] * 13,
        out_specs=(vmem,) * 4,
        scratch_shapes=landing(4, *arrays)
        + [
            pltpu.VMEM((sources, ROWS, capacity), jnp.float32),
            pltpu.VMEM((codes, ROWS, capacity), jnp.float32),
            pltpu.VMEM((cells, capacity, ROWS), jnp.float32),
            pltpu.VMEM((cells, capacity), jnp.float32),
        ],
        compiler_params=whole,
        name="density",
    )(*arrays)

    new_density = exchange(outgoing_density)
    new_border = swap_border(border_density)
    pairs = pair_source.shape[1]
    blocks = pairs + SPARE
    pair_rows = cells * PAIR_ROWS
    arrays = (
        pair_source, pair_shift, own, own_sent, incoming, other, wide_sorted, heat_sorted,
        sorted_density, lowest, highest, reach,
    )
    near_streams, far_streams, starts, orders, more = pl.pallas_call(
        functools.partial(stream_kernel, per_peer),
        out_shape=(
            f32(cells, blocks, ROWS, capacity),
            f32(cells, blocks, ROWS, capacity),
            i32(cells, pairs + 1),
            i32(pair_rows, capacity),
            f32(cells, capacity, ROWS),
        ),
        in_specs=[hbm] * 12,
        out_specs=(hbm, hbm, smem, vmem, vmem),
        scratch_shapes=landing(2, *arrays)
        + [
            pltpu.VMEM((sources, ROWS, capacity), jnp.float32),
            pltpu.VMEM((sources, ROWS, capacity), jnp.float32),
            pltpu.VMEM((codes, ROWS, capacity), jnp.float32),
            pltpu.VMEM((pair_rows, capacity), jnp.float32),
            pltpu.VMEM((pair_rows // capacity, capacity), jnp.int32),
            pltpu.SMEM((pair_rows // capacity, capacity), jnp.int32),
            pltpu.SemaphoreType.DMA,
            pltpu.VMEM((cells, blocks, ROWS, capacity), jnp.float32),
            pltpu.VMEM((cells, blocks, ROWS, capacity), jnp.float32),
            pltpu.SemaphoreType.DMA((2, cells)),
        ],
        compiler_params=whole,
        name="streams",
    )(*arrays)

    arrays = (
        pair_source, starts, actives,
        columns, more, orders, density, new_density, new_border, rank, active, velocity, time_bin,
    )
    acceleration, kicked = pl.pallas_call(
        functools.partial(force_kernel, per_peer),
        out_shape=(f32(3, cells, capacity), f32(3, cells, capacity)),
        in_specs=[hbm] * 15,
        out_specs=(vmem,) * 2,
        scratch_shapes=landing(3, *arrays)
        + [pltpu.VMEM(near_streams.shape, jnp.float32)] * 2
        + [pltpu.SemaphoreType.DMA((cells,))] * 2
        + [
            pltpu.VMEM((sources, ROWS, capacity), jnp.float32),
            pltpu.VMEM((blocks, ROWS, capacity), jnp.float32),
            pltpu.VMEM((cells, capacity, ROWS), jnp.float32),
            pltpu.VMEM((3, cells, capacity), jnp.float32),
        ],
        compiler_params=whole,
        name="force",
    )(*arrays, near_streams, far_streams)
    return density, acceleration, kicked


def solution(mesh):
    rows = P(("region", "cell"), None)
    planes = P(None, ("region", "cell"), None)
    return jax.shard_map(
        shards,
        mesh=mesh,
        in_specs=(
            planes, planes, rows, rows, rows, rows, P(("region", "cell")), rows, rows, rows, rows,
            rows,
        ),
        out_specs=(rows, planes, planes),
        check_vma=False,
    )
```

```python
import functools
import math

import jax
import jax.numpy as jnp
from jax import lax
from jax.experimental import pallas as pl
from jax.experimental.pallas import tpu as pltpu
from jax.sharding import PartitionSpec as P

ADIABATIC = 5.0 / 3.0
STEP_MAX = 0.2
LANES = 128
ROWS = 8
FORCE_UNROLL = 7
PAIR_ROWS = 32
FAR_AWAY = 1e9
SPARE = FORCE_UNROLL

X, Y, Z, MASS, VX, VY, VZ, WIDE = range(ROWS)
HEAT, DENS, LIVE = range(3)
SENT = 4
SPEED = 40.0
ACTIVE, STEP = SENT, SENT + 1
S_HEAT, S_RANK, S_REACH, S_CHOSEN = range(ROWS, ROWS + 4)
S_LOW, S_HIGH, S_ROWS = 2 * ROWS, 3 * ROWS, 4 * ROWS
F_RANK, F_ACTIVE, F_STEP, F_VX, F_VY, F_VZ, F_DENS = range(7)
INV6, HALF, SOUND, WARM, SUPPORT = range(5)


def lane_gather(values, index):
    return jnp.take_along_axis(values, index, axis=1, mode="promise_in_bounds")


def lanes_of(shape):
    return lax.broadcasted_iota(jnp.int32, shape, len(shape) - 1)


def start_copies(arrays, landed, sem):
    copies = [
        pltpu.make_async_copy(array, place, sem.at[index])
        for index, (array, place) in enumerate(zip(arrays, landed))
    ]
    for copy in copies:
        copy.start()
    return copies


def pack_kernel(count, *refs):
    arrays, (own, outgoing, border) = refs[:9], refs[9:12]
    landed, sem = refs[12:-1], refs[-1]
    for copy in start_copies(arrays, landed, sem):
        copy.wait()
    export, position, velocity, smoothing, mass, energy, density_old, active, time_bin = landed
    cells = smoothing.shape[0]
    shape = smoothing.shape
    lane = lanes_of(shape)
    row = lax.broadcasted_iota(jnp.int32, shape, 0)
    counts = jnp.zeros(shape, jnp.int32)
    for cell in range(cells):
        counts = jnp.where(row == cell, count[cell], counts)
    mass_live = jnp.where(lane < counts, mass[...], 0.0)
    zeros = jnp.zeros(shape, jnp.float32)
    rows = (
        position[0], position[1], position[2], mass_live,
        SPEED * velocity[0], SPEED * velocity[1], SPEED * velocity[2], 2.0 * smoothing[...],
        (ADIABATIC - 1.0) * energy[...], density_old[...], counts.astype(jnp.float32), zeros,
        jnp.where(active[...] > 0, 1.0, 0.0),
        STEP_MAX * jnp.exp2(-time_bin[...].astype(jnp.float32)), zeros, zeros,
    )
    for field, values in enumerate(rows):
        own[:, field, :] = values
    per_peer, peers = export.shape
    for peer in range(peers):
        for entry in range(per_peer):
            cell = export[entry, peer]
            outgoing[peer, entry * ROWS : (entry + 1) * ROWS, :] = own[cell, 0:ROWS, :]
            start = per_peer * ROWS + entry * SENT
            outgoing[peer, start : start + SENT, :] = own[cell, ROWS : ROWS + SENT, :]
    for side, cell in enumerate((cells - 1, 0)):
        border[side] = own[cell, 0 : ROWS + SENT, :]


def own_rows(own, field):
    return own[:, ROWS + field, :]


def sort_kernel(own, actives, bundle):
    cells = own.shape[0]
    shape = (cells, LANES)
    lane = lanes_of(shape)
    ones = own_rows(own, ACTIVE)
    is_active = ones > 0.5
    for cell in range(cells):
        actives[0, cell] = jnp.sum(ones[cell : cell + 1, :]).astype(jnp.int32)
    square = (LANES, LANES)
    upper = lax.broadcasted_iota(jnp.int32, square, 0) <= lanes_of(square)
    upper = jnp.where(upper, 1.0, 0.0).astype(jnp.bfloat16)
    seen = jnp.dot(ones.astype(jnp.bfloat16), upper, preferred_element_type=jnp.float32)
    seen = seen.astype(jnp.int32)
    chosen = lane_gather(seen, jnp.full(shape, LANES - 1, jnp.int32))
    others = lane + 1 - seen
    rank = jnp.where(is_active, seen - 1, chosen + others - 1)
    first_part = lane < chosen
    wanted = jnp.where(first_part, lane, lane - chosen)
    slot = jnp.zeros(shape, jnp.int32)
    step = LANES // 2
    while step:
        probe = slot + (step - 1)
        found = jnp.where(first_part, lane_gather(seen, probe), lane_gather(others, probe))
        slot = jnp.where(found <= wanted, slot + step, slot)
        step //= 2
    bundle[:, S_HEAT, :] = lane_gather(own_rows(own, HEAT), slot)
    bundle[:, S_RANK, :] = rank.astype(jnp.float32)
    bundle[:, S_CHOSEN, :] = chosen.astype(jnp.float32)
    for spare in range(S_CHOSEN + 1, S_LOW):
        bundle[:, spare, :] = jnp.zeros(shape, jnp.float32)
    place = lax.broadcasted_iota(jnp.int32, (ROWS, LANES), 0) <= Z
    for cell in range(cells):
        order = jnp.broadcast_to(slot[cell : cell + 1, :], (ROWS, LANES))
        tile = lane_gather(own[cell, 0:ROWS, :], order)
        bundle[cell, 0:ROWS, :] = tile
        target = lane < chosen[cell : cell + 1, :]
        low = jnp.min(jnp.where(target, tile, FAR_AWAY), axis=1, keepdims=True)
        high = jnp.max(jnp.where(target, tile, -FAR_AWAY), axis=1, keepdims=True)
        bundle[cell, S_LOW : S_LOW + ROWS, :] = jnp.where(place, low, -FAR_AWAY)
        bundle[cell, S_HIGH : S_HIGH + ROWS, :] = jnp.where(place, high, FAR_AWAY)
        bundle[cell, S_REACH : S_REACH + 1, :] = jnp.broadcast_to(high[WIDE : WIDE + 1, :], (1, LANES))


def source_tiles(own, incoming, border, per_peer):
    cells, peers = own.shape[0], incoming.shape[0]
    for cell in range(cells):
        yield (
            cell, lambda c=cell: own[c, 0:ROWS, :], lambda c=cell: own[c, ROWS : ROWS + SENT, :]
        )
    for peer in range(peers):
        for entry in range(per_peer):
            near, sent = entry * ROWS, per_peer * ROWS + entry * SENT
            yield (
                cells + peer * per_peer + entry,
                lambda p=peer, n=near: incoming[p, n : n + ROWS, :],
                lambda p=peer, n=sent: incoming[p, n : n + SENT, :],
            )
    for side in range(2):
        yield (
            cells + peers * per_peer + side,
            lambda b=side: border[b, 0:ROWS, :],
            lambda b=side: border[b, ROWS : ROWS + SENT, :],
        )


def fill_shifts(shifts):
    row = lax.broadcasted_iota(jnp.int32, (ROWS, LANES), 0)
    for code in range(shifts.shape[0]):
        first, second, third = code // 9 - 1.0, code // 3 % 3 - 1.0, code % 3 - 1.0
        shifts[code] = jnp.where(
            row == X, first, jnp.where(row == Y, second, jnp.where(row == Z, third, 0.0))
        )


def fill_streams(streams, tables, sources, starts, orders, cell):
    shape = (ROWS, LANES)
    lane = lanes_of(shape)
    pairs = sources.shape[1]
    moved = []
    for pair in range(pairs):
        order = jnp.broadcast_to(orders(pair), shape)
        moved.append([lane_gather(load(sources[cell, pair], pair), order) for load in tables])
    for pair in range(pairs):
        start = starts(pair)
        block = start >> 7
        fresh = lane >= (start & (LANES - 1))
        for which, stream in enumerate(streams):
            stream[block + 1] = moved[pair][which]
            pltpu.store(stream.at[block], moved[pair][which], mask=fresh)
    end = starts(pairs)
    block = end >> 7
    for stream in streams:
        stream[block] = jnp.where(lane < (end & (LANES - 1)), stream[block], 0.0)
        for extra in range(1, SPARE):
            stream[block + extra] = jnp.zeros(shape, jnp.float32)
    return (end + LANES - 1) >> 7


def spread(values, field):
    return jnp.broadcast_to(values[:, field : field + 1], (values.shape[0], LANES))


def over_targets(active, one_chunk):
    groups = (active + ROWS - 1) // ROWS

    def large(chunk, carry):
        one_chunk(pl.multiple_of(chunk * 4 * ROWS, ROWS), 4)
        return carry

    lax.fori_loop(0, groups // 4, large, 0)
    for size in (2, 1):

        @pl.when((groups & size) != 0)
        def _(size=size):
            done = groups & -(2 * size)
            one_chunk(pl.multiple_of(done * ROWS, ROWS), size)


def density_kernel(
    per_peer, pair_source, pair_shift, export, actives,
    own, incoming, border, bundle,
    density, densities, outgoing, outgoing_border,
    table, shifts, columns, sums, lines,
):
    fill_shifts(shifts)
    for cell in range(own.shape[0]):
        columns[cell] = bundle[cell, 0:ROWS, :].T
    cells, peers = own.shape[0], incoming.shape[0]
    for place, near, _ in source_tiles(own, incoming, border, per_peer):
        table[place] = near()

    def one_cell(cell, carry):
        def one_chunk(base, groups):
            size = groups * ROWS
            mine = columns[cell, pl.ds(base, size), :]
            place = [spread(mine, field) for field in (X, Y, Z)]
            wide = spread(mine, WIDE)
            smooth = 0.5 * wide

            total = jnp.zeros((size, LANES), jnp.float32)
            for pair in range(pair_source.shape[1]):
                source, code = pair_source[cell, pair], pair_shift[cell, pair]
                s = lambda field: table[source, field : field + 1, :]
                shift = lambda field: shifts[code, field : field + 1, :]
                apart = [place[c] - (s(c) + shift(c)) for c in range(3)]
                square = apart[0] * apart[0] + apart[1] * apart[1] + apart[2] * apart[2]
                radius = square * lax.rsqrt(jnp.maximum(square, 1e-24))
                outer = jnp.maximum(wide - radius, 0.0)
                inner = jnp.maximum(smooth - radius, 0.0)
                value = outer * outer * outer - 4.0 * (inner * inner * inner)
                total = total + s(MASS) * value
            sums[cell, pl.ds(base, size), 0:1] = jnp.sum(total, axis=1, keepdims=True)

        over_targets(actives[0, cell], one_chunk)
        return carry

    lax.fori_loop(0, cells, one_cell, 0)
    for cell in range(cells):
        lines[cell : cell + 1, :] = sums[cell].T[0:1, :]
    inverse = 2.0 / bundle[:, WIDE, :]
    inverse = inverse * inverse * inverse
    summed = lines[...] * (0.25 / math.pi) * (inverse * inverse)
    rank = bundle[:, S_RANK, :].astype(jnp.int32)
    density[...] = jnp.where(
        own_rows(own, ACTIVE) > 0.5, lane_gather(summed, rank), own_rows(own, DENS)
    )
    densities[0] = summed
    densities[1] = density[...]
    for peer in range(peers):
        for entry in range(per_peer):
            outgoing[peer, entry : entry + 1, :] = density[pl.ds(export[entry, peer], 1), :]
    outgoing_border[0:1, :] = density[cells - 1 : cells, :]
    outgoing_border[1:2, :] = density[0:1, :]


def stream_kernel(
    per_peer, pair_source, pair_shift, own, incoming, border, bundle, densities,
    near_streams, far_streams, starts, orders, columns, last,
    near_table, far_table, shifts, inside, totals_row, totals, sem,
):
    fill_shifts(shifts)
    cells, pairs = pair_source.shape
    tile_shape = (ROWS, LANES)
    row = lax.broadcasted_iota(jnp.int32, tile_shape, 0)
    lane = lanes_of(tile_shape).astype(jnp.float32)
    for place, near, sent in source_tiles(own, incoming, border, per_peer):
        tile, other = near(), sent()
        near_table[place] = tile
        wide, heat = tile[WIDE : WIDE + 1, :], other[HEAT : HEAT + 1, :]
        inverse = 2.0 * pl.reciprocal(wide, approx=True)
        inverse = inverse * inverse * inverse
        far_table[place, INV6 : INV6 + 1, :] = inverse * inverse
        far_table[place, HALF : HALF + 1, :] = 0.025 * wide
        far_table[place, SOUND : SOUND + 1, :] = jnp.sqrt(ADIABATIC * heat)
        far_table[place, WARM : WARM + 1, :] = heat
        far_table[place, SUPPORT : SUPPORT + 1, :] = jnp.where(
            lane[0:1, :] < other[LIVE : LIVE + 1, :], wide, -FAR_AWAY
        )

    def choose(cell, carry):
        low = bundle[cell, S_LOW : S_LOW + ROWS, :]
        high = bundle[cell, S_HIGH : S_HIGH + ROWS, :]
        widest = bundle[cell, S_REACH : S_REACH + 1, :]
        kept = []
        for pair in range(pairs):
            source = pair_source[cell, pair]
            tile = near_table[source] + shifts[pair_shift[cell, pair]]
            away = jnp.maximum(jnp.maximum(low - tile, tile - high), 0.0)
            distance = jnp.sum(away * away, axis=0, keepdims=True)
            support = far_table[source, SUPPORT : SUPPORT + 1, :]
            limit = jnp.maximum(support, widest)
            keep = (distance < limit * limit) & (support > 0.0)
            kept.append(jnp.where(keep, 1.0, 0.0))
        target = lane[0:1, :] < bundle[cell, S_CHOSEN : S_CHOSEN + 1, :]
        kept.append(jnp.where(target, 1.0, 0.0))
        kept += [jnp.zeros((1, LANES), jnp.float32)] * (PAIR_ROWS - pairs - 1)
        base = pl.multiple_of(cell * PAIR_ROWS, PAIR_ROWS)
        inside[pl.ds(base, PAIR_ROWS), :] = jnp.concatenate(kept, axis=0)
        return carry

    lax.fori_loop(0, cells, choose, 0)
    flags = inside[...].astype(jnp.bfloat16)
    all_lanes = jnp.ones((ROWS, LANES), jnp.bfloat16)
    sums = lax.dot_general(
        all_lanes, flags, (((1,), (1,)), ((), ())), preferred_element_type=jnp.float32
    )
    for line in range(totals_row.shape[0]):
        totals_row[line : line + 1, :] = sums[0:1, line * LANES : (line + 1) * LANES].astype(
            jnp.int32
        )
    copy = pltpu.make_async_copy(totals_row, totals, sem)
    copy.start()
    square = (LANES, LANES)
    upper = lax.broadcasted_iota(jnp.int32, square, 0) <= lanes_of(square)
    upper = jnp.where(upper, 1.0, 0.0).astype(jnp.bfloat16)
    seen = jnp.dot(flags, upper, preferred_element_type=jnp.float32)
    wanted = lanes_of(seen.shape).astype(jnp.float32)
    slot = jnp.zeros(seen.shape, jnp.int32)
    step = LANES // 2
    while step:
        found = lane_gather(seen, slot + (step - 1))
        slot = jnp.where(found <= wanted, slot + step, slot)
        step //= 2
    orders[...] = slot
    wide, heat, summed = bundle[:, WIDE, :], bundle[:, S_HEAT, :], densities[0]
    inverse = 2.0 * pl.reciprocal(wide, approx=True)
    inverse = inverse * inverse * inverse
    fields = (
        inverse * inverse, 0.025 * wide, jnp.sqrt(ADIABATIC * heat), 4.0 * summed, heat / summed,
    )
    for cell in range(cells):
        tile = jnp.zeros(tile_shape, jnp.float32)
        for which, values in enumerate(fields):
            tile = jnp.where(row == which, values[cell : cell + 1, :], tile)
        columns[cell] = jnp.concatenate([bundle[cell, 0:ROWS, :], tile], axis=0).T
    last[:, F_RANK, :] = bundle[:, S_RANK, :]
    last[:, F_ACTIVE, :] = own_rows(own, ACTIVE)
    last[:, F_STEP, :] = own_rows(own, STEP)
    for from_row, to_row in ((VX, F_VX), (VY, F_VY), (VZ, F_VZ)):
        last[:, to_row, :] = own[:, from_row, :] * (1.0 / SPEED)
    last[:, F_DENS, :] = densities[1]
    last[:, F_DENS + 1, :] = jnp.zeros((cells, LANES), jnp.float32)
    copy.wait()

    def one_cell(cell, carry):
        tables = (
            lambda source, pair: near_table[source] + shifts[pair_shift[cell, pair]],
            lambda source, pair: far_table[source],
        )
        start = jnp.int32(0)
        begins, turned = [], []
        for pair in range(pairs):
            begins.append(start)
            place = cell * PAIR_ROWS + pair
            turned.append(pltpu.roll(orders[pl.ds(place, 1), :], start & (LANES - 1), 1))
            start = start + totals[place >> 7, place & (LANES - 1)]
        begins.append(start)
        turned += [turned[-1]] * (PAIR_ROWS - pairs)
        for pair, begin in enumerate(begins):
            starts[cell, pair] = begin
        place = cell * PAIR_ROWS + pairs
        starts[cell, pairs + 1] = totals[place >> 7, place & (LANES - 1)]
        fill_streams(
            (near_streams.at[cell], far_streams.at[cell]), tables, pair_source,
            lambda pair: begins[pair], lambda pair: turned[pair], cell,
        )
        base = pl.multiple_of(cell * PAIR_ROWS, PAIR_ROWS)
        orders[pl.ds(base, PAIR_ROWS), :] = jnp.concatenate(turned, axis=0)
        return carry

    lax.fori_loop(0, cells, one_cell, 0)


def force_kernel(
    per_peer, pair_source, starts,
    columns, orders, last, new_density, new_border, near_streams, far_streams,
    acceleration, kicked,
    table, stream, sums, lines,
):
    cells, peers = last.shape[0], new_density.shape[0]
    pairs = pair_source.shape[1]
    for cell in range(cells):
        table[cell, 0:1, :] = last[cell, F_DENS : F_DENS + 1, :]
    for peer in range(peers):
        for entry in range(per_peer):
            place = cells + peer * per_peer + entry
            table[place, 0:1, :] = new_density[peer, entry : entry + 1, :]
    for side in range(2):
        table[cells + peers * per_peer + side, 0:1, :] = new_border[side : side + 1, :]

    def one_cell(cell, carry):
        near, far = near_streams.at[cell], far_streams.at[cell]
        used = fill_streams(
            (stream,), (lambda source, pair: table[source],), pair_source,
            lambda pair: starts[cell, pair],
            lambda pair: orders[pl.ds(cell * PAIR_ROWS + pair, 1), :], cell,
        )
        rounds = (used + FORCE_UNROLL - 1) // FORCE_UNROLL

        def one_chunk(base, groups):
            size = groups * ROWS
            mine = columns[cell, pl.ds(base, size), :]
            place = [spread(mine, field) for field in (X, Y, Z)]
            speed = [spread(mine, field) for field in (VX, VY, VZ)]
            wide = spread(mine, WIDE)
            inv6, half_, sound, dens4, press = [spread(mine, ROWS + field) for field in range(5)]

            def blocks(index, totals):
                for sub in range(FORCE_UNROLL):
                    block = index * FORCE_UNROLL + sub
                    s = lambda field: near[block, field : field + 1, :]
                    o = lambda field: far[block, field : field + 1, :]
                    dens = stream[block, 0:1, :]
                    their_press = o(WARM) * pl.reciprocal(jnp.maximum(dens, 1e-30), approx=True)
                    apart = [place[c] - s(c) for c in range(3)]
                    square = apart[0] * apart[0] + apart[1] * apart[1] + apart[2] * apart[2]
                    inverse = lax.rsqrt(jnp.maximum(square, 1e-24))
                    radius = square * inverse
                    double = radius + radius
                    outer = jnp.maximum(wide - radius, 0.0)
                    inner = jnp.maximum(wide - double, 0.0)
                    slope = inv6 * (outer * outer - inner * inner)
                    outer = jnp.maximum(s(WIDE) - radius, 0.0)
                    inner = jnp.maximum(s(WIDE) - double, 0.0)
                    slope = slope + o(INV6) * (outer * outer - inner * inner)
                    approach = (
                        (speed[0] - s(VX)) * apart[0]
                        + (speed[1] - s(VY)) * apart[1]
                        + (speed[2] - s(VZ)) * apart[2]
                    )
                    half = half_ + o(HALF)
                    slow = pl.reciprocal(square + half * half, approx=True)
                    mu = half * jnp.minimum(approach, 0.0) * slow
                    light = pl.reciprocal(dens4 + 4.0 * dens, approx=True)
                    viscous = mu * (mu - (sound + o(SOUND))) * light
                    weight = (press + their_press + viscous) * (slope * (inverse * s(MASS)))
                    totals = tuple(total + weight * a for total, a in zip(totals, apart))
                return totals

            zero = jnp.zeros((size, LANES), jnp.float32)
            totals = lax.fori_loop(0, rounds, blocks, (zero, zero, zero))
            for c in range(3):
                sums[cell, pl.ds(base, size), c : c + 1] = jnp.sum(
                    totals[c], axis=1, keepdims=True
                )

        over_targets(starts[cell, pairs + 1], one_chunk)
        return carry

    lax.fori_loop(0, cells, one_cell, 0)
    for cell in range(cells):
        turned = sums[cell].T
        for c in range(3):
            lines[c, cell : cell + 1, :] = turned[c : c + 1, :]
    rank = last[:, F_RANK, :].astype(jnp.int32)
    for c in range(3):
        gathered = lane_gather(lines[c] * (0.375 / math.pi), rank)
        value = jnp.where(last[:, F_ACTIVE, :] > 0.5, gathered, 0.0)
        acceleration[c] = value
        kicked[c] = last[:, F_VX + c, :] + value * last[:, F_STEP, :]


def shards(
    position, velocity, smoothing, particle_mass, energy, density_old, cell_count, active,
    time_bin, pair_source, pair_shift, export,
):
    cells, capacity = smoothing.shape
    peers, per_peer = export.shape
    sources = cells + peers * per_peer + 2
    codes = 27
    f32 = lambda *shape: jax.ShapeDtypeStruct(shape, jnp.float32)
    smem = pl.BlockSpec(memory_space=pltpu.SMEM)
    vmem = pl.BlockSpec(memory_space=pltpu.VMEM)
    hbm = pl.BlockSpec(memory_space=pltpu.HBM)
    whole = pltpu.CompilerParams(vmem_limit_bytes=64 * 2**20)
    params = pltpu.CompilerParams(vmem_limit_bytes=24 * 2**20)
    cost = pl.CostEstimate(flops=10**9, bytes_accessed=1000, transcendentals=0)
    i32 = lambda *shape: jax.ShapeDtypeStruct(shape, jnp.int32)
    sent_rows = per_peer * (ROWS + SENT)
    turned = export.T

    def landing(scalars, *arrays):
        return (
            [pltpu.SMEM(a.shape, a.dtype) for a in arrays[:scalars]]
            + [pltpu.VMEM(a.shape, a.dtype) for a in arrays[scalars:]]
            + [pltpu.SemaphoreType.DMA((len(arrays),))]
        )

    arrays = (
        turned, position, velocity, smoothing, particle_mass, energy, density_old, active, time_bin,
    )
    own, outgoing, border = pl.pallas_call(
        pack_kernel,
        out_shape=(
            f32(cells, 2 * ROWS, capacity),
            f32(peers, sent_rows, capacity),
            f32(2, ROWS + SENT, capacity),
        ),
        in_specs=[smem] + [hbm] * 9,
        out_specs=(vmem,) * 3,
        scratch_shapes=landing(1, *arrays),
        compiler_params=whole,
        cost_estimate=cost,
        name="pack",
    )(cell_count, *arrays)

    def exchange(pieces):
        return lax.all_to_all(pieces, "cell", split_axis=0, concat_axis=0, tiled=True)

    def swap_border(pieces):
        size = lax.axis_size("region")
        up = [(i, (i + 1) % size) for i in range(size)]
        down = [(j, i) for i, j in up]
        if size == 2:
            return lax.ppermute(pieces, "region", up)
        before = lax.ppermute(pieces[0:1], "region", up)
        after = lax.ppermute(pieces[1:2], "region", down)
        return jnp.concatenate([before, after], axis=0)

    incoming = exchange(outgoing)
    other = swap_border(border)
    actives, bundle = pl.pallas_call(
        sort_kernel,
        out_shape=(i32(1, cells), f32(cells, S_ROWS, capacity)),
        in_specs=[vmem],
        out_specs=(smem, vmem),
        compiler_params=params,
        cost_estimate=cost,
        name="sort",
    )(own)

    density, densities, outgoing_density, border_density = pl.pallas_call(
        functools.partial(density_kernel, per_peer),
        out_shape=(
            f32(cells, capacity),
            f32(2, cells, capacity),
            f32(peers, per_peer, capacity),
            f32(2, capacity),
        ),
        in_specs=[smem] * 4 + [vmem] * 4,
        out_specs=(vmem,) * 4,
        scratch_shapes=[
            pltpu.VMEM((sources, ROWS, capacity), jnp.float32),
            pltpu.VMEM((codes, ROWS, capacity), jnp.float32),
            pltpu.VMEM((cells, capacity, ROWS), jnp.float32),
            pltpu.VMEM((cells, capacity, ROWS), jnp.float32),
            pltpu.VMEM((cells, capacity), jnp.float32),
        ],
        compiler_params=params,
        cost_estimate=cost,
        name="density",
    )(pair_source, pair_shift, turned, actives, own, incoming, other, bundle)

    new_density = exchange(outgoing_density)
    new_border = swap_border(border_density)
    pairs = pair_source.shape[1]
    blocks = pairs + SPARE
    pair_rows = cells * PAIR_ROWS
    near_streams, far_streams, starts, orders, columns, last = pl.pallas_call(
        functools.partial(stream_kernel, per_peer),
        out_shape=(
            f32(cells, blocks, ROWS, capacity),
            f32(cells, blocks, ROWS, capacity),
            i32(cells, pairs + 2),
            i32(pair_rows, capacity),
            f32(cells, capacity, 2 * ROWS),
            f32(cells, ROWS, capacity),
        ),
        in_specs=[smem] * 2 + [vmem] * 5,
        out_specs=(vmem, vmem, smem, vmem, vmem, vmem),
        scratch_shapes=[
            pltpu.VMEM((sources, ROWS, capacity), jnp.float32),
            pltpu.VMEM((sources, ROWS, capacity), jnp.float32),
            pltpu.VMEM((codes, ROWS, capacity), jnp.float32),
            pltpu.VMEM((pair_rows, capacity), jnp.float32),
            pltpu.VMEM((pair_rows // capacity, capacity), jnp.int32),
            pltpu.SMEM((pair_rows // capacity, capacity), jnp.int32),
            pltpu.SemaphoreType.DMA,
        ],
        compiler_params=params,
        cost_estimate=cost,
        name="streams",
    )(pair_source, pair_shift, own, incoming, other, bundle, densities)

    acceleration, kicked = pl.pallas_call(
        functools.partial(force_kernel, per_peer),
        out_shape=(f32(3, cells, capacity), f32(3, cells, capacity)),
        in_specs=[smem] * 2 + [vmem] * 7,
        out_specs=(vmem,) * 2,
        scratch_shapes=[
            pltpu.VMEM((sources, ROWS, capacity), jnp.float32),
            pltpu.VMEM((blocks, ROWS, capacity), jnp.float32),
            pltpu.VMEM((cells, capacity, ROWS), jnp.float32),
            pltpu.VMEM((3, cells, capacity), jnp.float32),
        ],
        compiler_params=params,
        cost_estimate=cost,
        name="force",
    )(
        pair_source, starts, columns, orders, last, new_density, new_border, near_streams,
        far_streams,
    )
    return density, acceleration, kicked


def solution(mesh):
    rows = P(("region", "cell"), None)
    planes = P(None, ("region", "cell"), None)
    return jax.shard_map(
        shards,
        mesh=mesh,
        in_specs=(
            planes, planes, rows, rows, rows, rows, P(("region", "cell")), rows, rows, rows, rows,
            rows,
        ),
        out_specs=(rows, planes, planes),
        check_vma=False,
    )
```

```python
import functools
import math

import jax
import jax.numpy as jnp
from jax import lax
from jax.experimental import pallas as pl
from jax.experimental.pallas import tpu as pltpu
from jax.sharding import PartitionSpec as P

ADIABATIC = 5.0 / 3.0
STEP_MAX = 0.2
LANES = 128
ROWS = 8
FORCE_UNROLL = 7
PAIR_ROWS = 32
FAR_AWAY = 1e9
SPARE = FORCE_UNROLL

X, Y, Z, MASS, VX, VY, VZ, WIDE = range(ROWS)
SPREAD = (X, Y, Z, WIDE)
HEAT, DENS, LIVE = range(3)
SENT = 4
SPEED = 40.0
ACTIVE, STEP = SENT, SENT + 1
S_HEAT, S_RANK, S_REACH, S_CHOSEN = range(ROWS, ROWS + 4)
S_LOW, S_HIGH, S_ROWS = 2 * ROWS, 3 * ROWS, 4 * ROWS
F_RANK, F_ACTIVE, F_STEP, F_VX, F_VY, F_VZ, F_DENS = range(7)
INV6, HALF, SOUND, WARM, SUPPORT = range(5)


def lane_gather(values, index):
    return jnp.take_along_axis(values, index, axis=1, mode="promise_in_bounds")


def lanes_of(shape):
    return lax.broadcasted_iota(jnp.int32, shape, len(shape) - 1)


def start_copies(arrays, landed, sem):
    copies = [
        pltpu.make_async_copy(array, place, sem.at[index])
        for index, (array, place) in enumerate(zip(arrays, landed))
    ]
    for copy in copies:
        copy.start()
    return copies


def pack_kernel(*refs):
    arrays, (own, outgoing, border) = refs[:10], refs[10:13]
    landed, sem = refs[13:-1], refs[-1]
    for copy in start_copies(arrays, landed, sem):
        copy.wait()
    count, export, position, velocity, smoothing, mass, energy, density_old, active, time_bin = landed
    cells = smoothing.shape[0]
    shape = smoothing.shape
    lane = lanes_of(shape)
    row = lax.broadcasted_iota(jnp.int32, shape, 0)
    counts = jnp.zeros(shape, jnp.int32)
    for cell in range(cells):
        counts = jnp.where(row == cell, count[cell], counts)
    mass_live = jnp.where(lane < counts, mass[...], 0.0)
    zeros = jnp.zeros(shape, jnp.float32)
    rows = (
        position[0], position[1], position[2], mass_live,
        SPEED * velocity[0], SPEED * velocity[1], SPEED * velocity[2], 2.0 * smoothing[...],
        (ADIABATIC - 1.0) * energy[...], density_old[...], counts.astype(jnp.float32), zeros,
        jnp.where(active[...] > 0, 1.0, 0.0),
        STEP_MAX * jnp.exp2(-time_bin[...].astype(jnp.float32)), zeros, zeros,
    )
    for field, values in enumerate(rows):
        own[:, field, :] = values
    per_peer, peers = export.shape
    for peer in range(peers):
        for entry in range(per_peer):
            cell = export[entry, peer]
            outgoing[peer, entry * ROWS : (entry + 1) * ROWS, :] = own[cell, 0:ROWS, :]
            start = per_peer * ROWS + entry * SENT
            outgoing[peer, start : start + SENT, :] = own[cell, ROWS : ROWS + SENT, :]
    for side, cell in enumerate((cells - 1, 0)):
        border[side] = own[cell, 0 : ROWS + SENT, :]


def own_rows(own, field):
    return own[:, ROWS + field, :]


def sort_kernel(own, actives, bundle, spreads, columns):
    cells = own.shape[0]
    shape = (cells, LANES)
    lane = lanes_of(shape)
    ones = own_rows(own, ACTIVE)
    is_active = ones > 0.5
    for cell in range(cells):
        actives[0, cell] = jnp.sum(ones[cell : cell + 1, :]).astype(jnp.int32)
    square = (LANES, LANES)
    upper = lax.broadcasted_iota(jnp.int32, square, 0) <= lanes_of(square)
    upper = jnp.where(upper, 1.0, 0.0).astype(jnp.bfloat16)
    seen = jnp.dot(ones.astype(jnp.bfloat16), upper, preferred_element_type=jnp.float32)
    seen = seen.astype(jnp.int32)
    chosen = lane_gather(seen, jnp.full(shape, LANES - 1, jnp.int32))
    others = lane + 1 - seen
    rank = jnp.where(is_active, seen - 1, chosen + others - 1)
    first_part = lane < chosen
    wanted = jnp.where(first_part, lane, lane - chosen)
    slot = jnp.zeros(shape, jnp.int32)
    step = LANES // 2
    while step:
        probe = slot + (step - 1)
        found = jnp.where(first_part, lane_gather(seen, probe), lane_gather(others, probe))
        slot = jnp.where(found <= wanted, slot + step, slot)
        step //= 2
    bundle[:, S_HEAT, :] = lane_gather(own_rows(own, HEAT), slot)
    bundle[:, S_RANK, :] = rank.astype(jnp.float32)
    bundle[:, S_CHOSEN, :] = chosen.astype(jnp.float32)
    for spare in range(S_CHOSEN + 1, S_LOW):
        bundle[:, spare, :] = jnp.zeros(shape, jnp.float32)
    place = lax.broadcasted_iota(jnp.int32, (ROWS, LANES), 0) <= Z
    for cell in range(cells):
        order = jnp.broadcast_to(slot[cell : cell + 1, :], (ROWS, LANES))
        tile = lane_gather(own[cell, 0:ROWS, :], order)
        bundle[cell, 0:ROWS, :] = tile
        target = lane < chosen[cell : cell + 1, :]
        low = jnp.min(jnp.where(target, tile, FAR_AWAY), axis=1, keepdims=True)
        high = jnp.max(jnp.where(target, tile, -FAR_AWAY), axis=1, keepdims=True)
        bundle[cell, S_LOW : S_LOW + ROWS, :] = jnp.where(place, low, -FAR_AWAY)
        bundle[cell, S_HIGH : S_HIGH + ROWS, :] = jnp.where(place, high, FAR_AWAY)
        bundle[cell, S_REACH : S_REACH + 1, :] = jnp.broadcast_to(high[WIDE : WIDE + 1, :], (1, LANES))
        columns[cell] = tile.T

    def one_cell(cell, carry):
        def one_pair(pair, carry):
            base = pl.multiple_of(pair * 2 * ROWS, 2 * ROWS)
            mine = columns[cell, pl.ds(base, 2 * ROWS), :]
            for which, field in enumerate(SPREAD):
                tiles = spread(mine, field).reshape(2, ROWS, LANES)
                spreads[cell, pl.ds(pair * 2, 2), which * ROWS : (which + 1) * ROWS, :] = tiles
            return carry

        return lax.fori_loop(0, (actives[0, cell] + 2 * ROWS - 1) // (2 * ROWS), one_pair, carry)

    lax.fori_loop(0, cells, one_cell, 0)


def source_tiles(own, incoming, border, per_peer):
    cells, peers = own.shape[0], incoming.shape[0]
    for cell in range(cells):
        yield (
            cell, lambda c=cell: own[c, 0:ROWS, :], lambda c=cell: own[c, ROWS : ROWS + SENT, :]
        )
    for peer in range(peers):
        for entry in range(per_peer):
            near, sent = entry * ROWS, per_peer * ROWS + entry * SENT
            yield (
                cells + peer * per_peer + entry,
                lambda p=peer, n=near: incoming[p, n : n + ROWS, :],
                lambda p=peer, n=sent: incoming[p, n : n + SENT, :],
            )
    for side in range(2):
        yield (
            cells + peers * per_peer + side,
            lambda b=side: border[b, 0:ROWS, :],
            lambda b=side: border[b, ROWS : ROWS + SENT, :],
        )


def fill_shifts(shifts):
    row = lax.broadcasted_iota(jnp.int32, (ROWS, LANES), 0)
    for code in range(shifts.shape[0]):
        first, second, third = code // 9 - 1.0, code // 3 % 3 - 1.0, code % 3 - 1.0
        shifts[code] = jnp.where(
            row == X, first, jnp.where(row == Y, second, jnp.where(row == Z, third, 0.0))
        )


def fill_streams(streams, tables, sources, starts, orders, cell):
    shape = (ROWS, LANES)
    lane = lanes_of(shape)
    pairs = sources.shape[1]
    moved = []
    for pair in range(pairs):
        order = jnp.broadcast_to(orders(pair), shape)
        moved.append([lane_gather(load(sources[cell, pair], pair), order) for load in tables])
    for pair in range(pairs):
        start = starts(pair)
        block = start >> 7
        fresh = lane >= (start & (LANES - 1))
        for which, stream in enumerate(streams):
            stream[block + 1] = moved[pair][which]
            pltpu.store(stream.at[block], moved[pair][which], mask=fresh)
    end = starts(pairs)
    block = end >> 7
    for stream in streams:
        stream[block] = jnp.where(lane < (end & (LANES - 1)), stream[block], 0.0)
        for extra in range(1, SPARE):
            stream[block + extra] = jnp.zeros(shape, jnp.float32)


def spread(values, field):
    return jnp.broadcast_to(values[:, field : field + 1], (values.shape[0], LANES))


def over_targets(active, one_chunk):
    groups = (active + ROWS - 1) // ROWS

    def large(chunk, carry):
        one_chunk(pl.multiple_of(chunk * 4 * ROWS, ROWS), 4)
        return carry

    lax.fori_loop(0, groups // 4, large, 0)
    for size in (2, 1):

        @pl.when((groups & size) != 0)
        def _(size=size):
            done = groups & -(2 * size)
            one_chunk(pl.multiple_of(done * ROWS, ROWS), size)


def density_kernel(
    per_peer, pair_source, pair_shift, export, actives,
    own, incoming, border, bundle, spreads,
    density, densities, outgoing, outgoing_border,
    table, shifts, sums, lines,
):
    fill_shifts(shifts)
    cells, peers = own.shape[0], incoming.shape[0]
    for place, near, _ in source_tiles(own, incoming, border, per_peer):
        table[place] = near()

    def one_cell(cell, carry):
        def one_chunk(base, groups):
            size = groups * ROWS
            at = pl.ds(base // ROWS, groups)
            *place, wide = [
                spreads[cell, at, which * ROWS : (which + 1) * ROWS, :].reshape(size, LANES)
                for which in range(len(SPREAD))
            ]
            smooth = 0.5 * wide

            total = jnp.zeros((size, LANES), jnp.float32)
            for pair in range(pair_source.shape[1]):
                source, code = pair_source[cell, pair], pair_shift[cell, pair]
                s = lambda field: table[source, field : field + 1, :]
                shift = lambda field: shifts[code, field : field + 1, :]
                apart = [place[c] - (s(c) + shift(c)) for c in range(3)]
                square = apart[0] * apart[0] + apart[1] * apart[1] + apart[2] * apart[2]
                radius = square * lax.rsqrt(jnp.maximum(square, 1e-24))
                outer = jnp.maximum(wide - radius, 0.0)
                inner = jnp.maximum(smooth - radius, 0.0)
                value = outer * outer * outer - 4.0 * (inner * inner * inner)
                total = total + s(MASS) * value
            sums[cell, pl.ds(base, size), 0:1] = jnp.sum(total, axis=1, keepdims=True)

        over_targets(actives[0, cell], one_chunk)
        return carry

    lax.fori_loop(0, cells, one_cell, 0)
    for cell in range(cells):
        lines[cell : cell + 1, :] = sums[cell].T[0:1, :]
    inverse = 2.0 / bundle[:, WIDE, :]
    inverse = inverse * inverse * inverse
    summed = lines[...] * (0.25 / math.pi) * (inverse * inverse)
    rank = bundle[:, S_RANK, :].astype(jnp.int32)
    density[...] = jnp.where(
        own_rows(own, ACTIVE) > 0.5, lane_gather(summed, rank), own_rows(own, DENS)
    )
    densities[0] = summed
    densities[1] = density[...]
    for peer in range(peers):
        for entry in range(per_peer):
            outgoing[peer, entry : entry + 1, :] = density[pl.ds(export[entry, peer], 1), :]
    outgoing_border[0:1, :] = density[cells - 1 : cells, :]
    outgoing_border[1:2, :] = density[0:1, :]


def stream_kernel(
    per_peer, pair_source, pair_shift, own, incoming, border, bundle, densities,
    near_streams, far_streams, starts, orders, columns, last,
    near_table, far_table, shifts, inside, totals_row, totals, sem,
):
    fill_shifts(shifts)
    cells, pairs = pair_source.shape
    tile_shape = (ROWS, LANES)
    row = lax.broadcasted_iota(jnp.int32, tile_shape, 0)
    lane = lanes_of(tile_shape).astype(jnp.float32)
    for place, near, sent in source_tiles(own, incoming, border, per_peer):
        tile, other = near(), sent()
        near_table[place] = tile
        wide, heat = tile[WIDE : WIDE + 1, :], other[HEAT : HEAT + 1, :]
        inverse = 2.0 * pl.reciprocal(wide, approx=True)
        inverse = inverse * inverse * inverse
        far_table[place, INV6 : INV6 + 1, :] = inverse * inverse
        far_table[place, HALF : HALF + 1, :] = 0.025 * wide
        far_table[place, SOUND : SOUND + 1, :] = jnp.sqrt(ADIABATIC * heat)
        far_table[place, WARM : WARM + 1, :] = heat
        far_table[place, SUPPORT : SUPPORT + 1, :] = jnp.where(
            lane[0:1, :] < other[LIVE : LIVE + 1, :], wide, -FAR_AWAY
        )

    def choose(cell, carry):
        low = bundle[cell, S_LOW : S_LOW + ROWS, :]
        high = bundle[cell, S_HIGH : S_HIGH + ROWS, :]
        widest = bundle[cell, S_REACH : S_REACH + 1, :]
        kept = []
        for pair in range(pairs):
            source = pair_source[cell, pair]
            tile = near_table[source] + shifts[pair_shift[cell, pair]]
            away = jnp.maximum(jnp.maximum(low - tile, tile - high), 0.0)
            distance = jnp.sum(away * away, axis=0, keepdims=True)
            support = far_table[source, SUPPORT : SUPPORT + 1, :]
            limit = jnp.maximum(support, widest)
            keep = (distance < limit * limit) & (support > 0.0)
            kept.append(jnp.where(keep, 1.0, 0.0))
        target = lane[0:1, :] < bundle[cell, S_CHOSEN : S_CHOSEN + 1, :]
        kept.append(jnp.where(target, 1.0, 0.0))
        kept += [jnp.zeros((1, LANES), jnp.float32)] * (PAIR_ROWS - pairs - 1)
        base = pl.multiple_of(cell * PAIR_ROWS, PAIR_ROWS)
        inside[pl.ds(base, PAIR_ROWS), :] = jnp.concatenate(kept, axis=0)
        return carry

    lax.fori_loop(0, cells, choose, 0, unroll=4)
    flags = inside[...].astype(jnp.bfloat16)
    all_lanes = jnp.ones((ROWS, LANES), jnp.bfloat16)
    sums = lax.dot_general(
        all_lanes, flags, (((1,), (1,)), ((), ())), preferred_element_type=jnp.float32
    )
    for line in range(totals_row.shape[0]):
        totals_row[line : line + 1, :] = sums[0:1, line * LANES : (line + 1) * LANES].astype(
            jnp.int32
        )
    copy = pltpu.make_async_copy(totals_row, totals, sem)
    copy.start()
    square = (LANES, LANES)
    upper = lax.broadcasted_iota(jnp.int32, square, 0) <= lanes_of(square)
    upper = jnp.where(upper, 1.0, 0.0).astype(jnp.bfloat16)
    seen = jnp.dot(flags, upper, preferred_element_type=jnp.float32)
    wanted = lanes_of(seen.shape).astype(jnp.float32)
    slot = jnp.zeros(seen.shape, jnp.int32)
    step = LANES // 2
    while step:
        found = lane_gather(seen, slot + (step - 1))
        slot = jnp.where(found <= wanted, slot + step, slot)
        step //= 2
    orders[...] = slot
    wide, heat, summed = bundle[:, WIDE, :], bundle[:, S_HEAT, :], densities[0]
    inverse = 2.0 * pl.reciprocal(wide, approx=True)
    inverse = inverse * inverse * inverse
    fields = (
        inverse * inverse, 0.025 * wide, jnp.sqrt(ADIABATIC * heat), 4.0 * summed, heat / summed,
    )
    for cell in range(cells):
        tile = jnp.zeros(tile_shape, jnp.float32)
        for which, values in enumerate(fields):
            tile = jnp.where(row == which, values[cell : cell + 1, :], tile)
        columns[cell] = jnp.concatenate([bundle[cell, 0:ROWS, :], tile], axis=0).T
    last[:, F_RANK, :] = bundle[:, S_RANK, :]
    last[:, F_ACTIVE, :] = own_rows(own, ACTIVE)
    last[:, F_STEP, :] = own_rows(own, STEP)
    for from_row, to_row in ((VX, F_VX), (VY, F_VY), (VZ, F_VZ)):
        last[:, to_row, :] = own[:, from_row, :] * (1.0 / SPEED)
    last[:, F_DENS, :] = densities[1]
    last[:, F_DENS + 1, :] = jnp.zeros((cells, LANES), jnp.float32)
    copy.wait()

    def one_cell(cell, carry):
        tables = (
            lambda source, pair: near_table[source] + shifts[pair_shift[cell, pair]],
            lambda source, pair: far_table[source],
        )
        start = jnp.int32(0)
        begins, turned = [], []
        for pair in range(pairs):
            begins.append(start)
            place = cell * PAIR_ROWS + pair
            turned.append(pltpu.roll(orders[pl.ds(place, 1), :], start & (LANES - 1), 1))
            start = start + totals[place >> 7, place & (LANES - 1)]
        begins.append(start)
        turned += [turned[-1]] * (PAIR_ROWS - pairs)
        for pair, begin in enumerate(begins):
            starts[cell, pair] = begin
        place = cell * PAIR_ROWS + pairs
        starts[cell, pairs + 1] = totals[place >> 7, place & (LANES - 1)]
        fill_streams(
            (near_streams.at[cell], far_streams.at[cell]), tables, pair_source,
            lambda pair: begins[pair], lambda pair: turned[pair], cell,
        )
        base = pl.multiple_of(cell * PAIR_ROWS, PAIR_ROWS)
        orders[pl.ds(base, PAIR_ROWS), :] = jnp.concatenate(turned, axis=0)
        return carry

    lax.fori_loop(0, cells, one_cell, 0, unroll=2)


def force_kernel(
    per_peer, pair_source, starts,
    columns, orders, last, new_density, new_border, near_streams, far_streams,
    acceleration, kicked,
    table, streams, sums, lines,
):
    cells, peers = last.shape[0], new_density.shape[0]
    pairs = pair_source.shape[1]
    for cell in range(cells):
        table[cell, 0:1, :] = last[cell, F_DENS : F_DENS + 1, :]
    for peer in range(peers):
        for entry in range(per_peer):
            place = cells + peer * per_peer + entry
            table[place, 0:1, :] = new_density[peer, entry : entry + 1, :]
    for side in range(2):
        table[cells + peers * per_peer + side, 0:1, :] = new_border[side : side + 1, :]

    def one_stream(cell, carry):
        fill_streams(
            (streams.at[cell],), (lambda source, pair: table[source],), pair_source,
            lambda pair: starts[cell, pair],
            lambda pair: orders[pl.ds(cell * PAIR_ROWS + pair, 1), :], cell,
        )
        return carry

    lax.fori_loop(0, cells, one_stream, 0, unroll=4)

    def one_cell(cell, carry):
        near, far, stream = near_streams.at[cell], far_streams.at[cell], streams.at[cell]
        used = (starts[cell, pairs] + LANES - 1) >> 7
        rounds = (used + FORCE_UNROLL - 1) // FORCE_UNROLL

        def one_chunk(base, groups):
            size = groups * ROWS
            mine = columns[cell, pl.ds(base, size), :]
            place = [spread(mine, field) for field in (X, Y, Z)]
            speed = [spread(mine, field) for field in (VX, VY, VZ)]
            wide = spread(mine, WIDE)
            inv6, half_, sound, dens4, press = [spread(mine, ROWS + field) for field in range(5)]

            def blocks(index, totals):
                for sub in range(FORCE_UNROLL):
                    block = index * FORCE_UNROLL + sub
                    s = lambda field: near[block, field : field + 1, :]
                    o = lambda field: far[block, field : field + 1, :]
                    dens = stream[block, 0:1, :]
                    their_press = o(WARM) * pl.reciprocal(jnp.maximum(dens, 1e-30), approx=True)
                    apart = [place[c] - s(c) for c in range(3)]
                    square = apart[0] * apart[0] + apart[1] * apart[1] + apart[2] * apart[2]
                    inverse = lax.rsqrt(jnp.maximum(square, 1e-24))
                    radius = square * inverse
                    double = radius + radius
                    outer = jnp.maximum(wide - radius, 0.0)
                    inner = jnp.maximum(wide - double, 0.0)
                    slope = inv6 * (outer * outer - inner * inner)
                    outer = jnp.maximum(s(WIDE) - radius, 0.0)
                    inner = jnp.maximum(s(WIDE) - double, 0.0)
                    slope = slope + o(INV6) * (outer * outer - inner * inner)
                    approach = (
                        (speed[0] - s(VX)) * apart[0]
                        + (speed[1] - s(VY)) * apart[1]
                        + (speed[2] - s(VZ)) * apart[2]
                    )
                    half = half_ + o(HALF)
                    slow = pl.reciprocal(square + half * half, approx=True)
                    mu = half * jnp.minimum(approach, 0.0) * slow
                    light = pl.reciprocal(dens4 + 4.0 * dens, approx=True)
                    viscous = mu * (mu - (sound + o(SOUND))) * light
                    weight = (press + their_press + viscous) * (slope * (inverse * s(MASS)))
                    totals = tuple(total + weight * a for total, a in zip(totals, apart))
                return totals

            zero = jnp.zeros((size, LANES), jnp.float32)
            totals = lax.fori_loop(0, rounds, blocks, (zero, zero, zero))
            for c in range(3):
                sums[cell, pl.ds(base, size), c : c + 1] = jnp.sum(
                    totals[c], axis=1, keepdims=True
                )

        over_targets(starts[cell, pairs + 1], one_chunk)
        return carry

    lax.fori_loop(0, cells, one_cell, 0)
    for cell in range(cells):
        turned = sums[cell].T
        for c in range(3):
            lines[c, cell : cell + 1, :] = turned[c : c + 1, :]
    rank = last[:, F_RANK, :].astype(jnp.int32)
    for c in range(3):
        gathered = lane_gather(lines[c] * (0.375 / math.pi), rank)
        value = jnp.where(last[:, F_ACTIVE, :] > 0.5, gathered, 0.0)
        acceleration[c] = value
        kicked[c] = last[:, F_VX + c, :] + value * last[:, F_STEP, :]


def shards(
    position, velocity, smoothing, particle_mass, energy, density_old, cell_count, active,
    time_bin, pair_source, pair_shift, export,
):
    cells, capacity = smoothing.shape
    peers, per_peer = export.shape
    sources = cells + peers * per_peer + 2
    codes = 27
    f32 = lambda *shape: jax.ShapeDtypeStruct(shape, jnp.float32)
    smem = pl.BlockSpec(memory_space=pltpu.SMEM)
    vmem = pl.BlockSpec(memory_space=pltpu.VMEM)
    hbm = pl.BlockSpec(memory_space=pltpu.HBM)
    whole = pltpu.CompilerParams(vmem_limit_bytes=64 * 2**20)
    params = pltpu.CompilerParams(vmem_limit_bytes=24 * 2**20)
    cost = pl.CostEstimate(flops=10**9, bytes_accessed=1000, transcendentals=0)
    i32 = lambda *shape: jax.ShapeDtypeStruct(shape, jnp.int32)
    sent_rows = per_peer * (ROWS + SENT)
    turned = export.T

    def landing(scalars, *arrays):
        return (
            [pltpu.SMEM(a.shape, a.dtype) for a in arrays[:scalars]]
            + [pltpu.VMEM(a.shape, a.dtype) for a in arrays[scalars:]]
            + [pltpu.SemaphoreType.DMA((len(arrays),))]
        )

    arrays = (
        cell_count, turned, position, velocity, smoothing, particle_mass, energy, density_old,
        active, time_bin,
    )
    own, outgoing, border = pl.pallas_call(
        pack_kernel,
        out_shape=(
            f32(cells, 2 * ROWS, capacity),
            f32(peers, sent_rows, capacity),
            f32(2, ROWS + SENT, capacity),
        ),
        in_specs=[hbm] * 10,
        out_specs=(vmem,) * 3,
        scratch_shapes=landing(2, *arrays),
        compiler_params=whole,
        cost_estimate=cost,
        name="pack",
    )(*arrays)

    def exchange(pieces):
        return lax.all_to_all(pieces, "cell", split_axis=0, concat_axis=0, tiled=True)

    def swap_border(pieces):
        size = lax.axis_size("region")
        up = [(i, (i + 1) % size) for i in range(size)]
        down = [(j, i) for i, j in up]
        if size == 2:
            return lax.ppermute(pieces, "region", up)
        before = lax.ppermute(pieces[0:1], "region", up)
        after = lax.ppermute(pieces[1:2], "region", down)
        return jnp.concatenate([before, after], axis=0)

    incoming = exchange(outgoing)
    other = swap_border(border)
    actives, bundle, spreads = pl.pallas_call(
        sort_kernel,
        out_shape=(
            i32(1, cells),
            f32(cells, S_ROWS, capacity),
            f32(cells, capacity // ROWS, len(SPREAD) * ROWS, capacity),
        ),
        in_specs=[vmem],
        out_specs=(smem, vmem, vmem),
        scratch_shapes=[pltpu.VMEM((cells, capacity, ROWS), jnp.float32)],
        compiler_params=params,
        cost_estimate=cost,
        name="sort",
    )(own)

    density, densities, outgoing_density, border_density = pl.pallas_call(
        functools.partial(density_kernel, per_peer),
        out_shape=(
            f32(cells, capacity),
            f32(2, cells, capacity),
            f32(peers, per_peer, capacity),
            f32(2, capacity),
        ),
        in_specs=[smem] * 4 + [vmem] * 5,
        out_specs=(vmem,) * 4,
        scratch_shapes=[
            pltpu.VMEM((sources, ROWS, capacity), jnp.float32),
            pltpu.VMEM((codes, ROWS, capacity), jnp.float32),
            pltpu.VMEM((cells, capacity, ROWS), jnp.float32),
            pltpu.VMEM((cells, capacity), jnp.float32),
        ],
        compiler_params=params,
        cost_estimate=cost,
        name="density",
    )(pair_source, pair_shift, turned, actives, own, incoming, other, bundle, spreads)

    new_density = exchange(outgoing_density)
    new_border = swap_border(border_density)
    pairs = pair_source.shape[1]
    blocks = pairs + SPARE
    pair_rows = cells * PAIR_ROWS
    near_streams, far_streams, starts, orders, columns, last = pl.pallas_call(
        functools.partial(stream_kernel, per_peer),
        out_shape=(
            f32(cells, blocks, ROWS, capacity),
            f32(cells, blocks, ROWS, capacity),
            i32(cells, pairs + 2),
            i32(pair_rows, capacity),
            f32(cells, capacity, 2 * ROWS),
            f32(cells, ROWS, capacity),
        ),
        in_specs=[smem] * 2 + [vmem] * 5,
        out_specs=(vmem, vmem, smem, vmem, vmem, vmem),
        scratch_shapes=[
            pltpu.VMEM((sources, ROWS, capacity), jnp.float32),
            pltpu.VMEM((sources, ROWS, capacity), jnp.float32),
            pltpu.VMEM((codes, ROWS, capacity), jnp.float32),
            pltpu.VMEM((pair_rows, capacity), jnp.float32),
            pltpu.VMEM((pair_rows // capacity, capacity), jnp.int32),
            pltpu.SMEM((pair_rows // capacity, capacity), jnp.int32),
            pltpu.SemaphoreType.DMA,
        ],
        compiler_params=params,
        cost_estimate=cost,
        name="streams",
    )(pair_source, pair_shift, own, incoming, other, bundle, densities)

    acceleration, kicked = pl.pallas_call(
        functools.partial(force_kernel, per_peer),
        out_shape=(f32(3, cells, capacity), f32(3, cells, capacity)),
        in_specs=[smem] * 2 + [vmem] * 7,
        out_specs=(vmem,) * 2,
        scratch_shapes=[
            pltpu.VMEM((sources, ROWS, capacity), jnp.float32),
            pltpu.VMEM((cells, blocks, ROWS, capacity), jnp.float32),
            pltpu.VMEM((cells, capacity, ROWS), jnp.float32),
            pltpu.VMEM((3, cells, capacity), jnp.float32),
        ],
        compiler_params=params,
        cost_estimate=cost,
        name="force",
    )(
        pair_source, starts, columns, orders, last, new_density, new_border, near_streams,
        far_streams,
    )
    return density, acceleration, kicked


def solution(mesh):
    rows = P(("region", "cell"), None)
    planes = P(None, ("region", "cell"), None)
    return jax.shard_map(
        shards,
        mesh=mesh,
        in_specs=(
            planes, planes, rows, rows, rows, rows, P(("region", "cell")), rows, rows, rows, rows,
            rows,
        ),
        out_specs=(rows, planes, planes),
        check_vma=False,
    )
```

```python
import functools
import math

import jax
import jax.numpy as jnp
from jax import lax
from jax.experimental import pallas as pl
from jax.experimental.pallas import tpu as pltpu
from jax.sharding import PartitionSpec as P

ADIABATIC = 5.0 / 3.0
STEP_MAX = 0.2
LANES = 128
ROWS = 8
FORCE_UNROLL = 7
CHUNK = 16
TASKS = 4
PAIR_ROWS = 32
FAR_AWAY = 1e9
SPARE = FORCE_UNROLL

X, Y, Z, MASS, VX, VY, VZ, WIDE = range(ROWS)
SPREAD = (X, Y, Z, WIDE)
HEAT, DENS, LIVE = range(3)
SENT = 4
SPEED = 40.0
ACTIVE, STEP = SENT, SENT + 1
S_HEAT, S_RANK, S_REACH, S_CHOSEN = range(ROWS, ROWS + 4)
S_LOW, S_HIGH, S_ROWS = 2 * ROWS, 3 * ROWS, 4 * ROWS
F_RANK, F_ACTIVE, F_STEP, F_VX, F_VY, F_VZ, F_DENS = range(7)
INV6, HALF, SOUND, WARM, SUPPORT = range(5)


def lane_gather(values, index):
    return jnp.take_along_axis(values, index, axis=1, mode="promise_in_bounds")


def lanes_of(shape):
    return lax.broadcasted_iota(jnp.int32, shape, len(shape) - 1)


def start_copies(arrays, landed, sem):
    copies = [
        pltpu.make_async_copy(array, place, sem.at[index])
        for index, (array, place) in enumerate(zip(arrays, landed))
    ]
    for copy in copies:
        copy.start()
    return copies


def pack_kernel(*refs):
    arrays, (own, outgoing, border) = refs[:10], refs[10:13]
    landed, sem = refs[13:-1], refs[-1]
    for copy in start_copies(arrays, landed, sem):
        copy.wait()
    count, export, position, velocity, smoothing, mass, energy, density_old, active, time_bin = landed
    cells = smoothing.shape[0]
    shape = smoothing.shape
    lane = lanes_of(shape)
    row = lax.broadcasted_iota(jnp.int32, shape, 0)
    counts = jnp.zeros(shape, jnp.int32)
    for cell in range(cells):
        counts = jnp.where(row == cell, count[cell], counts)
    mass_live = jnp.where(lane < counts, mass[...], 0.0)
    zeros = jnp.zeros(shape, jnp.float32)
    rows = (
        position[0], position[1], position[2], mass_live,
        SPEED * velocity[0], SPEED * velocity[1], SPEED * velocity[2], 2.0 * smoothing[...],
        (ADIABATIC - 1.0) * energy[...], density_old[...], counts.astype(jnp.float32), zeros,
        jnp.where(active[...] > 0, 1.0, 0.0),
        STEP_MAX * jnp.exp2(-time_bin[...].astype(jnp.float32)), zeros, zeros,
    )
    for field, values in enumerate(rows):
        own[:, field, :] = values
    per_peer, peers = export.shape
    for peer in range(peers):
        for entry in range(per_peer):
            cell = export[entry, peer]
            outgoing[peer, entry * ROWS : (entry + 1) * ROWS, :] = own[cell, 0:ROWS, :]
            start = per_peer * ROWS + entry * SENT
            outgoing[peer, start : start + SENT, :] = own[cell, ROWS : ROWS + SENT, :]
    for side, cell in enumerate((cells - 1, 0)):
        border[side] = own[cell, 0 : ROWS + SENT, :]


def own_rows(own, field):
    return own[:, ROWS + field, :]


def sort_kernel(own, actives, bundle, spreads, columns):
    cells = own.shape[0]
    shape = (cells, LANES)
    lane = lanes_of(shape)
    ones = own_rows(own, ACTIVE)
    is_active = ones > 0.5
    for cell in range(cells):
        actives[0, cell] = jnp.sum(ones[cell : cell + 1, :]).astype(jnp.int32)
    square = (LANES, LANES)
    upper = lax.broadcasted_iota(jnp.int32, square, 0) <= lanes_of(square)
    upper = jnp.where(upper, 1.0, 0.0).astype(jnp.bfloat16)
    seen = jnp.dot(ones.astype(jnp.bfloat16), upper, preferred_element_type=jnp.float32)
    seen = seen.astype(jnp.int32)
    chosen = lane_gather(seen, jnp.full(shape, LANES - 1, jnp.int32))
    others = lane + 1 - seen
    rank = jnp.where(is_active, seen - 1, chosen + others - 1)
    first_part = lane < chosen
    wanted = jnp.where(first_part, lane, lane - chosen)
    slot = jnp.zeros(shape, jnp.int32)
    step = LANES // 2
    while step:
        probe = slot + (step - 1)
        found = jnp.where(first_part, lane_gather(seen, probe), lane_gather(others, probe))
        slot = jnp.where(found <= wanted, slot + step, slot)
        step //= 2
    bundle[:, S_HEAT, :] = lane_gather(own_rows(own, HEAT), slot)
    bundle[:, S_RANK, :] = rank.astype(jnp.float32)
    bundle[:, S_CHOSEN, :] = chosen.astype(jnp.float32)
    for spare in range(S_CHOSEN + 1, S_LOW):
        bundle[:, spare, :] = jnp.zeros(shape, jnp.float32)
    place = lax.broadcasted_iota(jnp.int32, (ROWS, LANES), 0) <= Z
    for cell in range(cells):
        order = jnp.broadcast_to(slot[cell : cell + 1, :], (ROWS, LANES))
        tile = lane_gather(own[cell, 0:ROWS, :], order)
        bundle[cell, 0:ROWS, :] = tile
        target = lane < chosen[cell : cell + 1, :]
        low = jnp.min(jnp.where(target, tile, FAR_AWAY), axis=1, keepdims=True)
        high = jnp.max(jnp.where(target, tile, -FAR_AWAY), axis=1, keepdims=True)
        bundle[cell, S_LOW : S_LOW + ROWS, :] = jnp.where(place, low, -FAR_AWAY)
        bundle[cell, S_HIGH : S_HIGH + ROWS, :] = jnp.where(place, high, FAR_AWAY)
        bundle[cell, S_REACH : S_REACH + 1, :] = jnp.broadcast_to(high[WIDE : WIDE + 1, :], (1, LANES))
        columns[cell] = tile.T

    def one_cell(cell, carry):
        def one_pair(pair, carry):
            base = pl.multiple_of(pair * 2 * ROWS, 2 * ROWS)
            mine = columns[cell, pl.ds(base, 2 * ROWS), :]
            for which, field in enumerate(SPREAD):
                tiles = spread(mine, field).reshape(2, ROWS, LANES)
                spreads[cell, pl.ds(pair * 2, 2), which * ROWS : (which + 1) * ROWS, :] = tiles
            return carry

        return lax.fori_loop(0, (actives[0, cell] + 2 * ROWS - 1) // (2 * ROWS), one_pair, carry)

    lax.fori_loop(0, cells, one_cell, 0)


def source_tiles(own, incoming, border, per_peer):
    cells, peers = own.shape[0], incoming.shape[0]
    for cell in range(cells):
        yield (
            cell, lambda c=cell: own[c, 0:ROWS, :], lambda c=cell: own[c, ROWS : ROWS + SENT, :]
        )
    for peer in range(peers):
        for entry in range(per_peer):
            near, sent = entry * ROWS, per_peer * ROWS + entry * SENT
            yield (
                cells + peer * per_peer + entry,
                lambda p=peer, n=near: incoming[p, n : n + ROWS, :],
                lambda p=peer, n=sent: incoming[p, n : n + SENT, :],
            )
    for side in range(2):
        yield (
            cells + peers * per_peer + side,
            lambda b=side: border[b, 0:ROWS, :],
            lambda b=side: border[b, ROWS : ROWS + SENT, :],
        )


def fill_shifts(shifts):
    row = lax.broadcasted_iota(jnp.int32, (ROWS, LANES), 0)
    for code in range(shifts.shape[0]):
        first, second, third = code // 9 - 1.0, code // 3 % 3 - 1.0, code % 3 - 1.0
        shifts[code] = jnp.where(
            row == X, first, jnp.where(row == Y, second, jnp.where(row == Z, third, 0.0))
        )


def fill_streams(streams, tables, sources, starts, orders, cell):
    shape = (ROWS, LANES)
    lane = lanes_of(shape)
    pairs = sources.shape[1]
    moved = []
    for pair in range(pairs):
        order = jnp.broadcast_to(orders(pair), shape)
        moved.append([lane_gather(load(sources[cell, pair], pair), order) for load in tables])
    for pair in range(pairs):
        start = starts(pair)
        block = start >> 7
        fresh = lane >= (start & (LANES - 1))
        for which, stream in enumerate(streams):
            stream[block + 1] = moved[pair][which]
            pltpu.store(stream.at[block], moved[pair][which], mask=fresh)
    end = starts(pairs)
    block = end >> 7
    for stream in streams:
        stream[block] = jnp.where(lane < (end & (LANES - 1)), stream[block], 0.0)
        for extra in range(1, SPARE):
            stream[block + extra] = jnp.zeros(shape, jnp.float32)


def spread(values, field):
    return jnp.broadcast_to(values[:, field : field + 1], (values.shape[0], LANES))


def over_targets(active, one_chunk):
    groups = (active + ROWS - 1) // ROWS

    def large(chunk, carry):
        one_chunk(pl.multiple_of(chunk * 4 * ROWS, ROWS), 4)
        return carry

    lax.fori_loop(0, groups // 4, large, 0)
    for size in (2, 1):

        @pl.when((groups & size) != 0)
        def _(size=size):
            done = groups & -(2 * size)
            one_chunk(pl.multiple_of(done * ROWS, ROWS), size)


def density_kernel(
    per_peer, pair_source, pair_shift, export, actives,
    own, incoming, border, bundle, spreads,
    density, densities, outgoing, outgoing_border,
    table, shifts, sums, lines,
):
    fill_shifts(shifts)
    cells, peers = own.shape[0], incoming.shape[0]
    for place, near, _ in source_tiles(own, incoming, border, per_peer):
        table[place] = near()

    def one_cell(cell, carry):
        def one_chunk(base, groups):
            size = groups * ROWS
            at = pl.ds(base // ROWS, groups)
            *place, wide = [
                spreads[cell, at, which * ROWS : (which + 1) * ROWS, :].reshape(size, LANES)
                for which in range(len(SPREAD))
            ]
            smooth = 0.5 * wide

            total = jnp.zeros((size, LANES), jnp.float32)
            for pair in range(pair_source.shape[1]):
                source, code = pair_source[cell, pair], pair_shift[cell, pair]
                s = lambda field: table[source, field : field + 1, :]
                shift = lambda field: shifts[code, field : field + 1, :]
                apart = [place[c] - (s(c) + shift(c)) for c in range(3)]
                square = apart[0] * apart[0] + apart[1] * apart[1] + apart[2] * apart[2]
                radius = square * lax.rsqrt(jnp.maximum(square, 1e-24))
                outer = jnp.maximum(wide - radius, 0.0)
                inner = jnp.maximum(smooth - radius, 0.0)
                value = outer * outer * outer - 4.0 * (inner * inner * inner)
                total = total + s(MASS) * value
            sums[cell, pl.ds(base, size), 0:1] = jnp.sum(total, axis=1, keepdims=True)

        over_targets(actives[0, cell], one_chunk)
        return carry

    lax.fori_loop(0, cells, one_cell, 0)
    for cell in range(cells):
        lines[cell : cell + 1, :] = sums[cell].T[0:1, :]
    inverse = 2.0 / bundle[:, WIDE, :]
    inverse = inverse * inverse * inverse
    summed = lines[...] * (0.25 / math.pi) * (inverse * inverse)
    rank = bundle[:, S_RANK, :].astype(jnp.int32)
    density[...] = jnp.where(
        own_rows(own, ACTIVE) > 0.5, lane_gather(summed, rank), own_rows(own, DENS)
    )
    densities[0] = summed
    densities[1] = density[...]
    for peer in range(peers):
        for entry in range(per_peer):
            outgoing[peer, entry : entry + 1, :] = density[pl.ds(export[entry, peer], 1), :]
    outgoing_border[0:1, :] = density[cells - 1 : cells, :]
    outgoing_border[1:2, :] = density[0:1, :]


def stream_kernel(
    per_peer, pair_source, pair_shift, own, incoming, border, bundle, densities,
    near_streams, far_streams, starts, orders, columns, last,
    near_table, far_table, shifts, inside, totals_row, totals, sem,
):
    fill_shifts(shifts)
    cells, pairs = pair_source.shape
    tile_shape = (ROWS, LANES)
    row = lax.broadcasted_iota(jnp.int32, tile_shape, 0)
    lane = lanes_of(tile_shape).astype(jnp.float32)
    for place, near, sent in source_tiles(own, incoming, border, per_peer):
        tile, other = near(), sent()
        near_table[place] = tile
        wide, heat = tile[WIDE : WIDE + 1, :], other[HEAT : HEAT + 1, :]
        inverse = 2.0 * pl.reciprocal(wide, approx=True)
        inverse = inverse * inverse * inverse
        far_table[place, INV6 : INV6 + 1, :] = inverse * inverse
        far_table[place, HALF : HALF + 1, :] = 0.025 * wide
        far_table[place, SOUND : SOUND + 1, :] = jnp.sqrt(ADIABATIC * heat)
        far_table[place, WARM : WARM + 1, :] = heat
        far_table[place, SUPPORT : SUPPORT + 1, :] = jnp.where(
            lane[0:1, :] < other[LIVE : LIVE + 1, :], wide, -FAR_AWAY
        )

    def choose(cell, carry):
        low = bundle[cell, S_LOW : S_LOW + ROWS, :]
        high = bundle[cell, S_HIGH : S_HIGH + ROWS, :]
        widest = bundle[cell, S_REACH : S_REACH + 1, :]
        kept = []
        for pair in range(pairs):
            source = pair_source[cell, pair]
            tile = near_table[source] + shifts[pair_shift[cell, pair]]
            away = jnp.maximum(jnp.maximum(low - tile, tile - high), 0.0)
            distance = jnp.sum(away * away, axis=0, keepdims=True)
            support = far_table[source, SUPPORT : SUPPORT + 1, :]
            limit = jnp.maximum(support, widest)
            keep = (distance < limit * limit) & (support > 0.0)
            kept.append(jnp.where(keep, 1.0, 0.0))
        target = lane[0:1, :] < bundle[cell, S_CHOSEN : S_CHOSEN + 1, :]
        kept.append(jnp.where(target, 1.0, 0.0))
        kept += [jnp.zeros((1, LANES), jnp.float32)] * (PAIR_ROWS - pairs - 1)
        base = pl.multiple_of(cell * PAIR_ROWS, PAIR_ROWS)
        inside[pl.ds(base, PAIR_ROWS), :] = jnp.concatenate(kept, axis=0)
        return carry

    lax.fori_loop(0, cells, choose, 0, unroll=4)
    flags = inside[...].astype(jnp.bfloat16)
    all_lanes = jnp.ones((ROWS, LANES), jnp.bfloat16)
    sums = lax.dot_general(
        all_lanes, flags, (((1,), (1,)), ((), ())), preferred_element_type=jnp.float32
    )
    for line in range(totals_row.shape[0]):
        totals_row[line : line + 1, :] = sums[0:1, line * LANES : (line + 1) * LANES].astype(
            jnp.int32
        )
    copy = pltpu.make_async_copy(totals_row, totals, sem)
    copy.start()
    square = (LANES, LANES)
    upper = lax.broadcasted_iota(jnp.int32, square, 0) <= lanes_of(square)
    upper = jnp.where(upper, 1.0, 0.0).astype(jnp.bfloat16)
    seen = jnp.dot(flags, upper, preferred_element_type=jnp.float32)
    wanted = lanes_of(seen.shape).astype(jnp.float32)
    slot = jnp.zeros(seen.shape, jnp.int32)
    step = LANES // 2
    while step:
        found = lane_gather(seen, slot + (step - 1))
        slot = jnp.where(found <= wanted, slot + step, slot)
        step //= 2
    orders[...] = slot
    wide, heat, summed = bundle[:, WIDE, :], bundle[:, S_HEAT, :], densities[0]
    inverse = 2.0 * pl.reciprocal(wide, approx=True)
    inverse = inverse * inverse * inverse
    fields = (
        inverse * inverse, 0.025 * wide, jnp.sqrt(ADIABATIC * heat), 4.0 * summed, heat / summed,
    )
    for cell in range(cells):
        tile = jnp.zeros(tile_shape, jnp.float32)
        for which, values in enumerate(fields):
            tile = jnp.where(row == which, values[cell : cell + 1, :], tile)
        columns[cell] = jnp.concatenate([bundle[cell, 0:ROWS, :], tile], axis=0).T
    last[:, F_RANK, :] = bundle[:, S_RANK, :]
    last[:, F_ACTIVE, :] = own_rows(own, ACTIVE)
    last[:, F_STEP, :] = own_rows(own, STEP)
    for from_row, to_row in ((VX, F_VX), (VY, F_VY), (VZ, F_VZ)):
        last[:, to_row, :] = own[:, from_row, :] * (1.0 / SPEED)
    last[:, F_DENS, :] = densities[1]
    last[:, F_DENS + 1, :] = jnp.zeros((cells, LANES), jnp.float32)
    copy.wait()

    def one_cell(cell, carry):
        tables = (
            lambda source, pair: near_table[source] + shifts[pair_shift[cell, pair]],
            lambda source, pair: far_table[source],
        )
        start = jnp.int32(0)
        begins, turned = [], []
        for pair in range(pairs):
            begins.append(start)
            place = cell * PAIR_ROWS + pair
            turned.append(pltpu.roll(orders[pl.ds(place, 1), :], start & (LANES - 1), 1))
            start = start + totals[place >> 7, place & (LANES - 1)]
        begins.append(start)
        turned += [turned[-1]] * (PAIR_ROWS - pairs)
        for pair, begin in enumerate(begins):
            starts[cell, pair] = begin
        place = cell * PAIR_ROWS + pairs
        starts[cell, pairs + 1] = totals[place >> 7, place & (LANES - 1)]
        fill_streams(
            (near_streams.at[cell], far_streams.at[cell]), tables, pair_source,
            lambda pair: begins[pair], lambda pair: turned[pair], cell,
        )
        base = pl.multiple_of(cell * PAIR_ROWS, PAIR_ROWS)
        orders[pl.ds(base, PAIR_ROWS), :] = jnp.concatenate(turned, axis=0)
        return carry

    lax.fori_loop(0, cells, one_cell, 0, unroll=2)


def force_kernel(
    per_peer, pair_source, starts,
    columns, orders, last, new_density, new_border, near_streams, far_streams,
    acceleration, kicked,
    table, streams, sums, lines, counts,
):
    cells, peers = last.shape[0], new_density.shape[0]
    pairs = pair_source.shape[1]
    for cell in range(cells):
        table[cell, 0:1, :] = last[cell, F_DENS : F_DENS + 1, :]
    for peer in range(peers):
        for entry in range(per_peer):
            place = cells + peer * per_peer + entry
            table[place, 0:1, :] = new_density[peer, entry : entry + 1, :]
    for side in range(2):
        table[cells + peers * per_peer + side, 0:1, :] = new_border[side : side + 1, :]

    def one_stream(cell, carry):
        fill_streams(
            (streams.at[cell],), (lambda source, pair: table[source],), pair_source,
            lambda pair: starts[cell, pair],
            lambda pair: orders[pl.ds(cell * PAIR_ROWS + pair, 1), :], cell,
        )
        return carry

    lax.fori_loop(0, cells, one_stream, 0, unroll=4)

    total = jnp.int32(0)
    for cell in range(cells):
        chunks = (starts[cell, pairs + 1] + CHUNK - 1) // CHUNK
        rounds = (((starts[cell, pairs] + LANES - 1) >> 7) + FORCE_UNROLL - 1) // FORCE_UNROLL
        counts[0, cell] = jnp.maximum(chunks, 1)
        counts[1, cell] = jnp.maximum(rounds, 1)
        total = total + counts[0, cell] * counts[1, cell]
        sums[cell] = jnp.zeros(sums.shape[1:], jnp.float32)
    counts[0, cells] = LANES // CHUNK
    counts[1, cells] = 1

    def one_task(task):
        cell, chunk, round_ = task
        real = jnp.minimum(cell, cells - 1)
        base = pl.multiple_of(chunk * CHUNK, CHUNK)
        first = round_ * FORCE_UNROLL
        near, far, stream = near_streams.at[real], far_streams.at[real], streams.at[real]
        mine = columns[real, pl.ds(base, CHUNK), :]
        place = [spread(mine, field) for field in (X, Y, Z)]
        speed = [spread(mine, field) for field in (VX, VY, VZ)]
        wide = spread(mine, WIDE)
        inv6, half_, sound, dens4, press = [spread(mine, ROWS + field) for field in range(5)]
        totals = None
        for sub in range(FORCE_UNROLL):
            block = first + sub
            s = lambda field: near[block, field : field + 1, :]
            o = lambda field: far[block, field : field + 1, :]
            dens = stream[block, 0:1, :]
            their_press = o(WARM) * pl.reciprocal(jnp.maximum(dens, 1e-30), approx=True)
            apart = [place[c] - s(c) for c in range(3)]
            square = apart[0] * apart[0] + apart[1] * apart[1] + apart[2] * apart[2]
            inverse = lax.rsqrt(jnp.maximum(square, 1e-24))
            radius = square * inverse
            double = radius + radius
            outer = jnp.maximum(wide - radius, 0.0)
            inner = jnp.maximum(wide - double, 0.0)
            slope = inv6 * (outer * outer - inner * inner)
            outer = jnp.maximum(s(WIDE) - radius, 0.0)
            inner = jnp.maximum(s(WIDE) - double, 0.0)
            slope = slope + o(INV6) * (outer * outer - inner * inner)
            approach = (
                (speed[0] - s(VX)) * apart[0]
                + (speed[1] - s(VY)) * apart[1]
                + (speed[2] - s(VZ)) * apart[2]
            )
            half = half_ + o(HALF)
            slow = pl.reciprocal(square + half * half, approx=True)
            mu = half * jnp.minimum(approach, 0.0) * slow
            light = pl.reciprocal(dens4 + 4.0 * dens, approx=True)
            viscous = mu * (mu - (sound + o(SOUND))) * light
            weight = (press + their_press + viscous) * (slope * (inverse * s(MASS)))
            terms = [weight * a for a in apart]
            totals = terms if totals is None else [t + a for t, a in zip(totals, terms)]
        found = jnp.concatenate([jnp.sum(t, axis=1, keepdims=True) for t in totals], axis=1)
        at = pl.ds(base, CHUNK)
        sums[cell, at, 0:3] = sums[cell, at, 0:3] + found
        round_ = round_ + 1
        wrapped = round_ >= counts[1, cell]
        chunk = jnp.where(wrapped, chunk + 1, chunk)
        done = chunk >= counts[0, cell]
        return (
            jnp.where(done, jnp.minimum(cell + 1, cells), cell),
            jnp.where(done, 0, chunk),
            jnp.where(wrapped, 0, round_),
        )

    def some_tasks(index, task):
        for _ in range(TASKS):
            task = one_task(task)
        return task

    zero = jnp.int32(0)
    lax.fori_loop(0, (total + TASKS - 1) // TASKS, some_tasks, (zero, zero, zero))
    for cell in range(cells):
        turned = sums[cell].T
        for c in range(3):
            lines[c, cell : cell + 1, :] = turned[c : c + 1, :]
    rank = last[:, F_RANK, :].astype(jnp.int32)
    for c in range(3):
        gathered = lane_gather(lines[c] * (0.375 / math.pi), rank)
        value = jnp.where(last[:, F_ACTIVE, :] > 0.5, gathered, 0.0)
        acceleration[c] = value
        kicked[c] = last[:, F_VX + c, :] + value * last[:, F_STEP, :]


def shards(
    position, velocity, smoothing, particle_mass, energy, density_old, cell_count, active,
    time_bin, pair_source, pair_shift, export,
):
    cells, capacity = smoothing.shape
    peers, per_peer = export.shape
    sources = cells + peers * per_peer + 2
    codes = 27
    f32 = lambda *shape: jax.ShapeDtypeStruct(shape, jnp.float32)
    smem = pl.BlockSpec(memory_space=pltpu.SMEM)
    vmem = pl.BlockSpec(memory_space=pltpu.VMEM)
    hbm = pl.BlockSpec(memory_space=pltpu.HBM)
    whole = pltpu.CompilerParams(vmem_limit_bytes=64 * 2**20)
    params = pltpu.CompilerParams(vmem_limit_bytes=24 * 2**20)
    cost = pl.CostEstimate(flops=10**9, bytes_accessed=1000, transcendentals=0)
    i32 = lambda *shape: jax.ShapeDtypeStruct(shape, jnp.int32)
    sent_rows = per_peer * (ROWS + SENT)
    turned = export.T

    def landing(scalars, *arrays):
        return (
            [pltpu.SMEM(a.shape, a.dtype) for a in arrays[:scalars]]
            + [pltpu.VMEM(a.shape, a.dtype) for a in arrays[scalars:]]
            + [pltpu.SemaphoreType.DMA((len(arrays),))]
        )

    arrays = (
        cell_count, turned, position, velocity, smoothing, particle_mass, energy, density_old,
        active, time_bin,
    )
    own, outgoing, border = pl.pallas_call(
        pack_kernel,
        out_shape=(
            f32(cells, 2 * ROWS, capacity),
            f32(peers, sent_rows, capacity),
            f32(2, ROWS + SENT, capacity),
        ),
        in_specs=[hbm] * 10,
        out_specs=(vmem,) * 3,
        scratch_shapes=landing(2, *arrays),
        compiler_params=whole,
        cost_estimate=cost,
        name="pack",
    )(*arrays)

    def exchange(pieces):
        return lax.all_to_all(pieces, "cell", split_axis=0, concat_axis=0, tiled=True)

    def swap_border(pieces):
        size = lax.axis_size("region")
        up = [(i, (i + 1) % size) for i in range(size)]
        down = [(j, i) for i, j in up]
        if size == 2:
            return lax.ppermute(pieces, "region", up)
        before = lax.ppermute(pieces[0:1], "region", up)
        after = lax.ppermute(pieces[1:2], "region", down)
        return jnp.concatenate([before, after], axis=0)

    incoming = exchange(outgoing)
    other = swap_border(border)
    actives, bundle, spreads = pl.pallas_call(
        sort_kernel,
        out_shape=(
            i32(1, cells),
            f32(cells, S_ROWS, capacity),
            f32(cells, capacity // ROWS, len(SPREAD) * ROWS, capacity),
        ),
        in_specs=[vmem],
        out_specs=(smem, vmem, vmem),
        scratch_shapes=[pltpu.VMEM((cells, capacity, ROWS), jnp.float32)],
        compiler_params=params,
        cost_estimate=cost,
        name="sort",
    )(own)

    density, densities, outgoing_density, border_density = pl.pallas_call(
        functools.partial(density_kernel, per_peer),
        out_shape=(
            f32(cells, capacity),
            f32(2, cells, capacity),
            f32(peers, per_peer, capacity),
            f32(2, capacity),
        ),
        in_specs=[smem] * 4 + [vmem] * 5,
        out_specs=(vmem,) * 4,
        scratch_shapes=[
            pltpu.VMEM((sources, ROWS, capacity), jnp.float32),
            pltpu.VMEM((codes, ROWS, capacity), jnp.float32),
            pltpu.VMEM((cells, capacity, ROWS), jnp.float32),
            pltpu.VMEM((cells, capacity), jnp.float32),
        ],
        compiler_params=params,
        cost_estimate=cost,
        name="density",
    )(pair_source, pair_shift, turned, actives, own, incoming, other, bundle, spreads)

    new_density = exchange(outgoing_density)
    new_border = swap_border(border_density)
    pairs = pair_source.shape[1]
    blocks = pairs + SPARE
    pair_rows = cells * PAIR_ROWS
    near_streams, far_streams, starts, orders, columns, last = pl.pallas_call(
        functools.partial(stream_kernel, per_peer),
        out_shape=(
            f32(cells, blocks, ROWS, capacity),
            f32(cells, blocks, ROWS, capacity),
            i32(cells, pairs + 2),
            i32(pair_rows, capacity),
            f32(cells, capacity, 2 * ROWS),
            f32(cells, ROWS, capacity),
        ),
        in_specs=[smem] * 2 + [vmem] * 5,
        out_specs=(vmem, vmem, smem, vmem, vmem, vmem),
        scratch_shapes=[
            pltpu.VMEM((sources, ROWS, capacity), jnp.float32),
            pltpu.VMEM((sources, ROWS, capacity), jnp.float32),
            pltpu.VMEM((codes, ROWS, capacity), jnp.float32),
            pltpu.VMEM((pair_rows, capacity), jnp.float32),
            pltpu.VMEM((pair_rows // capacity, capacity), jnp.int32),
            pltpu.SMEM((pair_rows // capacity, capacity), jnp.int32),
            pltpu.SemaphoreType.DMA,
        ],
        compiler_params=params,
        cost_estimate=cost,
        name="streams",
    )(pair_source, pair_shift, own, incoming, other, bundle, densities)

    acceleration, kicked = pl.pallas_call(
        functools.partial(force_kernel, per_peer),
        out_shape=(f32(3, cells, capacity), f32(3, cells, capacity)),
        in_specs=[smem] * 2 + [vmem] * 7,
        out_specs=(vmem,) * 2,
        scratch_shapes=[
            pltpu.VMEM((sources, ROWS, capacity), jnp.float32),
            pltpu.VMEM((cells, blocks, ROWS, capacity), jnp.float32),
            pltpu.VMEM((cells + 1, capacity, ROWS), jnp.float32),
            pltpu.VMEM((3, cells, capacity), jnp.float32),
            pltpu.SMEM((2, cells + 1), jnp.int32),
        ],
        compiler_params=params,
        cost_estimate=cost,
        name="force",
    )(
        pair_source, starts, columns, orders, last, new_density, new_border, near_streams,
        far_streams,
    )
    return density, acceleration, kicked


def solution(mesh):
    rows = P(("region", "cell"), None)
    planes = P(None, ("region", "cell"), None)
    return jax.shard_map(
        shards,
        mesh=mesh,
        in_specs=(
            planes, planes, rows, rows, rows, rows, P(("region", "cell")), rows, rows, rows, rows,
            rows,
        ),
        out_specs=(rows, planes, planes),
        check_vma=False,
    )
```

```python
import functools
import math

import jax
import jax.numpy as jnp
from jax import lax
from jax.experimental import pallas as pl
from jax.experimental.pallas import tpu as pltpu
from jax.sharding import PartitionSpec as P

ADIABATIC = 5.0 / 3.0
STEP_MAX = 0.2
LANES = 128
ROWS = 8
FORCE_UNROLL = 7
CHUNK = 16
TASKS = 4
PAIR_ROWS = 32
FAR_AWAY = 1e9
SPARE = FORCE_UNROLL

X, Y, Z, MASS, VX, VY, VZ, WIDE = range(ROWS)
SPREAD = (X, Y, Z, WIDE)
HEAT, DENS, LIVE = range(3)
SENT = 4
SPEED = 40.0
ACTIVE, STEP = SENT, SENT + 1
S_HEAT, S_RANK, S_REACH, S_CHOSEN = range(ROWS, ROWS + 4)
S_LOW, S_HIGH, S_ROWS = 2 * ROWS, 3 * ROWS, 4 * ROWS
F_RANK, F_ACTIVE, F_STEP, F_VX, F_VY, F_VZ, F_DENS = range(7)
INV6, HALF, SOUND, WARM, SUPPORT = range(5)


def lane_gather(values, index):
    return jnp.take_along_axis(values, index, axis=1, mode="promise_in_bounds")


def lanes_of(shape):
    return lax.broadcasted_iota(jnp.int32, shape, len(shape) - 1)


def start_copies(arrays, landed, sem):
    copies = [
        pltpu.make_async_copy(array, place, sem.at[index])
        for index, (array, place) in enumerate(zip(arrays, landed))
    ]
    for copy in copies:
        copy.start()
    return copies


def pack_kernel(*refs):
    arrays, (own, outgoing, border) = refs[:10], refs[10:13]
    landed, sem = refs[13:-1], refs[-1]
    for copy in start_copies(arrays, landed, sem):
        copy.wait()
    count, export, position, velocity, smoothing, mass, energy, density_old, active, time_bin = landed
    cells = smoothing.shape[0]
    shape = smoothing.shape
    lane = lanes_of(shape)
    row = lax.broadcasted_iota(jnp.int32, shape, 0)
    counts = jnp.zeros(shape, jnp.int32)
    for cell in range(cells):
        counts = jnp.where(row == cell, count[cell], counts)
    mass_live = jnp.where(lane < counts, mass[...], 0.0)
    zeros = jnp.zeros(shape, jnp.float32)
    rows = (
        position[0], position[1], position[2], mass_live,
        SPEED * velocity[0], SPEED * velocity[1], SPEED * velocity[2], 2.0 * smoothing[...],
        (ADIABATIC - 1.0) * energy[...], density_old[...], counts.astype(jnp.float32), zeros,
        jnp.where(active[...] > 0, 1.0, 0.0),
        STEP_MAX * jnp.exp2(-time_bin[...].astype(jnp.float32)), zeros, zeros,
    )
    for field, values in enumerate(rows):
        own[:, field, :] = values
    per_peer, peers = export.shape
    for peer in range(peers):
        for entry in range(per_peer):
            cell = export[entry, peer]
            outgoing[peer, entry * ROWS : (entry + 1) * ROWS, :] = own[cell, 0:ROWS, :]
            start = per_peer * ROWS + entry * SENT
            outgoing[peer, start : start + SENT, :] = own[cell, ROWS : ROWS + SENT, :]
    for side, cell in enumerate((cells - 1, 0)):
        border[side] = own[cell, 0 : ROWS + SENT, :]


def own_rows(own, field):
    return own[:, ROWS + field, :]


def sort_kernel(own, actives, bundle, spreads, columns):
    cells = own.shape[0]
    shape = (cells, LANES)
    lane = lanes_of(shape)
    ones = own_rows(own, ACTIVE)
    is_active = ones > 0.5
    for cell in range(cells):
        actives[0, cell] = jnp.sum(ones[cell : cell + 1, :]).astype(jnp.int32)
    square = (LANES, LANES)
    upper = lax.broadcasted_iota(jnp.int32, square, 0) <= lanes_of(square)
    upper = jnp.where(upper, 1.0, 0.0).astype(jnp.bfloat16)
    seen = jnp.dot(ones.astype(jnp.bfloat16), upper, preferred_element_type=jnp.float32)
    seen = seen.astype(jnp.int32)
    chosen = lane_gather(seen, jnp.full(shape, LANES - 1, jnp.int32))
    others = lane + 1 - seen
    rank = jnp.where(is_active, seen - 1, chosen + others - 1)
    first_part = lane < chosen
    wanted = jnp.where(first_part, lane, lane - chosen)
    slot = jnp.zeros(shape, jnp.int32)
    step = LANES // 2
    while step:
        probe = slot + (step - 1)
        found = jnp.where(first_part, lane_gather(seen, probe), lane_gather(others, probe))
        slot = jnp.where(found <= wanted, slot + step, slot)
        step //= 2
    bundle[:, S_HEAT, :] = lane_gather(own_rows(own, HEAT), slot)
    bundle[:, S_RANK, :] = rank.astype(jnp.float32)
    bundle[:, S_CHOSEN, :] = chosen.astype(jnp.float32)
    for spare in range(S_CHOSEN + 1, S_LOW):
        bundle[:, spare, :] = jnp.zeros(shape, jnp.float32)
    place = lax.broadcasted_iota(jnp.int32, (ROWS, LANES), 0) <= Z
    for cell in range(cells):
        order = jnp.broadcast_to(slot[cell : cell + 1, :], (ROWS, LANES))
        tile = lane_gather(own[cell, 0:ROWS, :], order)
        bundle[cell, 0:ROWS, :] = tile
        target = lane < chosen[cell : cell + 1, :]
        low = jnp.min(jnp.where(target, tile, FAR_AWAY), axis=1, keepdims=True)
        high = jnp.max(jnp.where(target, tile, -FAR_AWAY), axis=1, keepdims=True)
        bundle[cell, S_LOW : S_LOW + ROWS, :] = jnp.where(place, low, -FAR_AWAY)
        bundle[cell, S_HIGH : S_HIGH + ROWS, :] = jnp.where(place, high, FAR_AWAY)
        bundle[cell, S_REACH : S_REACH + 1, :] = jnp.broadcast_to(high[WIDE : WIDE + 1, :], (1, LANES))
        columns[cell] = tile.T

    def one_cell(cell, carry):
        def one_pair(pair, carry):
            base = pl.multiple_of(pair * 2 * ROWS, 2 * ROWS)
            mine = columns[cell, pl.ds(base, 2 * ROWS), :]
            for which, field in enumerate(SPREAD):
                tiles = spread(mine, field).reshape(2, ROWS, LANES)
                spreads[cell, pl.ds(pair * 2, 2), which * ROWS : (which + 1) * ROWS, :] = tiles
            return carry

        return lax.fori_loop(0, (actives[0, cell] + 2 * ROWS - 1) // (2 * ROWS), one_pair, carry)

    lax.fori_loop(0, cells, one_cell, 0)


def source_tiles(own, incoming, border, per_peer):
    cells, peers = own.shape[0], incoming.shape[0]
    for cell in range(cells):
        yield (
            cell, lambda c=cell: own[c, 0:ROWS, :], lambda c=cell: own[c, ROWS : ROWS + SENT, :]
        )
    for peer in range(peers):
        for entry in range(per_peer):
            near, sent = entry * ROWS, per_peer * ROWS + entry * SENT
            yield (
                cells + peer * per_peer + entry,
                lambda p=peer, n=near: incoming[p, n : n + ROWS, :],
                lambda p=peer, n=sent: incoming[p, n : n + SENT, :],
            )
    for side in range(2):
        yield (
            cells + peers * per_peer + side,
            lambda b=side: border[b, 0:ROWS, :],
            lambda b=side: border[b, ROWS : ROWS + SENT, :],
        )


def fill_shifts(shifts):
    row = lax.broadcasted_iota(jnp.int32, (ROWS, LANES), 0)
    for code in range(shifts.shape[0]):
        first, second, third = code // 9 - 1.0, code // 3 % 3 - 1.0, code % 3 - 1.0
        shifts[code] = jnp.where(
            row == X, first, jnp.where(row == Y, second, jnp.where(row == Z, third, 0.0))
        )


def fill_streams(streams, tables, sources, starts, orders, cell):
    shape = (ROWS, LANES)
    lane = lanes_of(shape)
    pairs = sources.shape[1]
    moved = []
    for pair in range(pairs):
        order = jnp.broadcast_to(orders(pair), shape)
        moved.append([lane_gather(load(sources[cell, pair], pair), order) for load in tables])
    for pair in range(pairs):
        start = starts(pair)
        block = start >> 7
        fresh = lane >= (start & (LANES - 1))
        for which, stream in enumerate(streams):
            stream[block + 1] = moved[pair][which]
            pltpu.store(stream.at[block], moved[pair][which], mask=fresh)
    end = starts(pairs)
    block = end >> 7
    for stream in streams:
        stream[block] = jnp.where(lane < (end & (LANES - 1)), stream[block], 0.0)
        for extra in range(1, SPARE):
            stream[block + extra] = jnp.zeros(shape, jnp.float32)


def spread(values, field):
    return jnp.broadcast_to(values[:, field : field + 1], (values.shape[0], LANES))


def over_targets(active, one_chunk):
    groups = (active + ROWS - 1) // ROWS

    def large(chunk, carry):
        one_chunk(pl.multiple_of(chunk * 4 * ROWS, ROWS), 4)
        return carry

    lax.fori_loop(0, groups // 4, large, 0)
    for size in (2, 1):

        @pl.when((groups & size) != 0)
        def _(size=size):
            done = groups & -(2 * size)
            one_chunk(pl.multiple_of(done * ROWS, ROWS), size)


def density_kernel(
    per_peer, pair_source, pair_shift, export, actives,
    own, incoming, border, bundle, spreads,
    density, densities, outgoing, outgoing_border,
    table, shifts, sums, lines,
):
    fill_shifts(shifts)
    cells, peers = own.shape[0], incoming.shape[0]
    for place, near, _ in source_tiles(own, incoming, border, per_peer):
        table[place] = near()

    def one_cell(cell, carry):
        def one_chunk(base, groups):
            size = groups * ROWS
            at = pl.ds(base // ROWS, groups)
            *place, wide = [
                spreads[cell, at, which * ROWS : (which + 1) * ROWS, :].reshape(size, LANES)
                for which in range(len(SPREAD))
            ]
            smooth = 0.5 * wide

            total = jnp.zeros((size, LANES), jnp.float32)
            for pair in range(pair_source.shape[1]):
                source, code = pair_source[cell, pair], pair_shift[cell, pair]
                s = lambda field: table[source, field : field + 1, :]
                shift = lambda field: shifts[code, field : field + 1, :]
                apart = [place[c] - (s(c) + shift(c)) for c in range(3)]
                square = apart[0] * apart[0] + apart[1] * apart[1] + apart[2] * apart[2]
                radius = square * lax.rsqrt(jnp.maximum(square, 1e-24))
                outer = jnp.maximum(wide - radius, 0.0)
                inner = jnp.maximum(smooth - radius, 0.0)
                value = outer * outer * outer - 4.0 * (inner * inner * inner)
                total = total + s(MASS) * value
            sums[cell, pl.ds(base, size), 0:1] = jnp.sum(total, axis=1, keepdims=True)

        over_targets(actives[0, cell], one_chunk)
        return carry

    lax.fori_loop(0, cells, one_cell, 0)
    for cell in range(cells):
        lines[cell : cell + 1, :] = sums[cell].T[0:1, :]
    inverse = 2.0 / bundle[:, WIDE, :]
    inverse = inverse * inverse * inverse
    summed = lines[...] * (0.25 / math.pi) * (inverse * inverse)
    rank = bundle[:, S_RANK, :].astype(jnp.int32)
    density[...] = jnp.where(
        own_rows(own, ACTIVE) > 0.5, lane_gather(summed, rank), own_rows(own, DENS)
    )
    densities[0] = summed
    densities[1] = density[...]
    for peer in range(peers):
        for entry in range(per_peer):
            outgoing[peer, entry : entry + 1, :] = density[pl.ds(export[entry, peer], 1), :]
    outgoing_border[0:1, :] = density[cells - 1 : cells, :]
    outgoing_border[1:2, :] = density[0:1, :]


def stream_kernel(
    per_peer, pair_source, pair_shift, own, incoming, border, bundle, densities,
    near_streams, far_streams, starts, orders, columns, last,
    near_table, far_table, shifts, inside, totals_row, totals, sem,
):
    fill_shifts(shifts)
    cells, pairs = pair_source.shape
    tile_shape = (ROWS, LANES)
    row = lax.broadcasted_iota(jnp.int32, tile_shape, 0)
    lane = lanes_of(tile_shape).astype(jnp.float32)
    for place, near, sent in source_tiles(own, incoming, border, per_peer):
        tile, other = near(), sent()
        near_table[place] = tile
        wide, heat = tile[WIDE : WIDE + 1, :], other[HEAT : HEAT + 1, :]
        inverse = 2.0 * pl.reciprocal(wide, approx=True)
        inverse = inverse * inverse * inverse
        far_table[place, INV6 : INV6 + 1, :] = inverse * inverse
        far_table[place, HALF : HALF + 1, :] = 0.025 * wide
        far_table[place, SOUND : SOUND + 1, :] = jnp.sqrt(ADIABATIC * heat)
        far_table[place, WARM : WARM + 1, :] = heat
        far_table[place, SUPPORT : SUPPORT + 1, :] = jnp.where(
            lane[0:1, :] < other[LIVE : LIVE + 1, :], wide, -FAR_AWAY
        )

    def choose(cell, carry):
        low = bundle[cell, S_LOW : S_LOW + ROWS, :]
        high = bundle[cell, S_HIGH : S_HIGH + ROWS, :]
        widest = bundle[cell, S_REACH : S_REACH + 1, :]
        kept = []
        for pair in range(pairs):
            source = pair_source[cell, pair]
            tile = near_table[source] + shifts[pair_shift[cell, pair]]
            away = jnp.maximum(jnp.maximum(low - tile, tile - high), 0.0)
            distance = jnp.sum(away * away, axis=0, keepdims=True)
            support = far_table[source, SUPPORT : SUPPORT + 1, :]
            limit = jnp.maximum(support, widest)
            keep = (distance < limit * limit) & (support > 0.0)
            kept.append(jnp.where(keep, 1.0, 0.0))
        target = lane[0:1, :] < bundle[cell, S_CHOSEN : S_CHOSEN + 1, :]
        kept.append(jnp.where(target, 1.0, 0.0))
        kept += [jnp.zeros((1, LANES), jnp.float32)] * (PAIR_ROWS - pairs - 1)
        base = pl.multiple_of(cell * PAIR_ROWS, PAIR_ROWS)
        inside[pl.ds(base, PAIR_ROWS), :] = jnp.concatenate(kept, axis=0)
        return carry

    lax.fori_loop(0, cells, choose, 0, unroll=4)
    flags = inside[...].astype(jnp.bfloat16)
    all_lanes = jnp.ones((ROWS, LANES), jnp.bfloat16)
    sums = lax.dot_general(
        all_lanes, flags, (((1,), (1,)), ((), ())), preferred_element_type=jnp.float32
    )
    for line in range(totals_row.shape[0]):
        totals_row[line : line + 1, :] = sums[0:1, line * LANES : (line + 1) * LANES].astype(
            jnp.int32
        )
    copy = pltpu.make_async_copy(totals_row, totals, sem)
    copy.start()
    square = (LANES, LANES)
    upper = lax.broadcasted_iota(jnp.int32, square, 0) <= lanes_of(square)
    upper = jnp.where(upper, 1.0, 0.0).astype(jnp.bfloat16)
    seen = jnp.dot(flags, upper, preferred_element_type=jnp.float32)
    wanted = lanes_of(seen.shape).astype(jnp.float32)
    slot = jnp.zeros(seen.shape, jnp.int32)
    step = LANES // 2
    while step:
        found = lane_gather(seen, slot + (step - 1))
        slot = jnp.where(found <= wanted, slot + step, slot)
        step //= 2
    orders[...] = slot
    wide, heat, summed = bundle[:, WIDE, :], bundle[:, S_HEAT, :], densities[0]
    inverse = 2.0 * pl.reciprocal(wide, approx=True)
    inverse = inverse * inverse * inverse
    fields = (
        inverse * inverse, 0.025 * wide, jnp.sqrt(ADIABATIC * heat), 4.0 * summed, heat / summed,
    )
    for cell in range(cells):
        tile = jnp.zeros(tile_shape, jnp.float32)
        for which, values in enumerate(fields):
            tile = jnp.where(row == which, values[cell : cell + 1, :], tile)
        columns[cell] = jnp.concatenate([bundle[cell, 0:ROWS, :], tile], axis=0).T
    last[:, F_RANK, :] = bundle[:, S_RANK, :]
    last[:, F_ACTIVE, :] = own_rows(own, ACTIVE)
    last[:, F_STEP, :] = own_rows(own, STEP)
    for from_row, to_row in ((VX, F_VX), (VY, F_VY), (VZ, F_VZ)):
        last[:, to_row, :] = own[:, from_row, :] * (1.0 / SPEED)
    last[:, F_DENS, :] = densities[1]
    last[:, F_DENS + 1, :] = jnp.zeros((cells, LANES), jnp.float32)
    copy.wait()

    def one_cell(cell, carry):
        tables = (
            lambda source, pair: near_table[source] + shifts[pair_shift[cell, pair]],
            lambda source, pair: far_table[source],
        )
        start = jnp.int32(0)
        begins, turned = [], []
        for pair in range(pairs):
            begins.append(start)
            place = cell * PAIR_ROWS + pair
            turned.append(pltpu.roll(orders[pl.ds(place, 1), :], start & (LANES - 1), 1))
            start = start + totals[place >> 7, place & (LANES - 1)]
        begins.append(start)
        turned += [turned[-1]] * (PAIR_ROWS - pairs)
        for pair, begin in enumerate(begins):
            starts[cell, pair] = begin
        place = cell * PAIR_ROWS + pairs
        starts[cell, pairs + 1] = totals[place >> 7, place & (LANES - 1)]
        fill_streams(
            (near_streams.at[cell], far_streams.at[cell]), tables, pair_source,
            lambda pair: begins[pair], lambda pair: turned[pair], cell,
        )
        base = pl.multiple_of(cell * PAIR_ROWS, PAIR_ROWS)
        orders[pl.ds(base, PAIR_ROWS), :] = jnp.concatenate(turned, axis=0)
        return carry

    lax.fori_loop(0, cells, one_cell, 0, unroll=2)


def force_kernel(
    per_peer, pair_source, starts,
    columns, orders, last, new_density, new_border, near_streams, far_streams,
    acceleration, kicked,
    table, streams, sums, lines, counts,
):
    cells, peers = last.shape[0], new_density.shape[0]
    pairs = pair_source.shape[1]
    for cell in range(cells):
        table[cell, 0:1, :] = last[cell, F_DENS : F_DENS + 1, :]
    for peer in range(peers):
        for entry in range(per_peer):
            place = cells + peer * per_peer + entry
            table[place, 0:1, :] = new_density[peer, entry : entry + 1, :]
    for side in range(2):
        table[cells + peers * per_peer + side, 0:1, :] = new_border[side : side + 1, :]

    def one_stream(cell, carry):
        fill_streams(
            (streams.at[cell],), (lambda source, pair: table[source],), pair_source,
            lambda pair: starts[cell, pair],
            lambda pair: orders[pl.ds(cell * PAIR_ROWS + pair, 1), :], cell,
        )
        return carry

    lax.fori_loop(0, cells, one_stream, 0, unroll=4)

    total = jnp.int32(0)
    for cell in range(cells):
        chunks = (starts[cell, pairs + 1] + CHUNK - 1) // CHUNK
        rounds = (((starts[cell, pairs] + LANES - 1) >> 7) + FORCE_UNROLL - 1) // FORCE_UNROLL
        counts[0, cell] = jnp.maximum(chunks, 1)
        counts[1, cell] = jnp.maximum(rounds, 1)
        total = total + counts[0, cell] * counts[1, cell]
        sums[cell] = jnp.zeros(sums.shape[1:], jnp.float32)
    counts[0, cells] = LANES // CHUNK
    counts[1, cells] = 1

    def one_task(task):
        cell, chunk, round_ = task
        real = jnp.minimum(cell, cells - 1)
        base = pl.multiple_of(chunk * CHUNK, CHUNK)
        first = round_ * FORCE_UNROLL
        near, far, stream = near_streams.at[real], far_streams.at[real], streams.at[real]
        mine = columns[real, pl.ds(base, CHUNK), :]
        place = [spread(mine, field) for field in (X, Y, Z)]
        speed = [spread(mine, field) for field in (VX, VY, VZ)]
        wide = spread(mine, WIDE)
        inv6, half_, sound, dens4, press = [spread(mine, ROWS + field) for field in range(5)]
        totals = None
        for sub in range(FORCE_UNROLL):
            block = first + sub
            s = lambda field: near[block, field : field + 1, :]
            o = lambda field: far[block, field : field + 1, :]
            dens = stream[block, 0:1, :]
            their_press = o(WARM) * pl.reciprocal(jnp.maximum(dens, 1e-30), approx=True)
            apart = [place[c] - s(c) for c in range(3)]
            square = apart[0] * apart[0] + apart[1] * apart[1] + apart[2] * apart[2]
            inverse = lax.rsqrt(jnp.maximum(square, 1e-24))
            radius = square * inverse
            double = radius + radius
            outer = jnp.maximum(wide - radius, 0.0)
            inner = jnp.maximum(wide - double, 0.0)
            slope = inv6 * (outer * outer - inner * inner)
            outer = jnp.maximum(s(WIDE) - radius, 0.0)
            inner = jnp.maximum(s(WIDE) - double, 0.0)
            slope = slope + o(INV6) * (outer * outer - inner * inner)
            approach = (
                (speed[0] - s(VX)) * apart[0]
                + (speed[1] - s(VY)) * apart[1]
                + (speed[2] - s(VZ)) * apart[2]
            )
            half = half_ + o(HALF)
            wall = square + half * half
            pull = half * jnp.minimum(approach, 0.0)
            shared = pl.reciprocal(wall * wall * (dens4 + 4.0 * dens), approx=True)
            viscous = pull * (pull - wall * (sound + o(SOUND))) * shared
            weight = (press + their_press + viscous) * (slope * (inverse * s(MASS)))
            terms = [weight * a for a in apart]
            totals = terms if totals is None else [t + a for t, a in zip(totals, terms)]
        found = jnp.concatenate([jnp.sum(t, axis=1, keepdims=True) for t in totals], axis=1)
        at = pl.ds(base, CHUNK)
        sums[cell, at, 0:3] = sums[cell, at, 0:3] + found
        round_ = round_ + 1
        wrapped = round_ >= counts[1, cell]
        chunk = jnp.where(wrapped, chunk + 1, chunk)
        done = chunk >= counts[0, cell]
        return (
            jnp.where(done, jnp.minimum(cell + 1, cells), cell),
            jnp.where(done, 0, chunk),
            jnp.where(wrapped, 0, round_),
        )

    def some_tasks(index, task):
        for _ in range(TASKS):
            task = one_task(task)
        return task

    zero = jnp.int32(0)
    lax.fori_loop(0, (total + TASKS - 1) // TASKS, some_tasks, (zero, zero, zero))
    for cell in range(cells):
        turned = sums[cell].T
        for c in range(3):
            lines[c, cell : cell + 1, :] = turned[c : c + 1, :]
    rank = last[:, F_RANK, :].astype(jnp.int32)
    for c in range(3):
        gathered = lane_gather(lines[c] * (0.375 / math.pi), rank)
        value = jnp.where(last[:, F_ACTIVE, :] > 0.5, gathered, 0.0)
        acceleration[c] = value
        kicked[c] = last[:, F_VX + c, :] + value * last[:, F_STEP, :]


def shards(
    position, velocity, smoothing, particle_mass, energy, density_old, cell_count, active,
    time_bin, pair_source, pair_shift, export,
):
    cells, capacity = smoothing.shape
    peers, per_peer = export.shape
    sources = cells + peers * per_peer + 2
    codes = 27
    f32 = lambda *shape: jax.ShapeDtypeStruct(shape, jnp.float32)
    smem = pl.BlockSpec(memory_space=pltpu.SMEM)
    vmem = pl.BlockSpec(memory_space=pltpu.VMEM)
    hbm = pl.BlockSpec(memory_space=pltpu.HBM)
    whole = pltpu.CompilerParams(vmem_limit_bytes=64 * 2**20)
    params = pltpu.CompilerParams(vmem_limit_bytes=24 * 2**20)
    cost = pl.CostEstimate(flops=10**9, bytes_accessed=1000, transcendentals=0)
    i32 = lambda *shape: jax.ShapeDtypeStruct(shape, jnp.int32)
    sent_rows = per_peer * (ROWS + SENT)
    turned = export.T

    def landing(scalars, *arrays):
        return (
            [pltpu.SMEM(a.shape, a.dtype) for a in arrays[:scalars]]
            + [pltpu.VMEM(a.shape, a.dtype) for a in arrays[scalars:]]
            + [pltpu.SemaphoreType.DMA((len(arrays),))]
        )

    arrays = (
        cell_count, turned, position, velocity, smoothing, particle_mass, energy, density_old,
        active, time_bin,
    )
    own, outgoing, border = pl.pallas_call(
        pack_kernel,
        out_shape=(
            f32(cells, 2 * ROWS, capacity),
            f32(peers, sent_rows, capacity),
            f32(2, ROWS + SENT, capacity),
        ),
        in_specs=[hbm] * 10,
        out_specs=(vmem,) * 3,
        scratch_shapes=landing(2, *arrays),
        compiler_params=whole,
        cost_estimate=cost,
        name="pack",
    )(*arrays)

    def exchange(pieces):
        return lax.all_to_all(pieces, "cell", split_axis=0, concat_axis=0, tiled=True)

    def swap_border(pieces):
        size = lax.axis_size("region")
        up = [(i, (i + 1) % size) for i in range(size)]
        down = [(j, i) for i, j in up]
        if size == 2:
            return lax.ppermute(pieces, "region", up)
        before = lax.ppermute(pieces[0:1], "region", up)
        after = lax.ppermute(pieces[1:2], "region", down)
        return jnp.concatenate([before, after], axis=0)

    incoming = exchange(outgoing)
    other = swap_border(border)
    actives, bundle, spreads = pl.pallas_call(
        sort_kernel,
        out_shape=(
            i32(1, cells),
            f32(cells, S_ROWS, capacity),
            f32(cells, capacity // ROWS, len(SPREAD) * ROWS, capacity),
        ),
        in_specs=[vmem],
        out_specs=(smem, vmem, vmem),
        scratch_shapes=[pltpu.VMEM((cells, capacity, ROWS), jnp.float32)],
        compiler_params=params,
        cost_estimate=cost,
        name="sort",
    )(own)

    density, densities, outgoing_density, border_density = pl.pallas_call(
        functools.partial(density_kernel, per_peer),
        out_shape=(
            f32(cells, capacity),
            f32(2, cells, capacity),
            f32(peers, per_peer, capacity),
            f32(2, capacity),
        ),
        in_specs=[smem] * 4 + [vmem] * 5,
        out_specs=(vmem,) * 4,
        scratch_shapes=[
            pltpu.VMEM((sources, ROWS, capacity), jnp.float32),
            pltpu.VMEM((codes, ROWS, capacity), jnp.float32),
            pltpu.VMEM((cells, capacity, ROWS), jnp.float32),
            pltpu.VMEM((cells, capacity), jnp.float32),
        ],
        compiler_params=params,
        cost_estimate=cost,
        name="density",
    )(pair_source, pair_shift, turned, actives, own, incoming, other, bundle, spreads)

    new_density = exchange(outgoing_density)
    new_border = swap_border(border_density)
    pairs = pair_source.shape[1]
    blocks = pairs + SPARE
    pair_rows = cells * PAIR_ROWS
    near_streams, far_streams, starts, orders, columns, last = pl.pallas_call(
        functools.partial(stream_kernel, per_peer),
        out_shape=(
            f32(cells, blocks, ROWS, capacity),
            f32(cells, blocks, ROWS, capacity),
            i32(cells, pairs + 2),
            i32(pair_rows, capacity),
            f32(cells, capacity, 2 * ROWS),
            f32(cells, ROWS, capacity),
        ),
        in_specs=[smem] * 2 + [vmem] * 5,
        out_specs=(vmem, vmem, smem, vmem, vmem, vmem),
        scratch_shapes=[
            pltpu.VMEM((sources, ROWS, capacity), jnp.float32),
            pltpu.VMEM((sources, ROWS, capacity), jnp.float32),
            pltpu.VMEM((codes, ROWS, capacity), jnp.float32),
            pltpu.VMEM((pair_rows, capacity), jnp.float32),
            pltpu.VMEM((pair_rows // capacity, capacity), jnp.int32),
            pltpu.SMEM((pair_rows // capacity, capacity), jnp.int32),
            pltpu.SemaphoreType.DMA,
        ],
        compiler_params=params,
        cost_estimate=cost,
        name="streams",
    )(pair_source, pair_shift, own, incoming, other, bundle, densities)

    acceleration, kicked = pl.pallas_call(
        functools.partial(force_kernel, per_peer),
        out_shape=(f32(3, cells, capacity), f32(3, cells, capacity)),
        in_specs=[smem] * 2 + [vmem] * 7,
        out_specs=(vmem,) * 2,
        scratch_shapes=[
            pltpu.VMEM((sources, ROWS, capacity), jnp.float32),
            pltpu.VMEM((cells, blocks, ROWS, capacity), jnp.float32),
            pltpu.VMEM((cells + 1, capacity, ROWS), jnp.float32),
            pltpu.VMEM((3, cells, capacity), jnp.float32),
            pltpu.SMEM((2, cells + 1), jnp.int32),
        ],
        compiler_params=params,
        cost_estimate=cost,
        name="force",
    )(
        pair_source, starts, columns, orders, last, new_density, new_border, near_streams,
        far_streams,
    )
    return density, acceleration, kicked


def solution(mesh):
    rows = P(("region", "cell"), None)
    planes = P(None, ("region", "cell"), None)
    return jax.shard_map(
        shards,
        mesh=mesh,
        in_specs=(
            planes, planes, rows, rows, rows, rows, P(("region", "cell")), rows, rows, rows, rows,
            rows,
        ),
        out_specs=(rows, planes, planes),
        check_vma=False,
    )
```

```python
import functools
import math

import jax
import jax.numpy as jnp
from jax import lax
from jax.experimental import pallas as pl
from jax.experimental.pallas import tpu as pltpu
from jax.sharding import PartitionSpec as P

ADIABATIC = 5.0 / 3.0
STEP_MAX = 0.2
LANES = 128
ROWS = 8
FORCE_UNROLL = 4
CHUNK = 8
TASKS = 14
PAIR_ROWS = 32
FAR_AWAY = 1e9
SPARE = FORCE_UNROLL

X, Y, Z, MASS, VX, VY, VZ, WIDE = range(ROWS)
SPREAD = (X, Y, Z, WIDE)
HEAT, DENS, LIVE = range(3)
SENT = 4
SPEED = 40.0
ACTIVE, STEP = SENT, SENT + 1
S_HEAT, S_RANK, S_REACH, S_CHOSEN = range(ROWS, ROWS + 4)
S_LOW, S_HIGH, S_ROWS = 2 * ROWS, 3 * ROWS, 4 * ROWS
F_RANK, F_ACTIVE, F_STEP, F_VX, F_VY, F_VZ, F_DENS = range(7)
INV6, HALF, SOUND, SUPPORT = range(4)
DENS4, PRESS = range(2)


def lane_gather(values, index):
    return jnp.take_along_axis(values, index, axis=1, mode="promise_in_bounds")


def lanes_of(shape):
    return lax.broadcasted_iota(jnp.int32, shape, len(shape) - 1)


def start_copies(arrays, landed, sem):
    copies = [
        pltpu.make_async_copy(array, place, sem.at[index])
        for index, (array, place) in enumerate(zip(arrays, landed))
    ]
    for copy in copies:
        copy.start()
    return copies


def pack_kernel(*refs):
    arrays, (own, outgoing, border) = refs[:10], refs[10:13]
    landed, sem = refs[13:-1], refs[-1]
    for copy in start_copies(arrays, landed, sem):
        copy.wait()
    count, export, position, velocity, smoothing, mass, energy, density_old, active, time_bin = landed
    cells = smoothing.shape[0]
    shape = smoothing.shape
    lane = lanes_of(shape)
    row = lax.broadcasted_iota(jnp.int32, shape, 0)
    counts = jnp.zeros(shape, jnp.int32)
    for cell in range(cells):
        counts = jnp.where(row == cell, count[cell], counts)
    mass_live = jnp.where(lane < counts, mass[...], 0.0)
    zeros = jnp.zeros(shape, jnp.float32)
    rows = (
        position[0], position[1], position[2], mass_live,
        SPEED * velocity[0], SPEED * velocity[1], SPEED * velocity[2], 2.0 * smoothing[...],
        (ADIABATIC - 1.0) * energy[...], density_old[...], counts.astype(jnp.float32), zeros,
        jnp.where(active[...] > 0, 1.0, 0.0),
        STEP_MAX * jnp.exp2(-time_bin[...].astype(jnp.float32)), zeros, zeros,
    )
    for field, values in enumerate(rows):
        own[:, field, :] = values
    per_peer, peers = export.shape
    for peer in range(peers):
        for entry in range(per_peer):
            cell = export[entry, peer]
            outgoing[peer, entry * ROWS : (entry + 1) * ROWS, :] = own[cell, 0:ROWS, :]
            start = per_peer * ROWS + entry * SENT
            outgoing[peer, start : start + SENT, :] = own[cell, ROWS : ROWS + SENT, :]
    for side, cell in enumerate((cells - 1, 0)):
        border[side] = own[cell, 0 : ROWS + SENT, :]


def own_rows(own, field):
    return own[:, ROWS + field, :]


def sort_kernel(own, actives, bundle, spreads, columns):
    cells = own.shape[0]
    shape = (cells, LANES)
    lane = lanes_of(shape)
    ones = own_rows(own, ACTIVE)
    is_active = ones > 0.5
    for cell in range(cells):
        actives[0, cell] = jnp.sum(ones[cell : cell + 1, :]).astype(jnp.int32)
    square = (LANES, LANES)
    upper = lax.broadcasted_iota(jnp.int32, square, 0) <= lanes_of(square)
    upper = jnp.where(upper, 1.0, 0.0).astype(jnp.bfloat16)
    seen = jnp.dot(ones.astype(jnp.bfloat16), upper, preferred_element_type=jnp.float32)
    seen = seen.astype(jnp.int32)
    chosen = lane_gather(seen, jnp.full(shape, LANES - 1, jnp.int32))
    others = lane + 1 - seen
    rank = jnp.where(is_active, seen - 1, chosen + others - 1)
    first_part = lane < chosen
    wanted = jnp.where(first_part, lane, lane - chosen)
    slot = jnp.zeros(shape, jnp.int32)
    step = LANES // 2
    while step:
        probe = slot + (step - 1)
        found = jnp.where(first_part, lane_gather(seen, probe), lane_gather(others, probe))
        slot = jnp.where(found <= wanted, slot + step, slot)
        step //= 2
    bundle[:, S_HEAT, :] = lane_gather(own_rows(own, HEAT), slot)
    bundle[:, S_RANK, :] = rank.astype(jnp.float32)
    bundle[:, S_CHOSEN, :] = chosen.astype(jnp.float32)
    for spare in range(S_CHOSEN + 1, S_LOW):
        bundle[:, spare, :] = jnp.zeros(shape, jnp.float32)
    place = lax.broadcasted_iota(jnp.int32, (ROWS, LANES), 0) <= Z
    for cell in range(cells):
        order = jnp.broadcast_to(slot[cell : cell + 1, :], (ROWS, LANES))
        tile = lane_gather(own[cell, 0:ROWS, :], order)
        bundle[cell, 0:ROWS, :] = tile
        target = lane < chosen[cell : cell + 1, :]
        low = jnp.min(jnp.where(target, tile, FAR_AWAY), axis=1, keepdims=True)
        high = jnp.max(jnp.where(target, tile, -FAR_AWAY), axis=1, keepdims=True)
        bundle[cell, S_LOW : S_LOW + ROWS, :] = jnp.where(place, low, -FAR_AWAY)
        bundle[cell, S_HIGH : S_HIGH + ROWS, :] = jnp.where(place, high, FAR_AWAY)
        bundle[cell, S_REACH : S_REACH + 1, :] = jnp.broadcast_to(high[WIDE : WIDE + 1, :], (1, LANES))
        columns[cell] = tile.T

    def one_cell(cell, carry):
        def one_pair(pair, carry):
            base = pl.multiple_of(pair * 2 * ROWS, 2 * ROWS)
            mine = columns[cell, pl.ds(base, 2 * ROWS), :]
            for which, field in enumerate(SPREAD):
                tiles = spread(mine, field).reshape(2, ROWS, LANES)
                spreads[cell, pl.ds(pair * 2, 2), which * ROWS : (which + 1) * ROWS, :] = tiles
            return carry

        return lax.fori_loop(0, (actives[0, cell] + 2 * ROWS - 1) // (2 * ROWS), one_pair, carry)

    lax.fori_loop(0, cells, one_cell, 0)


def source_tiles(own, incoming, border, per_peer):
    cells, peers = own.shape[0], incoming.shape[0]
    for cell in range(cells):
        yield (
            cell, lambda c=cell: own[c, 0:ROWS, :], lambda c=cell: own[c, ROWS : ROWS + SENT, :]
        )
    for peer in range(peers):
        for entry in range(per_peer):
            near, sent = entry * ROWS, per_peer * ROWS + entry * SENT
            yield (
                cells + peer * per_peer + entry,
                lambda p=peer, n=near: incoming[p, n : n + ROWS, :],
                lambda p=peer, n=sent: incoming[p, n : n + SENT, :],
            )
    for side in range(2):
        yield (
            cells + peers * per_peer + side,
            lambda b=side: border[b, 0:ROWS, :],
            lambda b=side: border[b, ROWS : ROWS + SENT, :],
        )


def fill_shifts(shifts):
    row = lax.broadcasted_iota(jnp.int32, (ROWS, LANES), 0)
    for code in range(shifts.shape[0]):
        first, second, third = code // 9 - 1.0, code // 3 % 3 - 1.0, code % 3 - 1.0
        shifts[code] = jnp.where(
            row == X, first, jnp.where(row == Y, second, jnp.where(row == Z, third, 0.0))
        )


def fill_streams(streams, tables, sources, starts, orders, cell):
    shape = (ROWS, LANES)
    lane = lanes_of(shape)
    pairs = sources.shape[1]
    moved = []
    for pair in range(pairs):
        order = jnp.broadcast_to(orders(pair), shape)
        moved.append([lane_gather(load(sources[cell, pair], pair), order) for load in tables])
    for pair in range(pairs):
        start = starts(pair)
        block = start >> 7
        fresh = lane >= (start & (LANES - 1))
        for which, stream in enumerate(streams):
            stream[block + 1] = moved[pair][which]
            pltpu.store(stream.at[block], moved[pair][which], mask=fresh)
    end = starts(pairs)
    block = end >> 7
    for stream in streams:
        stream[block] = jnp.where(lane < (end & (LANES - 1)), stream[block], 0.0)
        for extra in range(1, SPARE):
            stream[block + extra] = jnp.zeros(shape, jnp.float32)


def spread(values, field):
    return jnp.broadcast_to(values[:, field : field + 1], (values.shape[0], LANES))


def over_targets(active, one_chunk):
    groups = (active + ROWS - 1) // ROWS

    def large(chunk, carry):
        one_chunk(pl.multiple_of(chunk * 4 * ROWS, ROWS), 4)
        return carry

    lax.fori_loop(0, groups // 4, large, 0)
    for size in (2, 1):

        @pl.when((groups & size) != 0)
        def _(size=size):
            done = groups & -(2 * size)
            one_chunk(pl.multiple_of(done * ROWS, ROWS), size)


def density_kernel(
    per_peer, pair_source, pair_shift, export, actives,
    own, incoming, border, bundle, spreads,
    density, densities, outgoing, outgoing_border,
    table, shifts, sums, lines,
):
    fill_shifts(shifts)
    cells, peers = own.shape[0], incoming.shape[0]
    for place, near, _ in source_tiles(own, incoming, border, per_peer):
        table[place] = near()

    def one_cell(cell, carry):
        def one_chunk(base, groups):
            size = groups * ROWS
            at = pl.ds(base // ROWS, groups)
            *place, wide = [
                spreads[cell, at, which * ROWS : (which + 1) * ROWS, :].reshape(size, LANES)
                for which in range(len(SPREAD))
            ]
            smooth = 0.5 * wide

            total = jnp.zeros((size, LANES), jnp.float32)
            for pair in range(pair_source.shape[1]):
                source, code = pair_source[cell, pair], pair_shift[cell, pair]
                s = lambda field: table[source, field : field + 1, :]
                shift = lambda field: shifts[code, field : field + 1, :]
                apart = [place[c] - (s(c) + shift(c)) for c in range(3)]
                square = apart[0] * apart[0] + apart[1] * apart[1] + apart[2] * apart[2]
                radius = pl.reciprocal(lax.rsqrt(square), approx=True)
                outer = jnp.maximum(wide - radius, 0.0)
                inner = jnp.maximum(smooth - radius, 0.0)
                value = outer * outer * outer - 4.0 * (inner * inner * inner)
                total = total + s(MASS) * value
            sums[cell, pl.ds(base, size), 0:1] = jnp.sum(total, axis=1, keepdims=True)

        over_targets(actives[0, cell], one_chunk)
        return carry

    lax.fori_loop(0, cells, one_cell, 0)
    for cell in range(cells):
        lines[cell : cell + 1, :] = sums[cell].T[0:1, :]
    inverse = 2.0 / bundle[:, WIDE, :]
    inverse = inverse * inverse * inverse
    summed = lines[...] * (0.25 / math.pi) * (inverse * inverse)
    rank = bundle[:, S_RANK, :].astype(jnp.int32)
    density[...] = jnp.where(
        own_rows(own, ACTIVE) > 0.5, lane_gather(summed, rank), own_rows(own, DENS)
    )
    densities[0] = summed
    densities[1] = density[...]
    for peer in range(peers):
        for entry in range(per_peer):
            outgoing[peer, entry : entry + 1, :] = density[pl.ds(export[entry, peer], 1), :]
    outgoing_border[0:1, :] = density[cells - 1 : cells, :]
    outgoing_border[1:2, :] = density[0:1, :]


def stream_kernel(
    per_peer, pair_source, pair_shift, own, incoming, border, bundle, densities,
    near_streams, far_streams, starts, orders, columns, last, heats,
    near_table, far_table, shifts, inside, totals_row, totals, sem,
):
    fill_shifts(shifts)
    cells, pairs = pair_source.shape
    tile_shape = (ROWS, LANES)
    row = lax.broadcasted_iota(jnp.int32, tile_shape, 0)
    lane = lanes_of(tile_shape).astype(jnp.float32)
    for place, near, sent in source_tiles(own, incoming, border, per_peer):
        tile, other = near(), sent()
        near_table[place] = tile
        wide, heat = tile[WIDE : WIDE + 1, :], other[HEAT : HEAT + 1, :]
        inverse = 2.0 * pl.reciprocal(wide, approx=True)
        inverse = inverse * inverse * inverse
        far_table[place, INV6 : INV6 + 1, :] = inverse * inverse
        far_table[place, HALF : HALF + 1, :] = 0.025 * wide
        far_table[place, SOUND : SOUND + 1, :] = jnp.sqrt(ADIABATIC * heat)
        heats[place : place + 1, :] = heat
        far_table[place, SUPPORT : SUPPORT + 1, :] = jnp.where(
            lane[0:1, :] < other[LIVE : LIVE + 1, :], wide, -FAR_AWAY
        )

    def choose(cell, carry):
        low = bundle[cell, S_LOW : S_LOW + ROWS, :]
        high = bundle[cell, S_HIGH : S_HIGH + ROWS, :]
        widest = bundle[cell, S_REACH : S_REACH + 1, :]
        kept = []
        for pair in range(pairs):
            source = pair_source[cell, pair]
            tile = near_table[source] + shifts[pair_shift[cell, pair]]
            away = jnp.maximum(jnp.maximum(low - tile, tile - high), 0.0)
            distance = jnp.sum(away * away, axis=0, keepdims=True)
            support = far_table[source, SUPPORT : SUPPORT + 1, :]
            limit = jnp.maximum(support, widest)
            keep = (distance < limit * limit) & (support > 0.0)
            kept.append(jnp.where(keep, 1.0, 0.0))
        target = lane[0:1, :] < bundle[cell, S_CHOSEN : S_CHOSEN + 1, :]
        kept.append(jnp.where(target, 1.0, 0.0))
        kept += [jnp.zeros((1, LANES), jnp.float32)] * (PAIR_ROWS - pairs - 1)
        base = pl.multiple_of(cell * PAIR_ROWS, PAIR_ROWS)
        inside[pl.ds(base, PAIR_ROWS), :] = jnp.concatenate(kept, axis=0)
        return carry

    lax.fori_loop(0, cells, choose, 0, unroll=4)
    flags = inside[...].astype(jnp.bfloat16)
    all_lanes = jnp.ones((ROWS, LANES), jnp.bfloat16)
    sums = lax.dot_general(
        all_lanes, flags, (((1,), (1,)), ((), ())), preferred_element_type=jnp.float32
    )
    for line in range(totals_row.shape[0]):
        totals_row[line : line + 1, :] = sums[0:1, line * LANES : (line + 1) * LANES].astype(
            jnp.int32
        )
    copy = pltpu.make_async_copy(totals_row, totals, sem)
    copy.start()
    square = (LANES, LANES)
    upper = lax.broadcasted_iota(jnp.int32, square, 0) <= lanes_of(square)
    upper = jnp.where(upper, 1.0, 0.0).astype(jnp.bfloat16)
    seen = jnp.dot(flags, upper, preferred_element_type=jnp.float32)
    wanted = lanes_of(seen.shape).astype(jnp.float32)
    slot = jnp.zeros(seen.shape, jnp.int32)
    step = LANES // 2
    while step:
        found = lane_gather(seen, slot + (step - 1))
        slot = jnp.where(found <= wanted, slot + step, slot)
        step //= 2
    orders[...] = slot
    wide, heat, summed = bundle[:, WIDE, :], bundle[:, S_HEAT, :], densities[0]
    inverse = 2.0 * pl.reciprocal(wide, approx=True)
    inverse = inverse * inverse * inverse
    fields = (
        inverse * inverse, 0.025 * wide, jnp.sqrt(ADIABATIC * heat), 4.0 * summed, heat / summed,
    )
    for cell in range(cells):
        tile = jnp.zeros(tile_shape, jnp.float32)
        for which, values in enumerate(fields):
            tile = jnp.where(row == which, values[cell : cell + 1, :], tile)
        columns[cell] = jnp.concatenate([bundle[cell, 0:ROWS, :], tile], axis=0).T
    last[:, F_RANK, :] = bundle[:, S_RANK, :]
    last[:, F_ACTIVE, :] = own_rows(own, ACTIVE)
    last[:, F_STEP, :] = own_rows(own, STEP)
    for from_row, to_row in ((VX, F_VX), (VY, F_VY), (VZ, F_VZ)):
        last[:, to_row, :] = own[:, from_row, :] * (1.0 / SPEED)
    last[:, F_DENS, :] = densities[1]
    last[:, F_DENS + 1, :] = jnp.zeros((cells, LANES), jnp.float32)
    copy.wait()

    def one_cell(cell, carry):
        tables = (
            lambda source, pair: near_table[source] + shifts[pair_shift[cell, pair]],
            lambda source, pair: far_table[source],
        )
        start = jnp.int32(0)
        begins, turned = [], []
        for pair in range(pairs):
            begins.append(start)
            place = cell * PAIR_ROWS + pair
            turned.append(pltpu.roll(orders[pl.ds(place, 1), :], start & (LANES - 1), 1))
            start = start + totals[place >> 7, place & (LANES - 1)]
        begins.append(start)
        turned += [turned[-1]] * (PAIR_ROWS - pairs)
        for pair, begin in enumerate(begins):
            starts[cell, pair] = begin
        place = cell * PAIR_ROWS + pairs
        starts[cell, pairs + 1] = totals[place >> 7, place & (LANES - 1)]
        fill_streams(
            (near_streams.at[cell], far_streams.at[cell]), tables, pair_source,
            lambda pair: begins[pair], lambda pair: turned[pair], cell,
        )
        base = pl.multiple_of(cell * PAIR_ROWS, PAIR_ROWS)
        orders[pl.ds(base, PAIR_ROWS), :] = jnp.concatenate(turned, axis=0)
        return carry

    lax.fori_loop(0, cells, one_cell, 0, unroll=2)


def force_kernel(
    per_peer, pair_source, starts,
    columns, orders, last, heats, new_density, new_border, near_streams, far_streams,
    acceleration, kicked,
    table, densities, streams, sums, lines, counts,
):
    cells, peers = last.shape[0], new_density.shape[0]
    pairs = pair_source.shape[1]
    for cell in range(cells):
        densities[cell : cell + 1, :] = last[cell, F_DENS : F_DENS + 1, :]
    for peer in range(peers):
        place = cells + peer * per_peer
        densities[place : place + per_peer, :] = new_density[peer]
    place = cells + peers * per_peer
    densities[place : place + 2, :] = new_border[...]
    dens4 = 4.0 * densities[...]
    press = heats[...] * pl.reciprocal(densities[...], approx=True)
    for place in range(table.shape[0]):
        table[place, DENS4 : DENS4 + 1, :] = dens4[place : place + 1, :]
        table[place, PRESS : PRESS + 1, :] = press[place : place + 1, :]

    def one_stream(cell, carry):
        fill_streams(
            (streams.at[cell],), (lambda source, pair: table[source],), pair_source,
            lambda pair: starts[cell, pair],
            lambda pair: orders[pl.ds(cell * PAIR_ROWS + pair, 1), :], cell,
        )
        return carry

    lax.fori_loop(0, cells, one_stream, 0, unroll=4)

    total = jnp.int32(0)
    for cell in range(cells):
        chunks = (starts[cell, pairs + 1] + CHUNK - 1) // CHUNK
        rounds = (((starts[cell, pairs] + LANES - 1) >> 7) + FORCE_UNROLL - 1) // FORCE_UNROLL
        counts[0, cell] = jnp.maximum(chunks, 1)
        counts[1, cell] = jnp.maximum(rounds, 1)
        total = total + counts[0, cell] * counts[1, cell]
        sums[cell] = jnp.zeros(sums.shape[1:], jnp.float32)
    counts[0, cells] = LANES // CHUNK
    counts[1, cells] = 1

    def one_task(task):
        cell, chunk, round_ = task
        real = jnp.minimum(cell, cells - 1)
        base = pl.multiple_of(chunk * CHUNK, CHUNK)
        first = round_ * FORCE_UNROLL
        near, far, stream = near_streams.at[real], far_streams.at[real], streams.at[real]
        mine = columns[real, pl.ds(base, CHUNK), :]
        place = [spread(mine, field) for field in (X, Y, Z)]
        speed = [spread(mine, field) for field in (VX, VY, VZ)]
        wide = spread(mine, WIDE)
        inv6, half_, sound, dens4, press = [spread(mine, ROWS + field) for field in range(5)]
        totals = None
        for sub in range(FORCE_UNROLL):
            block = first + sub
            s = lambda field: near[block, field : field + 1, :]
            o = lambda field: far[block, field : field + 1, :]
            m = lambda field: stream[block, field : field + 1, :]
            apart = [place[c] - s(c) for c in range(3)]
            square = apart[0] * apart[0] + apart[1] * apart[1] + apart[2] * apart[2]
            inverse = lax.rsqrt(jnp.maximum(square, 1e-24))
            radius = pl.reciprocal(inverse, approx=True)
            outer = jnp.maximum(wide - radius, 0.0)
            least = jnp.minimum(outer, radius)
            slope = inv6 * (least * ((outer + outer) - least))
            outer = jnp.maximum(s(WIDE) - radius, 0.0)
            least = jnp.minimum(outer, radius)
            slope = slope + o(INV6) * (least * ((outer + outer) - least))
            approach = (
                (speed[0] - s(VX)) * apart[0]
                + (speed[1] - s(VY)) * apart[1]
                + (speed[2] - s(VZ)) * apart[2]
            )
            half = half_ + o(HALF)
            slow = pl.reciprocal(square + half * half, approx=True)
            mu = half * jnp.minimum(approach, 0.0) * slow
            light = pl.reciprocal(dens4 + m(DENS4), approx=True)
            viscous = mu * (mu - (sound + o(SOUND))) * light
            weight = (press + m(PRESS) + viscous) * (slope * (inverse * s(MASS)))
            terms = [weight * a for a in apart]
            totals = terms if totals is None else [t + a for t, a in zip(totals, terms)]
        found = jnp.concatenate([jnp.sum(t, axis=1, keepdims=True) for t in totals], axis=1)
        at = pl.ds(base, CHUNK)
        sums[cell, at, 0:3] = sums[cell, at, 0:3] + found
        round_ = round_ + 1
        wrapped = round_ >= counts[1, cell]
        chunk = jnp.where(wrapped, chunk + 1, chunk)
        done = chunk >= counts[0, cell]
        return (
            jnp.where(done, jnp.minimum(cell + 1, cells), cell),
            jnp.where(done, 0, chunk),
            jnp.where(wrapped, 0, round_),
        )

    def some_tasks(index, task):
        for _ in range(TASKS):
            task = one_task(task)
        return task

    zero = jnp.int32(0)
    lax.fori_loop(0, (total + TASKS - 1) // TASKS, some_tasks, (zero, zero, zero))
    for cell in range(cells):
        turned = sums[cell].T
        for c in range(3):
            lines[c, cell : cell + 1, :] = turned[c : c + 1, :]
    rank = last[:, F_RANK, :].astype(jnp.int32)
    for c in range(3):
        gathered = lane_gather(lines[c] * (0.375 / math.pi), rank)
        value = jnp.where(last[:, F_ACTIVE, :] > 0.5, gathered, 0.0)
        acceleration[c] = value
        kicked[c] = last[:, F_VX + c, :] + value * last[:, F_STEP, :]


def shards(
    position, velocity, smoothing, particle_mass, energy, density_old, cell_count, active,
    time_bin, pair_source, pair_shift, export,
):
    cells, capacity = smoothing.shape
    peers, per_peer = export.shape
    sources = cells + peers * per_peer + 2
    codes = 27
    f32 = lambda *shape: jax.ShapeDtypeStruct(shape, jnp.float32)
    smem = pl.BlockSpec(memory_space=pltpu.SMEM)
    vmem = pl.BlockSpec(memory_space=pltpu.VMEM)
    hbm = pl.BlockSpec(memory_space=pltpu.HBM)
    whole = pltpu.CompilerParams(vmem_limit_bytes=64 * 2**20)
    params = pltpu.CompilerParams(vmem_limit_bytes=24 * 2**20)
    cost = pl.CostEstimate(flops=10**9, bytes_accessed=1000, transcendentals=0)
    i32 = lambda *shape: jax.ShapeDtypeStruct(shape, jnp.int32)
    sent_rows = per_peer * (ROWS + SENT)
    turned = export.T

    def landing(scalars, *arrays):
        return (
            [pltpu.SMEM(a.shape, a.dtype) for a in arrays[:scalars]]
            + [pltpu.VMEM(a.shape, a.dtype) for a in arrays[scalars:]]
            + [pltpu.SemaphoreType.DMA((len(arrays),))]
        )

    arrays = (
        cell_count, turned, position, velocity, smoothing, particle_mass, energy, density_old,
        active, time_bin,
    )
    own, outgoing, border = pl.pallas_call(
        pack_kernel,
        out_shape=(
            f32(cells, 2 * ROWS, capacity),
            f32(peers, sent_rows, capacity),
            f32(2, ROWS + SENT, capacity),
        ),
        in_specs=[hbm] * 10,
        out_specs=(vmem,) * 3,
        scratch_shapes=landing(2, *arrays),
        compiler_params=whole,
        cost_estimate=cost,
        name="pack",
    )(*arrays)

    def exchange(pieces):
        return lax.all_to_all(pieces, "cell", split_axis=0, concat_axis=0, tiled=True)

    def swap_border(pieces):
        size = lax.axis_size("region")
        up = [(i, (i + 1) % size) for i in range(size)]
        down = [(j, i) for i, j in up]
        if size == 2:
            return lax.ppermute(pieces, "region", up)
        before = lax.ppermute(pieces[0:1], "region", up)
        after = lax.ppermute(pieces[1:2], "region", down)
        return jnp.concatenate([before, after], axis=0)

    incoming = exchange(outgoing)
    other = swap_border(border)
    actives, bundle, spreads = pl.pallas_call(
        sort_kernel,
        out_shape=(
            i32(1, cells),
            f32(cells, S_ROWS, capacity),
            f32(cells, capacity // ROWS, len(SPREAD) * ROWS, capacity),
        ),
        in_specs=[vmem],
        out_specs=(smem, vmem, vmem),
        scratch_shapes=[pltpu.VMEM((cells, capacity, ROWS), jnp.float32)],
        compiler_params=params,
        cost_estimate=cost,
        name="sort",
    )(own)

    density, densities, outgoing_density, border_density = pl.pallas_call(
        functools.partial(density_kernel, per_peer),
        out_shape=(
            f32(cells, capacity),
            f32(2, cells, capacity),
            f32(peers, per_peer, capacity),
            f32(2, capacity),
        ),
        in_specs=[smem] * 4 + [vmem] * 5,
        out_specs=(vmem,) * 4,
        scratch_shapes=[
            pltpu.VMEM((sources, ROWS, capacity), jnp.float32),
            pltpu.VMEM((codes, ROWS, capacity), jnp.float32),
            pltpu.VMEM((cells, capacity, ROWS), jnp.float32),
            pltpu.VMEM((cells, capacity), jnp.float32),
        ],
        compiler_params=params,
        cost_estimate=cost,
        name="density",
    )(pair_source, pair_shift, turned, actives, own, incoming, other, bundle, spreads)

    new_density = exchange(outgoing_density)
    new_border = swap_border(border_density)
    pairs = pair_source.shape[1]
    blocks = pairs + SPARE
    pair_rows = cells * PAIR_ROWS
    source_rows = -(-sources // ROWS) * ROWS
    near_streams, far_streams, starts, orders, columns, last, heats = pl.pallas_call(
        functools.partial(stream_kernel, per_peer),
        out_shape=(
            f32(cells, blocks, ROWS, capacity),
            f32(cells, blocks, ROWS, capacity),
            i32(cells, pairs + 2),
            i32(pair_rows, capacity),
            f32(cells, capacity, 2 * ROWS),
            f32(cells, ROWS, capacity),
            f32(source_rows, capacity),
        ),
        in_specs=[smem] * 2 + [vmem] * 5,
        out_specs=(vmem, vmem, smem, vmem, vmem, vmem, vmem),
        scratch_shapes=[
            pltpu.VMEM((sources, ROWS, capacity), jnp.float32),
            pltpu.VMEM((sources, ROWS, capacity), jnp.float32),
            pltpu.VMEM((codes, ROWS, capacity), jnp.float32),
            pltpu.VMEM((pair_rows, capacity), jnp.float32),
            pltpu.VMEM((pair_rows // capacity, capacity), jnp.int32),
            pltpu.SMEM((pair_rows // capacity, capacity), jnp.int32),
            pltpu.SemaphoreType.DMA,
        ],
        compiler_params=params,
        cost_estimate=cost,
        name="streams",
    )(pair_source, pair_shift, own, incoming, other, bundle, densities)

    acceleration, kicked = pl.pallas_call(
        functools.partial(force_kernel, per_peer),
        out_shape=(f32(3, cells, capacity), f32(3, cells, capacity)),
        in_specs=[smem] * 2 + [vmem] * 8,
        out_specs=(vmem,) * 2,
        scratch_shapes=[
            pltpu.VMEM((sources, ROWS, capacity), jnp.float32),
            pltpu.VMEM((source_rows, capacity), jnp.float32),
            pltpu.VMEM((cells, blocks, ROWS, capacity), jnp.float32),
            pltpu.VMEM((cells + 1, capacity, ROWS), jnp.float32),
            pltpu.VMEM((3, cells, capacity), jnp.float32),
            pltpu.SMEM((2, cells + 1), jnp.int32),
        ],
        compiler_params=params,
        cost_estimate=cost,
        name="force",
    )(
        pair_source, starts, columns, orders, last, heats, new_density, new_border, near_streams,
        far_streams,
    )
    return density, acceleration, kicked


def solution(mesh):
    rows = P(("region", "cell"), None)
    planes = P(None, ("region", "cell"), None)
    return jax.shard_map(
        shards,
        mesh=mesh,
        in_specs=(
            planes, planes, rows, rows, rows, rows, P(("region", "cell")), rows, rows, rows, rows,
            rows,
        ),
        out_specs=(rows, planes, planes),
        check_vma=False,
    )
```

```python
import functools
import math

import jax
import jax.numpy as jnp
from jax import lax
from jax.experimental import pallas as pl
from jax.experimental.pallas import tpu as pltpu
from jax.sharding import PartitionSpec as P

ADIABATIC = 5.0 / 3.0
STEP_MAX = 0.2
LANES = 128
ROWS = 8
FORCE_UNROLL = 7
PAIR_ROWS = 32
FAR_AWAY = 1e9
SPARE = FORCE_UNROLL

X, Y, Z, MASS, VX, VY, VZ, WIDE = range(ROWS)
SPREAD = (X, Y, Z, WIDE)
HEAT, DENS, LIVE = range(3)
SENT = 4
SPEED = 40.0
ACTIVE, STEP = SENT, SENT + 1
S_HEAT, S_RANK, S_REACH, S_CHOSEN = range(ROWS, ROWS + 4)
S_LOW, S_HIGH, S_ROWS = 2 * ROWS, 3 * ROWS, 4 * ROWS
F_RANK, F_ACTIVE, F_STEP, F_VX, F_VY, F_VZ, F_DENS = range(7)
INV6, HALF, SOUND, SUPPORT = range(4)
DENS4, PRESS = range(2)


def lane_gather(values, index):
    return jnp.take_along_axis(values, index, axis=1, mode="promise_in_bounds")


def lanes_of(shape):
    return lax.broadcasted_iota(jnp.int32, shape, len(shape) - 1)


def start_copies(arrays, landed, sem):
    copies = [
        pltpu.make_async_copy(array, place, sem.at[index])
        for index, (array, place) in enumerate(zip(arrays, landed))
    ]
    for copy in copies:
        copy.start()
    return copies


def pack_kernel(*refs):
    arrays, (own, outgoing, border) = refs[:10], refs[10:13]
    landed, sem = refs[13:-1], refs[-1]
    for copy in start_copies(arrays, landed, sem):
        copy.wait()
    count, export, position, velocity, smoothing, mass, energy, density_old, active, time_bin = landed
    cells = smoothing.shape[0]
    shape = smoothing.shape
    lane = lanes_of(shape)
    row = lax.broadcasted_iota(jnp.int32, shape, 0)
    counts = jnp.zeros(shape, jnp.int32)
    for cell in range(cells):
        counts = jnp.where(row == cell, count[cell], counts)
    mass_live = jnp.where(lane < counts, mass[...], 0.0)
    zeros = jnp.zeros(shape, jnp.float32)
    rows = (
        position[0], position[1], position[2], mass_live,
        SPEED * velocity[0], SPEED * velocity[1], SPEED * velocity[2], 2.0 * smoothing[...],
        (ADIABATIC - 1.0) * energy[...], density_old[...], counts.astype(jnp.float32), zeros,
        jnp.where(active[...] > 0, 1.0, 0.0),
        STEP_MAX * jnp.exp2(-time_bin[...].astype(jnp.float32)), zeros, zeros,
    )
    for field, values in enumerate(rows):
        own[:, field, :] = values
    per_peer, peers = export.shape
    for peer in range(peers):
        for entry in range(per_peer):
            cell = export[entry, peer]
            outgoing[peer, entry * ROWS : (entry + 1) * ROWS, :] = own[cell, 0:ROWS, :]
            start = per_peer * ROWS + entry * SENT
            outgoing[peer, start : start + SENT, :] = own[cell, ROWS : ROWS + SENT, :]
    for side, cell in enumerate((cells - 1, 0)):
        border[side] = own[cell, 0 : ROWS + SENT, :]


def own_rows(own, field):
    return own[:, ROWS + field, :]


def sort_kernel(own, actives, bundle, spreads, columns):
    cells = own.shape[0]
    shape = (cells, LANES)
    lane = lanes_of(shape)
    ones = own_rows(own, ACTIVE)
    is_active = ones > 0.5
    for cell in range(cells):
        actives[0, cell] = jnp.sum(ones[cell : cell + 1, :]).astype(jnp.int32)
    square = (LANES, LANES)
    upper = lax.broadcasted_iota(jnp.int32, square, 0) <= lanes_of(square)
    upper = jnp.where(upper, 1.0, 0.0).astype(jnp.bfloat16)
    seen = jnp.dot(ones.astype(jnp.bfloat16), upper, preferred_element_type=jnp.float32)
    seen = seen.astype(jnp.int32)
    chosen = lane_gather(seen, jnp.full(shape, LANES - 1, jnp.int32))
    others = lane + 1 - seen
    rank = jnp.where(is_active, seen - 1, chosen + others - 1)
    first_part = lane < chosen
    wanted = jnp.where(first_part, lane, lane - chosen)
    slot = jnp.zeros(shape, jnp.int32)
    step = LANES // 2
    while step:
        probe = slot + (step - 1)
        found = jnp.where(first_part, lane_gather(seen, probe), lane_gather(others, probe))
        slot = jnp.where(found <= wanted, slot + step, slot)
        step //= 2
    bundle[:, S_HEAT, :] = lane_gather(own_rows(own, HEAT), slot)
    bundle[:, S_RANK, :] = rank.astype(jnp.float32)
    bundle[:, S_CHOSEN, :] = chosen.astype(jnp.float32)
    for spare in range(S_CHOSEN + 1, S_LOW):
        bundle[:, spare, :] = jnp.zeros(shape, jnp.float32)
    place = lax.broadcasted_iota(jnp.int32, (ROWS, LANES), 0) <= Z
    for cell in range(cells):
        order = jnp.broadcast_to(slot[cell : cell + 1, :], (ROWS, LANES))
        tile = lane_gather(own[cell, 0:ROWS, :], order)
        bundle[cell, 0:ROWS, :] = tile
        target = lane < chosen[cell : cell + 1, :]
        low = jnp.min(jnp.where(target, tile, FAR_AWAY), axis=1, keepdims=True)
        high = jnp.max(jnp.where(target, tile, -FAR_AWAY), axis=1, keepdims=True)
        bundle[cell, S_LOW : S_LOW + ROWS, :] = jnp.where(place, low, -FAR_AWAY)
        bundle[cell, S_HIGH : S_HIGH + ROWS, :] = jnp.where(place, high, FAR_AWAY)
        bundle[cell, S_REACH : S_REACH + 1, :] = jnp.broadcast_to(high[WIDE : WIDE + 1, :], (1, LANES))
        columns[cell] = tile.T

    def one_cell(cell, carry):
        def one_pair(pair, carry):
            base = pl.multiple_of(pair * 2 * ROWS, 2 * ROWS)
            mine = columns[cell, pl.ds(base, 2 * ROWS), :]
            for which, field in enumerate(SPREAD):
                tiles = spread(mine, field).reshape(2, ROWS, LANES)
                spreads[cell, pl.ds(pair * 2, 2), which * ROWS : (which + 1) * ROWS, :] = tiles
            return carry

        return lax.fori_loop(0, (actives[0, cell] + 2 * ROWS - 1) // (2 * ROWS), one_pair, carry)

    lax.fori_loop(0, cells, one_cell, 0)


def source_tiles(own, incoming, border, per_peer):
    cells, peers = own.shape[0], incoming.shape[0]
    for cell in range(cells):
        yield (
            cell, lambda c=cell: own[c, 0:ROWS, :], lambda c=cell: own[c, ROWS : ROWS + SENT, :]
        )
    for peer in range(peers):
        for entry in range(per_peer):
            near, sent = entry * ROWS, per_peer * ROWS + entry * SENT
            yield (
                cells + peer * per_peer + entry,
                lambda p=peer, n=near: incoming[p, n : n + ROWS, :],
                lambda p=peer, n=sent: incoming[p, n : n + SENT, :],
            )
    for side in range(2):
        yield (
            cells + peers * per_peer + side,
            lambda b=side: border[b, 0:ROWS, :],
            lambda b=side: border[b, ROWS : ROWS + SENT, :],
        )


def fill_shifts(shifts):
    row = lax.broadcasted_iota(jnp.int32, (ROWS, LANES), 0)
    for code in range(shifts.shape[0]):
        first, second, third = code // 9 - 1.0, code // 3 % 3 - 1.0, code % 3 - 1.0
        shifts[code] = jnp.where(
            row == X, first, jnp.where(row == Y, second, jnp.where(row == Z, third, 0.0))
        )


def fill_streams(streams, tables, sources, starts, orders, cell):
    shape = (ROWS, LANES)
    lane = lanes_of(shape)
    pairs = sources.shape[1]
    moved = []
    for pair in range(pairs):
        order = jnp.broadcast_to(orders(pair), shape)
        moved.append([lane_gather(load(sources[cell, pair], pair), order) for load in tables])
    for pair in range(pairs):
        start = starts(pair)
        block = start >> 7
        fresh = lane >= (start & (LANES - 1))
        for which, stream in enumerate(streams):
            stream[block + 1] = moved[pair][which]
            pltpu.store(stream.at[block], moved[pair][which], mask=fresh)
    end = starts(pairs)
    block = end >> 7
    for stream in streams:
        stream[block] = jnp.where(lane < (end & (LANES - 1)), stream[block], 0.0)
        for extra in range(1, SPARE):
            stream[block + extra] = jnp.zeros(shape, jnp.float32)


def spread(values, field):
    return jnp.broadcast_to(values[:, field : field + 1], (values.shape[0], LANES))


def over_targets(active, one_chunk):
    groups = (active + ROWS - 1) // ROWS

    def large(chunk, carry):
        one_chunk(pl.multiple_of(chunk * 4 * ROWS, ROWS), 4)
        return carry

    lax.fori_loop(0, groups // 4, large, 0)
    for size in (2, 1):

        @pl.when((groups & size) != 0)
        def _(size=size):
            done = groups & -(2 * size)
            one_chunk(pl.multiple_of(done * ROWS, ROWS), size)


def density_kernel(
    per_peer, pair_source, pair_shift, export, actives,
    own, incoming, border, bundle, spreads,
    density, densities, outgoing, outgoing_border,
    table, shifts, sums, lines,
):
    fill_shifts(shifts)
    cells, peers = own.shape[0], incoming.shape[0]
    for place, near, _ in source_tiles(own, incoming, border, per_peer):
        table[place] = near()

    def one_cell(cell, carry):
        def one_chunk(base, groups):
            size = groups * ROWS
            at = pl.ds(base // ROWS, groups)
            *place, wide = [
                spreads[cell, at, which * ROWS : (which + 1) * ROWS, :].reshape(size, LANES)
                for which in range(len(SPREAD))
            ]
            smooth = 0.5 * wide

            total = jnp.zeros((size, LANES), jnp.float32)
            for pair in range(pair_source.shape[1]):
                source, code = pair_source[cell, pair], pair_shift[cell, pair]
                s = lambda field: table[source, field : field + 1, :]
                shift = lambda field: shifts[code, field : field + 1, :]
                apart = [place[c] - (s(c) + shift(c)) for c in range(3)]
                square = apart[0] * apart[0] + apart[1] * apart[1] + apart[2] * apart[2]
                radius = pl.reciprocal(lax.rsqrt(square), approx=True)
                outer = jnp.maximum(wide - radius, 0.0)
                inner = jnp.maximum(smooth - radius, 0.0)
                value = outer * outer * outer - 4.0 * (inner * inner * inner)
                total = total + s(MASS) * value
            sums[cell, pl.ds(base, size), 0:1] = jnp.sum(total, axis=1, keepdims=True)

        over_targets(actives[0, cell], one_chunk)
        return carry

    lax.fori_loop(0, cells, one_cell, 0)
    for cell in range(cells):
        lines[cell : cell + 1, :] = sums[cell].T[0:1, :]
    inverse = 2.0 / bundle[:, WIDE, :]
    inverse = inverse * inverse * inverse
    summed = lines[...] * (0.25 / math.pi) * (inverse * inverse)
    rank = bundle[:, S_RANK, :].astype(jnp.int32)
    density[...] = jnp.where(
        own_rows(own, ACTIVE) > 0.5, lane_gather(summed, rank), own_rows(own, DENS)
    )
    densities[0] = summed
    densities[1] = density[...]
    for peer in range(peers):
        for entry in range(per_peer):
            outgoing[peer, entry : entry + 1, :] = density[pl.ds(export[entry, peer], 1), :]
    outgoing_border[0:1, :] = density[cells - 1 : cells, :]
    outgoing_border[1:2, :] = density[0:1, :]


def stream_kernel(
    per_peer, pair_source, pair_shift, own, incoming, border, bundle, densities,
    near_streams, far_streams, starts, orders, columns, last, heats,
    near_table, far_table, shifts, inside, totals_row, totals, sem,
):
    fill_shifts(shifts)
    cells, pairs = pair_source.shape
    tile_shape = (ROWS, LANES)
    row = lax.broadcasted_iota(jnp.int32, tile_shape, 0)
    lane = lanes_of(tile_shape).astype(jnp.float32)
    for place, near, sent in source_tiles(own, incoming, border, per_peer):
        tile, other = near(), sent()
        near_table[place] = tile
        wide, heat = tile[WIDE : WIDE + 1, :], other[HEAT : HEAT + 1, :]
        inverse = 2.0 * pl.reciprocal(wide, approx=True)
        inverse = inverse * inverse * inverse
        far_table[place, INV6 : INV6 + 1, :] = inverse * inverse
        far_table[place, HALF : HALF + 1, :] = 0.025 * wide
        far_table[place, SOUND : SOUND + 1, :] = jnp.sqrt(ADIABATIC * heat)
        heats[place : place + 1, :] = heat
        far_table[place, SUPPORT : SUPPORT + 1, :] = jnp.where(
            lane[0:1, :] < other[LIVE : LIVE + 1, :], wide, -FAR_AWAY
        )

    def choose(cell, carry):
        low = bundle[cell, S_LOW : S_LOW + ROWS, :]
        high = bundle[cell, S_HIGH : S_HIGH + ROWS, :]
        widest = bundle[cell, S_REACH : S_REACH + 1, :]
        kept = []
        for pair in range(pairs):
            source = pair_source[cell, pair]
            tile = near_table[source] + shifts[pair_shift[cell, pair]]
            away = jnp.maximum(jnp.maximum(low - tile, tile - high), 0.0)
            distance = jnp.sum(away * away, axis=0, keepdims=True)
            support = far_table[source, SUPPORT : SUPPORT + 1, :]
            limit = jnp.maximum(support, widest)
            keep = (distance < limit * limit) & (support > 0.0)
            kept.append(jnp.where(keep, 1.0, 0.0))
        target = lane[0:1, :] < bundle[cell, S_CHOSEN : S_CHOSEN + 1, :]
        kept.append(jnp.where(target, 1.0, 0.0))
        kept += [jnp.zeros((1, LANES), jnp.float32)] * (PAIR_ROWS - pairs - 1)
        base = pl.multiple_of(cell * PAIR_ROWS, PAIR_ROWS)
        inside[pl.ds(base, PAIR_ROWS), :] = jnp.concatenate(kept, axis=0)
        return carry

    lax.fori_loop(0, cells, choose, 0, unroll=4)
    flags = inside[...].astype(jnp.bfloat16)
    all_lanes = jnp.ones((ROWS, LANES), jnp.bfloat16)
    sums = lax.dot_general(
        all_lanes, flags, (((1,), (1,)), ((), ())), preferred_element_type=jnp.float32
    )
    for line in range(totals_row.shape[0]):
        totals_row[line : line + 1, :] = sums[0:1, line * LANES : (line + 1) * LANES].astype(
            jnp.int32
        )
    copy = pltpu.make_async_copy(totals_row, totals, sem)
    copy.start()
    square = (LANES, LANES)
    upper = lax.broadcasted_iota(jnp.int32, square, 0) <= lanes_of(square)
    upper = jnp.where(upper, 1.0, 0.0).astype(jnp.bfloat16)
    seen = jnp.dot(flags, upper, preferred_element_type=jnp.float32)
    wanted = lanes_of(seen.shape).astype(jnp.float32)
    slot = jnp.zeros(seen.shape, jnp.int32)
    step = LANES // 2
    while step:
        found = lane_gather(seen, slot + (step - 1))
        slot = jnp.where(found <= wanted, slot + step, slot)
        step //= 2
    orders[...] = slot
    heat, summed = bundle[:, S_HEAT, :], densities[0]
    fields = (jnp.sqrt(ADIABATIC * heat), 4.0 * summed)
    for cell in range(cells):
        tile = jnp.zeros(tile_shape, jnp.float32)
        for which, values in enumerate(fields):
            tile = jnp.where(row == which, values[cell : cell + 1, :], tile)
        columns[cell] = jnp.concatenate([bundle[cell, 0:ROWS, :], tile], axis=0).T
    last[:, F_RANK, :] = bundle[:, S_RANK, :]
    last[:, F_ACTIVE, :] = own_rows(own, ACTIVE)
    last[:, F_STEP, :] = own_rows(own, STEP)
    for from_row, to_row in ((VX, F_VX), (VY, F_VY), (VZ, F_VZ)):
        last[:, to_row, :] = own[:, from_row, :] * (1.0 / SPEED)
    last[:, F_DENS, :] = densities[1]
    last[:, F_DENS + 1, :] = jnp.zeros((cells, LANES), jnp.float32)
    copy.wait()

    def one_cell(cell, carry):
        tables = (
            lambda source, pair: near_table[source] + shifts[pair_shift[cell, pair]],
            lambda source, pair: far_table[source],
        )
        start = jnp.int32(0)
        begins, turned = [], []
        for pair in range(pairs):
            begins.append(start)
            place = cell * PAIR_ROWS + pair
            turned.append(pltpu.roll(orders[pl.ds(place, 1), :], start & (LANES - 1), 1))
            start = start + totals[place >> 7, place & (LANES - 1)]
        begins.append(start)
        turned += [turned[-1]] * (PAIR_ROWS - pairs)
        for pair, begin in enumerate(begins):
            starts[cell, pair] = begin
        place = cell * PAIR_ROWS + pairs
        starts[cell, pairs + 1] = totals[place >> 7, place & (LANES - 1)]
        fill_streams(
            (near_streams.at[cell], far_streams.at[cell]), tables, pair_source,
            lambda pair: begins[pair], lambda pair: turned[pair], cell,
        )
        base = pl.multiple_of(cell * PAIR_ROWS, PAIR_ROWS)
        orders[pl.ds(base, PAIR_ROWS), :] = jnp.concatenate(turned, axis=0)
        return carry

    lax.fori_loop(0, cells, one_cell, 0, unroll=2)


def force_kernel(
    per_peer, pair_source, starts,
    columns, orders, last, heats, new_density, new_border, near_streams, far_streams,
    acceleration, kicked,
    table, densities, streams, sums, lines,
):
    cells, peers = last.shape[0], new_density.shape[0]
    pairs = pair_source.shape[1]
    for cell in range(cells):
        densities[cell : cell + 1, :] = last[cell, F_DENS : F_DENS + 1, :]
    for peer in range(peers):
        place = cells + peer * per_peer
        densities[place : place + per_peer, :] = new_density[peer]
    place = cells + peers * per_peer
    densities[place : place + 2, :] = new_border[...]
    dens4 = 4.0 * densities[...]
    press = heats[...] * pl.reciprocal(densities[...], approx=True)
    for place in range(table.shape[0]):
        table[place, DENS4 : DENS4 + 1, :] = dens4[place : place + 1, :]
        table[place, PRESS : PRESS + 1, :] = press[place : place + 1, :]

    def one_stream(cell, carry):
        fill_streams(
            (streams.at[cell],), (lambda source, pair: table[source],), pair_source,
            lambda pair: starts[cell, pair],
            lambda pair: orders[pl.ds(cell * PAIR_ROWS + pair, 1), :], cell,
        )
        return carry

    lax.fori_loop(0, cells, one_stream, 0, unroll=4)

    def one_cell(cell, carry):
        near, far, stream = near_streams.at[cell], far_streams.at[cell], streams.at[cell]
        used = (starts[cell, pairs] + LANES - 1) >> 7
        rounds = (used + FORCE_UNROLL - 1) // FORCE_UNROLL

        def one_chunk(base, groups):
            size = groups * ROWS
            mine = columns[cell, pl.ds(base, size), :]
            place = [spread(mine, field) for field in (X, Y, Z)]
            wide = spread(mine, WIDE)
            speed = [spread(mine, field) for field in (VX, VY, VZ)]
            sound, dens4 = [spread(mine, ROWS + field) for field in range(2)]
            inv6 = 2.0 * pl.reciprocal(wide, approx=True)
            inv6 = inv6 * inv6 * inv6
            inv6 = inv6 * inv6
            half_ = 0.025 * wide
            press = sound * sound * ((4.0 / ADIABATIC) * pl.reciprocal(dens4, approx=True))

            def blocks(index, totals):
                for sub in range(FORCE_UNROLL):
                    block = index * FORCE_UNROLL + sub
                    s = lambda field: near[block, field : field + 1, :]
                    o = lambda field: far[block, field : field + 1, :]
                    m = lambda field: stream[block, field : field + 1, :]
                    apart = [place[c] - s(c) for c in range(3)]
                    square = apart[0] * apart[0] + apart[1] * apart[1] + apart[2] * apart[2]
                    inverse = lax.rsqrt(jnp.maximum(square, 1e-24))
                    radius = pl.reciprocal(inverse, approx=True)
                    outer = jnp.maximum(wide - radius, 0.0)
                    least = jnp.minimum(outer, radius)
                    slope = inv6 * (least * ((outer + outer) - least))
                    outer = jnp.maximum(s(WIDE) - radius, 0.0)
                    least = jnp.minimum(outer, radius)
                    slope = slope + o(INV6) * (least * ((outer + outer) - least))
                    approach = (
                        (speed[0] - s(VX)) * apart[0]
                        + (speed[1] - s(VY)) * apart[1]
                        + (speed[2] - s(VZ)) * apart[2]
                    )
                    half = half_ + o(HALF)
                    slow = pl.reciprocal(square + half * half, approx=True)
                    mu = half * jnp.minimum(approach, 0.0) * slow
                    light = pl.reciprocal(dens4 + m(DENS4), approx=True)
                    viscous = mu * (mu - (sound + o(SOUND))) * light
                    weight = (press + m(PRESS) + viscous) * (slope * (inverse * s(MASS)))
                    terms = [weight * a for a in apart]
                    totals = terms if totals is None else [t + a for t, a in zip(totals, terms)]
                return tuple(totals)

            totals = lax.fori_loop(1, rounds, blocks, blocks(0, None))
            for c in range(3):
                sums[cell, pl.ds(base, size), c : c + 1] = jnp.sum(
                    totals[c], axis=1, keepdims=True
                )

        over_targets(starts[cell, pairs + 1], one_chunk)
        return carry

    lax.fori_loop(0, cells, one_cell, 0)
    for cell in range(cells):
        turned = sums[cell].T
        for c in range(3):
            lines[c, cell : cell + 1, :] = turned[c : c + 1, :]
    rank = last[:, F_RANK, :].astype(jnp.int32)
    for c in range(3):
        gathered = lane_gather(lines[c] * (0.375 / math.pi), rank)
        value = jnp.where(last[:, F_ACTIVE, :] > 0.5, gathered, 0.0)
        acceleration[c] = value
        kicked[c] = last[:, F_VX + c, :] + value * last[:, F_STEP, :]


def shards(
    position, velocity, smoothing, particle_mass, energy, density_old, cell_count, active,
    time_bin, pair_source, pair_shift, export,
):
    cells, capacity = smoothing.shape
    peers, per_peer = export.shape
    sources = cells + peers * per_peer + 2
    codes = 27
    f32 = lambda *shape: jax.ShapeDtypeStruct(shape, jnp.float32)
    smem = pl.BlockSpec(memory_space=pltpu.SMEM)
    vmem = pl.BlockSpec(memory_space=pltpu.VMEM)
    hbm = pl.BlockSpec(memory_space=pltpu.HBM)
    whole = pltpu.CompilerParams(vmem_limit_bytes=64 * 2**20)
    params = pltpu.CompilerParams(vmem_limit_bytes=24 * 2**20)
    cost = pl.CostEstimate(flops=10**9, bytes_accessed=1000, transcendentals=0)
    i32 = lambda *shape: jax.ShapeDtypeStruct(shape, jnp.int32)
    sent_rows = per_peer * (ROWS + SENT)
    turned = export.T

    def landing(scalars, *arrays):
        return (
            [pltpu.SMEM(a.shape, a.dtype) for a in arrays[:scalars]]
            + [pltpu.VMEM(a.shape, a.dtype) for a in arrays[scalars:]]
            + [pltpu.SemaphoreType.DMA((len(arrays),))]
        )

    arrays = (
        cell_count, turned, position, velocity, smoothing, particle_mass, energy, density_old,
        active, time_bin,
    )
    own, outgoing, border = pl.pallas_call(
        pack_kernel,
        out_shape=(
            f32(cells, 2 * ROWS, capacity),
            f32(peers, sent_rows, capacity),
            f32(2, ROWS + SENT, capacity),
        ),
        in_specs=[hbm] * 10,
        out_specs=(vmem,) * 3,
        scratch_shapes=landing(2, *arrays),
        compiler_params=whole,
        cost_estimate=cost,
        name="pack",
    )(*arrays)

    def exchange(pieces):
        return lax.all_to_all(pieces, "cell", split_axis=0, concat_axis=0, tiled=True)

    def swap_border(pieces):
        size = lax.axis_size("region")
        up = [(i, (i + 1) % size) for i in range(size)]
        down = [(j, i) for i, j in up]
        if size == 2:
            return lax.ppermute(pieces, "region", up)
        before = lax.ppermute(pieces[0:1], "region", up)
        after = lax.ppermute(pieces[1:2], "region", down)
        return jnp.concatenate([before, after], axis=0)

    incoming = exchange(outgoing)
    other = swap_border(border)
    actives, bundle, spreads = pl.pallas_call(
        sort_kernel,
        out_shape=(
            i32(1, cells),
            f32(cells, S_ROWS, capacity),
            f32(cells, capacity // ROWS, len(SPREAD) * ROWS, capacity),
        ),
        in_specs=[vmem],
        out_specs=(smem, vmem, vmem),
        scratch_shapes=[pltpu.VMEM((cells, capacity, ROWS), jnp.float32)],
        compiler_params=params,
        cost_estimate=cost,
        name="sort",
    )(own)

    density, densities, outgoing_density, border_density = pl.pallas_call(
        functools.partial(density_kernel, per_peer),
        out_shape=(
            f32(cells, capacity),
            f32(2, cells, capacity),
            f32(peers, per_peer, capacity),
            f32(2, capacity),
        ),
        in_specs=[smem] * 4 + [vmem] * 5,
        out_specs=(vmem,) * 4,
        scratch_shapes=[
            pltpu.VMEM((sources, ROWS, capacity), jnp.float32),
            pltpu.VMEM((codes, ROWS, capacity), jnp.float32),
            pltpu.VMEM((cells, capacity, ROWS), jnp.float32),
            pltpu.VMEM((cells, capacity), jnp.float32),
        ],
        compiler_params=params,
        cost_estimate=cost,
        name="density",
    )(pair_source, pair_shift, turned, actives, own, incoming, other, bundle, spreads)

    new_density = exchange(outgoing_density)
    new_border = swap_border(border_density)
    pairs = pair_source.shape[1]
    blocks = pairs + SPARE
    pair_rows = cells * PAIR_ROWS
    source_rows = -(-sources // ROWS) * ROWS
    near_streams, far_streams, starts, orders, columns, last, heats = pl.pallas_call(
        functools.partial(stream_kernel, per_peer),
        out_shape=(
            f32(cells, blocks, ROWS, capacity),
            f32(cells, blocks, ROWS, capacity),
            i32(cells, pairs + 2),
            i32(pair_rows, capacity),
            f32(cells, capacity, 2 * ROWS),
            f32(cells, ROWS, capacity),
            f32(source_rows, capacity),
        ),
        in_specs=[smem] * 2 + [vmem] * 5,
        out_specs=(vmem, vmem, smem, vmem, vmem, vmem, vmem),
        scratch_shapes=[
            pltpu.VMEM((sources, ROWS, capacity), jnp.float32),
            pltpu.VMEM((sources, ROWS, capacity), jnp.float32),
            pltpu.VMEM((codes, ROWS, capacity), jnp.float32),
            pltpu.VMEM((pair_rows, capacity), jnp.float32),
            pltpu.VMEM((pair_rows // capacity, capacity), jnp.int32),
            pltpu.SMEM((pair_rows // capacity, capacity), jnp.int32),
            pltpu.SemaphoreType.DMA,
        ],
        compiler_params=params,
        cost_estimate=cost,
        name="streams",
    )(pair_source, pair_shift, own, incoming, other, bundle, densities)

    acceleration, kicked = pl.pallas_call(
        functools.partial(force_kernel, per_peer),
        out_shape=(f32(3, cells, capacity), f32(3, cells, capacity)),
        in_specs=[smem] * 2 + [vmem] * 8,
        out_specs=(vmem,) * 2,
        scratch_shapes=[
            pltpu.VMEM((sources, ROWS, capacity), jnp.float32),
            pltpu.VMEM((source_rows, capacity), jnp.float32),
            pltpu.VMEM((cells, blocks, ROWS, capacity), jnp.float32),
            pltpu.VMEM((cells, capacity, ROWS), jnp.float32),
            pltpu.VMEM((3, cells, capacity), jnp.float32),
        ],
        compiler_params=params,
        cost_estimate=cost,
        name="force",
    )(
        pair_source, starts, columns, orders, last, heats, new_density, new_border, near_streams,
        far_streams,
    )
    return density, acceleration, kicked


def solution(mesh):
    rows = P(("region", "cell"), None)
    planes = P(None, ("region", "cell"), None)
    return jax.shard_map(
        shards,
        mesh=mesh,
        in_specs=(
            planes, planes, rows, rows, rows, rows, P(("region", "cell")), rows, rows, rows, rows,
            rows,
        ),
        out_specs=(rows, planes, planes),
        check_vma=False,
    )
```

```python
import functools
import math

import jax
import jax.numpy as jnp
from jax import lax
from jax.experimental import pallas as pl
from jax.experimental.pallas import tpu as pltpu
from jax.sharding import PartitionSpec as P

ADIABATIC = 5.0 / 3.0
STEP_MAX = 0.2
LANES = 128
ROWS = 8
FORCE_UNROLL = 7
PAIR_ROWS = 32
FAR_AWAY = 1e9
SPARE = FORCE_UNROLL

X, Y, Z, MASS, VX, VY, VZ, WIDE = range(ROWS)
SPREAD = (X, Y, Z, WIDE)
HEAT, DENS, LIVE = range(3)
SENT = 4
SPEED = 40.0
ACTIVE, STEP = SENT, SENT + 1
S_HEAT, S_RANK, S_REACH, S_CHOSEN = range(ROWS, ROWS + 4)
S_LOW, S_HIGH, S_ROWS = 2 * ROWS, 3 * ROWS, 4 * ROWS
F_RANK, F_ACTIVE, F_STEP, F_VX, F_VY, F_VZ, F_DENS = range(7)
INV6, HALF, SOUND, SUPPORT = range(4)
DENS4, PRESS = range(2)


def lane_gather(values, index):
    return jnp.take_along_axis(values, index, axis=1, mode="promise_in_bounds")


def lanes_of(shape):
    return lax.broadcasted_iota(jnp.int32, shape, len(shape) - 1)


def start_copies(arrays, landed, sem):
    copies = [
        pltpu.make_async_copy(array, place, sem.at[index])
        for index, (array, place) in enumerate(zip(arrays, landed))
    ]
    for copy in copies:
        copy.start()
    return copies


def pack_kernel(*refs):
    arrays, (own, outgoing, border) = refs[:10], refs[10:13]
    landed, sem = refs[13:-1], refs[-1]
    for copy in start_copies(arrays, landed, sem):
        copy.wait()
    count, export, position, velocity, smoothing, mass, energy, density_old, active, time_bin = landed
    cells = smoothing.shape[0]
    shape = smoothing.shape
    lane = lanes_of(shape)
    row = lax.broadcasted_iota(jnp.int32, shape, 0)
    counts = jnp.zeros(shape, jnp.int32)
    for cell in range(cells):
        counts = jnp.where(row == cell, count[cell], counts)
    mass_live = jnp.where(lane < counts, mass[...], 0.0)
    zeros = jnp.zeros(shape, jnp.float32)
    rows = (
        position[0], position[1], position[2], mass_live,
        SPEED * velocity[0], SPEED * velocity[1], SPEED * velocity[2], 2.0 * smoothing[...],
        (ADIABATIC - 1.0) * energy[...], density_old[...], counts.astype(jnp.float32), zeros,
        jnp.where(active[...] > 0, 1.0, 0.0),
        STEP_MAX * jnp.exp2(-time_bin[...].astype(jnp.float32)), zeros, zeros,
    )
    for field, values in enumerate(rows):
        own[:, field, :] = values
    per_peer, peers = export.shape
    for peer in range(peers):
        for entry in range(per_peer):
            cell = export[entry, peer]
            outgoing[peer, entry * ROWS : (entry + 1) * ROWS, :] = own[cell, 0:ROWS, :]
            start = per_peer * ROWS + entry * SENT
            outgoing[peer, start : start + SENT, :] = own[cell, ROWS : ROWS + SENT, :]
    for side, cell in enumerate((cells - 1, 0)):
        border[side] = own[cell, 0 : ROWS + SENT, :]


def own_rows(own, field):
    return own[:, ROWS + field, :]


def sort_kernel(own, actives, bundle, spreads, columns):
    cells = own.shape[0]
    shape = (cells, LANES)
    lane = lanes_of(shape)
    ones = own_rows(own, ACTIVE)
    is_active = ones > 0.5
    for cell in range(cells):
        actives[0, cell] = jnp.sum(ones[cell : cell + 1, :]).astype(jnp.int32)
    square = (LANES, LANES)
    upper = lax.broadcasted_iota(jnp.int32, square, 0) <= lanes_of(square)
    upper = jnp.where(upper, 1.0, 0.0).astype(jnp.bfloat16)
    seen = jnp.dot(ones.astype(jnp.bfloat16), upper, preferred_element_type=jnp.float32)
    seen = seen.astype(jnp.int32)
    chosen = lane_gather(seen, jnp.full(shape, LANES - 1, jnp.int32))
    others = lane + 1 - seen
    rank = jnp.where(is_active, seen - 1, chosen + others - 1)
    first_part = lane < chosen
    wanted = jnp.where(first_part, lane, lane - chosen)
    slot = jnp.zeros(shape, jnp.int32)
    step = LANES // 2
    while step:
        probe = slot + (step - 1)
        found = jnp.where(first_part, lane_gather(seen, probe), lane_gather(others, probe))
        slot = jnp.where(found <= wanted, slot + step, slot)
        step //= 2
    bundle[:, S_HEAT, :] = lane_gather(own_rows(own, HEAT), slot)
    bundle[:, S_RANK, :] = rank.astype(jnp.float32)
    bundle[:, S_CHOSEN, :] = chosen.astype(jnp.float32)
    for spare in range(S_CHOSEN + 1, S_LOW):
        bundle[:, spare, :] = jnp.zeros(shape, jnp.float32)
    place = lax.broadcasted_iota(jnp.int32, (ROWS, LANES), 0) <= Z
    for cell in range(cells):
        order = jnp.broadcast_to(slot[cell : cell + 1, :], (ROWS, LANES))
        tile = lane_gather(own[cell, 0:ROWS, :], order)
        bundle[cell, 0:ROWS, :] = tile
        target = lane < chosen[cell : cell + 1, :]
        low = jnp.min(jnp.where(target, tile, FAR_AWAY), axis=1, keepdims=True)
        high = jnp.max(jnp.where(target, tile, -FAR_AWAY), axis=1, keepdims=True)
        bundle[cell, S_LOW : S_LOW + ROWS, :] = jnp.where(place, low, -FAR_AWAY)
        bundle[cell, S_HIGH : S_HIGH + ROWS, :] = jnp.where(place, high, FAR_AWAY)
        bundle[cell, S_REACH : S_REACH + 1, :] = jnp.broadcast_to(high[WIDE : WIDE + 1, :], (1, LANES))
        columns[cell, :, 0:ROWS] = tile.T

    def one_cell(cell, carry):
        def one_pair(pair, carry):
            base = pl.multiple_of(pair * 2 * ROWS, 2 * ROWS)
            mine = columns[cell, pl.ds(base, 2 * ROWS), :]
            for which, field in enumerate(SPREAD):
                tiles = spread(mine, field).reshape(2, ROWS, LANES)
                spreads[cell, pl.ds(pair * 2, 2), which * ROWS : (which + 1) * ROWS, :] = tiles
            return carry

        return lax.fori_loop(0, (actives[0, cell] + 2 * ROWS - 1) // (2 * ROWS), one_pair, carry)

    lax.fori_loop(0, cells, one_cell, 0)


def source_tiles(own, incoming, border, per_peer):
    cells, peers = own.shape[0], incoming.shape[0]
    for cell in range(cells):
        yield (
            cell, lambda c=cell: own[c, 0:ROWS, :], lambda c=cell: own[c, ROWS : ROWS + SENT, :]
        )
    for peer in range(peers):
        for entry in range(per_peer):
            near, sent = entry * ROWS, per_peer * ROWS + entry * SENT
            yield (
                cells + peer * per_peer + entry,
                lambda p=peer, n=near: incoming[p, n : n + ROWS, :],
                lambda p=peer, n=sent: incoming[p, n : n + SENT, :],
            )
    for side in range(2):
        yield (
            cells + peers * per_peer + side,
            lambda b=side: border[b, 0:ROWS, :],
            lambda b=side: border[b, ROWS : ROWS + SENT, :],
        )


def fill_shifts(shifts):
    row = lax.broadcasted_iota(jnp.int32, (ROWS, LANES), 0)
    for code in range(shifts.shape[0]):
        first, second, third = code // 9 - 1.0, code // 3 % 3 - 1.0, code % 3 - 1.0
        shifts[code] = jnp.where(
            row == X, first, jnp.where(row == Y, second, jnp.where(row == Z, third, 0.0))
        )


def fill_streams(streams, tables, sources, starts, orders, cell):
    shape = (ROWS, LANES)
    lane = lanes_of(shape)
    pairs = sources.shape[1]
    moved = []
    for pair in range(pairs):
        order = jnp.broadcast_to(orders(pair), shape)
        moved.append([lane_gather(load(sources[cell, pair], pair), order) for load in tables])
    for pair in range(pairs):
        start = starts(pair)
        block = start >> 7
        fresh = lane >= (start & (LANES - 1))
        for which, stream in enumerate(streams):
            stream[block + 1] = moved[pair][which]
            pltpu.store(stream.at[block], moved[pair][which], mask=fresh)
    end = starts(pairs)
    block = end >> 7
    for stream in streams:
        stream[block] = jnp.where(lane < (end & (LANES - 1)), stream[block], 0.0)
        for extra in range(1, SPARE):
            stream[block + extra] = jnp.zeros(shape, jnp.float32)


def spread(values, field):
    return lane_gather(values, jnp.full(values.shape, field, jnp.int32))


def over_targets(active, one_chunk):
    groups = (active + ROWS - 1) // ROWS

    def large(chunk, carry):
        one_chunk(pl.multiple_of(chunk * 4 * ROWS, ROWS), 4)
        return carry

    lax.fori_loop(0, groups // 4, large, 0)
    for size in (2, 1):

        @pl.when((groups & size) != 0)
        def _(size=size):
            done = groups & -(2 * size)
            one_chunk(pl.multiple_of(done * ROWS, ROWS), size)


def density_kernel(
    per_peer, pair_source, pair_shift, export, actives,
    own, incoming, border, bundle, spreads,
    density, densities, outgoing, outgoing_border,
    table, shifts, sums, lines,
):
    fill_shifts(shifts)
    cells, peers = own.shape[0], incoming.shape[0]
    for place, near, _ in source_tiles(own, incoming, border, per_peer):
        table[place] = near()

    def one_cell(cell, carry):
        def one_chunk(base, groups):
            size = groups * ROWS
            at = pl.ds(base // ROWS, groups)
            *place, wide = [
                spreads[cell, at, which * ROWS : (which + 1) * ROWS, :].reshape(size, LANES)
                for which in range(len(SPREAD))
            ]
            smooth = 0.5 * wide

            total = jnp.zeros((size, LANES), jnp.float32)
            for pair in range(pair_source.shape[1]):
                source, code = pair_source[cell, pair], pair_shift[cell, pair]
                s = lambda field: table[source, field : field + 1, :]
                shift = lambda field: shifts[code, field : field + 1, :]
                apart = [place[c] - (s(c) + shift(c)) for c in range(3)]
                square = apart[0] * apart[0] + apart[1] * apart[1] + apart[2] * apart[2]
                radius = pl.reciprocal(lax.rsqrt(square), approx=True)
                outer = jnp.maximum(wide - radius, 0.0)
                inner = jnp.maximum(smooth - radius, 0.0)
                value = outer * outer * outer - 4.0 * (inner * inner * inner)
                total = total + s(MASS) * value
            sums[cell, pl.ds(base, size), 0:1] = jnp.sum(total, axis=1, keepdims=True)

        over_targets(actives[0, cell], one_chunk)
        return carry

    lax.fori_loop(0, cells, one_cell, 0)
    for cell in range(cells):
        lines[cell : cell + 1, :] = sums[cell].T[0:1, :]
    inverse = 2.0 / bundle[:, WIDE, :]
    inverse = inverse * inverse * inverse
    summed = lines[...] * (0.25 / math.pi) * (inverse * inverse)
    rank = bundle[:, S_RANK, :].astype(jnp.int32)
    density[...] = jnp.where(
        own_rows(own, ACTIVE) > 0.5, lane_gather(summed, rank), own_rows(own, DENS)
    )
    densities[0] = summed
    densities[1] = density[...]
    for peer in range(peers):
        for entry in range(per_peer):
            outgoing[peer, entry : entry + 1, :] = density[pl.ds(export[entry, peer], 1), :]
    outgoing_border[0:1, :] = density[cells - 1 : cells, :]
    outgoing_border[1:2, :] = density[0:1, :]


def stream_kernel(
    per_peer, pair_source, pair_shift, own, incoming, border, bundle, densities,
    near_streams, far_streams, starts, orders, columns, last, heats,
    near_table, far_table, shifts, inside, totals_row, totals, sem,
):
    fill_shifts(shifts)
    cells, pairs = pair_source.shape
    tile_shape = (ROWS, LANES)
    row = lax.broadcasted_iota(jnp.int32, tile_shape, 0)
    lane = lanes_of(tile_shape).astype(jnp.float32)
    for place, near, sent in source_tiles(own, incoming, border, per_peer):
        tile, other = near(), sent()
        near_table[place] = tile
        wide, heat = tile[WIDE : WIDE + 1, :], other[HEAT : HEAT + 1, :]
        inverse = 2.0 * pl.reciprocal(wide, approx=True)
        inverse = inverse * inverse * inverse
        far_table[place, INV6 : INV6 + 1, :] = inverse * inverse
        far_table[place, HALF : HALF + 1, :] = 0.025 * wide
        far_table[place, SOUND : SOUND + 1, :] = jnp.sqrt(ADIABATIC * heat)
        heats[place : place + 1, :] = heat
        far_table[place, SUPPORT : SUPPORT + 1, :] = jnp.where(
            lane[0:1, :] < other[LIVE : LIVE + 1, :], wide, -FAR_AWAY
        )

    def choose(cell, carry):
        low = bundle[cell, S_LOW : S_LOW + ROWS, :]
        high = bundle[cell, S_HIGH : S_HIGH + ROWS, :]
        widest = bundle[cell, S_REACH : S_REACH + 1, :]
        kept = []
        for pair in range(pairs):
            source = pair_source[cell, pair]
            tile = near_table[source] + shifts[pair_shift[cell, pair]]
            away = jnp.maximum(jnp.maximum(low - tile, tile - high), 0.0)
            distance = jnp.sum(away * away, axis=0, keepdims=True)
            support = far_table[source, SUPPORT : SUPPORT + 1, :]
            limit = jnp.maximum(support, widest)
            keep = (distance < limit * limit) & (support > 0.0)
            kept.append(jnp.where(keep, 1.0, 0.0))
        target = lane[0:1, :] < bundle[cell, S_CHOSEN : S_CHOSEN + 1, :]
        kept.append(jnp.where(target, 1.0, 0.0))
        kept += [jnp.zeros((1, LANES), jnp.float32)] * (PAIR_ROWS - pairs - 1)
        base = pl.multiple_of(cell * PAIR_ROWS, PAIR_ROWS)
        inside[pl.ds(base, PAIR_ROWS), :] = jnp.concatenate(kept, axis=0)
        return carry

    lax.fori_loop(0, cells, choose, 0, unroll=4)
    flags = inside[...].astype(jnp.bfloat16)
    all_lanes = jnp.ones((ROWS, LANES), jnp.bfloat16)
    sums = lax.dot_general(
        all_lanes, flags, (((1,), (1,)), ((), ())), preferred_element_type=jnp.float32
    )
    for line in range(totals_row.shape[0]):
        totals_row[line : line + 1, :] = sums[0:1, line * LANES : (line + 1) * LANES].astype(
            jnp.int32
        )
    copy = pltpu.make_async_copy(totals_row, totals, sem)
    copy.start()
    square = (LANES, LANES)
    upper = lax.broadcasted_iota(jnp.int32, square, 0) <= lanes_of(square)
    upper = jnp.where(upper, 1.0, 0.0).astype(jnp.bfloat16)
    seen = jnp.dot(flags, upper, preferred_element_type=jnp.float32)
    wanted = lanes_of(seen.shape).astype(jnp.float32)
    slot = jnp.zeros(seen.shape, jnp.int32)
    step = LANES // 2
    while step:
        found = lane_gather(seen, slot + (step - 1))
        slot = jnp.where(found <= wanted, slot + step, slot)
        step //= 2
    orders[...] = slot
    heat, summed = bundle[:, S_HEAT, :], densities[0]
    fields = (jnp.sqrt(ADIABATIC * heat), 4.0 * summed)
    for cell in range(cells):
        tile = jnp.zeros(tile_shape, jnp.float32)
        for which, values in enumerate(fields):
            tile = jnp.where(row == which, values[cell : cell + 1, :], tile)
        columns[cell, :, 0 : 2 * ROWS] = jnp.concatenate([bundle[cell, 0:ROWS, :], tile], axis=0).T
    last[:, F_RANK, :] = bundle[:, S_RANK, :]
    last[:, F_ACTIVE, :] = own_rows(own, ACTIVE)
    last[:, F_STEP, :] = own_rows(own, STEP)
    for from_row, to_row in ((VX, F_VX), (VY, F_VY), (VZ, F_VZ)):
        last[:, to_row, :] = own[:, from_row, :] * (1.0 / SPEED)
    last[:, F_DENS, :] = densities[1]
    last[:, F_DENS + 1, :] = jnp.zeros((cells, LANES), jnp.float32)
    copy.wait()

    def one_cell(cell, carry):
        tables = (
            lambda source, pair: near_table[source] + shifts[pair_shift[cell, pair]],
            lambda source, pair: far_table[source],
        )
        start = jnp.int32(0)
        begins, turned = [], []
        for pair in range(pairs):
            begins.append(start)
            place = cell * PAIR_ROWS + pair
            turned.append(pltpu.roll(orders[pl.ds(place, 1), :], start & (LANES - 1), 1))
            start = start + totals[place >> 7, place & (LANES - 1)]
        begins.append(start)
        turned += [turned[-1]] * (PAIR_ROWS - pairs)
        for pair, begin in enumerate(begins):
            starts[cell, pair] = begin
        place = cell * PAIR_ROWS + pairs
        starts[cell, pairs + 1] = totals[place >> 7, place & (LANES - 1)]
        fill_streams(
            (near_streams.at[cell], far_streams.at[cell]), tables, pair_source,
            lambda pair: begins[pair], lambda pair: turned[pair], cell,
        )
        base = pl.multiple_of(cell * PAIR_ROWS, PAIR_ROWS)
        orders[pl.ds(base, PAIR_ROWS), :] = jnp.concatenate(turned, axis=0)
        return carry

    lax.fori_loop(0, cells, one_cell, 0, unroll=2)


def force_kernel(
    per_peer, pair_source, starts,
    columns, orders, last, heats, new_density, new_border, near_streams, far_streams, spreads,
    acceleration, kicked,
    table, densities, streams, sums, lines,
):
    cells, peers = last.shape[0], new_density.shape[0]
    pairs = pair_source.shape[1]
    for cell in range(cells):
        densities[cell : cell + 1, :] = last[cell, F_DENS : F_DENS + 1, :]
    for peer in range(peers):
        place = cells + peer * per_peer
        densities[place : place + per_peer, :] = new_density[peer]
    place = cells + peers * per_peer
    densities[place : place + 2, :] = new_border[...]
    dens4 = 4.0 * densities[...]
    press = heats[...] * pl.reciprocal(densities[...], approx=True)
    for place in range(table.shape[0]):
        table[place, DENS4 : DENS4 + 1, :] = dens4[place : place + 1, :]
        table[place, PRESS : PRESS + 1, :] = press[place : place + 1, :]

    def one_stream(cell, carry):
        fill_streams(
            (streams.at[cell],), (lambda source, pair: table[source],), pair_source,
            lambda pair: starts[cell, pair],
            lambda pair: orders[pl.ds(cell * PAIR_ROWS + pair, 1), :], cell,
        )
        return carry

    lax.fori_loop(0, cells, one_stream, 0, unroll=4)

    def one_cell(cell, carry):
        near, far, stream = near_streams.at[cell], far_streams.at[cell], streams.at[cell]
        used = (starts[cell, pairs] + LANES - 1) >> 7
        rounds = (used + FORCE_UNROLL - 1) // FORCE_UNROLL

        def one_chunk(base, groups):
            size = groups * ROWS
            mine = columns[cell, pl.ds(base, size), :]
            at = pl.ds(base // ROWS, groups)
            *place, wide = [
                spreads[cell, at, which * ROWS : (which + 1) * ROWS, :].reshape(size, LANES)
                for which in range(len(SPREAD))
            ]
            speed = [spread(mine, field) for field in (VX, VY, VZ)]
            sound, dens4 = [spread(mine, ROWS + field) for field in range(2)]
            inv6 = 2.0 * pl.reciprocal(wide, approx=True)
            inv6 = inv6 * inv6 * inv6
            inv6 = inv6 * inv6
            half_ = 0.025 * wide
            press = sound * sound * ((4.0 / ADIABATIC) * pl.reciprocal(dens4, approx=True))

            def blocks(index, totals):
                for sub in range(FORCE_UNROLL):
                    block = index * FORCE_UNROLL + sub
                    s = lambda field: near[block, field : field + 1, :]
                    o = lambda field: far[block, field : field + 1, :]
                    m = lambda field: stream[block, field : field + 1, :]
                    apart = [place[c] - s(c) for c in range(3)]
                    square = apart[0] * apart[0] + apart[1] * apart[1] + apart[2] * apart[2]
                    inverse = lax.rsqrt(jnp.maximum(square, 1e-24))
                    radius = pl.reciprocal(inverse, approx=True)
                    outer = jnp.maximum(wide - radius, 0.0)
                    least = jnp.minimum(outer, radius)
                    slope = inv6 * (least * ((outer + outer) - least))
                    outer = jnp.maximum(s(WIDE) - radius, 0.0)
                    least = jnp.minimum(outer, radius)
                    slope = slope + o(INV6) * (least * ((outer + outer) - least))
                    approach = (
                        (speed[0] - s(VX)) * apart[0]
                        + (speed[1] - s(VY)) * apart[1]
                        + (speed[2] - s(VZ)) * apart[2]
                    )
                    half = half_ + o(HALF)
                    slow = pl.reciprocal(square + half * half, approx=True)
                    mu = half * jnp.minimum(approach, 0.0) * slow
                    light = pl.reciprocal(dens4 + m(DENS4), approx=True)
                    viscous = mu * (mu - (sound + o(SOUND))) * light
                    weight = (press + m(PRESS) + viscous) * (slope * (inverse * s(MASS)))
                    terms = [weight * a for a in apart]
                    totals = terms if totals is None else [t + a for t, a in zip(totals, terms)]
                return tuple(totals)

            totals = lax.fori_loop(1, rounds, blocks, blocks(0, None))
            for c in range(3):
                sums[cell, pl.ds(base, size), c : c + 1] = jnp.sum(
                    totals[c], axis=1, keepdims=True
                )

        over_targets(starts[cell, pairs + 1], one_chunk)
        return carry

    lax.fori_loop(0, cells, one_cell, 0)
    for cell in range(cells):
        turned = sums[cell].T
        for c in range(3):
            lines[c, cell : cell + 1, :] = turned[c : c + 1, :]
    rank = last[:, F_RANK, :].astype(jnp.int32)
    for c in range(3):
        gathered = lane_gather(lines[c] * (0.375 / math.pi), rank)
        value = jnp.where(last[:, F_ACTIVE, :] > 0.5, gathered, 0.0)
        acceleration[c] = value
        kicked[c] = last[:, F_VX + c, :] + value * last[:, F_STEP, :]


def shards(
    position, velocity, smoothing, particle_mass, energy, density_old, cell_count, active,
    time_bin, pair_source, pair_shift, export,
):
    cells, capacity = smoothing.shape
    peers, per_peer = export.shape
    sources = cells + peers * per_peer + 2
    codes = 27
    f32 = lambda *shape: jax.ShapeDtypeStruct(shape, jnp.float32)
    smem = pl.BlockSpec(memory_space=pltpu.SMEM)
    vmem = pl.BlockSpec(memory_space=pltpu.VMEM)
    hbm = pl.BlockSpec(memory_space=pltpu.HBM)
    whole = pltpu.CompilerParams(vmem_limit_bytes=64 * 2**20)
    params = pltpu.CompilerParams(vmem_limit_bytes=24 * 2**20)
    cost = pl.CostEstimate(flops=10**9, bytes_accessed=1000, transcendentals=0)
    i32 = lambda *shape: jax.ShapeDtypeStruct(shape, jnp.int32)
    sent_rows = per_peer * (ROWS + SENT)
    turned = export.T

    def landing(scalars, *arrays):
        return (
            [pltpu.SMEM(a.shape, a.dtype) for a in arrays[:scalars]]
            + [pltpu.VMEM(a.shape, a.dtype) for a in arrays[scalars:]]
            + [pltpu.SemaphoreType.DMA((len(arrays),))]
        )

    arrays = (
        cell_count, turned, position, velocity, smoothing, particle_mass, energy, density_old,
        active, time_bin,
    )
    own, outgoing, border = pl.pallas_call(
        pack_kernel,
        out_shape=(
            f32(cells, 2 * ROWS, capacity),
            f32(peers, sent_rows, capacity),
            f32(2, ROWS + SENT, capacity),
        ),
        in_specs=[hbm] * 10,
        out_specs=(vmem,) * 3,
        scratch_shapes=landing(2, *arrays),
        compiler_params=whole,
        cost_estimate=cost,
        name="pack",
    )(*arrays)

    def exchange(pieces):
        return lax.all_to_all(pieces, "cell", split_axis=0, concat_axis=0, tiled=True)

    def swap_border(pieces):
        size = lax.axis_size("region")
        up = [(i, (i + 1) % size) for i in range(size)]
        down = [(j, i) for i, j in up]
        if size == 2:
            return lax.ppermute(pieces, "region", up)
        before = lax.ppermute(pieces[0:1], "region", up)
        after = lax.ppermute(pieces[1:2], "region", down)
        return jnp.concatenate([before, after], axis=0)

    incoming = exchange(outgoing)
    other = swap_border(border)
    actives, bundle, spreads = pl.pallas_call(
        sort_kernel,
        out_shape=(
            i32(1, cells),
            f32(cells, S_ROWS, capacity),
            f32(cells, capacity // ROWS, len(SPREAD) * ROWS, capacity),
        ),
        in_specs=[vmem],
        out_specs=(smem, vmem, vmem),
        scratch_shapes=[pltpu.VMEM((cells, capacity, LANES), jnp.float32)],
        compiler_params=params,
        cost_estimate=cost,
        name="sort",
    )(own)

    density, densities, outgoing_density, border_density = pl.pallas_call(
        functools.partial(density_kernel, per_peer),
        out_shape=(
            f32(cells, capacity),
            f32(2, cells, capacity),
            f32(peers, per_peer, capacity),
            f32(2, capacity),
        ),
        in_specs=[smem] * 4 + [vmem] * 5,
        out_specs=(vmem,) * 4,
        scratch_shapes=[
            pltpu.VMEM((sources, ROWS, capacity), jnp.float32),
            pltpu.VMEM((codes, ROWS, capacity), jnp.float32),
            pltpu.VMEM((cells, capacity, ROWS), jnp.float32),
            pltpu.VMEM((cells, capacity), jnp.float32),
        ],
        compiler_params=params,
        cost_estimate=cost,
        name="density",
    )(pair_source, pair_shift, turned, actives, own, incoming, other, bundle, spreads)

    new_density = exchange(outgoing_density)
    new_border = swap_border(border_density)
    pairs = pair_source.shape[1]
    blocks = pairs + SPARE
    pair_rows = cells * PAIR_ROWS
    source_rows = -(-sources // ROWS) * ROWS
    near_streams, far_streams, starts, orders, columns, last, heats = pl.pallas_call(
        functools.partial(stream_kernel, per_peer),
        out_shape=(
            f32(cells, blocks, ROWS, capacity),
            f32(cells, blocks, ROWS, capacity),
            i32(cells, pairs + 2),
            i32(pair_rows, capacity),
            f32(cells, capacity, LANES),
            f32(cells, ROWS, capacity),
            f32(source_rows, capacity),
        ),
        in_specs=[smem] * 2 + [vmem] * 5,
        out_specs=(vmem, vmem, smem, vmem, vmem, vmem, vmem),
        scratch_shapes=[
            pltpu.VMEM((sources, ROWS, capacity), jnp.float32),
            pltpu.VMEM((sources, ROWS, capacity), jnp.float32),
            pltpu.VMEM((codes, ROWS, capacity), jnp.float32),
            pltpu.VMEM((pair_rows, capacity), jnp.float32),
            pltpu.VMEM((pair_rows // capacity, capacity), jnp.int32),
            pltpu.SMEM((pair_rows // capacity, capacity), jnp.int32),
            pltpu.SemaphoreType.DMA,
        ],
        compiler_params=params,
        cost_estimate=cost,
        name="streams",
    )(pair_source, pair_shift, own, incoming, other, bundle, densities)

    acceleration, kicked = pl.pallas_call(
        functools.partial(force_kernel, per_peer),
        out_shape=(f32(3, cells, capacity), f32(3, cells, capacity)),
        in_specs=[smem] * 2 + [vmem] * 9,
        out_specs=(vmem,) * 2,
        scratch_shapes=[
            pltpu.VMEM((sources, ROWS, capacity), jnp.float32),
            pltpu.VMEM((source_rows, capacity), jnp.float32),
            pltpu.VMEM((cells, blocks, ROWS, capacity), jnp.float32),
            pltpu.VMEM((cells, capacity, ROWS), jnp.float32),
            pltpu.VMEM((3, cells, capacity), jnp.float32),
        ],
        compiler_params=params,
        cost_estimate=cost,
        name="force",
    )(
        pair_source, starts, columns, orders, last, heats, new_density, new_border, near_streams,
        far_streams, spreads,
    )
    return density, acceleration, kicked


def solution(mesh):
    rows = P(("region", "cell"), None)
    planes = P(None, ("region", "cell"), None)
    return jax.shard_map(
        shards,
        mesh=mesh,
        in_specs=(
            planes, planes, rows, rows, rows, rows, P(("region", "cell")), rows, rows, rows, rows,
            rows,
        ),
        out_specs=(rows, planes, planes),
        check_vma=False,
    )
```

```python
import functools
import math

import jax
import jax.numpy as jnp
from jax import lax
from jax.experimental import pallas as pl
from jax.experimental.pallas import tpu as pltpu
from jax.sharding import PartitionSpec as P

ADIABATIC = 5.0 / 3.0
STEP_MAX = 0.2
LANES = 128
ROWS = 8
FORCE_UNROLL = 7
PAIR_ROWS = 32
FAR_AWAY = 1e9
SPARE = FORCE_UNROLL

X, Y, Z, MASS, VX, VY, VZ, WIDE = range(ROWS)
SPREAD = (X, Y, Z, WIDE)
HEAT, DENS, LIVE = range(3)
SENT = 4
SPEED = 40.0
ACTIVE, STEP = SENT, SENT + 1
S_HEAT, S_RANK, S_REACH, S_CHOSEN = range(ROWS, ROWS + 4)
S_LOW, S_HIGH, S_ROWS = 2 * ROWS, 3 * ROWS, 4 * ROWS
F_RANK, F_ACTIVE, F_STEP, F_VX, F_VY, F_VZ, F_DENS = range(7)
DENS4, PRESS, INV6, HALF, SOUND = range(5)


def lane_gather(values, index):
    return jnp.take_along_axis(values, index, axis=1, mode="promise_in_bounds")


def lanes_of(shape):
    return lax.broadcasted_iota(jnp.int32, shape, len(shape) - 1)


def start_copies(arrays, landed, sem):
    copies = [
        pltpu.make_async_copy(array, place, sem.at[index])
        for index, (array, place) in enumerate(zip(arrays, landed))
    ]
    for copy in copies:
        copy.start()
    return copies


def pack_kernel(*refs):
    arrays, (own, outgoing, border) = refs[:10], refs[10:13]
    landed, sem = refs[13:-1], refs[-1]
    for copy in start_copies(arrays, landed, sem):
        copy.wait()
    count, export, position, velocity, smoothing, mass, energy, density_old, active, time_bin = landed
    cells = smoothing.shape[0]
    shape = smoothing.shape
    lane = lanes_of(shape)
    row = lax.broadcasted_iota(jnp.int32, shape, 0)
    counts = jnp.zeros(shape, jnp.int32)
    for cell in range(cells):
        counts = jnp.where(row == cell, count[cell], counts)
    mass_live = jnp.where(lane < counts, mass[...], 0.0)
    zeros = jnp.zeros(shape, jnp.float32)
    rows = (
        position[0], position[1], position[2], mass_live,
        SPEED * velocity[0], SPEED * velocity[1], SPEED * velocity[2], 2.0 * smoothing[...],
        (ADIABATIC - 1.0) * energy[...], density_old[...], counts.astype(jnp.float32), zeros,
        jnp.where(active[...] > 0, 1.0, 0.0),
        STEP_MAX * jnp.exp2(-time_bin[...].astype(jnp.float32)), zeros, zeros,
    )
    for field, values in enumerate(rows):
        own[:, field, :] = values
    per_peer, peers = export.shape
    for peer in range(peers):
        for entry in range(per_peer):
            cell = export[entry, peer]
            outgoing[peer, entry * ROWS : (entry + 1) * ROWS, :] = own[cell, 0:ROWS, :]
            start = per_peer * ROWS + entry * SENT
            outgoing[peer, start : start + SENT, :] = own[cell, ROWS : ROWS + SENT, :]
    for side, cell in enumerate((cells - 1, 0)):
        border[side] = own[cell, 0 : ROWS + SENT, :]


def own_rows(own, field):
    return own[:, ROWS + field, :]


def sort_kernel(own, actives, bundle, spreads, columns):
    cells = own.shape[0]
    shape = (cells, LANES)
    lane = lanes_of(shape)
    ones = own_rows(own, ACTIVE)
    is_active = ones > 0.5
    for cell in range(cells):
        actives[0, cell] = jnp.sum(ones[cell : cell + 1, :]).astype(jnp.int32)
    square = (LANES, LANES)
    upper = lax.broadcasted_iota(jnp.int32, square, 0) <= lanes_of(square)
    upper = jnp.where(upper, 1.0, 0.0).astype(jnp.bfloat16)
    seen = jnp.dot(ones.astype(jnp.bfloat16), upper, preferred_element_type=jnp.float32)
    seen = seen.astype(jnp.int32)
    chosen = lane_gather(seen, jnp.full(shape, LANES - 1, jnp.int32))
    others = lane + 1 - seen
    rank = jnp.where(is_active, seen - 1, chosen + others - 1)
    first_part = lane < chosen
    wanted = jnp.where(first_part, lane, lane - chosen)
    slot = jnp.zeros(shape, jnp.int32)
    step = LANES // 2
    while step:
        probe = slot + (step - 1)
        found = jnp.where(first_part, lane_gather(seen, probe), lane_gather(others, probe))
        slot = jnp.where(found <= wanted, slot + step, slot)
        step //= 2
    bundle[:, S_HEAT, :] = lane_gather(own_rows(own, HEAT), slot)
    bundle[:, S_RANK, :] = rank.astype(jnp.float32)
    bundle[:, S_CHOSEN, :] = chosen.astype(jnp.float32)
    for spare in range(S_CHOSEN + 1, S_LOW):
        bundle[:, spare, :] = jnp.zeros(shape, jnp.float32)
    place = lax.broadcasted_iota(jnp.int32, (ROWS, LANES), 0) <= Z
    for cell in range(cells):
        order = jnp.broadcast_to(slot[cell : cell + 1, :], (ROWS, LANES))
        tile = lane_gather(own[cell, 0:ROWS, :], order)
        bundle[cell, 0:ROWS, :] = tile
        target = lane < chosen[cell : cell + 1, :]
        low = jnp.min(jnp.where(target, tile, FAR_AWAY), axis=1, keepdims=True)
        high = jnp.max(jnp.where(target, tile, -FAR_AWAY), axis=1, keepdims=True)
        bundle[cell, S_LOW : S_LOW + ROWS, :] = jnp.where(place, low, -FAR_AWAY)
        bundle[cell, S_HIGH : S_HIGH + ROWS, :] = jnp.where(place, high, FAR_AWAY)
        bundle[cell, S_REACH : S_REACH + 1, :] = jnp.broadcast_to(high[WIDE : WIDE + 1, :], (1, LANES))
        columns[cell, :, 0:ROWS] = tile.T

    def one_cell(cell, carry):
        def one_pair(pair, carry):
            base = pl.multiple_of(pair * 2 * ROWS, 2 * ROWS)
            mine = columns[cell, pl.ds(base, 2 * ROWS), :]
            for which, field in enumerate(SPREAD):
                tiles = spread(mine, field).reshape(2, ROWS, LANES)
                spreads[cell, pl.ds(pair * 2, 2), which * ROWS : (which + 1) * ROWS, :] = tiles
            return carry

        return lax.fori_loop(0, (actives[0, cell] + 2 * ROWS - 1) // (2 * ROWS), one_pair, carry)

    lax.fori_loop(0, cells, one_cell, 0)


def source_tiles(own, incoming, border, per_peer):
    cells, peers = own.shape[0], incoming.shape[0]
    for cell in range(cells):
        yield (
            cell, lambda c=cell: own[c, 0:ROWS, :], lambda c=cell: own[c, ROWS : ROWS + SENT, :]
        )
    for peer in range(peers):
        for entry in range(per_peer):
            near, sent = entry * ROWS, per_peer * ROWS + entry * SENT
            yield (
                cells + peer * per_peer + entry,
                lambda p=peer, n=near: incoming[p, n : n + ROWS, :],
                lambda p=peer, n=sent: incoming[p, n : n + SENT, :],
            )
    for side in range(2):
        yield (
            cells + peers * per_peer + side,
            lambda b=side: border[b, 0:ROWS, :],
            lambda b=side: border[b, ROWS : ROWS + SENT, :],
        )


def fill_shifts(shifts):
    row = lax.broadcasted_iota(jnp.int32, (ROWS, LANES), 0)
    for code in range(shifts.shape[0]):
        first, second, third = code // 9 - 1.0, code // 3 % 3 - 1.0, code % 3 - 1.0
        shifts[code] = jnp.where(
            row == X, first, jnp.where(row == Y, second, jnp.where(row == Z, third, 0.0))
        )


def fill_stream(stream, load, sources, starts, orders, cell):
    shape = (ROWS, LANES)
    lane = lanes_of(shape)
    pairs = sources.shape[1]
    moved = []
    for pair in range(pairs):
        order = jnp.broadcast_to(orders(pair), shape)
        moved.append(lane_gather(load(sources[cell, pair], pair), order))
    for pair in range(pairs):
        start = starts(pair)
        block = start >> 7
        stream[block + 1] = moved[pair]
        pltpu.store(stream.at[block], moved[pair], mask=lane >= (start & (LANES - 1)))
    end = starts(pairs)
    block = end >> 7
    stream[block] = jnp.where(lane < (end & (LANES - 1)), stream[block], 0.0)
    for extra in range(1, SPARE):
        stream[block + extra] = jnp.zeros(shape, jnp.float32)


def spread(values, field):
    return lane_gather(values, jnp.full(values.shape, field, jnp.int32))


def over_targets(active, one_chunk):
    groups = (active + ROWS - 1) // ROWS

    def large(chunk, carry):
        one_chunk(pl.multiple_of(chunk * 4 * ROWS, ROWS), 4)
        return carry

    lax.fori_loop(0, groups // 4, large, 0)
    for size in (2, 1):

        @pl.when((groups & size) != 0)
        def _(size=size):
            done = groups & -(2 * size)
            one_chunk(pl.multiple_of(done * ROWS, ROWS), size)


def density_kernel(
    per_peer, pair_source, pair_shift, export, actives,
    own, incoming, border, bundle, spreads,
    density, densities, outgoing, outgoing_border,
    table, shifts, sums, lines,
):
    fill_shifts(shifts)
    cells, peers = own.shape[0], incoming.shape[0]
    for place, near, _ in source_tiles(own, incoming, border, per_peer):
        table[place] = near()

    def one_cell(cell, carry):
        def one_chunk(base, groups):
            size = groups * ROWS
            at = pl.ds(base // ROWS, groups)
            *place, wide = [
                spreads[cell, at, which * ROWS : (which + 1) * ROWS, :].reshape(size, LANES)
                for which in range(len(SPREAD))
            ]
            smooth = 0.5 * wide

            total = jnp.zeros((size, LANES), jnp.float32)
            for pair in range(pair_source.shape[1]):
                source, code = pair_source[cell, pair], pair_shift[cell, pair]
                s = lambda field: table[source, field : field + 1, :]
                shift = lambda field: shifts[code, field : field + 1, :]
                apart = [place[c] - (s(c) + shift(c)) for c in range(3)]
                square = apart[0] * apart[0] + apart[1] * apart[1] + apart[2] * apart[2]
                radius = pl.reciprocal(lax.rsqrt(square), approx=True)
                outer = jnp.maximum(wide - radius, 0.0)
                inner = jnp.maximum(smooth - radius, 0.0)
                value = outer * outer * outer - 4.0 * (inner * inner * inner)
                total = total + s(MASS) * value
            sums[cell, pl.ds(base, size), 0:1] = jnp.sum(total, axis=1, keepdims=True)

        over_targets(actives[0, cell], one_chunk)
        return carry

    lax.fori_loop(0, cells, one_cell, 0)
    for cell in range(cells):
        lines[cell : cell + 1, :] = sums[cell].T[0:1, :]
    inverse = 2.0 / bundle[:, WIDE, :]
    inverse = inverse * inverse * inverse
    summed = lines[...] * (0.25 / math.pi) * (inverse * inverse)
    rank = bundle[:, S_RANK, :].astype(jnp.int32)
    density[...] = jnp.where(
        own_rows(own, ACTIVE) > 0.5, lane_gather(summed, rank), own_rows(own, DENS)
    )
    densities[0] = summed
    densities[1] = density[...]
    for peer in range(peers):
        for entry in range(per_peer):
            outgoing[peer, entry : entry + 1, :] = density[pl.ds(export[entry, peer], 1), :]
    outgoing_border[0:1, :] = density[cells - 1 : cells, :]
    outgoing_border[1:2, :] = density[0:1, :]


def stream_kernel(
    per_peer, pair_source, pair_shift, own, incoming, border, bundle, densities,
    near_streams, starts, orders, columns, last, traits,
    near_table, supports, shifts, inside, totals_row, totals, sem,
):
    fill_shifts(shifts)
    cells, pairs = pair_source.shape
    tile_shape = (ROWS, LANES)
    row = lax.broadcasted_iota(jnp.int32, tile_shape, 0)
    lane = lanes_of(tile_shape).astype(jnp.float32)
    for place, near, sent in source_tiles(own, incoming, border, per_peer):
        tile, other = near(), sent()
        near_table[place] = tile
        wide, at = tile[WIDE : WIDE + 1, :], slice(place, place + 1)
        traits[0, at, :] = other[HEAT : HEAT + 1, :]
        traits[1, at, :] = wide
        supports[at, :] = jnp.where(lane[0:1, :] < other[LIVE : LIVE + 1, :], wide, -FAR_AWAY)

    def choose(cell, carry):
        low = bundle[cell, S_LOW : S_LOW + ROWS, :]
        high = bundle[cell, S_HIGH : S_HIGH + ROWS, :]
        widest = bundle[cell, S_REACH : S_REACH + 1, :]
        kept = []
        for pair in range(pairs):
            source = pair_source[cell, pair]
            tile = near_table[source] + shifts[pair_shift[cell, pair]]
            away = jnp.maximum(jnp.maximum(low - tile, tile - high), 0.0)
            distance = jnp.sum(away * away, axis=0, keepdims=True)
            support = supports[pl.ds(source, 1), :]
            limit = jnp.maximum(support, widest)
            keep = (distance < limit * limit) & (support > 0.0)
            kept.append(jnp.where(keep, 1.0, 0.0))
        target = lane[0:1, :] < bundle[cell, S_CHOSEN : S_CHOSEN + 1, :]
        kept.append(jnp.where(target, 1.0, 0.0))
        kept += [jnp.zeros((1, LANES), jnp.float32)] * (PAIR_ROWS - pairs - 1)
        base = pl.multiple_of(cell * PAIR_ROWS, PAIR_ROWS)
        inside[pl.ds(base, PAIR_ROWS), :] = jnp.concatenate(kept, axis=0)
        return carry

    lax.fori_loop(0, cells, choose, 0, unroll=4)
    flags = inside[...].astype(jnp.bfloat16)
    all_lanes = jnp.ones((ROWS, LANES), jnp.bfloat16)
    sums = lax.dot_general(
        all_lanes, flags, (((1,), (1,)), ((), ())), preferred_element_type=jnp.float32
    )
    for line in range(totals_row.shape[0]):
        totals_row[line : line + 1, :] = sums[0:1, line * LANES : (line + 1) * LANES].astype(
            jnp.int32
        )
    copy = pltpu.make_async_copy(totals_row, totals, sem)
    copy.start()
    square = (LANES, LANES)
    upper = lax.broadcasted_iota(jnp.int32, square, 0) <= lanes_of(square)
    upper = jnp.where(upper, 1.0, 0.0).astype(jnp.bfloat16)
    seen = jnp.dot(flags, upper, preferred_element_type=jnp.float32)
    wanted = lanes_of(seen.shape).astype(jnp.float32)
    slot = jnp.zeros(seen.shape, jnp.int32)
    step = LANES // 2
    while step:
        found = lane_gather(seen, slot + (step - 1))
        slot = jnp.where(found <= wanted, slot + step, slot)
        step //= 2
    orders[...] = slot
    heat, summed = bundle[:, S_HEAT, :], densities[0]
    fields = (jnp.sqrt(ADIABATIC * heat), 4.0 * summed)
    for cell in range(cells):
        tile = jnp.zeros(tile_shape, jnp.float32)
        for which, values in enumerate(fields):
            tile = jnp.where(row == which, values[cell : cell + 1, :], tile)
        columns[cell, :, 0 : 2 * ROWS] = jnp.concatenate([bundle[cell, 0:ROWS, :], tile], axis=0).T
    last[:, F_RANK, :] = bundle[:, S_RANK, :]
    last[:, F_ACTIVE, :] = own_rows(own, ACTIVE)
    last[:, F_STEP, :] = own_rows(own, STEP)
    for from_row, to_row in ((VX, F_VX), (VY, F_VY), (VZ, F_VZ)):
        last[:, to_row, :] = own[:, from_row, :] * (1.0 / SPEED)
    last[:, F_DENS, :] = densities[1]
    last[:, F_DENS + 1, :] = jnp.zeros((cells, LANES), jnp.float32)
    copy.wait()

    def one_cell(cell, carry):
        load = lambda source, pair: near_table[source] + shifts[pair_shift[cell, pair]]
        start = jnp.int32(0)
        begins, turned = [], []
        for pair in range(pairs):
            begins.append(start)
            place = cell * PAIR_ROWS + pair
            turned.append(pltpu.roll(orders[pl.ds(place, 1), :], start & (LANES - 1), 1))
            start = start + totals[place >> 7, place & (LANES - 1)]
        begins.append(start)
        turned += [turned[-1]] * (PAIR_ROWS - pairs)
        for pair, begin in enumerate(begins):
            starts[cell, pair] = begin
        place = cell * PAIR_ROWS + pairs
        starts[cell, pairs + 1] = totals[place >> 7, place & (LANES - 1)]
        fill_stream(
            near_streams.at[cell], load, pair_source,
            lambda pair: begins[pair], lambda pair: turned[pair], cell,
        )
        base = pl.multiple_of(cell * PAIR_ROWS, PAIR_ROWS)
        orders[pl.ds(base, PAIR_ROWS), :] = jnp.concatenate(turned, axis=0)
        return carry

    lax.fori_loop(0, cells, one_cell, 0, unroll=2)


def force_kernel(
    per_peer, pair_source, starts,
    columns, orders, last, traits, new_density, new_border, near_streams,
    acceleration, kicked,
    table, densities, streams, sums, lines,
):
    cells, peers = last.shape[0], new_density.shape[0]
    pairs = pair_source.shape[1]
    for cell in range(cells):
        densities[cell : cell + 1, :] = last[cell, F_DENS : F_DENS + 1, :]
    for peer in range(peers):
        place = cells + peer * per_peer
        densities[place : place + per_peer, :] = new_density[peer]
    place = cells + peers * per_peer
    densities[place : place + 2, :] = new_border[...]
    heat, wide = traits[0], traits[1]
    inverse = 2.0 * pl.reciprocal(wide, approx=True)
    inverse = inverse * inverse * inverse
    table[:, DENS4, :] = 4.0 * densities[...]
    table[:, PRESS, :] = heat * pl.reciprocal(densities[...], approx=True)
    table[:, INV6, :] = inverse * inverse
    table[:, HALF, :] = 0.025 * wide
    table[:, SOUND, :] = jnp.sqrt(ADIABATIC * heat)

    def one_stream(cell, carry):
        fill_stream(
            streams.at[cell], lambda source, pair: table[source], pair_source,
            lambda pair: starts[cell, pair],
            lambda pair: orders[pl.ds(cell * PAIR_ROWS + pair, 1), :], cell,
        )
        return carry

    lax.fori_loop(0, cells, one_stream, 0, unroll=4)

    def one_cell(cell, carry):
        near, far = near_streams.at[cell], streams.at[cell]
        used = (starts[cell, pairs] + LANES - 1) >> 7
        rounds = (used + FORCE_UNROLL - 1) // FORCE_UNROLL

        def one_chunk(base, groups):
            size = groups * ROWS
            mine = columns[cell, pl.ds(base, size), :]
            place = [spread(mine, field) for field in (X, Y, Z)]
            wide = spread(mine, WIDE)
            speed = [spread(mine, field) for field in (VX, VY, VZ)]
            sound, dens4 = [spread(mine, ROWS + field) for field in range(2)]
            inv6 = 2.0 * pl.reciprocal(wide, approx=True)
            inv6 = inv6 * inv6 * inv6
            inv6 = inv6 * inv6
            half_ = 0.025 * wide
            press = sound * sound * ((4.0 / ADIABATIC) * pl.reciprocal(dens4, approx=True))

            def blocks(index, totals):
                for sub in range(FORCE_UNROLL):
                    block = index * FORCE_UNROLL + sub
                    s = lambda field: near[block, field : field + 1, :]
                    o = lambda field: far[block, field : field + 1, :]
                    apart = [place[c] - s(c) for c in range(3)]
                    square = apart[0] * apart[0] + apart[1] * apart[1] + apart[2] * apart[2]
                    inverse = lax.rsqrt(jnp.maximum(square, 1e-24))
                    radius = pl.reciprocal(inverse, approx=True)
                    outer = jnp.maximum(wide - radius, 0.0)
                    least = jnp.minimum(outer, radius)
                    slope = inv6 * (least * ((outer + outer) - least))
                    outer = jnp.maximum(s(WIDE) - radius, 0.0)
                    least = jnp.minimum(outer, radius)
                    slope = slope + o(INV6) * (least * ((outer + outer) - least))
                    approach = (
                        (speed[0] - s(VX)) * apart[0]
                        + (speed[1] - s(VY)) * apart[1]
                        + (speed[2] - s(VZ)) * apart[2]
                    )
                    half = half_ + o(HALF)
                    slow = pl.reciprocal(square + half * half, approx=True)
                    mu = half * jnp.minimum(approach, 0.0) * slow
                    light = pl.reciprocal(dens4 + o(DENS4), approx=True)
                    viscous = mu * (mu - (sound + o(SOUND))) * light
                    weight = (press + o(PRESS) + viscous) * (slope * (inverse * s(MASS)))
                    terms = [weight * a for a in apart]
                    totals = terms if totals is None else [t + a for t, a in zip(totals, terms)]
                return tuple(totals)

            totals = lax.fori_loop(1, rounds, blocks, blocks(0, None))
            for c in range(3):
                sums[cell, pl.ds(base, size), c : c + 1] = jnp.sum(
                    totals[c], axis=1, keepdims=True
                )

        over_targets(starts[cell, pairs + 1], one_chunk)
        return carry

    lax.fori_loop(0, cells, one_cell, 0)
    for cell in range(cells):
        turned = sums[cell].T
        for c in range(3):
            lines[c, cell : cell + 1, :] = turned[c : c + 1, :]
    rank = last[:, F_RANK, :].astype(jnp.int32)
    for c in range(3):
        gathered = lane_gather(lines[c] * (0.375 / math.pi), rank)
        value = jnp.where(last[:, F_ACTIVE, :] > 0.5, gathered, 0.0)
        acceleration[c] = value
        kicked[c] = last[:, F_VX + c, :] + value * last[:, F_STEP, :]


def shards(
    position, velocity, smoothing, particle_mass, energy, density_old, cell_count, active,
    time_bin, pair_source, pair_shift, export,
):
    cells, capacity = smoothing.shape
    peers, per_peer = export.shape
    sources = cells + peers * per_peer + 2
    codes = 27
    f32 = lambda *shape: jax.ShapeDtypeStruct(shape, jnp.float32)
    smem = pl.BlockSpec(memory_space=pltpu.SMEM)
    vmem = pl.BlockSpec(memory_space=pltpu.VMEM)
    hbm = pl.BlockSpec(memory_space=pltpu.HBM)
    whole = pltpu.CompilerParams(vmem_limit_bytes=64 * 2**20)
    params = pltpu.CompilerParams(vmem_limit_bytes=24 * 2**20)
    cost = pl.CostEstimate(flops=10**9, bytes_accessed=1000, transcendentals=0)
    i32 = lambda *shape: jax.ShapeDtypeStruct(shape, jnp.int32)
    sent_rows = per_peer * (ROWS + SENT)
    turned = export.T

    def landing(scalars, *arrays):
        return (
            [pltpu.SMEM(a.shape, a.dtype) for a in arrays[:scalars]]
            + [pltpu.VMEM(a.shape, a.dtype) for a in arrays[scalars:]]
            + [pltpu.SemaphoreType.DMA((len(arrays),))]
        )

    arrays = (
        cell_count, turned, position, velocity, smoothing, particle_mass, energy, density_old,
        active, time_bin,
    )
    own, outgoing, border = pl.pallas_call(
        pack_kernel,
        out_shape=(
            f32(cells, 2 * ROWS, capacity),
            f32(peers, sent_rows, capacity),
            f32(2, ROWS + SENT, capacity),
        ),
        in_specs=[hbm] * 10,
        out_specs=(vmem,) * 3,
        scratch_shapes=landing(2, *arrays),
        compiler_params=whole,
        cost_estimate=cost,
        name="pack",
    )(*arrays)

    def exchange(pieces):
        return lax.all_to_all(pieces, "cell", split_axis=0, concat_axis=0, tiled=True)

    def swap_border(pieces):
        size = lax.axis_size("region")
        up = [(i, (i + 1) % size) for i in range(size)]
        down = [(j, i) for i, j in up]
        if size == 2:
            return lax.ppermute(pieces, "region", up)
        before = lax.ppermute(pieces[0:1], "region", up)
        after = lax.ppermute(pieces[1:2], "region", down)
        return jnp.concatenate([before, after], axis=0)

    incoming = exchange(outgoing)
    other = swap_border(border)
    actives, bundle, spreads = pl.pallas_call(
        sort_kernel,
        out_shape=(
            i32(1, cells),
            f32(cells, S_ROWS, capacity),
            f32(cells, capacity // ROWS, len(SPREAD) * ROWS, capacity),
        ),
        in_specs=[vmem],
        out_specs=(smem, vmem, vmem),
        scratch_shapes=[pltpu.VMEM((cells, capacity, LANES), jnp.float32)],
        compiler_params=params,
        cost_estimate=cost,
        name="sort",
    )(own)

    density, densities, outgoing_density, border_density = pl.pallas_call(
        functools.partial(density_kernel, per_peer),
        out_shape=(
            f32(cells, capacity),
            f32(2, cells, capacity),
            f32(peers, per_peer, capacity),
            f32(2, capacity),
        ),
        in_specs=[smem] * 4 + [vmem] * 5,
        out_specs=(vmem,) * 4,
        scratch_shapes=[
            pltpu.VMEM((sources, ROWS, capacity), jnp.float32),
            pltpu.VMEM((codes, ROWS, capacity), jnp.float32),
            pltpu.VMEM((cells, capacity, ROWS), jnp.float32),
            pltpu.VMEM((cells, capacity), jnp.float32),
        ],
        compiler_params=params,
        cost_estimate=cost,
        name="density",
    )(pair_source, pair_shift, turned, actives, own, incoming, other, bundle, spreads)

    new_density = exchange(outgoing_density)
    new_border = swap_border(border_density)
    pairs = pair_source.shape[1]
    blocks = pairs + SPARE
    pair_rows = cells * PAIR_ROWS
    source_rows = -(-sources // ROWS) * ROWS
    near_streams, starts, orders, columns, last, traits = pl.pallas_call(
        functools.partial(stream_kernel, per_peer),
        out_shape=(
            f32(cells, blocks, ROWS, capacity),
            i32(cells, pairs + 2),
            i32(pair_rows, capacity),
            f32(cells, capacity, LANES),
            f32(cells, ROWS, capacity),
            f32(2, source_rows, capacity),
        ),
        in_specs=[smem] * 2 + [vmem] * 5,
        out_specs=(vmem, smem, vmem, vmem, vmem, vmem),
        scratch_shapes=[
            pltpu.VMEM((sources, ROWS, capacity), jnp.float32),
            pltpu.VMEM((source_rows, capacity), jnp.float32),
            pltpu.VMEM((codes, ROWS, capacity), jnp.float32),
            pltpu.VMEM((pair_rows, capacity), jnp.float32),
            pltpu.VMEM((pair_rows // capacity, capacity), jnp.int32),
            pltpu.SMEM((pair_rows // capacity, capacity), jnp.int32),
            pltpu.SemaphoreType.DMA,
        ],
        compiler_params=params,
        cost_estimate=cost,
        name="streams",
    )(pair_source, pair_shift, own, incoming, other, bundle, densities)

    acceleration, kicked = pl.pallas_call(
        functools.partial(force_kernel, per_peer),
        out_shape=(f32(3, cells, capacity), f32(3, cells, capacity)),
        in_specs=[smem] * 2 + [vmem] * 7,
        out_specs=(vmem,) * 2,
        scratch_shapes=[
            pltpu.VMEM((source_rows, ROWS, capacity), jnp.float32),
            pltpu.VMEM((source_rows, capacity), jnp.float32),
            pltpu.VMEM((cells, blocks, ROWS, capacity), jnp.float32),
            pltpu.VMEM((cells, capacity, ROWS), jnp.float32),
            pltpu.VMEM((3, cells, capacity), jnp.float32),
        ],
        compiler_params=params,
        cost_estimate=cost,
        name="force",
    )(
        pair_source, starts, columns, orders, last, traits, new_density, new_border, near_streams,
    )
    return density, acceleration, kicked


def solution(mesh):
    rows = P(("region", "cell"), None)
    planes = P(None, ("region", "cell"), None)
    return jax.shard_map(
        shards,
        mesh=mesh,
        in_specs=(
            planes, planes, rows, rows, rows, rows, P(("region", "cell")), rows, rows, rows, rows,
            rows,
        ),
        out_specs=(rows, planes, planes),
        check_vma=False,
    )
```

```python
import functools
import math

import jax
import jax.numpy as jnp
from jax import lax
from jax.experimental import pallas as pl
from jax.experimental.pallas import tpu as pltpu
from jax.sharding import PartitionSpec as P

ADIABATIC = 5.0 / 3.0
STEP_MAX = 0.2
LANES = 128
ROWS = 8
FORCE_UNROLL = 7
PAIR_ROWS = 32
FAR_AWAY = 1e9
SPARE = FORCE_UNROLL

X, Y, Z, MASS, VX, VY, VZ, WIDE = range(ROWS)
SPREAD = (X, Y, Z, WIDE)
HEAT, DENS, LIVE = range(3)
SENT = 4
SPEED = 40.0
ACTIVE, STEP = SENT, SENT + 1
S_HEAT, S_RANK, S_REACH, S_CHOSEN = range(ROWS, ROWS + 4)
S_LOW, S_HIGH, S_ROWS = 2 * ROWS, 3 * ROWS, 4 * ROWS
F_RANK, F_ACTIVE, F_STEP, F_VX, F_VY, F_VZ, F_DENS = range(7)
DENS4, PRESS, INV6, HALF, SOUND = range(5)


def lane_gather(values, index):
    return jnp.take_along_axis(values, index, axis=1, mode="promise_in_bounds")


def lanes_of(shape):
    return lax.broadcasted_iota(jnp.int32, shape, len(shape) - 1)


def start_copies(arrays, landed, sem):
    copies = [
        pltpu.make_async_copy(array, place, sem.at[index])
        for index, (array, place) in enumerate(zip(arrays, landed))
    ]
    for copy in copies:
        copy.start()
    return copies


def pack_kernel(*refs):
    arrays, (own, outgoing, border) = refs[:10], refs[10:13]
    landed, sem = refs[13:-1], refs[-1]
    for copy in start_copies(arrays, landed, sem):
        copy.wait()
    count, export, position, velocity, smoothing, mass, energy, density_old, active, time_bin = landed
    cells = smoothing.shape[0]
    shape = smoothing.shape
    lane = lanes_of(shape)
    row = lax.broadcasted_iota(jnp.int32, shape, 0)
    counts = jnp.zeros(shape, jnp.int32)
    for cell in range(cells):
        counts = jnp.where(row == cell, count[cell], counts)
    mass_live = jnp.where(lane < counts, mass[...], 0.0)
    zeros = jnp.zeros(shape, jnp.float32)
    rows = (
        position[0], position[1], position[2], mass_live,
        SPEED * velocity[0], SPEED * velocity[1], SPEED * velocity[2], 2.0 * smoothing[...],
        (ADIABATIC - 1.0) * energy[...], density_old[...], counts.astype(jnp.float32), zeros,
        jnp.where(active[...] > 0, 1.0, 0.0),
        STEP_MAX * jnp.exp2(-time_bin[...].astype(jnp.float32)), zeros, zeros,
    )
    for field, values in enumerate(rows):
        own[:, field, :] = values
    per_peer, peers = export.shape
    for peer in range(peers):
        for entry in range(per_peer):
            cell = export[entry, peer]
            outgoing[peer, entry * ROWS : (entry + 1) * ROWS, :] = own[cell, 0:ROWS, :]
            start = per_peer * ROWS + entry * SENT
            outgoing[peer, start : start + SENT, :] = own[cell, ROWS : ROWS + SENT, :]
    for side, cell in enumerate((cells - 1, 0)):
        border[side] = own[cell, 0 : ROWS + SENT, :]


def own_rows(own, field):
    return own[:, ROWS + field, :]


def sort_kernel(own, actives, bundle, spreads, columns):
    cells = own.shape[0]
    shape = (cells, LANES)
    lane = lanes_of(shape)
    ones = own_rows(own, ACTIVE)
    is_active = ones > 0.5
    for cell in range(cells):
        actives[0, cell] = jnp.sum(ones[cell : cell + 1, :]).astype(jnp.int32)
    square = (LANES, LANES)
    upper = lax.broadcasted_iota(jnp.int32, square, 0) <= lanes_of(square)
    upper = jnp.where(upper, 1.0, 0.0).astype(jnp.bfloat16)
    seen = jnp.dot(ones.astype(jnp.bfloat16), upper, preferred_element_type=jnp.float32)
    seen = seen.astype(jnp.int32)
    chosen = lane_gather(seen, jnp.full(shape, LANES - 1, jnp.int32))
    others = lane + 1 - seen
    rank = jnp.where(is_active, seen - 1, chosen + others - 1)
    first_part = lane < chosen
    wanted = jnp.where(first_part, lane, lane - chosen)
    slot = jnp.zeros(shape, jnp.int32)
    step = LANES // 2
    while step:
        probe = slot + (step - 1)
        found = jnp.where(first_part, lane_gather(seen, probe), lane_gather(others, probe))
        slot = jnp.where(found <= wanted, slot + step, slot)
        step //= 2
    bundle[:, S_HEAT, :] = lane_gather(own_rows(own, HEAT), slot)
    bundle[:, S_RANK, :] = rank.astype(jnp.float32)
    bundle[:, S_CHOSEN, :] = chosen.astype(jnp.float32)
    for spare in range(S_CHOSEN + 1, S_LOW):
        bundle[:, spare, :] = jnp.zeros(shape, jnp.float32)
    place = lax.broadcasted_iota(jnp.int32, (ROWS, LANES), 0) <= Z
    for cell in range(cells):
        order = jnp.broadcast_to(slot[cell : cell + 1, :], (ROWS, LANES))
        tile = lane_gather(own[cell, 0:ROWS, :], order)
        bundle[cell, 0:ROWS, :] = tile
        target = lane < chosen[cell : cell + 1, :]
        low = jnp.min(jnp.where(target, tile, FAR_AWAY), axis=1, keepdims=True)
        high = jnp.max(jnp.where(target, tile, -FAR_AWAY), axis=1, keepdims=True)
        bundle[cell, S_LOW : S_LOW + ROWS, :] = jnp.where(place, low, -FAR_AWAY)
        bundle[cell, S_HIGH : S_HIGH + ROWS, :] = jnp.where(place, high, FAR_AWAY)
        bundle[cell, S_REACH : S_REACH + 1, :] = jnp.broadcast_to(high[WIDE : WIDE + 1, :], (1, LANES))
        columns[cell, :, 0:ROWS] = tile.T

    def one_cell(cell, carry):
        def one_pair(pair, carry):
            base = pl.multiple_of(pair * 2 * ROWS, 2 * ROWS)
            mine = columns[cell, pl.ds(base, 2 * ROWS), :]
            for which, field in enumerate(SPREAD):
                tiles = spread(mine, field).reshape(2, ROWS, LANES)
                spreads[cell, pl.ds(pair * 2, 2), which * ROWS : (which + 1) * ROWS, :] = tiles
            return carry

        return lax.fori_loop(0, (actives[0, cell] + 2 * ROWS - 1) // (2 * ROWS), one_pair, carry)

    lax.fori_loop(0, cells, one_cell, 0)


def source_tiles(own, incoming, border, per_peer):
    cells, peers = own.shape[0], incoming.shape[0]
    for cell in range(cells):
        yield (
            cell, lambda c=cell: own[c, 0:ROWS, :], lambda c=cell: own[c, ROWS : ROWS + SENT, :]
        )
    for peer in range(peers):
        for entry in range(per_peer):
            near, sent = entry * ROWS, per_peer * ROWS + entry * SENT
            yield (
                cells + peer * per_peer + entry,
                lambda p=peer, n=near: incoming[p, n : n + ROWS, :],
                lambda p=peer, n=sent: incoming[p, n : n + SENT, :],
            )
    for side in range(2):
        yield (
            cells + peers * per_peer + side,
            lambda b=side: border[b, 0:ROWS, :],
            lambda b=side: border[b, ROWS : ROWS + SENT, :],
        )


def fill_shifts(shifts):
    row = lax.broadcasted_iota(jnp.int32, (ROWS, LANES), 0)
    for code in range(shifts.shape[0]):
        first, second, third = code // 9 - 1.0, code // 3 % 3 - 1.0, code % 3 - 1.0
        shifts[code] = jnp.where(
            row == X, first, jnp.where(row == Y, second, jnp.where(row == Z, third, 0.0))
        )


def start_of(starts, cell, pair):
    place = cell * PAIR_ROWS + pair
    return starts[place >> 7, place & (LANES - 1)]


def fill_stream(stream, load, sources, starts, orders, cell):
    shape = (ROWS, LANES)
    lane = lanes_of(shape)
    pairs = sources.shape[1]
    moved = []
    for pair in range(pairs):
        order = jnp.broadcast_to(orders[pl.ds(cell * PAIR_ROWS + pair, 1), :], shape)
        moved.append(lane_gather(load(sources[cell, pair], pair), order))
    for pair in range(pairs):
        start = start_of(starts, cell, pair)
        block = start >> 7
        stream[block + 1] = moved[pair]
        pltpu.store(stream.at[block], moved[pair], mask=lane >= (start & (LANES - 1)))
    end = start_of(starts, cell, pairs)
    block = end >> 7
    stream[block] = jnp.where(lane < (end & (LANES - 1)), stream[block], 0.0)
    for extra in range(1, SPARE):
        stream[block + extra] = jnp.zeros(shape, jnp.float32)


def spread(values, field):
    return lane_gather(values, jnp.full(values.shape, field, jnp.int32))


def over_targets(active, one_chunk):
    groups = (active + ROWS - 1) // ROWS

    def large(chunk, carry):
        one_chunk(pl.multiple_of(chunk * 4 * ROWS, ROWS), 4)
        return carry

    lax.fori_loop(0, groups // 4, large, 0)
    for size in (2, 1):

        @pl.when((groups & size) != 0)
        def _(size=size):
            done = groups & -(2 * size)
            one_chunk(pl.multiple_of(done * ROWS, ROWS), size)


def density_kernel(
    per_peer, pair_source, pair_shift, export, actives,
    own, incoming, border, bundle, spreads,
    density, densities, outgoing, outgoing_border,
    table, shifts, sums, lines,
):
    fill_shifts(shifts)
    cells, peers = own.shape[0], incoming.shape[0]
    for place, near, _ in source_tiles(own, incoming, border, per_peer):
        table[place] = near()

    def one_cell(cell, carry):
        def one_chunk(base, groups):
            size = groups * ROWS
            at = pl.ds(base // ROWS, groups)
            *place, wide = [
                spreads[cell, at, which * ROWS : (which + 1) * ROWS, :].reshape(size, LANES)
                for which in range(len(SPREAD))
            ]
            smooth = 0.5 * wide

            total = jnp.zeros((size, LANES), jnp.float32)
            for pair in range(pair_source.shape[1]):
                source, code = pair_source[cell, pair], pair_shift[cell, pair]
                s = lambda field: table[source, field : field + 1, :]
                shift = lambda field: shifts[code, field : field + 1, :]
                apart = [place[c] - (s(c) + shift(c)) for c in range(3)]
                square = apart[0] * apart[0] + apart[1] * apart[1] + apart[2] * apart[2]
                radius = pl.reciprocal(lax.rsqrt(square), approx=True)
                outer = jnp.maximum(wide - radius, 0.0)
                inner = jnp.maximum(smooth - radius, 0.0)
                value = outer * outer * outer - 4.0 * (inner * inner * inner)
                total = total + s(MASS) * value
            sums[cell, pl.ds(base, size), 0:1] = jnp.sum(total, axis=1, keepdims=True)

        over_targets(actives[0, cell], one_chunk)
        return carry

    lax.fori_loop(0, cells, one_cell, 0)
    for cell in range(cells):
        lines[cell : cell + 1, :] = sums[cell].T[0:1, :]
    inverse = 2.0 / bundle[:, WIDE, :]
    inverse = inverse * inverse * inverse
    summed = lines[...] * (0.25 / math.pi) * (inverse * inverse)
    rank = bundle[:, S_RANK, :].astype(jnp.int32)
    density[...] = jnp.where(
        own_rows(own, ACTIVE) > 0.5, lane_gather(summed, rank), own_rows(own, DENS)
    )
    densities[0] = summed
    densities[1] = density[...]
    for peer in range(peers):
        for entry in range(per_peer):
            outgoing[peer, entry : entry + 1, :] = density[pl.ds(export[entry, peer], 1), :]
    outgoing_border[0:1, :] = density[cells - 1 : cells, :]
    outgoing_border[1:2, :] = density[0:1, :]


def stream_kernel(
    per_peer, pair_source, pair_shift, own, incoming, border, bundle, densities,
    near_streams, starts, orders, columns, last, traits,
    near_table, supports, shifts, squares, reaches, starts_row, sem,
):
    fill_shifts(shifts)
    cells, pairs = pair_source.shape
    tile_shape = (ROWS, LANES)
    row = lax.broadcasted_iota(jnp.int32, tile_shape, 0)
    lane = lanes_of(tile_shape).astype(jnp.float32)
    for place, near, sent in source_tiles(own, incoming, border, per_peer):
        tile, other = near(), sent()
        near_table[place] = tile
        wide, at = tile[WIDE : WIDE + 1, :], slice(place, place + 1)
        traits[0, at, :] = other[HEAT : HEAT + 1, :]
        traits[1, at, :] = wide
        supports[at, :] = jnp.where(lane[0:1, :] < other[LIVE : LIVE + 1, :], wide, -FAR_AWAY)

    def measure(cell, carry):
        low = bundle[cell, S_LOW : S_LOW + ROWS, :]
        high = bundle[cell, S_HIGH : S_HIGH + ROWS, :]
        for pair in range(pairs):
            source = pair_source[cell, pair]
            tile = near_table[source] + shifts[pair_shift[cell, pair]]
            away = jnp.maximum(jnp.maximum(low - tile, tile - high), 0.0)
            squares[cell, pair * ROWS : (pair + 1) * ROWS, :] = away * away
            place = pl.ds(cell * PAIR_ROWS + pair, 1)
            reaches[place, :] = supports[pl.ds(source, 1), :]
        return carry

    lax.fori_loop(0, cells, measure, 0, unroll=2)
    shape = (PAIR_ROWS, pairs * ROWS)
    adder = lax.broadcasted_iota(jnp.int32, shape, 0) == (lanes_of(shape) // ROWS)
    adder = jnp.where(adder, 1.0, 0.0).astype(jnp.bfloat16)
    pair_row = lax.broadcasted_iota(jnp.int32, (PAIR_ROWS, LANES), 0)
    flags = []
    for cell in range(cells):
        distance = jnp.dot(
            adder, squares[cell].astype(jnp.bfloat16), preferred_element_type=jnp.float32
        )
        support = reaches[cell * PAIR_ROWS : (cell + 1) * PAIR_ROWS, :]
        limit = jnp.maximum(support, bundle[cell, S_REACH : S_REACH + 1, :])
        keep = (distance < 1.02 * limit * limit) & (support > 0.0) & (pair_row < pairs)
        target = lane[0:1, :] < bundle[cell, S_CHOSEN : S_CHOSEN + 1, :]
        keep = keep | ((pair_row == pairs) & target)
        flags.append(jnp.where(keep, 1.0, 0.0))
    flags = jnp.concatenate(flags, axis=0).astype(jnp.bfloat16)
    rows = flags.shape[0]
    shape = (rows, rows)
    first, second = lax.broadcasted_iota(jnp.int32, shape, 0), lanes_of(shape)
    same = (first // PAIR_ROWS) == (second // PAIR_ROWS)
    earlier = jnp.where(same & (second < first), 1.0, 0.0).astype(jnp.bfloat16)
    later = jnp.where(same & (first < second), 1.0, 0.0).astype(jnp.bfloat16)
    dot = functools.partial(jnp.dot, preferred_element_type=jnp.float32)
    sums = lax.dot_general(
        jnp.ones((ROWS, LANES), jnp.bfloat16), flags, (((1,), (1,)), ((), ())),
        preferred_element_type=jnp.float32,
    )
    sums = dot(sums.astype(jnp.bfloat16), later)
    for line in range(starts_row.shape[0]):
        starts_row[line : line + 1, :] = sums[0:1, line * LANES : (line + 1) * LANES].astype(
            jnp.int32
        )
    copy = pltpu.make_async_copy(starts_row, starts, sem)
    copy.start()
    square = (LANES, LANES)
    upper = lax.broadcasted_iota(jnp.int32, square, 0) <= lanes_of(square)
    upper = jnp.where(upper, 1.0, 0.0).astype(jnp.bfloat16)
    seen = dot(flags, upper)
    begins = dot(earlier, dot(flags, jnp.ones(square, jnp.bfloat16)).astype(jnp.bfloat16))
    wanted = (lanes_of(seen.shape) - begins.astype(jnp.int32)) & (LANES - 1)
    wanted = wanted.astype(jnp.float32)
    slot = jnp.zeros(seen.shape, jnp.int32)
    step = LANES // 2
    while step:
        found = lane_gather(seen, slot + (step - 1))
        slot = jnp.where(found <= wanted, slot + step, slot)
        step //= 2
    orders[...] = slot
    heat, summed = bundle[:, S_HEAT, :], densities[0]
    fields = (jnp.sqrt(ADIABATIC * heat), 4.0 * summed)
    for cell in range(cells):
        tile = jnp.zeros(tile_shape, jnp.float32)
        for which, values in enumerate(fields):
            tile = jnp.where(row == which, values[cell : cell + 1, :], tile)
        columns[cell, :, 0 : 2 * ROWS] = jnp.concatenate([bundle[cell, 0:ROWS, :], tile], axis=0).T
    last[:, F_RANK, :] = bundle[:, S_RANK, :]
    last[:, F_ACTIVE, :] = own_rows(own, ACTIVE)
    last[:, F_STEP, :] = own_rows(own, STEP)
    for from_row, to_row in ((VX, F_VX), (VY, F_VY), (VZ, F_VZ)):
        last[:, to_row, :] = own[:, from_row, :] * (1.0 / SPEED)
    last[:, F_DENS, :] = densities[1]
    last[:, F_DENS + 1, :] = jnp.zeros((cells, LANES), jnp.float32)
    copy.wait()

    def one_cell(cell, carry):
        load = lambda source, pair: near_table[source] + shifts[pair_shift[cell, pair]]
        fill_stream(near_streams.at[cell], load, pair_source, starts, orders, cell)
        return carry

    lax.fori_loop(0, cells, one_cell, 0, unroll=2)


def force_kernel(
    per_peer, pair_source, starts,
    columns, orders, last, traits, new_density, new_border, near_streams,
    acceleration, kicked,
    table, densities, streams, sums, lines,
):
    cells, peers = last.shape[0], new_density.shape[0]
    pairs = pair_source.shape[1]
    for cell in range(cells):
        densities[cell : cell + 1, :] = last[cell, F_DENS : F_DENS + 1, :]
    for peer in range(peers):
        place = cells + peer * per_peer
        densities[place : place + per_peer, :] = new_density[peer]
    place = cells + peers * per_peer
    densities[place : place + 2, :] = new_border[...]
    heat, wide = traits[0], traits[1]
    inverse = 2.0 * pl.reciprocal(wide, approx=True)
    inverse = inverse * inverse * inverse
    table[:, DENS4, :] = 4.0 * densities[...]
    table[:, PRESS, :] = heat * pl.reciprocal(densities[...], approx=True)
    table[:, INV6, :] = inverse * inverse
    table[:, HALF, :] = 0.025 * wide
    table[:, SOUND, :] = jnp.sqrt(ADIABATIC * heat)

    def one_stream(cell, carry):
        fill_stream(
            streams.at[cell], lambda source, pair: table[source], pair_source, starts, orders, cell
        )
        return carry

    lax.fori_loop(0, cells, one_stream, 0, unroll=4)

    def one_cell(cell, carry):
        near, far = near_streams.at[cell], streams.at[cell]
        end = start_of(starts, cell, pairs)
        used = (end + LANES - 1) >> 7
        rounds = (used + FORCE_UNROLL - 1) // FORCE_UNROLL

        def one_chunk(base, groups):
            size = groups * ROWS
            mine = columns[cell, pl.ds(base, size), :]
            place = [spread(mine, field) for field in (X, Y, Z)]
            wide = spread(mine, WIDE)
            speed = [spread(mine, field) for field in (VX, VY, VZ)]
            sound, dens4 = [spread(mine, ROWS + field) for field in range(2)]
            inv6 = 2.0 * pl.reciprocal(wide, approx=True)
            inv6 = inv6 * inv6 * inv6
            inv6 = inv6 * inv6
            half_ = 0.025 * wide
            press = sound * sound * ((4.0 / ADIABATIC) * pl.reciprocal(dens4, approx=True))

            def blocks(index, totals):
                for sub in range(FORCE_UNROLL):
                    block = index * FORCE_UNROLL + sub
                    s = lambda field: near[block, field : field + 1, :]
                    o = lambda field: far[block, field : field + 1, :]
                    apart = [place[c] - s(c) for c in range(3)]
                    square = apart[0] * apart[0] + apart[1] * apart[1] + apart[2] * apart[2]
                    inverse = lax.rsqrt(jnp.maximum(square, 1e-24))
                    radius = pl.reciprocal(inverse, approx=True)
                    outer = jnp.maximum(wide - radius, 0.0)
                    least = jnp.minimum(outer, radius)
                    slope = inv6 * (least * ((outer + outer) - least))
                    outer = jnp.maximum(s(WIDE) - radius, 0.0)
                    least = jnp.minimum(outer, radius)
                    slope = slope + o(INV6) * (least * ((outer + outer) - least))
                    approach = (
                        (speed[0] - s(VX)) * apart[0]
                        + (speed[1] - s(VY)) * apart[1]
                        + (speed[2] - s(VZ)) * apart[2]
                    )
                    half = half_ + o(HALF)
                    slow = pl.reciprocal(square + half * half, approx=True)
                    mu = half * jnp.minimum(approach, 0.0) * slow
                    light = pl.reciprocal(dens4 + o(DENS4), approx=True)
                    viscous = mu * (mu - (sound + o(SOUND))) * light
                    weight = (press + o(PRESS) + viscous) * (slope * (inverse * s(MASS)))
                    terms = [weight * a for a in apart]
                    totals = terms if totals is None else [t + a for t, a in zip(totals, terms)]
                return tuple(totals)

            totals = lax.fori_loop(1, rounds, blocks, blocks(0, None))
            for c in range(3):
                sums[cell, pl.ds(base, size), c : c + 1] = jnp.sum(
                    totals[c], axis=1, keepdims=True
                )

        over_targets(start_of(starts, cell, pairs + 1) - end, one_chunk)
        return carry

    lax.fori_loop(0, cells, one_cell, 0)
    for cell in range(cells):
        turned = sums[cell].T
        for c in range(3):
            lines[c, cell : cell + 1, :] = turned[c : c + 1, :]
    rank = last[:, F_RANK, :].astype(jnp.int32)
    for c in range(3):
        gathered = lane_gather(lines[c] * (0.375 / math.pi), rank)
        value = jnp.where(last[:, F_ACTIVE, :] > 0.5, gathered, 0.0)
        acceleration[c] = value
        kicked[c] = last[:, F_VX + c, :] + value * last[:, F_STEP, :]


def shards(
    position, velocity, smoothing, particle_mass, energy, density_old, cell_count, active,
    time_bin, pair_source, pair_shift, export,
):
    cells, capacity = smoothing.shape
    peers, per_peer = export.shape
    sources = cells + peers * per_peer + 2
    codes = 27
    f32 = lambda *shape: jax.ShapeDtypeStruct(shape, jnp.float32)
    smem = pl.BlockSpec(memory_space=pltpu.SMEM)
    vmem = pl.BlockSpec(memory_space=pltpu.VMEM)
    hbm = pl.BlockSpec(memory_space=pltpu.HBM)
    whole = pltpu.CompilerParams(vmem_limit_bytes=64 * 2**20)
    params = pltpu.CompilerParams(vmem_limit_bytes=24 * 2**20)
    cost = pl.CostEstimate(flops=10**9, bytes_accessed=1000, transcendentals=0)
    i32 = lambda *shape: jax.ShapeDtypeStruct(shape, jnp.int32)
    sent_rows = per_peer * (ROWS + SENT)
    turned = export.T

    def landing(scalars, *arrays):
        return (
            [pltpu.SMEM(a.shape, a.dtype) for a in arrays[:scalars]]
            + [pltpu.VMEM(a.shape, a.dtype) for a in arrays[scalars:]]
            + [pltpu.SemaphoreType.DMA((len(arrays),))]
        )

    arrays = (
        cell_count, turned, position, velocity, smoothing, particle_mass, energy, density_old,
        active, time_bin,
    )
    own, outgoing, border = pl.pallas_call(
        pack_kernel,
        out_shape=(
            f32(cells, 2 * ROWS, capacity),
            f32(peers, sent_rows, capacity),
            f32(2, ROWS + SENT, capacity),
        ),
        in_specs=[hbm] * 10,
        out_specs=(vmem,) * 3,
        scratch_shapes=landing(2, *arrays),
        compiler_params=whole,
        cost_estimate=cost,
        name="pack",
    )(*arrays)

    def exchange(pieces):
        return lax.all_to_all(pieces, "cell", split_axis=0, concat_axis=0, tiled=True)

    def swap_border(pieces):
        size = lax.axis_size("region")
        up = [(i, (i + 1) % size) for i in range(size)]
        down = [(j, i) for i, j in up]
        if size == 2:
            return lax.ppermute(pieces, "region", up)
        before = lax.ppermute(pieces[0:1], "region", up)
        after = lax.ppermute(pieces[1:2], "region", down)
        return jnp.concatenate([before, after], axis=0)

    incoming = exchange(outgoing)
    other = swap_border(border)
    actives, bundle, spreads = pl.pallas_call(
        sort_kernel,
        out_shape=(
            i32(1, cells),
            f32(cells, S_ROWS, capacity),
            f32(cells, capacity // ROWS, len(SPREAD) * ROWS, capacity),
        ),
        in_specs=[vmem],
        out_specs=(smem, vmem, vmem),
        scratch_shapes=[pltpu.VMEM((cells, capacity, LANES), jnp.float32)],
        compiler_params=params,
        cost_estimate=cost,
        name="sort",
    )(own)

    density, densities, outgoing_density, border_density = pl.pallas_call(
        functools.partial(density_kernel, per_peer),
        out_shape=(
            f32(cells, capacity),
            f32(2, cells, capacity),
            f32(peers, per_peer, capacity),
            f32(2, capacity),
        ),
        in_specs=[smem] * 4 + [vmem] * 5,
        out_specs=(vmem,) * 4,
        scratch_shapes=[
            pltpu.VMEM((sources, ROWS, capacity), jnp.float32),
            pltpu.VMEM((codes, ROWS, capacity), jnp.float32),
            pltpu.VMEM((cells, capacity, ROWS), jnp.float32),
            pltpu.VMEM((cells, capacity), jnp.float32),
        ],
        compiler_params=params,
        cost_estimate=cost,
        name="density",
    )(pair_source, pair_shift, turned, actives, own, incoming, other, bundle, spreads)

    new_density = exchange(outgoing_density)
    new_border = swap_border(border_density)
    pairs = pair_source.shape[1]
    blocks = pairs + SPARE
    pair_rows = cells * PAIR_ROWS
    source_rows = -(-sources // ROWS) * ROWS
    near_streams, starts, orders, columns, last, traits = pl.pallas_call(
        functools.partial(stream_kernel, per_peer),
        out_shape=(
            f32(cells, blocks, ROWS, capacity),
            i32(pair_rows // capacity, capacity),
            i32(pair_rows, capacity),
            f32(cells, capacity, LANES),
            f32(cells, ROWS, capacity),
            f32(2, source_rows, capacity),
        ),
        in_specs=[smem] * 2 + [vmem] * 5,
        out_specs=(vmem, smem, vmem, vmem, vmem, vmem),
        scratch_shapes=[
            pltpu.VMEM((sources, ROWS, capacity), jnp.float32),
            pltpu.VMEM((source_rows, capacity), jnp.float32),
            pltpu.VMEM((codes, ROWS, capacity), jnp.float32),
            pltpu.VMEM((cells, pairs * ROWS, capacity), jnp.float32),
            pltpu.VMEM((pair_rows, capacity), jnp.float32),
            pltpu.VMEM((pair_rows // capacity, capacity), jnp.int32),
            pltpu.SemaphoreType.DMA,
        ],
        compiler_params=params,
        cost_estimate=cost,
        name="streams",
    )(pair_source, pair_shift, own, incoming, other, bundle, densities)

    acceleration, kicked = pl.pallas_call(
        functools.partial(force_kernel, per_peer),
        out_shape=(f32(3, cells, capacity), f32(3, cells, capacity)),
        in_specs=[smem] * 2 + [vmem] * 7,
        out_specs=(vmem,) * 2,
        scratch_shapes=[
            pltpu.VMEM((source_rows, ROWS, capacity), jnp.float32),
            pltpu.VMEM((source_rows, capacity), jnp.float32),
            pltpu.VMEM((cells, blocks, ROWS, capacity), jnp.float32),
            pltpu.VMEM((cells, capacity, ROWS), jnp.float32),
            pltpu.VMEM((3, cells, capacity), jnp.float32),
        ],
        compiler_params=params,
        cost_estimate=cost,
        name="force",
    )(
        pair_source, starts, columns, orders, last, traits, new_density, new_border, near_streams,
    )
    return density, acceleration, kicked


def solution(mesh):
    rows = P(("region", "cell"), None)
    planes = P(None, ("region", "cell"), None)
    return jax.shard_map(
        shards,
        mesh=mesh,
        in_specs=(
            planes, planes, rows, rows, rows, rows, P(("region", "cell")), rows, rows, rows, rows,
            rows,
        ),
        out_specs=(rows, planes, planes),
        check_vma=False,
    )
```

```python
import functools
import math

import jax
import jax.numpy as jnp
from jax import lax
from jax.experimental import pallas as pl
from jax.experimental.pallas import tpu as pltpu
from jax.sharding import PartitionSpec as P

ADIABATIC = 5.0 / 3.0
STEP_MAX = 0.2
LANES = 128
ROWS = 8
FORCE_UNROLL = 7
PAIR_ROWS = 32
FAR_AWAY = 1e9
SPARE = FORCE_UNROLL

X, Y, Z, MASS, VX, VY, VZ, WIDE = range(ROWS)
SPREAD = (X, Y, Z, WIDE)
HEAT, DENS, LIVE = range(3)
SENT = 4
SPEED = 40.0
ACTIVE, STEP = SENT, SENT + 1
S_HEAT, S_RANK, S_REACH, S_CHOSEN = range(ROWS, ROWS + 4)
S_LOW, S_HIGH, S_ROWS = 2 * ROWS, 3 * ROWS, 4 * ROWS
F_RANK, F_ACTIVE, F_STEP, F_VX, F_VY, F_VZ, F_DENS = range(7)
DENS4, PRESS, INV6, HALF, SOUND = range(5)


def lane_gather(values, index):
    return jnp.take_along_axis(values, index, axis=1, mode="promise_in_bounds")


def lanes_of(shape):
    return lax.broadcasted_iota(jnp.int32, shape, len(shape) - 1)


def start_copies(arrays, landed, sem):
    copies = [
        pltpu.make_async_copy(array, place, sem.at[index])
        for index, (array, place) in enumerate(zip(arrays, landed))
    ]
    for copy in copies:
        copy.start()
    return copies


def pack_kernel(*refs):
    arrays, (own, outgoing, border) = refs[:10], refs[10:13]
    landed, sem = refs[13:-1], refs[-1]
    for copy in start_copies(arrays, landed, sem):
        copy.wait()
    count, export, position, velocity, smoothing, mass, energy, density_old, active, time_bin = landed
    cells = smoothing.shape[0]
    shape = smoothing.shape
    lane = lanes_of(shape)
    row = lax.broadcasted_iota(jnp.int32, shape, 0)
    counts = jnp.zeros(shape, jnp.int32)
    for cell in range(cells):
        counts = jnp.where(row == cell, count[cell], counts)
    mass_live = jnp.where(lane < counts, mass[...], 0.0)
    zeros = jnp.zeros(shape, jnp.float32)
    rows = (
        position[0], position[1], position[2], mass_live,
        SPEED * velocity[0], SPEED * velocity[1], SPEED * velocity[2], 2.0 * smoothing[...],
        (ADIABATIC - 1.0) * energy[...], density_old[...], counts.astype(jnp.float32), zeros,
        jnp.where(active[...] > 0, 1.0, 0.0),
        STEP_MAX * jnp.exp2(-time_bin[...].astype(jnp.float32)), zeros, zeros,
    )
    for field, values in enumerate(rows):
        own[:, field, :] = values
    per_peer, peers = export.shape
    for peer in range(peers):
        for entry in range(per_peer):
            cell = export[entry, peer]
            outgoing[peer, entry * ROWS : (entry + 1) * ROWS, :] = own[cell, 0:ROWS, :]
            start = per_peer * ROWS + entry * SENT
            outgoing[peer, start : start + SENT, :] = own[cell, ROWS : ROWS + SENT, :]
    for side, cell in enumerate((cells - 1, 0)):
        border[side] = own[cell, 0 : ROWS + SENT, :]


def own_rows(own, field):
    return own[:, ROWS + field, :]


def sort_kernel(own, actives, bundle, spreads, columns):
    cells = own.shape[0]
    shape = (cells, LANES)
    lane = lanes_of(shape)
    ones = own_rows(own, ACTIVE)
    is_active = ones > 0.5
    for cell in range(cells):
        actives[0, cell] = jnp.sum(ones[cell : cell + 1, :]).astype(jnp.int32)
    square = (LANES, LANES)
    upper = lax.broadcasted_iota(jnp.int32, square, 0) <= lanes_of(square)
    upper = jnp.where(upper, 1.0, 0.0).astype(jnp.bfloat16)
    seen = jnp.dot(ones.astype(jnp.bfloat16), upper, preferred_element_type=jnp.float32)
    seen = seen.astype(jnp.int32)
    chosen = lane_gather(seen, jnp.full(shape, LANES - 1, jnp.int32))
    others = lane + 1 - seen
    rank = jnp.where(is_active, seen - 1, chosen + others - 1)
    first_part = lane < chosen
    wanted = jnp.where(first_part, lane, lane - chosen)
    slot = jnp.zeros(shape, jnp.int32)
    step = LANES // 2
    while step:
        probe = slot + (step - 1)
        found = jnp.where(first_part, lane_gather(seen, probe), lane_gather(others, probe))
        slot = jnp.where(found <= wanted, slot + step, slot)
        step //= 2
    bundle[:, S_HEAT, :] = lane_gather(own_rows(own, HEAT), slot)
    bundle[:, S_RANK, :] = rank.astype(jnp.float32)
    bundle[:, S_CHOSEN, :] = chosen.astype(jnp.float32)
    for spare in range(S_CHOSEN + 1, S_LOW):
        bundle[:, spare, :] = jnp.zeros(shape, jnp.float32)
    place = lax.broadcasted_iota(jnp.int32, (ROWS, LANES), 0) <= Z
    for cell in range(cells):
        order = jnp.broadcast_to(slot[cell : cell + 1, :], (ROWS, LANES))
        tile = lane_gather(own[cell, 0:ROWS, :], order)
        bundle[cell, 0:ROWS, :] = tile
        target = lane < chosen[cell : cell + 1, :]
        low = jnp.min(jnp.where(target, tile, FAR_AWAY), axis=1, keepdims=True)
        high = jnp.max(jnp.where(target, tile, -FAR_AWAY), axis=1, keepdims=True)
        bundle[cell, S_LOW : S_LOW + ROWS, :] = jnp.where(place, low, -FAR_AWAY)
        bundle[cell, S_HIGH : S_HIGH + ROWS, :] = jnp.where(place, high, FAR_AWAY)
        bundle[cell, S_REACH : S_REACH + 1, :] = jnp.broadcast_to(high[WIDE : WIDE + 1, :], (1, LANES))
        columns[cell, :, 0:ROWS] = tile.T

    def one_cell(cell, carry):
        def one_pair(pair, carry):
            base = pl.multiple_of(pair * 2 * ROWS, 2 * ROWS)
            mine = columns[cell, pl.ds(base, 2 * ROWS), :]
            for which, field in enumerate(SPREAD):
                tiles = spread(mine, field).reshape(2, ROWS, LANES)
                spreads[cell, pl.ds(pair * 2, 2), which * ROWS : (which + 1) * ROWS, :] = tiles
            return carry

        return lax.fori_loop(0, (actives[0, cell] + 2 * ROWS - 1) // (2 * ROWS), one_pair, carry)

    lax.fori_loop(0, cells, one_cell, 0)


def source_tiles(own, incoming, border, per_peer):
    cells, peers = own.shape[0], incoming.shape[0]
    for cell in range(cells):
        yield (
            cell, lambda c=cell: own[c, 0:ROWS, :], lambda c=cell: own[c, ROWS : ROWS + SENT, :]
        )
    for peer in range(peers):
        for entry in range(per_peer):
            near, sent = entry * ROWS, per_peer * ROWS + entry * SENT
            yield (
                cells + peer * per_peer + entry,
                lambda p=peer, n=near: incoming[p, n : n + ROWS, :],
                lambda p=peer, n=sent: incoming[p, n : n + SENT, :],
            )
    for side in range(2):
        yield (
            cells + peers * per_peer + side,
            lambda b=side: border[b, 0:ROWS, :],
            lambda b=side: border[b, ROWS : ROWS + SENT, :],
        )


def fill_shifts(shifts):
    row = lax.broadcasted_iota(jnp.int32, (ROWS, LANES), 0)
    for code in range(shifts.shape[0]):
        first, second, third = code // 9 - 1.0, code // 3 % 3 - 1.0, code % 3 - 1.0
        shifts[code] = jnp.where(
            row == X, first, jnp.where(row == Y, second, jnp.where(row == Z, third, 0.0))
        )


def start_of(starts, cell, pair):
    per_line = LANES // PAIR_ROWS
    return starts[cell // per_line, (cell % per_line) * PAIR_ROWS + pair]


def fill_stream(stream, load, sources, starts, orders, cell):
    shape = (ROWS, LANES)
    lane = lanes_of(shape)
    pairs = sources.shape[1]
    moved = []
    for pair in range(pairs):
        order = jnp.broadcast_to(orders[pl.ds(cell * PAIR_ROWS + pair, 1), :], shape)
        moved.append(lane_gather(load(sources[cell, pair], pair), order))
    for pair in range(pairs):
        start = start_of(starts, cell, pair)
        block = start >> 7
        stream[block + 1] = moved[pair]
        pltpu.store(stream.at[block], moved[pair], mask=lane >= (start & (LANES - 1)))
    end = start_of(starts, cell, pairs)
    block = end >> 7
    stream[block] = jnp.where(lane < (end & (LANES - 1)), stream[block], 0.0)
    for extra in range(1, SPARE):
        stream[block + extra] = jnp.zeros(shape, jnp.float32)


def spread(values, field):
    return lane_gather(values, jnp.full(values.shape, field, jnp.int32))


def over_targets(active, one_chunk):
    groups = (active + ROWS - 1) // ROWS
    large = jnp.maximum(groups - 2, 0) // 4
    rest = groups - 4 * large
    large = jnp.where(rest == 4, large + 1, large)

    def large_chunk(chunk, carry):
        one_chunk(pl.multiple_of(chunk * 4 * ROWS, ROWS), 4)
        return carry

    lax.fori_loop(0, large, large_chunk, 0)
    for size in (1, 2, 3, 5):

        @pl.when(rest == size)
        def _(size=size):
            one_chunk(pl.multiple_of(large * 4 * ROWS, ROWS), size)


def density_kernel(
    per_peer, pair_source, pair_shift, export, actives,
    own, incoming, border, bundle, spreads,
    density, densities, outgoing, outgoing_border,
    table, shifts, sums, lines,
):
    fill_shifts(shifts)
    cells, peers = own.shape[0], incoming.shape[0]
    for place, near, _ in source_tiles(own, incoming, border, per_peer):
        table[place] = near()

    def one_cell(cell, carry):
        def one_chunk(base, groups):
            size = groups * ROWS
            at = pl.ds(base // ROWS, groups)
            *place, wide = [
                spreads[cell, at, which * ROWS : (which + 1) * ROWS, :].reshape(size, LANES)
                for which in range(len(SPREAD))
            ]
            smooth = 0.5 * wide

            total = jnp.zeros((size, LANES), jnp.float32)
            for pair in range(pair_source.shape[1]):
                source, code = pair_source[cell, pair], pair_shift[cell, pair]
                s = lambda field: table[source, field : field + 1, :]
                shift = lambda field: shifts[code, field : field + 1, :]
                apart = [place[c] - (s(c) + shift(c)) for c in range(3)]
                square = apart[0] * apart[0] + apart[1] * apart[1] + apart[2] * apart[2]
                radius = pl.reciprocal(lax.rsqrt(square), approx=True)
                outer = jnp.maximum(wide - radius, 0.0)
                inner = jnp.maximum(smooth - radius, 0.0)
                value = outer * outer * outer - 4.0 * (inner * inner * inner)
                total = total + s(MASS) * value
            sums[cell, pl.ds(base, size), 0:1] = jnp.sum(total, axis=1, keepdims=True)

        over_targets(actives[0, cell], one_chunk)
        return carry

    lax.fori_loop(0, cells, one_cell, 0)
    for cell in range(cells):
        lines[cell : cell + 1, :] = sums[cell].T[0:1, :]
    inverse = 2.0 / bundle[:, WIDE, :]
    inverse = inverse * inverse * inverse
    summed = lines[...] * (0.25 / math.pi) * (inverse * inverse)
    rank = bundle[:, S_RANK, :].astype(jnp.int32)
    density[...] = jnp.where(
        own_rows(own, ACTIVE) > 0.5, lane_gather(summed, rank), own_rows(own, DENS)
    )
    densities[0] = summed
    densities[1] = density[...]
    for peer in range(peers):
        for entry in range(per_peer):
            outgoing[peer, entry : entry + 1, :] = density[pl.ds(export[entry, peer], 1), :]
    outgoing_border[0:1, :] = density[cells - 1 : cells, :]
    outgoing_border[1:2, :] = density[0:1, :]


def stream_kernel(
    per_peer, pair_source, pair_shift, own, incoming, border, bundle, densities,
    near_streams, starts, orders, columns, last, traits,
    near_table, supports, shifts, squares, reaches, starts_row, sem,
):
    fill_shifts(shifts)
    cells, pairs = pair_source.shape
    tile_shape = (ROWS, LANES)
    row = lax.broadcasted_iota(jnp.int32, tile_shape, 0)
    lane = lanes_of(tile_shape).astype(jnp.float32)
    for place, near, sent in source_tiles(own, incoming, border, per_peer):
        tile, other = near(), sent()
        near_table[place] = tile
        wide, at = tile[WIDE : WIDE + 1, :], slice(place, place + 1)
        traits[0, at, :] = other[HEAT : HEAT + 1, :]
        traits[1, at, :] = wide
        supports[at, :] = jnp.where(lane[0:1, :] < other[LIVE : LIVE + 1, :], wide, -FAR_AWAY)

    def measure(cell, carry):
        low = bundle[cell, S_LOW : S_LOW + ROWS, :]
        high = bundle[cell, S_HIGH : S_HIGH + ROWS, :]
        for pair in range(pairs):
            source = pair_source[cell, pair]
            tile = near_table[source] + shifts[pair_shift[cell, pair]]
            away = jnp.maximum(jnp.maximum(low - tile, tile - high), 0.0)
            squares[cell, pair * ROWS : (pair + 1) * ROWS, :] = away * away
            place = pl.ds(cell * PAIR_ROWS + pair, 1)
            reaches[place, :] = supports[pl.ds(source, 1), :]
        return carry

    lax.fori_loop(0, cells, measure, 0, unroll=2)
    shape = (PAIR_ROWS, pairs * ROWS)
    adder = lax.broadcasted_iota(jnp.int32, shape, 0) == (lanes_of(shape) // ROWS)
    adder = jnp.where(adder, 1.0, 0.0).astype(jnp.bfloat16)
    pair_row = lax.broadcasted_iota(jnp.int32, (PAIR_ROWS, LANES), 0)
    flags = []
    for cell in range(cells):
        distance = jnp.dot(
            adder, squares[cell].astype(jnp.bfloat16), preferred_element_type=jnp.float32
        )
        support = reaches[cell * PAIR_ROWS : (cell + 1) * PAIR_ROWS, :]
        limit = jnp.maximum(support, bundle[cell, S_REACH : S_REACH + 1, :])
        keep = (distance < 1.005 * limit * limit) & (support > 0.0) & (pair_row < pairs)
        target = lane[0:1, :] < bundle[cell, S_CHOSEN : S_CHOSEN + 1, :]
        keep = keep | ((pair_row == pairs) & target)
        flags.append(jnp.where(keep, 1.0, 0.0))
    flags = jnp.concatenate(flags, axis=0).astype(jnp.bfloat16)
    rows = flags.shape[0]
    shape = (rows, rows)
    first, second = lax.broadcasted_iota(jnp.int32, shape, 0), lanes_of(shape)
    same = (first // PAIR_ROWS) == (second // PAIR_ROWS)
    earlier = jnp.where(same & (second < first), 1.0, 0.0).astype(jnp.bfloat16)
    later = jnp.where(same & (first < second), 1.0, 0.0).astype(jnp.bfloat16)
    dot = functools.partial(jnp.dot, preferred_element_type=jnp.float32)
    sums = lax.dot_general(
        jnp.ones((ROWS, LANES), jnp.bfloat16), flags, (((1,), (1,)), ((), ())),
        preferred_element_type=jnp.float32,
    )
    sums = dot(sums.astype(jnp.bfloat16), later)
    for line in range(starts_row.shape[0]):
        starts_row[line : line + 1, :] = sums[0:1, line * LANES : (line + 1) * LANES].astype(
            jnp.int32
        )
    copy = pltpu.make_async_copy(starts_row, starts, sem)
    copy.start()
    square = (LANES, LANES)
    upper = lax.broadcasted_iota(jnp.int32, square, 0) <= lanes_of(square)
    upper = jnp.where(upper, 1.0, 0.0).astype(jnp.bfloat16)
    seen = dot(flags, upper)
    begins = dot(earlier, dot(flags, jnp.ones(square, jnp.bfloat16)).astype(jnp.bfloat16))
    wanted = (lanes_of(seen.shape) - begins.astype(jnp.int32)) & (LANES - 1)
    wanted = wanted.astype(jnp.float32)
    slot = jnp.zeros(seen.shape, jnp.int32)
    step = LANES // 2
    while step:
        found = lane_gather(seen, slot + (step - 1))
        slot = jnp.where(found <= wanted, slot + step, slot)
        step //= 2
    orders[...] = slot
    heat, summed = bundle[:, S_HEAT, :], densities[0]
    fields = (jnp.sqrt(ADIABATIC * heat), 4.0 * summed)
    for cell in range(cells):
        tile = jnp.zeros(tile_shape, jnp.float32)
        for which, values in enumerate(fields):
            tile = jnp.where(row == which, values[cell : cell + 1, :], tile)
        columns[cell, :, 0 : 2 * ROWS] = jnp.concatenate([bundle[cell, 0:ROWS, :], tile], axis=0).T
    last[:, F_RANK, :] = bundle[:, S_RANK, :]
    last[:, F_ACTIVE, :] = own_rows(own, ACTIVE)
    last[:, F_STEP, :] = own_rows(own, STEP)
    for from_row, to_row in ((VX, F_VX), (VY, F_VY), (VZ, F_VZ)):
        last[:, to_row, :] = own[:, from_row, :] * (1.0 / SPEED)
    last[:, F_DENS, :] = densities[1]
    last[:, F_DENS + 1, :] = jnp.zeros((cells, LANES), jnp.float32)
    copy.wait()

    def one_cell(cell, carry):
        load = lambda source, pair: near_table[source] + shifts[pair_shift[cell, pair]]
        fill_stream(near_streams.at[cell], load, pair_source, starts, orders, cell)
        return carry

    lax.fori_loop(0, cells, one_cell, 0, unroll=2)


def force_kernel(
    per_peer, pair_source, starts,
    columns, orders, last, traits, new_density, new_border, near_streams,
    acceleration, kicked,
    table, densities, streams, sums, lines,
):
    cells, peers = last.shape[0], new_density.shape[0]
    pairs = pair_source.shape[1]
    for cell in range(cells):
        densities[cell : cell + 1, :] = last[cell, F_DENS : F_DENS + 1, :]
    for peer in range(peers):
        place = cells + peer * per_peer
        densities[place : place + per_peer, :] = new_density[peer]
    place = cells + peers * per_peer
    densities[place : place + 2, :] = new_border[...]
    heat, wide = traits[0], traits[1]
    inverse = 2.0 * pl.reciprocal(wide, approx=True)
    inverse = inverse * inverse * inverse
    table[:, DENS4, :] = 4.0 * densities[...]
    table[:, PRESS, :] = heat * pl.reciprocal(densities[...], approx=True)
    table[:, INV6, :] = inverse * inverse
    table[:, HALF, :] = 0.025 * wide
    table[:, SOUND, :] = jnp.sqrt(ADIABATIC * heat)

    def one_stream(cell, carry):
        fill_stream(
            streams.at[cell], lambda source, pair: table[source], pair_source, starts, orders, cell
        )
        return carry

    lax.fori_loop(0, cells, one_stream, 0, unroll=4)

    def one_cell(cell, carry):
        near, far = near_streams.at[cell], streams.at[cell]
        end = start_of(starts, cell, pairs)
        used = (end + LANES - 1) >> 7
        rounds = (used + FORCE_UNROLL - 1) // FORCE_UNROLL

        def one_chunk(base, groups):
            size = groups * ROWS
            mine = columns[cell, pl.ds(base, size), :]
            place = [spread(mine, field) for field in (X, Y, Z)]
            wide = spread(mine, WIDE)
            speed = [spread(mine, field) for field in (VX, VY, VZ)]
            sound, dens4 = [spread(mine, ROWS + field) for field in range(2)]
            inv6 = 2.0 * pl.reciprocal(wide, approx=True)
            inv6 = inv6 * inv6 * inv6
            inv6 = inv6 * inv6
            half_ = 0.025 * wide
            press = sound * sound * ((4.0 / ADIABATIC) * pl.reciprocal(dens4, approx=True))

            def blocks(index, totals):
                for sub in range(FORCE_UNROLL):
                    block = index * FORCE_UNROLL + sub
                    s = lambda field: near[block, field : field + 1, :]
                    o = lambda field: far[block, field : field + 1, :]
                    apart = [place[c] - s(c) for c in range(3)]
                    square = apart[0] * apart[0] + apart[1] * apart[1] + apart[2] * apart[2]
                    inverse = lax.rsqrt(jnp.maximum(square, 1e-24))
                    radius = pl.reciprocal(inverse, approx=True)
                    outer = jnp.maximum(wide - radius, 0.0)
                    least = jnp.minimum(outer, radius)
                    slope = inv6 * (least * ((outer + outer) - least))
                    outer = jnp.maximum(s(WIDE) - radius, 0.0)
                    least = jnp.minimum(outer, radius)
                    slope = slope + o(INV6) * (least * ((outer + outer) - least))
                    approach = (
                        (speed[0] - s(VX)) * apart[0]
                        + (speed[1] - s(VY)) * apart[1]
                        + (speed[2] - s(VZ)) * apart[2]
                    )
                    half = half_ + o(HALF)
                    slow = pl.reciprocal(square + half * half, approx=True)
                    mu = half * jnp.minimum(approach, 0.0) * slow
                    light = pl.reciprocal(dens4 + o(DENS4), approx=True)
                    viscous = mu * (mu - (sound + o(SOUND))) * light
                    weight = (press + o(PRESS) + viscous) * (slope * (inverse * s(MASS)))
                    terms = [weight * a for a in apart]
                    totals = terms if totals is None else [t + a for t, a in zip(totals, terms)]
                return tuple(totals)

            totals = lax.fori_loop(1, rounds, blocks, blocks(0, None))
            for c in range(3):
                sums[cell, pl.ds(base, size), c : c + 1] = jnp.sum(
                    totals[c], axis=1, keepdims=True
                )

        over_targets(start_of(starts, cell, pairs + 1) - end, one_chunk)
        return carry

    lax.fori_loop(0, cells, one_cell, 0)
    for cell in range(cells):
        turned = sums[cell].T
        for c in range(3):
            lines[c, cell : cell + 1, :] = turned[c : c + 1, :]
    rank = last[:, F_RANK, :].astype(jnp.int32)
    for c in range(3):
        gathered = lane_gather(lines[c] * (0.375 / math.pi), rank)
        value = jnp.where(last[:, F_ACTIVE, :] > 0.5, gathered, 0.0)
        acceleration[c] = value
        kicked[c] = last[:, F_VX + c, :] + value * last[:, F_STEP, :]


def shards(
    position, velocity, smoothing, particle_mass, energy, density_old, cell_count, active,
    time_bin, pair_source, pair_shift, export,
):
    cells, capacity = smoothing.shape
    peers, per_peer = export.shape
    sources = cells + peers * per_peer + 2
    codes = 27
    f32 = lambda *shape: jax.ShapeDtypeStruct(shape, jnp.float32)
    smem = pl.BlockSpec(memory_space=pltpu.SMEM)
    vmem = pl.BlockSpec(memory_space=pltpu.VMEM)
    hbm = pl.BlockSpec(memory_space=pltpu.HBM)
    whole = pltpu.CompilerParams(vmem_limit_bytes=64 * 2**20)
    params = pltpu.CompilerParams(vmem_limit_bytes=24 * 2**20)
    cost = pl.CostEstimate(flops=10**9, bytes_accessed=1000, transcendentals=0)
    i32 = lambda *shape: jax.ShapeDtypeStruct(shape, jnp.int32)
    sent_rows = per_peer * (ROWS + SENT)
    turned = export.T

    def landing(scalars, *arrays):
        return (
            [pltpu.SMEM(a.shape, a.dtype) for a in arrays[:scalars]]
            + [pltpu.VMEM(a.shape, a.dtype) for a in arrays[scalars:]]
            + [pltpu.SemaphoreType.DMA((len(arrays),))]
        )

    arrays = (
        cell_count, turned, position, velocity, smoothing, particle_mass, energy, density_old,
        active, time_bin,
    )
    own, outgoing, border = pl.pallas_call(
        pack_kernel,
        out_shape=(
            f32(cells, 2 * ROWS, capacity),
            f32(peers, sent_rows, capacity),
            f32(2, ROWS + SENT, capacity),
        ),
        in_specs=[hbm] * 10,
        out_specs=(vmem,) * 3,
        scratch_shapes=landing(2, *arrays),
        compiler_params=whole,
        cost_estimate=cost,
        name="pack",
    )(*arrays)

    def exchange(pieces):
        return lax.all_to_all(pieces, "cell", split_axis=0, concat_axis=0, tiled=True)

    def swap_border(pieces):
        size = lax.axis_size("region")
        up = [(i, (i + 1) % size) for i in range(size)]
        down = [(j, i) for i, j in up]
        if size == 2:
            return lax.ppermute(pieces, "region", up)
        before = lax.ppermute(pieces[0:1], "region", up)
        after = lax.ppermute(pieces[1:2], "region", down)
        return jnp.concatenate([before, after], axis=0)

    incoming = exchange(outgoing)
    other = swap_border(border)
    actives, bundle, spreads = pl.pallas_call(
        sort_kernel,
        out_shape=(
            i32(1, cells),
            f32(cells, S_ROWS, capacity),
            f32(cells, capacity // ROWS, len(SPREAD) * ROWS, capacity),
        ),
        in_specs=[vmem],
        out_specs=(smem, vmem, vmem),
        scratch_shapes=[pltpu.VMEM((cells, capacity, LANES), jnp.float32)],
        compiler_params=params,
        cost_estimate=cost,
        name="sort",
    )(own)

    density, densities, outgoing_density, border_density = pl.pallas_call(
        functools.partial(density_kernel, per_peer),
        out_shape=(
            f32(cells, capacity),
            f32(2, cells, capacity),
            f32(peers, per_peer, capacity),
            f32(2, capacity),
        ),
        in_specs=[smem] * 4 + [vmem] * 5,
        out_specs=(vmem,) * 4,
        scratch_shapes=[
            pltpu.VMEM((sources, ROWS, capacity), jnp.float32),
            pltpu.VMEM((codes, ROWS, capacity), jnp.float32),
            pltpu.VMEM((cells, capacity, ROWS), jnp.float32),
            pltpu.VMEM((cells, capacity), jnp.float32),
        ],
        compiler_params=params,
        cost_estimate=cost,
        name="density",
    )(pair_source, pair_shift, turned, actives, own, incoming, other, bundle, spreads)

    new_density = exchange(outgoing_density)
    new_border = swap_border(border_density)
    pairs = pair_source.shape[1]
    blocks = pairs + SPARE
    pair_rows = cells * PAIR_ROWS
    source_rows = -(-sources // ROWS) * ROWS
    near_streams, starts, orders, columns, last, traits = pl.pallas_call(
        functools.partial(stream_kernel, per_peer),
        out_shape=(
            f32(cells, blocks, ROWS, capacity),
            i32(pair_rows // capacity, capacity),
            i32(pair_rows, capacity),
            f32(cells, capacity, LANES),
            f32(cells, ROWS, capacity),
            f32(2, source_rows, capacity),
        ),
        in_specs=[smem] * 2 + [vmem] * 5,
        out_specs=(vmem, smem, vmem, vmem, vmem, vmem),
        scratch_shapes=[
            pltpu.VMEM((sources, ROWS, capacity), jnp.float32),
            pltpu.VMEM((source_rows, capacity), jnp.float32),
            pltpu.VMEM((codes, ROWS, capacity), jnp.float32),
            pltpu.VMEM((cells, pairs * ROWS, capacity), jnp.float32),
            pltpu.VMEM((pair_rows, capacity), jnp.float32),
            pltpu.VMEM((pair_rows // capacity, capacity), jnp.int32),
            pltpu.SemaphoreType.DMA,
        ],
        compiler_params=params,
        cost_estimate=cost,
        name="streams",
    )(pair_source, pair_shift, own, incoming, other, bundle, densities)

    acceleration, kicked = pl.pallas_call(
        functools.partial(force_kernel, per_peer),
        out_shape=(f32(3, cells, capacity), f32(3, cells, capacity)),
        in_specs=[smem] * 2 + [vmem] * 7,
        out_specs=(vmem,) * 2,
        scratch_shapes=[
            pltpu.VMEM((source_rows, ROWS, capacity), jnp.float32),
            pltpu.VMEM((source_rows, capacity), jnp.float32),
            pltpu.VMEM((cells, blocks, ROWS, capacity), jnp.float32),
            pltpu.VMEM((cells, capacity, ROWS), jnp.float32),
            pltpu.VMEM((3, cells, capacity), jnp.float32),
        ],
        compiler_params=params,
        cost_estimate=cost,
        name="force",
    )(
        pair_source, starts, columns, orders, last, traits, new_density, new_border, near_streams,
    )
    return density, acceleration, kicked


def solution(mesh):
    rows = P(("region", "cell"), None)
    planes = P(None, ("region", "cell"), None)
    return jax.shard_map(
        shards,
        mesh=mesh,
        in_specs=(
            planes, planes, rows, rows, rows, rows, P(("region", "cell")), rows, rows, rows, rows,
            rows,
        ),
        out_specs=(rows, planes, planes),
        check_vma=False,
    )
```

```python
import functools
import math

import jax
import jax.numpy as jnp
from jax import lax
from jax.experimental import pallas as pl
from jax.experimental.pallas import tpu as pltpu
from jax.sharding import PartitionSpec as P

ADIABATIC = 5.0 / 3.0
STEP_MAX = 0.2
LANES = 128
ROWS = 8
FORCE_UNROLL = 7
PAIR_ROWS = 32
FAR_AWAY = 1e9
SPARE = FORCE_UNROLL

X, Y, Z, MASS, VX, VY, VZ, WIDE = range(ROWS)
SPREAD = (X, Y, Z, WIDE)
HEAT, DENS, LIVE = range(3)
SENT = 4
SPEED = 40.0
ACTIVE, STEP = SENT, SENT + 1
S_HEAT, S_RANK, S_REACH, S_CHOSEN = range(ROWS, ROWS + 4)
S_LOW, S_HIGH, S_ROWS = 2 * ROWS, 3 * ROWS, 4 * ROWS
F_RANK, F_ACTIVE, F_STEP, F_VX, F_VY, F_VZ, F_DENS = range(7)
DENS4, PRESS, INV6, HALF, SOUND = range(5)


def lane_gather(values, index):
    return jnp.take_along_axis(values, index, axis=1, mode="promise_in_bounds")


def lanes_of(shape):
    return lax.broadcasted_iota(jnp.int32, shape, len(shape) - 1)


def start_copies(arrays, landed, sem):
    copies = [
        pltpu.make_async_copy(array, place, sem.at[index])
        for index, (array, place) in enumerate(zip(arrays, landed))
    ]
    for copy in copies:
        copy.start()
    return copies


def pack_kernel(*refs):
    arrays, (own, outgoing, border) = refs[:10], refs[10:13]
    landed, sem = refs[13:-1], refs[-1]
    for copy in start_copies(arrays, landed, sem):
        copy.wait()
    count, export, position, velocity, smoothing, mass, energy, density_old, active, time_bin = landed
    cells = smoothing.shape[0]
    shape = smoothing.shape
    lane = lanes_of(shape)
    row = lax.broadcasted_iota(jnp.int32, shape, 0)
    counts = jnp.zeros(shape, jnp.int32)
    for cell in range(cells):
        counts = jnp.where(row == cell, count[cell], counts)
    mass_live = jnp.where(lane < counts, mass[...], 0.0)
    zeros = jnp.zeros(shape, jnp.float32)
    rows = (
        position[0], position[1], position[2], mass_live,
        SPEED * velocity[0], SPEED * velocity[1], SPEED * velocity[2], 2.0 * smoothing[...],
        (ADIABATIC - 1.0) * energy[...], density_old[...], counts.astype(jnp.float32), zeros,
        jnp.where(active[...] > 0, 1.0, 0.0),
        STEP_MAX * jnp.exp2(-time_bin[...].astype(jnp.float32)), zeros, zeros,
    )
    for field, values in enumerate(rows):
        own[:, field, :] = values
    per_peer, peers = export.shape
    for peer in range(peers):
        for entry in range(per_peer):
            cell = export[entry, peer]
            outgoing[peer, entry * ROWS : (entry + 1) * ROWS, :] = own[cell, 0:ROWS, :]
            start = per_peer * ROWS + entry * SENT
            outgoing[peer, start : start + SENT, :] = own[cell, ROWS : ROWS + SENT, :]
    for side, cell in enumerate((cells - 1, 0)):
        border[side] = own[cell, 0 : ROWS + SENT, :]


def own_rows(own, field):
    return own[:, ROWS + field, :]


def sort_kernel(own, actives, bundle, spreads, columns):
    cells = own.shape[0]
    shape = (cells, LANES)
    lane = lanes_of(shape)
    ones = own_rows(own, ACTIVE)
    is_active = ones > 0.5
    for cell in range(cells):
        actives[0, cell] = jnp.sum(ones[cell : cell + 1, :]).astype(jnp.int32)
    square = (LANES, LANES)
    upper = lax.broadcasted_iota(jnp.int32, square, 0) <= lanes_of(square)
    upper = jnp.where(upper, 1.0, 0.0).astype(jnp.bfloat16)
    seen = jnp.dot(ones.astype(jnp.bfloat16), upper, preferred_element_type=jnp.float32)
    seen = seen.astype(jnp.int32)
    chosen = lane_gather(seen, jnp.full(shape, LANES - 1, jnp.int32))
    others = lane + 1 - seen
    rank = jnp.where(is_active, seen - 1, chosen + others - 1)
    first_part = lane < chosen
    wanted = jnp.where(first_part, lane, lane - chosen)
    slot = jnp.zeros(shape, jnp.int32)
    step = LANES // 2
    while step:
        probe = slot + (step - 1)
        found = jnp.where(first_part, lane_gather(seen, probe), lane_gather(others, probe))
        slot = jnp.where(found <= wanted, slot + step, slot)
        step //= 2
    bundle[:, S_HEAT, :] = lane_gather(own_rows(own, HEAT), slot)
    bundle[:, S_RANK, :] = rank.astype(jnp.float32)
    bundle[:, S_CHOSEN, :] = chosen.astype(jnp.float32)
    for spare in range(S_CHOSEN + 1, S_LOW):
        bundle[:, spare, :] = jnp.zeros(shape, jnp.float32)
    place = lax.broadcasted_iota(jnp.int32, (ROWS, LANES), 0) <= Z
    for cell in range(cells):
        order = jnp.broadcast_to(slot[cell : cell + 1, :], (ROWS, LANES))
        tile = lane_gather(own[cell, 0:ROWS, :], order)
        bundle[cell, 0:ROWS, :] = tile
        target = lane < chosen[cell : cell + 1, :]
        low = jnp.min(jnp.where(target, tile, FAR_AWAY), axis=1, keepdims=True)
        high = jnp.max(jnp.where(target, tile, -FAR_AWAY), axis=1, keepdims=True)
        bundle[cell, S_LOW : S_LOW + ROWS, :] = jnp.where(place, low, -FAR_AWAY)
        bundle[cell, S_HIGH : S_HIGH + ROWS, :] = jnp.where(place, high, FAR_AWAY)
        bundle[cell, S_REACH : S_REACH + 1, :] = jnp.broadcast_to(high[WIDE : WIDE + 1, :], (1, LANES))
        columns[cell, :, 0:ROWS] = tile.T

    def one_cell(cell, carry):
        def one_pair(pair, carry):
            base = pl.multiple_of(pair * 2 * ROWS, 2 * ROWS)
            mine = columns[cell, pl.ds(base, 2 * ROWS), :]
            for which, field in enumerate(SPREAD):
                tiles = spread(mine, field).reshape(2, ROWS, LANES)
                spreads[cell, pl.ds(pair * 2, 2), which * ROWS : (which + 1) * ROWS, :] = tiles
            return carry

        return lax.fori_loop(0, (actives[0, cell] + 2 * ROWS - 1) // (2 * ROWS), one_pair, carry)

    lax.fori_loop(0, cells, one_cell, 0)


def source_tiles(own, incoming, border, per_peer):
    cells, peers = own.shape[0], incoming.shape[0]
    for cell in range(cells):
        yield (
            cell, lambda c=cell: own[c, 0:ROWS, :], lambda c=cell: own[c, ROWS : ROWS + SENT, :]
        )
    for peer in range(peers):
        for entry in range(per_peer):
            near, sent = entry * ROWS, per_peer * ROWS + entry * SENT
            yield (
                cells + peer * per_peer + entry,
                lambda p=peer, n=near: incoming[p, n : n + ROWS, :],
                lambda p=peer, n=sent: incoming[p, n : n + SENT, :],
            )
    for side in range(2):
        yield (
            cells + peers * per_peer + side,
            lambda b=side: border[b, 0:ROWS, :],
            lambda b=side: border[b, ROWS : ROWS + SENT, :],
        )


def fill_shifts(shifts):
    row = lax.broadcasted_iota(jnp.int32, (ROWS, LANES), 0)
    for code in range(shifts.shape[0]):
        first, second, third = code // 9 - 1.0, code // 3 % 3 - 1.0, code % 3 - 1.0
        shifts[code] = jnp.where(
            row == X, first, jnp.where(row == Y, second, jnp.where(row == Z, third, 0.0))
        )


def start_of(starts, cell, pair):
    per_line = LANES // PAIR_ROWS
    return starts[cell // per_line, (cell % per_line) * PAIR_ROWS + pair]


def fill_stream(stream, load, sources, starts, orders, cell):
    shape = (ROWS, LANES)
    lane = lanes_of(shape)
    pairs = sources.shape[1]
    moved = []
    for pair in range(pairs):
        order = jnp.broadcast_to(orders[pl.ds(cell * PAIR_ROWS + pair, 1), :], shape)
        moved.append(lane_gather(load(sources[cell, pair], pair), order))
    for pair in range(pairs):
        start = start_of(starts, cell, pair)
        block = start >> 7
        stream[block + 1] = moved[pair]
        pltpu.store(stream.at[block], moved[pair], mask=lane >= (start & (LANES - 1)))
    end = start_of(starts, cell, pairs)
    block = end >> 7
    stream[block] = jnp.where(lane < (end & (LANES - 1)), stream[block], 0.0)
    for extra in range(1, SPARE):
        stream[block + extra] = jnp.zeros(shape, jnp.float32)


def spread(values, field):
    return lane_gather(values, jnp.full(values.shape, field, jnp.int32))


def over_targets(active, one_chunk):
    groups = (active + ROWS - 1) // ROWS
    large = jnp.maximum(groups - 2, 0) // 4
    rest = groups - 4 * large
    large = jnp.where(rest == 4, large + 1, large)

    def large_chunk(chunk, carry):
        one_chunk(pl.multiple_of(chunk * 4 * ROWS, ROWS), 4)
        return carry

    lax.fori_loop(0, large, large_chunk, 0)
    for size in (1, 2, 3, 5):

        @pl.when(rest == size)
        def _(size=size):
            one_chunk(pl.multiple_of(large * 4 * ROWS, ROWS), size)


def density_kernel(
    per_peer, pair_source, pair_shift, export, actives,
    own, incoming, border, bundle, spreads,
    density, densities, outgoing, outgoing_border,
    table, shifts, sums, lines,
):
    fill_shifts(shifts)
    cells, peers = own.shape[0], incoming.shape[0]
    for place, near, _ in source_tiles(own, incoming, border, per_peer):
        table[place] = near()

    def one_cell(cell, carry):
        def one_chunk(base, groups):
            size = groups * ROWS
            at = pl.ds(base // ROWS, groups)
            *place, wide = [
                spreads[cell, at, which * ROWS : (which + 1) * ROWS, :].reshape(size, LANES)
                for which in range(len(SPREAD))
            ]
            smooth = 0.5 * wide

            total = jnp.zeros((size, LANES), jnp.float32)
            for pair in range(pair_source.shape[1]):
                source, code = pair_source[cell, pair], pair_shift[cell, pair]
                s = lambda field: table[source, field : field + 1, :]
                shift = lambda field: shifts[code, field : field + 1, :]
                apart = [place[c] - (s(c) + shift(c)) for c in range(3)]
                square = apart[0] * apart[0] + apart[1] * apart[1] + apart[2] * apart[2]
                radius = pl.reciprocal(lax.rsqrt(square), approx=True)
                outer = jnp.maximum(wide - radius, 0.0)
                inner = jnp.maximum(smooth - radius, 0.0)
                value = outer * outer * outer - 4.0 * (inner * inner * inner)
                total = total + s(MASS) * value
            sums[cell, pl.ds(base, size), 0:1] = jnp.sum(total, axis=1, keepdims=True)

        over_targets(actives[0, cell], one_chunk)
        return carry

    lax.fori_loop(0, cells, one_cell, 0)
    for cell in range(cells):
        lines[cell : cell + 1, :] = sums[cell].T[0:1, :]
    inverse = 2.0 / bundle[:, WIDE, :]
    inverse = inverse * inverse * inverse
    summed = lines[...] * (0.25 / math.pi) * (inverse * inverse)
    rank = bundle[:, S_RANK, :].astype(jnp.int32)
    density[...] = jnp.where(
        own_rows(own, ACTIVE) > 0.5, lane_gather(summed, rank), own_rows(own, DENS)
    )
    densities[0] = summed
    densities[1] = density[...]
    for peer in range(peers):
        for entry in range(per_peer):
            outgoing[peer, entry : entry + 1, :] = density[pl.ds(export[entry, peer], 1), :]
    outgoing_border[0:1, :] = density[cells - 1 : cells, :]
    outgoing_border[1:2, :] = density[0:1, :]


def stream_kernel(
    per_peer, pair_source, pair_shift, own, incoming, border, bundle, densities,
    near_streams, starts, orders, columns, last, traits,
    near_table, supports, shifts, squares, reaches, starts_row, sem,
):
    fill_shifts(shifts)
    cells, pairs = pair_source.shape
    tile_shape = (ROWS, LANES)
    row = lax.broadcasted_iota(jnp.int32, tile_shape, 0)
    lane = lanes_of(tile_shape).astype(jnp.float32)
    for place, near, sent in source_tiles(own, incoming, border, per_peer):
        tile, other = near(), sent()
        near_table[place] = tile
        wide, at = tile[WIDE : WIDE + 1, :], slice(place, place + 1)
        traits[0, at, :] = other[HEAT : HEAT + 1, :]
        traits[1, at, :] = wide
        supports[at, :] = jnp.where(lane[0:1, :] < other[LIVE : LIVE + 1, :], wide, -FAR_AWAY)

    def measure(cell, carry):
        low = bundle[cell, S_LOW : S_LOW + ROWS, :]
        high = bundle[cell, S_HIGH : S_HIGH + ROWS, :]
        for pair in range(pairs):
            source = pair_source[cell, pair]
            tile = near_table[source] + shifts[pair_shift[cell, pair]]
            away = jnp.maximum(jnp.maximum(low - tile, tile - high), 0.0)
            squares[cell, pair * ROWS : (pair + 1) * ROWS, :] = away * away
            place = pl.ds(cell * PAIR_ROWS + pair, 1)
            reaches[place, :] = supports[pl.ds(source, 1), :]
        return carry

    lax.fori_loop(0, cells, measure, 0, unroll=4)
    shape = (PAIR_ROWS, pairs * ROWS)
    adder = lax.broadcasted_iota(jnp.int32, shape, 0) == (lanes_of(shape) // ROWS)
    adder = jnp.where(adder, 1.0, 0.0).astype(jnp.bfloat16)
    pair_row = lax.broadcasted_iota(jnp.int32, (PAIR_ROWS, LANES), 0)
    flags = []
    for cell in range(cells):
        distance = jnp.dot(
            adder, squares[cell].astype(jnp.bfloat16), preferred_element_type=jnp.float32
        )
        support = reaches[cell * PAIR_ROWS : (cell + 1) * PAIR_ROWS, :]
        limit = jnp.maximum(support, bundle[cell, S_REACH : S_REACH + 1, :])
        keep = (distance < 1.005 * limit * limit) & (support > 0.0) & (pair_row < pairs)
        target = lane[0:1, :] < bundle[cell, S_CHOSEN : S_CHOSEN + 1, :]
        keep = keep | ((pair_row == pairs) & target)
        flags.append(jnp.where(keep, 1.0, 0.0))
    flags = jnp.concatenate(flags, axis=0).astype(jnp.bfloat16)
    rows = flags.shape[0]
    shape = (rows, rows)
    first, second = lax.broadcasted_iota(jnp.int32, shape, 0), lanes_of(shape)
    same = (first // PAIR_ROWS) == (second // PAIR_ROWS)
    earlier = jnp.where(same & (second < first), 1.0, 0.0).astype(jnp.bfloat16)
    later = jnp.where(same & (first < second), 1.0, 0.0).astype(jnp.bfloat16)
    dot = functools.partial(jnp.dot, preferred_element_type=jnp.float32)
    sums = lax.dot_general(
        jnp.ones((ROWS, LANES), jnp.bfloat16), flags, (((1,), (1,)), ((), ())),
        preferred_element_type=jnp.float32,
    )
    sums = dot(sums.astype(jnp.bfloat16), later)
    for line in range(starts_row.shape[0]):
        starts_row[line : line + 1, :] = sums[0:1, line * LANES : (line + 1) * LANES].astype(
            jnp.int32
        )
    copy = pltpu.make_async_copy(starts_row, starts, sem)
    copy.start()
    square = (LANES, LANES)
    upper = lax.broadcasted_iota(jnp.int32, square, 0) <= lanes_of(square)
    upper = jnp.where(upper, 1.0, 0.0).astype(jnp.bfloat16)
    seen = dot(flags, upper)
    begins = dot(earlier, dot(flags, jnp.ones(square, jnp.bfloat16)).astype(jnp.bfloat16))
    wanted = (lanes_of(seen.shape) - begins.astype(jnp.int32)) & (LANES - 1)
    wanted = wanted.astype(jnp.float32)
    slot = jnp.zeros(seen.shape, jnp.int32)
    step = LANES // 2
    while step:
        found = lane_gather(seen, slot + (step - 1))
        slot = jnp.where(found <= wanted, slot + step, slot)
        step //= 2
    orders[...] = slot
    heat, summed = bundle[:, S_HEAT, :], densities[0]
    fields = (jnp.sqrt(ADIABATIC * heat), 4.0 * summed)
    for cell in range(cells):
        tile = jnp.zeros(tile_shape, jnp.float32)
        for which, values in enumerate(fields):
            tile = jnp.where(row == which, values[cell : cell + 1, :], tile)
        columns[cell, :, 0 : 2 * ROWS] = jnp.concatenate([bundle[cell, 0:ROWS, :], tile], axis=0).T
    last[:, F_RANK, :] = bundle[:, S_RANK, :]
    last[:, F_ACTIVE, :] = own_rows(own, ACTIVE)
    last[:, F_STEP, :] = own_rows(own, STEP)
    for from_row, to_row in ((VX, F_VX), (VY, F_VY), (VZ, F_VZ)):
        last[:, to_row, :] = own[:, from_row, :] * (1.0 / SPEED)
    last[:, F_DENS, :] = densities[1]
    last[:, F_DENS + 1, :] = jnp.zeros((cells, LANES), jnp.float32)
    copy.wait()

    def one_cell(cell, carry):
        load = lambda source, pair: near_table[source] + shifts[pair_shift[cell, pair]]
        fill_stream(near_streams.at[cell], load, pair_source, starts, orders, cell)
        return carry

    lax.fori_loop(0, cells, one_cell, 0, unroll=4)


def force_kernel(
    per_peer, pair_source, starts,
    columns, orders, last, traits, new_density, new_border, near_streams, spreads,
    acceleration, kicked,
    table, densities, streams, sums, lines,
):
    cells, peers = last.shape[0], new_density.shape[0]
    pairs = pair_source.shape[1]
    for cell in range(cells):
        densities[cell : cell + 1, :] = last[cell, F_DENS : F_DENS + 1, :]
    for peer in range(peers):
        place = cells + peer * per_peer
        densities[place : place + per_peer, :] = new_density[peer]
    place = cells + peers * per_peer
    densities[place : place + 2, :] = new_border[...]
    heat, wide = traits[0], traits[1]
    inverse = 2.0 * pl.reciprocal(wide, approx=True)
    inverse = inverse * inverse * inverse
    table[:, DENS4, :] = 4.0 * densities[...]
    table[:, PRESS, :] = heat * pl.reciprocal(densities[...], approx=True)
    table[:, INV6, :] = inverse * inverse
    table[:, HALF, :] = 0.025 * wide
    table[:, SOUND, :] = jnp.sqrt(ADIABATIC * heat)

    def one_stream(cell, carry):
        fill_stream(
            streams.at[cell], lambda source, pair: table[source], pair_source, starts, orders, cell
        )
        return carry

    lax.fori_loop(0, cells, one_stream, 0, unroll=8)

    def one_cell(cell, carry):
        near, far = near_streams.at[cell], streams.at[cell]
        end = start_of(starts, cell, pairs)
        used = (end + LANES - 1) >> 7
        rounds = (used + FORCE_UNROLL - 1) // FORCE_UNROLL

        def one_chunk(base, groups):
            size = groups * ROWS
            mine = columns[cell, pl.ds(base, size), :]
            at = pl.ds(base // ROWS, groups)
            *place, wide = [
                spreads[cell, at, which * ROWS : (which + 1) * ROWS, :].reshape(size, LANES)
                for which in range(len(SPREAD))
            ]
            speed = [spread(mine, field) for field in (VX, VY, VZ)]
            sound, dens4 = [spread(mine, ROWS + field) for field in range(2)]
            inv6 = 2.0 * pl.reciprocal(wide, approx=True)
            inv6 = inv6 * inv6 * inv6
            inv6 = inv6 * inv6
            half_ = 0.025 * wide
            press = sound * sound * ((4.0 / ADIABATIC) * pl.reciprocal(dens4, approx=True))

            def blocks(index, totals):
                for sub in range(FORCE_UNROLL):
                    block = index * FORCE_UNROLL + sub
                    s = lambda field: near[block, field : field + 1, :]
                    o = lambda field: far[block, field : field + 1, :]
                    apart = [place[c] - s(c) for c in range(3)]
                    square = apart[0] * apart[0] + apart[1] * apart[1] + apart[2] * apart[2]
                    inverse = lax.rsqrt(jnp.maximum(square, 1e-24))
                    radius = pl.reciprocal(inverse, approx=True)
                    outer = jnp.maximum(wide - radius, 0.0)
                    least = jnp.minimum(outer, radius)
                    slope = inv6 * (least * ((outer + outer) - least))
                    outer = jnp.maximum(s(WIDE) - radius, 0.0)
                    least = jnp.minimum(outer, radius)
                    slope = slope + o(INV6) * (least * ((outer + outer) - least))
                    approach = (
                        (speed[0] - s(VX)) * apart[0]
                        + (speed[1] - s(VY)) * apart[1]
                        + (speed[2] - s(VZ)) * apart[2]
                    )
                    half = half_ + o(HALF)
                    slow = pl.reciprocal(square + half * half, approx=True)
                    mu = half * jnp.minimum(approach, 0.0) * slow
                    light = pl.reciprocal(dens4 + o(DENS4), approx=True)
                    viscous = mu * (mu - (sound + o(SOUND))) * light
                    weight = (press + o(PRESS) + viscous) * (slope * (inverse * s(MASS)))
                    terms = [weight * a for a in apart]
                    totals = terms if totals is None else [t + a for t, a in zip(totals, terms)]
                return tuple(totals)

            totals = lax.fori_loop(1, rounds, blocks, blocks(0, None))
            for c in range(3):
                sums[cell, pl.ds(base, size), c : c + 1] = jnp.sum(
                    totals[c], axis=1, keepdims=True
                )

        over_targets(start_of(starts, cell, pairs + 1) - end, one_chunk)
        return carry

    lax.fori_loop(0, cells, one_cell, 0)
    for cell in range(cells):
        turned = sums[cell].T
        for c in range(3):
            lines[c, cell : cell + 1, :] = turned[c : c + 1, :]
    rank = last[:, F_RANK, :].astype(jnp.int32)
    for c in range(3):
        gathered = lane_gather(lines[c] * (0.375 / math.pi), rank)
        value = jnp.where(last[:, F_ACTIVE, :] > 0.5, gathered, 0.0)
        acceleration[c] = value
        kicked[c] = last[:, F_VX + c, :] + value * last[:, F_STEP, :]


def shards(
    position, velocity, smoothing, particle_mass, energy, density_old, cell_count, active,
    time_bin, pair_source, pair_shift, export,
):
    cells, capacity = smoothing.shape
    peers, per_peer = export.shape
    sources = cells + peers * per_peer + 2
    codes = 27
    f32 = lambda *shape: jax.ShapeDtypeStruct(shape, jnp.float32)
    smem = pl.BlockSpec(memory_space=pltpu.SMEM)
    vmem = pl.BlockSpec(memory_space=pltpu.VMEM)
    hbm = pl.BlockSpec(memory_space=pltpu.HBM)
    whole = pltpu.CompilerParams(vmem_limit_bytes=64 * 2**20)
    params = pltpu.CompilerParams(vmem_limit_bytes=24 * 2**20)
    cost = pl.CostEstimate(flops=10**9, bytes_accessed=1000, transcendentals=0)
    i32 = lambda *shape: jax.ShapeDtypeStruct(shape, jnp.int32)
    sent_rows = per_peer * (ROWS + SENT)
    turned = export.T

    def landing(scalars, *arrays):
        return (
            [pltpu.SMEM(a.shape, a.dtype) for a in arrays[:scalars]]
            + [pltpu.VMEM(a.shape, a.dtype) for a in arrays[scalars:]]
            + [pltpu.SemaphoreType.DMA((len(arrays),))]
        )

    arrays = (
        cell_count, turned, position, velocity, smoothing, particle_mass, energy, density_old,
        active, time_bin,
    )
    own, outgoing, border = pl.pallas_call(
        pack_kernel,
        out_shape=(
            f32(cells, 2 * ROWS, capacity),
            f32(peers, sent_rows, capacity),
            f32(2, ROWS + SENT, capacity),
        ),
        in_specs=[hbm] * 10,
        out_specs=(vmem,) * 3,
        scratch_shapes=landing(2, *arrays),
        compiler_params=whole,
        cost_estimate=cost,
        name="pack",
    )(*arrays)

    def exchange(pieces):
        return lax.all_to_all(pieces, "cell", split_axis=0, concat_axis=0, tiled=True)

    def swap_border(pieces):
        size = lax.axis_size("region")
        up = [(i, (i + 1) % size) for i in range(size)]
        down = [(j, i) for i, j in up]
        if size == 2:
            return lax.ppermute(pieces, "region", up)
        before = lax.ppermute(pieces[0:1], "region", up)
        after = lax.ppermute(pieces[1:2], "region", down)
        return jnp.concatenate([before, after], axis=0)

    incoming = exchange(outgoing)
    other = swap_border(border)
    actives, bundle, spreads = pl.pallas_call(
        sort_kernel,
        out_shape=(
            i32(1, cells),
            f32(cells, S_ROWS, capacity),
            f32(cells, capacity // ROWS, len(SPREAD) * ROWS, capacity),
        ),
        in_specs=[vmem],
        out_specs=(smem, vmem, vmem),
        scratch_shapes=[pltpu.VMEM((cells, capacity, LANES), jnp.float32)],
        compiler_params=params,
        cost_estimate=cost,
        name="sort",
    )(own)

    density, densities, outgoing_density, border_density = pl.pallas_call(
        functools.partial(density_kernel, per_peer),
        out_shape=(
            f32(cells, capacity),
            f32(2, cells, capacity),
            f32(peers, per_peer, capacity),
            f32(2, capacity),
        ),
        in_specs=[smem] * 4 + [vmem] * 5,
        out_specs=(vmem,) * 4,
        scratch_shapes=[
            pltpu.VMEM((sources, ROWS, capacity), jnp.float32),
            pltpu.VMEM((codes, ROWS, capacity), jnp.float32),
            pltpu.VMEM((cells, capacity, ROWS), jnp.float32),
            pltpu.VMEM((cells, capacity), jnp.float32),
        ],
        compiler_params=params,
        cost_estimate=cost,
        name="density",
    )(pair_source, pair_shift, turned, actives, own, incoming, other, bundle, spreads)

    new_density = exchange(outgoing_density)
    new_border = swap_border(border_density)
    pairs = pair_source.shape[1]
    blocks = pairs + SPARE
    pair_rows = cells * PAIR_ROWS
    source_rows = -(-sources // ROWS) * ROWS
    near_streams, starts, orders, columns, last, traits = pl.pallas_call(
        functools.partial(stream_kernel, per_peer),
        out_shape=(
            f32(cells, blocks, ROWS, capacity),
            i32(pair_rows // capacity, capacity),
            i32(pair_rows, capacity),
            f32(cells, capacity, LANES),
            f32(cells, ROWS, capacity),
            f32(2, source_rows, capacity),
        ),
        in_specs=[smem] * 2 + [vmem] * 5,
        out_specs=(vmem, smem, vmem, vmem, vmem, vmem),
        scratch_shapes=[
            pltpu.VMEM((sources, ROWS, capacity), jnp.float32),
            pltpu.VMEM((source_rows, capacity), jnp.float32),
            pltpu.VMEM((codes, ROWS, capacity), jnp.float32),
            pltpu.VMEM((cells, pairs * ROWS, capacity), jnp.float32),
            pltpu.VMEM((pair_rows, capacity), jnp.float32),
            pltpu.VMEM((pair_rows // capacity, capacity), jnp.int32),
            pltpu.SemaphoreType.DMA,
        ],
        compiler_params=params,
        cost_estimate=cost,
        name="streams",
    )(pair_source, pair_shift, own, incoming, other, bundle, densities)

    acceleration, kicked = pl.pallas_call(
        functools.partial(force_kernel, per_peer),
        out_shape=(f32(3, cells, capacity), f32(3, cells, capacity)),
        in_specs=[smem] * 2 + [vmem] * 8,
        out_specs=(vmem,) * 2,
        scratch_shapes=[
            pltpu.VMEM((source_rows, ROWS, capacity), jnp.float32),
            pltpu.VMEM((source_rows, capacity), jnp.float32),
            pltpu.VMEM((cells, blocks, ROWS, capacity), jnp.float32),
            pltpu.VMEM((cells, capacity, ROWS), jnp.float32),
            pltpu.VMEM((3, cells, capacity), jnp.float32),
        ],
        compiler_params=params,
        cost_estimate=cost,
        name="force",
    )(
        pair_source, starts, columns, orders, last, traits, new_density, new_border, near_streams,
        spreads,
    )
    return density, acceleration, kicked


def solution(mesh):
    rows = P(("region", "cell"), None)
    planes = P(None, ("region", "cell"), None)
    return jax.shard_map(
        shards,
        mesh=mesh,
        in_specs=(
            planes, planes, rows, rows, rows, rows, P(("region", "cell")), rows, rows, rows, rows,
            rows,
        ),
        out_specs=(rows, planes, planes),
        check_vma=False,
    )
```

```python
import functools
import math

import jax
import jax.numpy as jnp
from jax import lax
from jax.experimental import pallas as pl
from jax.experimental.pallas import tpu as pltpu
from jax.sharding import PartitionSpec as P

ADIABATIC = 5.0 / 3.0
STEP_MAX = 0.2
LANES = 128
ROWS = 8
FORCE_UNROLL = 7
PAIR_ROWS = 32
FAR_AWAY = 1e9
SPARE = FORCE_UNROLL

X, Y, Z, MASS, VX, VY, VZ, WIDE = range(ROWS)
SPREAD = (X, Y, Z, WIDE)
HEAT, DENS, LIVE = range(3)
SENT = 4
SPEED = 40.0
ACTIVE, STEP = SENT, SENT + 1
S_HEAT, S_RANK, S_REACH, S_CHOSEN = range(ROWS, ROWS + 4)
S_LOW, S_HIGH, S_ROWS = 2 * ROWS, 3 * ROWS, 4 * ROWS
F_RANK, F_ACTIVE, F_STEP, F_VX, F_VY, F_VZ, F_DENS = range(7)
DENS4, PRESS, INV6, HALF, SOUND = range(5)


def lane_gather(values, index):
    return jnp.take_along_axis(values, index, axis=1, mode="promise_in_bounds")


def lanes_of(shape):
    return lax.broadcasted_iota(jnp.int32, shape, len(shape) - 1)


def start_copies(arrays, landed, sem):
    copies = [
        pltpu.make_async_copy(array, place, sem.at[index])
        for index, (array, place) in enumerate(zip(arrays, landed))
    ]
    for copy in copies:
        copy.start()
    return copies


def pack_kernel(*refs):
    arrays, (own, outgoing, border) = refs[:10], refs[10:13]
    landed, sem = refs[13:-1], refs[-1]
    for copy in start_copies(arrays, landed, sem):
        copy.wait()
    count, export, position, velocity, smoothing, mass, energy, density_old, active, time_bin = landed
    cells = smoothing.shape[0]
    shape = smoothing.shape
    lane = lanes_of(shape)
    row = lax.broadcasted_iota(jnp.int32, shape, 0)
    counts = jnp.zeros(shape, jnp.int32)
    for cell in range(cells):
        counts = jnp.where(row == cell, count[cell], counts)
    mass_live = jnp.where(lane < counts, mass[...], 0.0)
    zeros = jnp.zeros(shape, jnp.float32)
    rows = (
        position[0], position[1], position[2], mass_live,
        SPEED * velocity[0], SPEED * velocity[1], SPEED * velocity[2], 2.0 * smoothing[...],
        (ADIABATIC - 1.0) * energy[...], density_old[...], counts.astype(jnp.float32), zeros,
        jnp.where(active[...] > 0, 1.0, 0.0),
        STEP_MAX * jnp.exp2(-time_bin[...].astype(jnp.float32)), zeros, zeros,
    )
    for field, values in enumerate(rows):
        own[:, field, :] = values
    per_peer, peers = export.shape
    for peer in range(peers):
        for entry in range(per_peer):
            cell = export[entry, peer]
            outgoing[peer, entry * ROWS : (entry + 1) * ROWS, :] = own[cell, 0:ROWS, :]
            start = per_peer * ROWS + entry * SENT
            outgoing[peer, start : start + SENT, :] = own[cell, ROWS : ROWS + SENT, :]
    for side, cell in enumerate((cells - 1, 0)):
        border[side] = own[cell, 0 : ROWS + SENT, :]


def own_rows(own, field):
    return own[:, ROWS + field, :]


def sort_kernel(own, actives, bundle, spreads, columns):
    cells = own.shape[0]
    shape = (cells, LANES)
    lane = lanes_of(shape)
    ones = own_rows(own, ACTIVE)
    is_active = ones > 0.5
    for cell in range(cells):
        actives[0, cell] = jnp.sum(ones[cell : cell + 1, :]).astype(jnp.int32)
    square = (LANES, LANES)
    upper = lax.broadcasted_iota(jnp.int32, square, 0) <= lanes_of(square)
    upper = jnp.where(upper, 1.0, 0.0).astype(jnp.bfloat16)
    seen = jnp.dot(ones.astype(jnp.bfloat16), upper, preferred_element_type=jnp.float32)
    seen = seen.astype(jnp.int32)
    chosen = lane_gather(seen, jnp.full(shape, LANES - 1, jnp.int32))
    others = lane + 1 - seen
    rank = jnp.where(is_active, seen - 1, chosen + others - 1)
    first_part = lane < chosen
    wanted = jnp.where(first_part, lane, lane - chosen)
    slot = jnp.zeros(shape, jnp.int32)
    step = LANES // 2
    while step:
        probe = slot + (step - 1)
        found = jnp.where(first_part, lane_gather(seen, probe), lane_gather(others, probe))
        slot = jnp.where(found <= wanted, slot + step, slot)
        step //= 2
    bundle[:, S_HEAT, :] = lane_gather(own_rows(own, HEAT), slot)
    bundle[:, S_RANK, :] = rank.astype(jnp.float32)
    bundle[:, S_CHOSEN, :] = chosen.astype(jnp.float32)
    for spare in range(S_CHOSEN + 1, S_LOW):
        bundle[:, spare, :] = jnp.zeros(shape, jnp.float32)
    place = lax.broadcasted_iota(jnp.int32, (ROWS, LANES), 0) <= Z
    for cell in range(cells):
        order = jnp.broadcast_to(slot[cell : cell + 1, :], (ROWS, LANES))
        tile = lane_gather(own[cell, 0:ROWS, :], order)
        bundle[cell, 0:ROWS, :] = tile
        target = lane < chosen[cell : cell + 1, :]
        low = jnp.min(jnp.where(target, tile, FAR_AWAY), axis=1, keepdims=True)
        high = jnp.max(jnp.where(target, tile, -FAR_AWAY), axis=1, keepdims=True)
        bundle[cell, S_LOW : S_LOW + ROWS, :] = jnp.where(place, low, -FAR_AWAY)
        bundle[cell, S_HIGH : S_HIGH + ROWS, :] = jnp.where(place, high, FAR_AWAY)
        bundle[cell, S_REACH : S_REACH + 1, :] = jnp.broadcast_to(high[WIDE : WIDE + 1, :], (1, LANES))
        columns[cell, :, 0:ROWS] = tile.T

    def one_cell(cell, carry):
        def one_pair(pair, carry):
            base = pl.multiple_of(pair * 2 * ROWS, 2 * ROWS)
            mine = columns[cell, pl.ds(base, 2 * ROWS), :]
            for which, field in enumerate(SPREAD):
                tiles = spread(mine, field).reshape(2, ROWS, LANES)
                spreads[cell, pl.ds(pair * 2, 2), which * ROWS : (which + 1) * ROWS, :] = tiles
            return carry

        return lax.fori_loop(0, (actives[0, cell] + 2 * ROWS - 1) // (2 * ROWS), one_pair, carry)

    lax.fori_loop(0, cells, one_cell, 0)


def source_tiles(own, incoming, border, per_peer):
    cells, peers = own.shape[0], incoming.shape[0]
    for cell in range(cells):
        yield (
            cell, lambda c=cell: own[c, 0:ROWS, :], lambda c=cell: own[c, ROWS : ROWS + SENT, :]
        )
    for peer in range(peers):
        for entry in range(per_peer):
            near, sent = entry * ROWS, per_peer * ROWS + entry * SENT
            yield (
                cells + peer * per_peer + entry,
                lambda p=peer, n=near: incoming[p, n : n + ROWS, :],
                lambda p=peer, n=sent: incoming[p, n : n + SENT, :],
            )
    for side in range(2):
        yield (
            cells + peers * per_peer + side,
            lambda b=side: border[b, 0:ROWS, :],
            lambda b=side: border[b, ROWS : ROWS + SENT, :],
        )


def fill_shifts(shifts):
    row = lax.broadcasted_iota(jnp.int32, (ROWS, LANES), 0)
    for code in range(shifts.shape[0]):
        first, second, third = code // 9 - 1.0, code // 3 % 3 - 1.0, code % 3 - 1.0
        shifts[code] = jnp.where(
            row == X, first, jnp.where(row == Y, second, jnp.where(row == Z, third, 0.0))
        )


def start_of(starts, cell, pair):
    per_line = LANES // PAIR_ROWS
    return starts[cell // per_line, (cell % per_line) * PAIR_ROWS + pair]


def fill_stream(stream, load, sources, starts, orders, cell):
    shape = (ROWS, LANES)
    lane = lanes_of(shape)
    pairs = sources.shape[1]
    moved = []
    for pair in range(pairs):
        order = jnp.broadcast_to(orders[pl.ds(cell * PAIR_ROWS + pair, 1), :], shape)
        moved.append(lane_gather(load(sources[cell, pair], pair), order))
    for pair in range(pairs):
        start = start_of(starts, cell, pair)
        block = start >> 7
        stream[block + 1] = moved[pair]
        pltpu.store(stream.at[block], moved[pair], mask=lane >= (start & (LANES - 1)))
    end = start_of(starts, cell, pairs)
    block = end >> 7
    stream[block] = jnp.where(lane < (end & (LANES - 1)), stream[block], 0.0)
    for extra in range(1, SPARE):
        stream[block + extra] = jnp.zeros(shape, jnp.float32)


def spread(values, field):
    return lane_gather(values, jnp.full(values.shape, field, jnp.int32))


def over_targets(active, one_chunk):
    groups = (active + ROWS - 1) // ROWS
    large = jnp.maximum(groups - 2, 0) // 4
    rest = groups - 4 * large
    large = jnp.where(rest == 4, large + 1, large)

    def large_chunk(chunk, carry):
        one_chunk(pl.multiple_of(chunk * 4 * ROWS, ROWS), 4)
        return carry

    lax.fori_loop(0, large, large_chunk, 0)
    for size in (1, 2, 3, 5):

        @pl.when(rest == size)
        def _(size=size):
            one_chunk(pl.multiple_of(large * 4 * ROWS, ROWS), size)


def density_kernel(
    per_peer, pair_source, pair_shift, export, actives,
    own, incoming, border, bundle, spreads,
    density, densities, outgoing, outgoing_border,
    table, shifts, sums, lines,
):
    fill_shifts(shifts)
    cells, peers = own.shape[0], incoming.shape[0]
    for place, near, _ in source_tiles(own, incoming, border, per_peer):
        table[place] = near()

    def one_cell(cell, carry):
        def one_chunk(base, groups):
            size = groups * ROWS
            at = pl.ds(base // ROWS, groups)
            *place, wide = [
                spreads[cell, at, which * ROWS : (which + 1) * ROWS, :].reshape(size, LANES)
                for which in range(len(SPREAD))
            ]
            smooth = 0.5 * wide

            total = jnp.zeros((size, LANES), jnp.float32)
            for pair in range(pair_source.shape[1]):
                source, code = pair_source[cell, pair], pair_shift[cell, pair]
                s = lambda field: table[source, field : field + 1, :]
                shift = lambda field: shifts[code, field : field + 1, :]
                apart = [place[c] - (s(c) + shift(c)) for c in range(3)]
                square = apart[0] * apart[0] + apart[1] * apart[1] + apart[2] * apart[2]
                radius = pl.reciprocal(lax.rsqrt(square), approx=True)
                outer = jnp.maximum(wide - radius, 0.0)
                inner = jnp.maximum(smooth - radius, 0.0)
                value = outer * outer * outer - 4.0 * (inner * inner * inner)
                total = total + s(MASS) * value
            sums[cell, pl.ds(base, size), 0:1] = jnp.sum(total, axis=1, keepdims=True)

        over_targets(actives[0, cell], one_chunk)
        return carry

    lax.fori_loop(0, cells, one_cell, 0)
    for cell in range(cells):
        lines[cell : cell + 1, :] = sums[cell].T[0:1, :]
    inverse = 2.0 / bundle[:, WIDE, :]
    inverse = inverse * inverse * inverse
    summed = lines[...] * (0.25 / math.pi) * (inverse * inverse)
    rank = bundle[:, S_RANK, :].astype(jnp.int32)
    density[...] = jnp.where(
        own_rows(own, ACTIVE) > 0.5, lane_gather(summed, rank), own_rows(own, DENS)
    )
    densities[0] = summed
    densities[1] = density[...]
    for peer in range(peers):
        for entry in range(per_peer):
            outgoing[peer, entry : entry + 1, :] = density[pl.ds(export[entry, peer], 1), :]
    outgoing_border[0:1, :] = density[cells - 1 : cells, :]
    outgoing_border[1:2, :] = density[0:1, :]


def stream_kernel(
    per_peer, pair_source, pair_shift, own, incoming, border, bundle, densities, spreads,
    near_streams, starts, orders, columns, last, traits,
    near_table, supports, shifts, squares, reaches, starts_row, sem,
):
    del spreads
    fill_shifts(shifts)
    cells, pairs = pair_source.shape
    tile_shape = (ROWS, LANES)
    row = lax.broadcasted_iota(jnp.int32, tile_shape, 0)
    lane = lanes_of(tile_shape).astype(jnp.float32)
    for place, near, sent in source_tiles(own, incoming, border, per_peer):
        tile, other = near(), sent()
        near_table[place] = tile
        wide, at = tile[WIDE : WIDE + 1, :], slice(place, place + 1)
        traits[0, at, :] = other[HEAT : HEAT + 1, :]
        traits[1, at, :] = wide
        supports[at, :] = jnp.where(lane[0:1, :] < other[LIVE : LIVE + 1, :], wide, -FAR_AWAY)

    def measure(cell, carry):
        low = bundle[cell, S_LOW : S_LOW + ROWS, :]
        high = bundle[cell, S_HIGH : S_HIGH + ROWS, :]
        for pair in range(pairs):
            source = pair_source[cell, pair]
            tile = near_table[source] + shifts[pair_shift[cell, pair]]
            away = jnp.maximum(jnp.maximum(low - tile, tile - high), 0.0)
            squares[cell, pair * ROWS : (pair + 1) * ROWS, :] = away * away
            place = pl.ds(cell * PAIR_ROWS + pair, 1)
            reaches[place, :] = supports[pl.ds(source, 1), :]
        return carry

    lax.fori_loop(0, cells, measure, 0, unroll=4)
    shape = (PAIR_ROWS, pairs * ROWS)
    adder = lax.broadcasted_iota(jnp.int32, shape, 0) == (lanes_of(shape) // ROWS)
    adder = jnp.where(adder, 1.0, 0.0).astype(jnp.bfloat16)
    pair_row = lax.broadcasted_iota(jnp.int32, (PAIR_ROWS, LANES), 0)
    flags = []
    for cell in range(cells):
        distance = jnp.dot(
            adder, squares[cell].astype(jnp.bfloat16), preferred_element_type=jnp.float32
        )
        support = reaches[cell * PAIR_ROWS : (cell + 1) * PAIR_ROWS, :]
        limit = jnp.maximum(support, bundle[cell, S_REACH : S_REACH + 1, :])
        keep = (distance < 1.005 * limit * limit) & (support > 0.0) & (pair_row < pairs)
        target = lane[0:1, :] < bundle[cell, S_CHOSEN : S_CHOSEN + 1, :]
        keep = keep | ((pair_row == pairs) & target)
        flags.append(jnp.where(keep, 1.0, 0.0))
    flags = jnp.concatenate(flags, axis=0).astype(jnp.bfloat16)
    rows = flags.shape[0]
    shape = (rows, rows)
    first, second = lax.broadcasted_iota(jnp.int32, shape, 0), lanes_of(shape)
    same = (first // PAIR_ROWS) == (second // PAIR_ROWS)
    earlier = jnp.where(same & (second < first), 1.0, 0.0).astype(jnp.bfloat16)
    later = jnp.where(same & (first < second), 1.0, 0.0).astype(jnp.bfloat16)
    dot = functools.partial(jnp.dot, preferred_element_type=jnp.float32)
    sums = lax.dot_general(
        jnp.ones((ROWS, LANES), jnp.bfloat16), flags, (((1,), (1,)), ((), ())),
        preferred_element_type=jnp.float32,
    )
    sums = dot(sums.astype(jnp.bfloat16), later)
    for line in range(starts_row.shape[0]):
        starts_row[line : line + 1, :] = sums[0:1, line * LANES : (line + 1) * LANES].astype(
            jnp.int32
        )
    copy = pltpu.make_async_copy(starts_row, starts, sem)
    copy.start()
    square = (LANES, LANES)
    upper = lax.broadcasted_iota(jnp.int32, square, 0) <= lanes_of(square)
    upper = jnp.where(upper, 1.0, 0.0).astype(jnp.bfloat16)
    seen = dot(flags, upper)
    begins = dot(earlier, dot(flags, jnp.ones(square, jnp.bfloat16)).astype(jnp.bfloat16))
    wanted = (lanes_of(seen.shape) - begins.astype(jnp.int32)) & (LANES - 1)
    wanted = wanted.astype(jnp.float32)
    slot = jnp.zeros(seen.shape, jnp.int32)
    step = LANES // 2
    while step:
        found = lane_gather(seen, slot + (step - 1))
        slot = jnp.where(found <= wanted, slot + step, slot)
        step //= 2
    orders[...] = slot
    heat, summed = bundle[:, S_HEAT, :], densities[0]
    fields = (jnp.sqrt(ADIABATIC * heat), 4.0 * summed)
    for cell in range(cells):
        tile = jnp.zeros(tile_shape, jnp.float32)
        for which, values in enumerate(fields):
            tile = jnp.where(row == which, values[cell : cell + 1, :], tile)
        columns[cell, :, 0 : 2 * ROWS] = jnp.concatenate([bundle[cell, 0:ROWS, :], tile], axis=0).T
    last[:, F_RANK, :] = bundle[:, S_RANK, :]
    last[:, F_ACTIVE, :] = own_rows(own, ACTIVE)
    last[:, F_STEP, :] = own_rows(own, STEP)
    for from_row, to_row in ((VX, F_VX), (VY, F_VY), (VZ, F_VZ)):
        last[:, to_row, :] = own[:, from_row, :] * (1.0 / SPEED)
    last[:, F_DENS, :] = densities[1]
    last[:, F_DENS + 1, :] = jnp.zeros((cells, LANES), jnp.float32)
    copy.wait()

    def one_cell(cell, carry):
        load = lambda source, pair: near_table[source] + shifts[pair_shift[cell, pair]]
        fill_stream(near_streams.at[cell], load, pair_source, starts, orders, cell)
        return carry

    lax.fori_loop(0, cells, one_cell, 0, unroll=4)


def force_kernel(
    per_peer, pair_source, starts,
    columns, orders, last, traits, new_density, new_border, near_streams, spreads,
    acceleration, kicked,
    table, densities, streams, sums, lines,
):
    cells, peers = last.shape[0], new_density.shape[0]
    pairs = pair_source.shape[1]
    for cell in range(cells):
        densities[cell : cell + 1, :] = last[cell, F_DENS : F_DENS + 1, :]
    for peer in range(peers):
        place = cells + peer * per_peer
        densities[place : place + per_peer, :] = new_density[peer]
    place = cells + peers * per_peer
    densities[place : place + 2, :] = new_border[...]
    heat, wide = traits[0], traits[1]
    inverse = 2.0 * pl.reciprocal(wide, approx=True)
    inverse = inverse * inverse * inverse
    table[:, DENS4, :] = 4.0 * densities[...]
    table[:, PRESS, :] = heat * pl.reciprocal(densities[...], approx=True)
    table[:, INV6, :] = inverse * inverse
    table[:, HALF, :] = 0.025 * wide
    table[:, SOUND, :] = jnp.sqrt(ADIABATIC * heat)

    def one_stream(cell, carry):
        fill_stream(
            streams.at[cell], lambda source, pair: table[source], pair_source, starts, orders, cell
        )
        return carry

    lax.fori_loop(0, cells, one_stream, 0, unroll=8)

    def one_cell(cell, carry):
        near, far = near_streams.at[cell], streams.at[cell]
        end = start_of(starts, cell, pairs)
        used = (end + LANES - 1) >> 7
        rounds = (used + FORCE_UNROLL - 1) // FORCE_UNROLL

        def one_chunk(base, groups):
            size = groups * ROWS
            mine = columns[cell, pl.ds(base, size), :]
            at = pl.ds(base // ROWS, groups)
            *place, wide = [
                spreads[cell, at, which * ROWS : (which + 1) * ROWS, :].reshape(size, LANES)
                for which in range(len(SPREAD))
            ]
            speed = [spread(mine, field) for field in (VX, VY, VZ)]
            sound, dens4 = [spread(mine, ROWS + field) for field in range(2)]
            inv6 = 2.0 * pl.reciprocal(wide, approx=True)
            inv6 = inv6 * inv6 * inv6
            inv6 = inv6 * inv6
            half_ = 0.025 * wide
            press = sound * sound * ((4.0 / ADIABATIC) * pl.reciprocal(dens4, approx=True))

            def blocks(index, totals):
                for sub in range(FORCE_UNROLL):
                    block = index * FORCE_UNROLL + sub
                    s = lambda field: near[block, field : field + 1, :]
                    o = lambda field: far[block, field : field + 1, :]
                    apart = [place[c] - s(c) for c in range(3)]
                    square = apart[0] * apart[0] + apart[1] * apart[1] + apart[2] * apart[2]
                    inverse = lax.rsqrt(jnp.maximum(square, 1e-24))
                    radius = pl.reciprocal(inverse, approx=True)
                    outer = jnp.maximum(wide - radius, 0.0)
                    least = jnp.minimum(outer, radius)
                    slope = inv6 * (least * ((outer + outer) - least))
                    outer = jnp.maximum(s(WIDE) - radius, 0.0)
                    least = jnp.minimum(outer, radius)
                    slope = slope + o(INV6) * (least * ((outer + outer) - least))
                    approach = (
                        (speed[0] - s(VX)) * apart[0]
                        + (speed[1] - s(VY)) * apart[1]
                        + (speed[2] - s(VZ)) * apart[2]
                    )
                    half = half_ + o(HALF)
                    slow = pl.reciprocal(square + half * half, approx=True)
                    mu = half * jnp.minimum(approach, 0.0) * slow
                    light = pl.reciprocal(dens4 + o(DENS4), approx=True)
                    viscous = mu * (mu - (sound + o(SOUND))) * light
                    weight = (press + o(PRESS) + viscous) * (slope * (inverse * s(MASS)))
                    terms = [weight * a for a in apart]
                    totals = terms if totals is None else [t + a for t, a in zip(totals, terms)]
                return tuple(totals)

            totals = lax.fori_loop(1, rounds, blocks, blocks(0, None))
            for c in range(3):
                sums[cell, pl.ds(base, size), c : c + 1] = jnp.sum(
                    totals[c], axis=1, keepdims=True
                )

        over_targets(start_of(starts, cell, pairs + 1) - end, one_chunk)
        return carry

    lax.fori_loop(0, cells, one_cell, 0)
    for cell in range(cells):
        turned = sums[cell].T
        for c in range(3):
            lines[c, cell : cell + 1, :] = turned[c : c + 1, :]
    rank = last[:, F_RANK, :].astype(jnp.int32)
    for c in range(3):
        gathered = lane_gather(lines[c] * (0.375 / math.pi), rank)
        value = jnp.where(last[:, F_ACTIVE, :] > 0.5, gathered, 0.0)
        acceleration[c] = value
        kicked[c] = last[:, F_VX + c, :] + value * last[:, F_STEP, :]


def shards(
    position, velocity, smoothing, particle_mass, energy, density_old, cell_count, active,
    time_bin, pair_source, pair_shift, export,
):
    cells, capacity = smoothing.shape
    peers, per_peer = export.shape
    sources = cells + peers * per_peer + 2
    codes = 27
    f32 = lambda *shape: jax.ShapeDtypeStruct(shape, jnp.float32)
    smem = pl.BlockSpec(memory_space=pltpu.SMEM)
    vmem = pl.BlockSpec(memory_space=pltpu.VMEM)
    hbm = pl.BlockSpec(memory_space=pltpu.HBM)
    whole = pltpu.CompilerParams(vmem_limit_bytes=64 * 2**20)
    params = pltpu.CompilerParams(vmem_limit_bytes=24 * 2**20)
    cost = pl.CostEstimate(flops=10**9, bytes_accessed=1000, transcendentals=0)
    i32 = lambda *shape: jax.ShapeDtypeStruct(shape, jnp.int32)
    sent_rows = per_peer * (ROWS + SENT)
    turned = export.T

    def landing(scalars, *arrays):
        return (
            [pltpu.SMEM(a.shape, a.dtype) for a in arrays[:scalars]]
            + [pltpu.VMEM(a.shape, a.dtype) for a in arrays[scalars:]]
            + [pltpu.SemaphoreType.DMA((len(arrays),))]
        )

    arrays = (
        cell_count, turned, position, velocity, smoothing, particle_mass, energy, density_old,
        active, time_bin,
    )
    own, outgoing, border = pl.pallas_call(
        pack_kernel,
        out_shape=(
            f32(cells, 2 * ROWS, capacity),
            f32(peers, sent_rows, capacity),
            f32(2, ROWS + SENT, capacity),
        ),
        in_specs=[hbm] * 10,
        out_specs=(vmem,) * 3,
        scratch_shapes=landing(2, *arrays),
        compiler_params=whole,
        cost_estimate=cost,
        name="pack",
    )(*arrays)

    def exchange(pieces):
        return lax.all_to_all(pieces, "cell", split_axis=0, concat_axis=0, tiled=True)

    def swap_border(pieces):
        size = lax.axis_size("region")
        up = [(i, (i + 1) % size) for i in range(size)]
        down = [(j, i) for i, j in up]
        if size == 2:
            return lax.ppermute(pieces, "region", up)
        before = lax.ppermute(pieces[0:1], "region", up)
        after = lax.ppermute(pieces[1:2], "region", down)
        return jnp.concatenate([before, after], axis=0)

    incoming = exchange(outgoing)
    other = swap_border(border)
    actives, bundle, spreads = pl.pallas_call(
        sort_kernel,
        out_shape=(
            i32(1, cells),
            f32(cells, S_ROWS, capacity),
            f32(cells, capacity // ROWS, len(SPREAD) * ROWS, capacity),
        ),
        in_specs=[vmem],
        out_specs=(smem, vmem, vmem),
        scratch_shapes=[pltpu.VMEM((cells, capacity, LANES), jnp.float32)],
        compiler_params=params,
        cost_estimate=cost,
        name="sort",
    )(own)

    density, densities, outgoing_density, border_density = pl.pallas_call(
        functools.partial(density_kernel, per_peer),
        out_shape=(
            f32(cells, capacity),
            f32(2, cells, capacity),
            f32(peers, per_peer, capacity),
            f32(2, capacity),
        ),
        in_specs=[smem] * 4 + [vmem] * 5,
        out_specs=(vmem,) * 4,
        scratch_shapes=[
            pltpu.VMEM((sources, ROWS, capacity), jnp.float32),
            pltpu.VMEM((codes, ROWS, capacity), jnp.float32),
            pltpu.VMEM((cells, capacity, ROWS), jnp.float32),
            pltpu.VMEM((cells, capacity), jnp.float32),
        ],
        compiler_params=params,
        cost_estimate=cost,
        name="density",
    )(pair_source, pair_shift, turned, actives, own, incoming, other, bundle, spreads)

    new_density = exchange(outgoing_density)
    new_border = swap_border(border_density)
    pairs = pair_source.shape[1]
    blocks = pairs + SPARE
    pair_rows = cells * PAIR_ROWS
    source_rows = -(-sources // ROWS) * ROWS
    near_streams, starts, orders, columns, last, traits = pl.pallas_call(
        functools.partial(stream_kernel, per_peer),
        out_shape=(
            f32(cells, blocks, ROWS, capacity),
            i32(pair_rows // capacity, capacity),
            i32(pair_rows, capacity),
            f32(cells, capacity, LANES),
            f32(cells, ROWS, capacity),
            f32(2, source_rows, capacity),
        ),
        in_specs=[smem] * 2 + [vmem] * 6,
        out_specs=(vmem, smem, vmem, vmem, vmem, vmem),
        scratch_shapes=[
            pltpu.VMEM((sources, ROWS, capacity), jnp.float32),
            pltpu.VMEM((source_rows, capacity), jnp.float32),
            pltpu.VMEM((codes, ROWS, capacity), jnp.float32),
            pltpu.VMEM((cells, pairs * ROWS, capacity), jnp.float32),
            pltpu.VMEM((pair_rows, capacity), jnp.float32),
            pltpu.VMEM((pair_rows // capacity, capacity), jnp.int32),
            pltpu.SemaphoreType.DMA,
        ],
        compiler_params=params,
        cost_estimate=cost,
        name="streams",
    )(pair_source, pair_shift, own, incoming, other, bundle, densities, spreads)

    acceleration, kicked = pl.pallas_call(
        functools.partial(force_kernel, per_peer),
        out_shape=(f32(3, cells, capacity), f32(3, cells, capacity)),
        in_specs=[smem] * 2 + [vmem] * 8,
        out_specs=(vmem,) * 2,
        scratch_shapes=[
            pltpu.VMEM((source_rows, ROWS, capacity), jnp.float32),
            pltpu.VMEM((source_rows, capacity), jnp.float32),
            pltpu.VMEM((cells, blocks, ROWS, capacity), jnp.float32),
            pltpu.VMEM((cells, capacity, ROWS), jnp.float32),
            pltpu.VMEM((3, cells, capacity), jnp.float32),
        ],
        compiler_params=params,
        cost_estimate=cost,
        name="force",
    )(
        pair_source, starts, columns, orders, last, traits, new_density, new_border, near_streams,
        spreads,
    )
    return density, acceleration, kicked


def solution(mesh):
    rows = P(("region", "cell"), None)
    planes = P(None, ("region", "cell"), None)
    return jax.shard_map(
        shards,
        mesh=mesh,
        in_specs=(
            planes, planes, rows, rows, rows, rows, P(("region", "cell")), rows, rows, rows, rows,
            rows,
        ),
        out_specs=(rows, planes, planes),
        check_vma=False,
    )
```
